32 devices in a mesh: dp: 8 (over y, x, core), fsdp: 4 (over z).
Axes of the slice: x: 2, y: 2, z: 4, core: 2. Of those that a mesh axis runs over, the one named last changes fastest.
Arguments:
- tokens: bfloat16 [8, 2048, 1024], P('dp', 'fsdp'), may hold values from -6 to 6
- memory_keys: bfloat16 [8, 1024, 1024], P('dp', 'fsdp'), may hold values from -6 to 6
- memory_values: bfloat16 [8, 1024, 1024], P('dp', 'fsdp'), may hold values from -6 to 6
- chosen: int32 [8, 8, 4], P('dp', 'fsdp'), may hold values from 0 to 7, all different within a row
- counts: int32 [8, 8, 4], P('dp', 'fsdp'), may hold values from 1 to 128
- w_query: bfloat16 [1024, 1024], P(('dp', 'fsdp')), may hold values from -0.1875 to 0.1875
- w_key: bfloat16 [1024, 1024], P(('dp', 'fsdp')), may hold values from -0.1875 to 0.1875
- w_value: bfloat16 [1024, 1024], P(('dp', 'fsdp')), may hold values from -0.1875 to 0.1875
- w_out: bfloat16 [1024, 1024], P(('dp', 'fsdp')), may hold values from -1.5 to 1.5
- w_gate: bfloat16 [1024, 2816], P(('dp', 'fsdp')), may hold values from -0.1875 to 0.1875
- w_up: bfloat16 [1024, 2816], P(('dp', 'fsdp')), may hold values from -0.1875 to 0.1875
- w_down: bfloat16 [2816, 1024], P(('dp', 'fsdp')), may hold values from -0.109375 to 0.109375
- gain_attn: bfloat16 [1024], P(('dp', 'fsdp')), may hold values from 0.5 to 1.5
- gain_ffn: bfloat16 [1024], P(('dp', 'fsdp')), may hold values from 0.5 to 1.5
- cotangent: bfloat16 [8, 2048, 1024], P('dp', 'fsdp'), may hold values from -6 to 6
Outputs:
- mixed: bfloat16 [8, 2048, 1024], P('dp', 'fsdp')
- tokens_grad: bfloat16 [8, 2048, 1024], P('dp', 'fsdp')
- grad_w_query: float32 [1024, 1024], P(('dp', 'fsdp'))
- grad_w_key: float32 [1024, 1024], P(('dp', 'fsdp'))
- grad_w_value: float32 [1024, 1024], P(('dp', 'fsdp'))
- grad_w_out: float32 [1024, 1024], P(('dp', 'fsdp'))
- grad_w_gate: float32 [1024, 2816], P(('dp', 'fsdp'))
- grad_w_up: float32 [1024, 2816], P(('dp', 'fsdp'))
- grad_w_down: float32 [2816, 1024], P(('dp', 'fsdp'))
- grad_gain_attn: float32 [1024], P(('dp', 'fsdp'))
- grad_gain_ffn: float32 [1024], P(('dp', 'fsdp'))
The draws below stay inside these ranges and needn't reach their ends.
Inputs may be any that keep to these rules, and one draw needn't show every extreme that they name: `chosen`: each query block names 4 different memory blocks of its own sequence, and for every block index, some query block of some sequence names it (not necessarily of every sequence).
All inputs are finite; a program needn't handle non-finite values.
Results may differ from the reference program's by a relative error of at most 0.017.
Values may be sent and summed in bfloat16 or wider, within the bound.
No kernel may reach another device: no remote copies, remote signals or barrier semaphores. Data moves between devices by JAX's collectives and lax.ppermute only.
A program may use at most 256 MiB of HBM per device.

```python
import math
import jax
import jax.numpy as jnp
from jax import lax

D = 1024
HEADS = 8
HEAD_DIM = 128
FF = 2816
LEN = 2048
QBLK = 256
MBLK = 128
TOPB = 4
SEQS = 8
MEM = 1024
NQB = 8
NMB = 8


def with_ends(result, own_key, low, high):
    spot = [jax.random.randint(jax.random.fold_in(own_key, axis), (), 0, length) for axis, length in enumerate(result.shape)]
    main_axis = result.shape.index(max(result.shape))
    neighbour = spot[:main_axis] + [(spot[main_axis] + 1) % result.shape[main_axis]] + spot[main_axis + 1:]
    return result.at[tuple(spot)].set(low).at[tuple(neighbour)].set(high)


def level_of(rng, extent, split, smallest, high):
    loudness = 1.0
    for dim, blocks in split:
        steps = jax.random.uniform(jax.random.fold_in(jax.random.fold_in(rng, 6), dim), (blocks,), jnp.float32, smallest / len(split), high / len(split))
        loudness = loudness * jnp.repeat(jnp.exp(steps), extent[dim] // blocks).reshape((-1,) + (1,) * (len(extent) - 1 - dim))
    return loudness


def picks_of(stream_key, rows, number_of, top, lift):
    sequence = jax.random.permutation(jax.random.fold_in(stream_key, 1), number_of)
    favour = sequence
    for power in range(3):
        favour = favour * favour // number_of
    favour = favour * lift // number_of
    tickets = jax.random.randint(jax.random.fold_in(stream_key, 2), (rows, number_of), 0, 4096) + favour
    holders = jax.random.permutation(jax.random.fold_in(stream_key, 3), rows)[jnp.arange(number_of) % rows]
    tickets = jnp.where(jnp.arange(rows)[:, None] == holders[None, :], 1 << 14, tickets)
    score = tickets * number_of + jnp.arange(number_of)
    return lax.top_k(score.astype(jnp.int32), top)[1].astype(jnp.int32)


def scatter_about(own_key, shape, deviation, reach, cuts=(), kind=jnp.bfloat16):
    values = deviation * jax.random.normal(own_key, shape, jnp.float32)
    if cuts:
        values = values * level_of(own_key, shape, cuts, -0.22, 0.18)
    return jnp.clip(values, -reach, reach).astype(kind)


def setup_inputs(seed: int = 0) -> dict:
    key_list = jax.random.split(jax.random.key(seed), 16)
    return {
        "tokens": scatter_about(key_list[0], (SEQS, LEN, D), 1.0, 6.0, ((0, 8), (1, 4))),
        "memory_keys": scatter_about(key_list[1], (SEQS, MEM, D), 1.0, 6.0, ((0, 8), (1, 4))),
        "memory_values": scatter_about(key_list[2], (SEQS, MEM, D), 1.0, 6.0, ((0, 8), (1, 4))),
        "chosen": picks_of(key_list[3], SEQS * NQB, NMB, TOPB, 0).reshape((SEQS, NQB, TOPB)),
        "counts": with_ends(jax.random.randint(key_list[4], (SEQS, NQB, TOPB), 1, MBLK + 1), jax.random.fold_in(key_list[4], 1), 1, MBLK).astype(jnp.int32),
        "w_query": scatter_about(key_list[5], (D, D), D ** -0.5, 0.1875, ((0, 32),)),
        "w_key": scatter_about(key_list[6], (D, D), D ** -0.5, 0.1875, ((0, 32),)),
        "w_value": scatter_about(key_list[7], (D, D), D ** -0.5, 0.1875, ((0, 32),)),
        "w_out": scatter_about(key_list[8], (D, D), (D // 64) ** -0.5, 1.5, ((0, 32),)),
        "w_gate": scatter_about(key_list[9], (D, FF), D ** -0.5, 0.1875, ((0, 32),)),
        "w_up": scatter_about(key_list[10], (D, FF), D ** -0.5, 0.1875, ((0, 32),)),
        "w_down": scatter_about(key_list[11], (FF, D), FF ** -0.5, 0.109375, ((0, 32),)),
        "gain_attn": jnp.clip(1.0 + 0.1 * jax.random.normal(key_list[12], (D,), jnp.float32), 0.5, 1.5).astype(jnp.bfloat16),
        "gain_ffn": jnp.clip(1.0 + 0.1 * jax.random.normal(key_list[13], (D,), jnp.float32), 0.5, 1.5).astype(jnp.bfloat16),
        "cotangent": scatter_about(key_list[14], (SEQS, LEN, D), 1.0, 6.0, ((0, 8), (1, 4))),
    }


@jax.custom_vjp
def low(v):
    return lax.optimization_barrier(v.astype(jnp.bfloat16)).astype(jnp.float32)

@jax.custom_vjp
def low_back(v):
    return v

def low_keep(v):
    return (low(v), None)

def low_pass(kept, grad):
    return (grad,)

def back_keep(v):
    return (v, None)

def back_low(kept, grad):
    return (low(grad),)
low.defvjp(low_keep, low_pass)
low_back.defvjp(back_keep, back_low)
EPSILON = 1e-06
NEGATIVE = -1e+30
HIGHEST = lax.Precision.HIGHEST

def matmul(left, right):
    return jnp.dot(left, right, precision=HIGHEST)

def norm_rows(values, gain):
    return values * lax.rsqrt(lax.optimization_barrier(jnp.mean(values * values, -1, keepdims=True)) + EPSILON) * gain

def rotary(values, positions):
    half_dim = HEAD_DIM // 2
    frequency = 10000.0 ** (-jnp.arange(half_dim, dtype=jnp.float32) / half_dim)
    angles = positions.astype(jnp.float32)[:, None] * frequency[None, :]
    cosine = jnp.cos(angles)[:, None, :]
    sine_part = jnp.sin(angles)[:, None, :]
    shaped = values.reshape(values.shape[:-1] + (HEADS, HEAD_DIM))
    front_half = shaped[..., :half_dim]
    back_half = shaped[..., half_dim:]
    turned = jnp.concatenate([front_half * cosine - back_half * sine_part, back_half * cosine + front_half * sine_part], -1)
    return turned.reshape(values.shape)

def forward_one(weights, inputs, mem_keys, mem_values, chosen_one, counts_one):
    w_query, w_key, w_value, w_out, w_gate, w_up, w_down, gain_attn, gain_ffn = weights
    score_scale = 1.0 / math.sqrt(HEAD_DIM)
    block_count = LEN // QBLK
    positions = jnp.arange(LEN, dtype=jnp.int32)
    normed = low(norm_rows(inputs, gain_attn))
    queries = low(rotary(low_back(matmul(normed, w_query)), positions))
    key_rows = low(rotary(low_back(matmul(normed, w_key)), positions))
    value_rows = low(low_back(matmul(normed, w_value)))
    offsets = jnp.arange(MBLK, dtype=jnp.int32)
    mem_rows = (chosen_one[:, :, None] * MBLK + offsets[None, None, :]).reshape(block_count, TOPB * MBLK)
    valid_rows = (offsets[None, None, :] < counts_one[:, :, None]).reshape(block_count, TOPB * MBLK)
    picked_keys = mem_keys[mem_rows].reshape(block_count, TOPB * MBLK, HEADS, HEAD_DIM)
    picked_values = mem_values[mem_rows].reshape(block_count, TOPB * MBLK, HEADS, HEAD_DIM)
    query_heads = queries.reshape(LEN, HEADS, HEAD_DIM)
    key_heads = key_rows.reshape(LEN, HEADS, HEAD_DIM)
    value_heads = value_rows.reshape(LEN, HEADS, HEAD_DIM)
    local_part = jnp.einsum('qhd,khd->hqk', query_heads, key_heads, precision=HIGHEST) * score_scale
    causal = positions[:, None] >= positions[None, :]
    local_part = jnp.where(causal[None], local_part, NEGATIVE)
    blocked = query_heads.reshape(block_count, QBLK, HEADS, HEAD_DIM)
    remote = jnp.einsum('bqhd,bmhd->hbqm', blocked, picked_keys, precision=HIGHEST) * score_scale
    remote = jnp.where(valid_rows[None, :, None, :], remote, NEGATIVE).reshape(HEADS, LEN, TOPB * MBLK)
    scores = low_back(jnp.concatenate([local_part, remote], -1))
    maximum = lax.optimization_barrier(jnp.max(scores, -1, keepdims=True))
    exponent = jnp.exp(scores - maximum)
    probs = low(exponent / lax.optimization_barrier(jnp.sum(exponent, -1, keepdims=True)))
    local_out = jnp.einsum('hqk,khd->qhd', probs[..., :LEN], value_heads, precision=HIGHEST)
    remote_probs = probs[..., LEN:].reshape(HEADS, block_count, QBLK, TOPB * MBLK)
    remote_out = jnp.einsum('hbqm,bmhd->bqhd', remote_probs, picked_values, precision=HIGHEST)
    attended = (local_out + remote_out.reshape(LEN, HEADS, HEAD_DIM)).reshape(LEN, HEADS * HEAD_DIM)
    attended = low(low_back(attended))
    middle = inputs + low_back(matmul(attended, w_out))
    normed_two = low(norm_rows(middle, gain_ffn))
    gate_act = low_back(matmul(normed_two, w_gate))
    up_act = low_back(matmul(normed_two, w_up))
    hidden = low(jax.nn.silu(gate_act) * up_act)
    return middle + matmul(hidden, w_down)

def reference(tokens, memory_keys, memory_values, chosen, counts, w_query, w_key, w_value, w_out, w_gate, w_up, w_down, gain_attn, gain_ffn, cotangent):
    weights = tuple((w.astype(jnp.float32) for w in (w_query, w_key, w_value, w_out, w_gate, w_up, w_down, gain_attn, gain_ffn)))

    def seq_step(totals, pieces):
        inputs, mem_keys, mem_values, chosen_one, counts_one, grad_output = pieces

        def forward_fn(weight_set, token_rows):
            return forward_one(weight_set, token_rows, mem_keys.astype(jnp.float32), mem_values.astype(jnp.float32), chosen_one, counts_one)
        mixed_one, pullback = jax.vjp(forward_fn, weights, inputs.astype(jnp.float32))
        grad_weights, grad_tokens = pullback(grad_output.astype(jnp.float32))
        totals = jax.tree.map(jnp.add, totals, grad_weights)
        return (totals, (mixed_one.astype(jnp.bfloat16), grad_tokens.astype(jnp.bfloat16)))
    zero_sums = tuple((jnp.zeros_like(w) for w in weights))
    totals, (mixed, tokens_grad) = lax.scan(seq_step, zero_sums, (tokens, memory_keys, memory_values, chosen, counts, cotangent))
    return (mixed, tokens_grad, totals[0], totals[1], totals[2], totals[3], totals[4], totals[5], totals[6], totals[7], totals[8])
```

```python
import functools
import math

import jax
import jax.numpy as jnp
import numpy as np
from jax import lax
from jax.experimental import pallas as pl
from jax.experimental.pallas import tpu as pltpu
from jax.sharding import PartitionSpec as P

HEAD_DIM = 128
QBLK = 256
MBLK = 128
EPSILON = 1e-06
NEGATIVE = -1e30
SCALE = 1.0 / math.sqrt(HEAD_DIM)
LOG2E = math.log2(math.e)
MIB = 1 << 20
F32 = jnp.float32
BF16 = jnp.bfloat16
NT = (((1,), (1,)), ((), ()))
TN = (((0,), (0,)), ((), ()))


def dot(left, right, dims=(((1,), (0,)), ((), ()))):
    return lax.dot_general(left, right, dims, preferred_element_type=F32)


def rotary_tables(length):
    half_dim = HEAD_DIM // 2
    frequency = 10000.0 ** (-jnp.arange(half_dim, dtype=F32) / half_dim)
    angles = jnp.arange(length, dtype=jnp.int32).astype(F32)[:, None] * frequency[None, :]
    cosine, sine = jnp.cos(angles), jnp.sin(angles)
    return jnp.concatenate([cosine, cosine], 1), jnp.concatenate([-sine, sine], 1)


def qkv_kernel(heads, tok_ref, gain_ref, w_ref, cos_ref, sin_ref, qkv_ref, normed_ref):
    rows = tok_ref[...].astype(F32)
    factor = lax.rsqrt(jnp.mean(rows * rows, -1, keepdims=True) + EPSILON)
    normed = (rows * factor * gain_ref[...]).astype(BF16)
    normed_ref[...] = normed
    cosine, sine = cos_ref[...], sin_ref[...]
    for part in range(3):
        for head in range(heads):
            columns = slice((part * heads + head) * HEAD_DIM, (part * heads + head + 1) * HEAD_DIM)
            value = dot(normed, w_ref[:, columns])
            if part < 2:
                value = value * cosine + pltpu.roll(value, HEAD_DIM // 2, 1) * sine
            qkv_ref[:, columns] = value.astype(BF16)


def project_qkv(tokens_all, gain, w_qkv, cosine, sine, heads):
    length, width = tokens_all.shape
    columns = w_qkv.shape[1]
    block = QBLK
    return pl.pallas_call(
        functools.partial(qkv_kernel, heads),
        grid=(length // block,),
        in_specs=[
            pl.BlockSpec((block, width), lambda i: (i, 0)),
            pl.BlockSpec((1, width), lambda i: (0, 0)),
            pl.BlockSpec((width, columns), lambda i: (0, 0)),
            pl.BlockSpec((block, HEAD_DIM), lambda i: (i, 0)),
            pl.BlockSpec((block, HEAD_DIM), lambda i: (i, 0)),
        ],
        out_specs=[
            pl.BlockSpec((block, columns), lambda i: (i, 0)),
            pl.BlockSpec((block, width), lambda i: (i, 0)),
        ],
        out_shape=[
            jax.ShapeDtypeStruct((length, columns), BF16),
            jax.ShapeDtypeStruct((length, width), BF16),
        ],
        compiler_params=pltpu.CompilerParams(vmem_limit_bytes=48 * MIB),
        cost_estimate=pl.CostEstimate(
            flops=2 * length * width * columns, bytes_accessed=4 * length * (width + columns), transcendentals=0
        ),
        name="project_qkv",
    )(tokens_all, gain, w_qkv, cosine, sine)


def memory_bias(counts_ref, base, top, axis):
    shape = (1, top * MBLK) if axis == 1 else (top * MBLK, 1)
    column = lax.broadcasted_iota(jnp.int32, shape, axis)
    limit = jnp.zeros(shape, jnp.int32)
    for entry in range(top):
        inside = (column >= entry * MBLK) & (column < entry * MBLK + counts_ref[base + entry])
        limit = jnp.where(inside, 1, limit)
    return jnp.where(limit > 0, 0.0, NEGATIVE)


def pick_memory(ref, chosen_ref, base, top, columns):
    rows = [
        ref[pl.ds(pl.multiple_of(chosen_ref[base + entry] * MBLK, MBLK), MBLK), columns]
        for entry in range(top)
    ]
    return jnp.concatenate(rows, 0)


def forward_kernel(heads, top, chosen_ref, counts_ref, q_ref, k_ref, v_ref, mk_ref, mv_ref, out_ref, lse_ref):
    block = pl.program_id(0)
    base = block * top
    bias = memory_bias(counts_ref, base, top, 1)
    row = lax.broadcasted_iota(jnp.int32, (QBLK, QBLK), 0)
    column = lax.broadcasted_iota(jnp.int32, (QBLK, QBLK), 1)
    causal = row >= column
    own = pl.ds(pl.multiple_of(block * QBLK, QBLK), QBLK)
    unit = SCALE * LOG2E
    states = []
    for head in range(heads):
        columns = slice(head * HEAD_DIM, (head + 1) * HEAD_DIM)
        query = q_ref[:, columns]
        remote = dot(query, pick_memory(mk_ref, chosen_ref, base, top, columns), NT) * unit + bias
        local = jnp.where(causal, dot(query, k_ref[own, columns], NT) * unit, NEGATIVE)
        peak = jnp.maximum(jnp.max(remote, -1, keepdims=True), jnp.max(local, -1, keepdims=True))
        remote = jnp.exp2(remote - peak)
        local = jnp.exp2(local - peak)
        total = jnp.sum(remote, -1, keepdims=True) + jnp.sum(local, -1, keepdims=True)
        acc = dot(remote.astype(BF16), pick_memory(mv_ref, chosen_ref, base, top, columns))
        acc = acc + dot(local.astype(BF16), v_ref[own, columns])
        states.append((peak, total, acc))

    def step(index, states):
        rows = pl.ds(pl.multiple_of(index * QBLK, QBLK), QBLK)
        after = []
        for head in range(heads):
            columns = slice(head * HEAD_DIM, (head + 1) * HEAD_DIM)
            peak, total, acc = states[head]
            scores = dot(q_ref[:, columns], k_ref[rows, columns], NT) * unit
            higher = jnp.maximum(peak, jnp.max(scores, -1, keepdims=True))
            shrink = jnp.exp2(peak - higher)
            weights = jnp.exp2(scores - higher)
            total = total * shrink + jnp.sum(weights, -1, keepdims=True)
            acc = acc * shrink + dot(weights.astype(BF16), v_ref[rows, columns])
            after.append((higher, total, acc))
        return tuple(after)

    states = lax.fori_loop(0, block, step, tuple(states))
    for head in range(heads):
        columns = slice(head * HEAD_DIM, (head + 1) * HEAD_DIM)
        peak, total, acc = states[head]
        out_ref[:, columns] = (acc / total).astype(BF16)
        lse_ref[:, head : head + 1] = peak + jnp.log2(total)


def attend_forward(chosen, counts, qkv, memory, heads, top):
    length = qkv.shape[0]
    wide = heads * HEAD_DIM
    blocks = length // QBLK
    mem_rows = memory.shape[0]
    return pl.pallas_call(
        functools.partial(forward_kernel, heads, top),
        grid_spec=pltpu.PrefetchScalarGridSpec(
            num_scalar_prefetch=2,
            grid=(blocks,),
            in_specs=[
                pl.BlockSpec((QBLK, wide), lambda i, *_: (i, 0)),
                pl.BlockSpec((length, wide), lambda i, *_: (0, 1)),
                pl.BlockSpec((length, wide), lambda i, *_: (0, 2)),
                pl.BlockSpec((mem_rows, wide), lambda i, *_: (0, 0)),
                pl.BlockSpec((mem_rows, wide), lambda i, *_: (0, 1)),
            ],
            out_specs=[
                pl.BlockSpec((QBLK, wide), lambda i, *_: (i, 0)),
                pl.BlockSpec((QBLK, heads), lambda i, *_: (i, 0)),
            ],
        ),
        out_shape=[
            jax.ShapeDtypeStruct((length, wide), BF16),
            jax.ShapeDtypeStruct((length, heads), F32),
        ],
        compiler_params=pltpu.CompilerParams(vmem_limit_bytes=48 * MIB),
        cost_estimate=pl.CostEstimate(
            flops=4 * heads * length * HEAD_DIM * (length // 2 + top * MBLK),
            bytes_accessed=8 * length * wide,
            transcendentals=heads * length * (length // 2 + top * MBLK),
        ),
        name="attend_forward",
    )(chosen, counts, qkv, qkv, qkv, memory, memory)


def backward_kernel(
    heads, top, blocks, chosen_ref, counts_ref, q_ref, k_ref, v_ref, mk_ref, mv_ref, go_ref, out_ref, lse_ref,
    cos_ref, sin_ref, grad_ref, gk_ref, gv_ref,
):
    block = blocks - 1 - pl.program_id(0)
    base = block * top
    unit = SCALE * LOG2E
    bias = memory_bias(counts_ref, base, top, 0)
    key_at = lax.broadcasted_iota(jnp.int32, (QBLK, QBLK), 0)
    query_at = lax.broadcasted_iota(jnp.int32, (QBLK, QBLK), 1)
    causal = query_at >= key_at
    own = pl.ds(pl.multiple_of(block * QBLK, QBLK), QBLK)

    @pl.when(pl.program_id(0) == 0)
    def _():
        gk_ref[...] = jnp.zeros_like(gk_ref)
        gv_ref[...] = jnp.zeros_like(gv_ref)

    def spread(column):
        return jnp.transpose(jnp.broadcast_to(column, (QBLK, HEAD_DIM)))[:1]

    stats = []
    for head in range(heads):
        columns = slice(head * HEAD_DIM, (head + 1) * HEAD_DIM)
        grad = go_ref[:, columns]
        delta = jnp.sum(grad.astype(F32) * out_ref[:, columns].astype(F32), -1, keepdims=True)
        stats.append((spread(lse_ref[:, head : head + 1]), spread(delta)))

    def pair(head, keys, values, mask):
        columns = slice(head * HEAD_DIM, (head + 1) * HEAD_DIM)
        lse, delta = stats[head]
        scores = mask(dot(keys, q_ref[:, columns], NT) * unit)
        weights = jnp.exp2(scores - lse)
        grad_weights = dot(values, go_ref[:, columns], NT)
        grad_scores = (weights * (grad_weights - delta)).astype(BF16)
        return weights.astype(BF16), grad_scores

    def update(head, rows, weights, grad_scores):
        columns = slice(head * HEAD_DIM, (head + 1) * HEAD_DIM)
        gk_ref[rows, columns] += dot(grad_scores, q_ref[:, columns])
        gv_ref[rows, columns] += dot(weights, go_ref[:, columns])

    totals = []
    for head in range(heads):
        columns = slice(head * HEAD_DIM, (head + 1) * HEAD_DIM)
        keys = pick_memory(mk_ref, chosen_ref, base, top, columns)
        values = pick_memory(mv_ref, chosen_ref, base, top, columns)
        _, grad_scores = pair(head, keys, values, lambda scores: scores + bias)
        total = dot(grad_scores, keys, TN)
        keys = k_ref[own, columns]
        weights, grad_scores = pair(
            head, keys, v_ref[own, columns], lambda scores: jnp.where(causal, scores, NEGATIVE)
        )
        update(head, own, weights, grad_scores)
        totals.append(total + dot(grad_scores, keys, TN))

    def step(index, totals):
        rows = pl.ds(pl.multiple_of(index * QBLK, QBLK), QBLK)
        after = []
        for head in range(heads):
            columns = slice(head * HEAD_DIM, (head + 1) * HEAD_DIM)
            keys = k_ref[rows, columns]
            weights, grad_scores = pair(head, keys, v_ref[rows, columns], lambda scores: scores)
            update(head, rows, weights, grad_scores)
            after.append(totals[head] + dot(grad_scores, keys, TN))
        return tuple(after)

    totals = lax.fori_loop(0, block, step, tuple(totals))
    cosine, sine = cos_ref[...], sin_ref[...]

    def unturn(value):
        return value * cosine - pltpu.roll(value, HEAD_DIM // 2, 1) * sine

    wide = heads * HEAD_DIM
    for head in range(heads):
        columns = slice(head * HEAD_DIM, (head + 1) * HEAD_DIM)
        at = head * HEAD_DIM
        grad_ref[:, at : at + HEAD_DIM] = unturn(totals[head] * SCALE).astype(BF16)
        grad_key = gk_ref[own, columns] * SCALE
        grad_ref[:, wide + at : wide + at + HEAD_DIM] = unturn(grad_key).astype(BF16)
        grad_ref[:, 2 * wide + at : 2 * wide + at + HEAD_DIM] = gv_ref[own, columns].astype(BF16)


def attend_backward(chosen, counts, qkv, memory, grad_out, out, lse, cosine, sine, heads, top):
    length = qkv.shape[0]
    wide = heads * HEAD_DIM
    blocks = length // QBLK
    mem_rows = memory.shape[0]
    last = blocks - 1
    return pl.pallas_call(
        functools.partial(backward_kernel, heads, top, blocks),
        grid_spec=pltpu.PrefetchScalarGridSpec(
            num_scalar_prefetch=2,
            grid=(blocks,),
            in_specs=[
                pl.BlockSpec((QBLK, wide), lambda i, *_: (last - i, 0)),
                pl.BlockSpec((length, wide), lambda i, *_: (0, 1)),
                pl.BlockSpec((length, wide), lambda i, *_: (0, 2)),
                pl.BlockSpec((mem_rows, wide), lambda i, *_: (0, 0)),
                pl.BlockSpec((mem_rows, wide), lambda i, *_: (0, 1)),
                pl.BlockSpec((QBLK, wide), lambda i, *_: (last - i, 0)),
                pl.BlockSpec((QBLK, wide), lambda i, *_: (last - i, 0)),
                pl.BlockSpec((QBLK, heads), lambda i, *_: (last - i, 0)),
                pl.BlockSpec((QBLK, HEAD_DIM), lambda i, *_: (last - i, 0)),
                pl.BlockSpec((QBLK, HEAD_DIM), lambda i, *_: (last - i, 0)),
            ],
            out_specs=pl.BlockSpec((QBLK, 3 * wide), lambda i, *_: (last - i, 0)),
            scratch_shapes=[pltpu.VMEM((length, wide), F32), pltpu.VMEM((length, wide), F32)],
        ),
        out_shape=jax.ShapeDtypeStruct((length, 3 * wide), BF16),
        compiler_params=pltpu.CompilerParams(vmem_limit_bytes=48 * MIB),
        cost_estimate=pl.CostEstimate(
            flops=10 * heads * length * HEAD_DIM * (length // 2 + top * MBLK),
            bytes_accessed=16 * length * wide,
            transcendentals=heads * length * (length // 2 + top * MBLK),
        ),
        name="attend_backward",
    )(chosen, counts, qkv, qkv, qkv, memory, memory, grad_out, out, lse, cosine, sine)


def chain_gather(block, axis):
    size = lax.axis_size(axis)
    place = lax.axis_index(axis)
    up = [(i, i + 1) for i in range(size - 1)]
    down = [(i + 1, i) for i in range(size - 1)]
    from_below, from_above = [], []
    rising = falling = block
    for _ in range(size - 1):
        rising = lax.ppermute(rising, axis, up)
        falling = lax.ppermute(falling, axis, down)
        from_below.append(rising)
        from_above.append(falling)
    ordered = []
    for index in range(size):
        cases = []
        for mine in range(size):
            if mine == index:
                cases.append(block)
            elif mine > index:
                cases.append(from_below[mine - index - 1])
            else:
                cases.append(from_above[index - mine - 1])
        ordered.append(lax.select_n(place, *cases) if size > 2 else lax.select_n(place > 0, *cases))
    return ordered


def body(
    tokens, memory_keys, memory_values, chosen, counts, w_query, w_key, w_value, w_out, w_gate, w_up, w_down,
    gain_attn, gain_ffn, cotangent,
):
    ring, span = lax.axis_size("fsdp"), lax.axis_size("dp")
    rows, width = tokens.shape[1:]
    heads = width // HEAD_DIM // ring
    wide = heads * HEAD_DIM
    length = rows * ring
    top = chosen.shape[2]
    hidden_width = w_gate.shape[1]
    share = w_query.shape[0]
    mine = tokens[0]

    extra = 8 if share % 8 == 0 else 8 - share % 8
    parts = [w.reshape(share, ring, wide).transpose(1, 0, 2) for w in (w_query, w_key, w_value)]
    gains = jnp.pad(jnp.concatenate([gain_attn, gain_ffn]), (0, 3 * wide - 2 * share))
    gains = jnp.broadcast_to(gains, (ring, extra, 3 * wide))
    parcel = jnp.concatenate([jnp.concatenate(parts, 2), gains], 1)
    parcel = lax.all_to_all(parcel, "fsdp", 0, 0, tiled=True)
    parcel = lax.all_gather(parcel, "dp", axis=0, tiled=True)
    w_qkv = parcel[:, :share].reshape(width, 3 * wide)
    gain_one = parcel[:, share, :share].reshape(1, width).astype(F32)
    gain_two = parcel[:, share, share : 2 * share].reshape(1, width).astype(F32)

    picks = lax.all_gather(jnp.stack([chosen[0], counts[0]]), "fsdp", axis=1, tiled=True)
    chosen_all, counts_all = picks[0].reshape(-1), picks[1].reshape(-1)
    memory = jnp.concatenate(
        [m[0].reshape(-1, ring, wide).transpose(1, 0, 2) for m in (memory_keys, memory_values)], 2
    )
    memory = lax.all_to_all(memory, "fsdp", 0, 0, tiled=True).reshape(-1, 2 * wide)

    gathered = jnp.concatenate(chain_gather(mine, "fsdp"), 0)

    def whole(shard):
        near = lax.all_gather(shard, "fsdp", axis=0, tiled=True)
        return lax.all_gather(near, "dp", axis=0, tiled=True)

    first = whole(jnp.concatenate([w_gate, w_up, w_out], 1))
    down_full = whole(w_down)
    gate_up = first[:, : 2 * hidden_width]
    out_full = first[:, 2 * hidden_width :]

    cosine, sine = rotary_tables(length)
    qkv, normed = project_qkv(gathered, gain_one, w_qkv, cosine, sine, heads)
    attended_heads, lse = attend_forward(chosen_all, counts_all, qkv, memory, heads, top)
    attended = lax.all_to_all(attended_heads, "fsdp", 0, 1, tiled=True)

    middle = mine.astype(F32) + dot(attended, out_full)
    factor = lax.rsqrt(jnp.mean(middle * middle, -1, keepdims=True) + EPSILON)
    normed_two = (middle * factor * gain_two).astype(BF16)
    acts = dot(normed_two, gate_up)
    gate_act, up_act = acts[:, :hidden_width], acts[:, hidden_width:]
    sigmoid = jax.nn.sigmoid(gate_act)
    hidden = (gate_act * sigmoid * up_act).astype(BF16)
    mixed = (middle + dot(hidden, down_full)).astype(BF16)

    upstream = cotangent[0]
    grad_down = dot(hidden, upstream, TN).astype(BF16)
    grad_hidden = dot(upstream, down_full, NT)
    grad_gate = grad_hidden * up_act * sigmoid * (1.0 + gate_act * (1.0 - sigmoid))
    grad_up = grad_hidden * gate_act * sigmoid
    grad_acts = jnp.concatenate([grad_gate.astype(BF16), grad_up.astype(BF16)], 1)
    grad_gate_up = dot(normed_two, grad_acts, TN).astype(BF16)
    grad_normed_two = dot(grad_acts, gate_up, NT)

    def norm_back(values, factor, gain, grad):
        scaled = grad * gain
        inner = jnp.mean(scaled * values, -1, keepdims=True)
        return factor * scaled - values * factor**3 * inner

    gain_two_grad = jnp.sum(grad_normed_two * middle * factor, 0)
    grad_middle = upstream.astype(F32) + norm_back(middle, factor, gain_two, grad_normed_two)
    grad_branch = grad_middle.astype(BF16)
    grad_attended = dot(grad_branch, out_full, NT).astype(BF16)
    grad_heads = lax.all_to_all(grad_attended, "fsdp", 1, 0, tiled=True)
    grad_out = dot(attended, grad_branch, TN).astype(BF16)

    grad_qkv = attend_backward(
        chosen_all, counts_all, qkv, memory, grad_heads, attended_heads, lse, cosine, sine, heads, top
    )
    grad_w_qkv = dot(normed, grad_qkv, TN).astype(BF16)
    partial = dot(grad_qkv, w_qkv, NT)
    tokens_f32 = gathered.astype(F32)
    factor_all = lax.rsqrt(jnp.mean(tokens_f32 * tokens_f32, -1, keepdims=True) + EPSILON)
    gain_one_grad = jnp.sum(partial * tokens_f32 * factor_all, 0)
    grad_normed = lax.psum_scatter(
        partial.astype(BF16), "fsdp", scatter_dimension=0, tiled=True
    ).astype(F32)
    own = mine.astype(F32)
    own_factor = lax.rsqrt(jnp.mean(own * own, -1, keepdims=True) + EPSILON)
    tokens_grad = (grad_middle + norm_back(own, own_factor, gain_one, grad_normed)).astype(BF16)

    def reduced(grad):
        near = lax.psum_scatter(grad, "dp", scatter_dimension=0, tiled=True)
        return lax.psum_scatter(near, "fsdp", scatter_dimension=0, tiled=True).astype(F32)

    down_share = reduced(grad_down)
    gate_up_share = reduced(grad_gate_up)
    gain_columns = jnp.pad(jnp.stack([gain_one_grad, gain_two_grad], 1), ((0, 0), (0, HEAD_DIM - 2)))
    late = jnp.concatenate([grad_w_qkv, grad_out, gain_columns.astype(BF16)], 1)
    late = lax.psum_scatter(late, "dp", scatter_dimension=0, tiled=True)
    late = late.reshape(ring, share, late.shape[1])
    late = lax.all_to_all(late, "fsdp", 0, 0, tiled=True).astype(F32)
    projections = [
        late[:, :, part * wide : (part + 1) * wide].transpose(1, 0, 2).reshape(share, width) for part in range(3)
    ]
    out_share = jnp.sum(late[:, :, 3 * wide : 3 * wide + width], 0)
    gain_shares = jnp.sum(late[:, :, 3 * wide + width :], 0)
    return (
        mixed[None],
        tokens_grad[None],
        *projections,
        out_share,
        gate_up_share[:, :hidden_width],
        gate_up_share[:, hidden_width:],
        down_share,
        gain_shares[:, 0],
        gain_shares[:, 1],
    )


def solution(mesh):
    both = ("dp", "fsdp")
    rows, matrix, vector = P("dp", "fsdp", None), P(both, None), P(both)
    in_specs = (rows,) * 5 + (matrix,) * 7 + (vector,) * 2 + (rows,)
    out_specs = (rows,) * 2 + (matrix,) * 7 + (vector,) * 2
    return jax.shard_map(body, mesh=mesh, in_specs=in_specs, out_specs=out_specs, check_vma=False)
```

```python
import functools
import math

import jax
import jax.numpy as jnp
import numpy as np
from jax import lax
from jax.experimental import pallas as pl
from jax.experimental.pallas import tpu as pltpu
from jax.sharding import PartitionSpec as P

HEAD_DIM = 128
QBLK = 256
MBLK = 128
EPSILON = 1e-06
NEGATIVE = -1e30
SCALE = 1.0 / math.sqrt(HEAD_DIM)
LOG2E = math.log2(math.e)
MIB = 1 << 20
F32 = jnp.float32
BF16 = jnp.bfloat16
NT = (((1,), (1,)), ((), ()))
TN = (((0,), (0,)), ((), ()))


def dot(left, right, dims=(((1,), (0,)), ((), ()))):
    return lax.dot_general(left, right, dims, preferred_element_type=F32)


def rotary_tables(length):
    half_dim = HEAD_DIM // 2
    frequency = 10000.0 ** (-jnp.arange(half_dim, dtype=F32) / half_dim)
    angles = jnp.arange(length, dtype=jnp.int32).astype(F32)[:, None] * frequency[None, :]
    cosine, sine = jnp.cos(angles), jnp.sin(angles)
    return jnp.concatenate([cosine, cosine], 1), jnp.concatenate([-sine, sine], 1)


def qkv_kernel(heads, tok_ref, gain_ref, w_ref, cos_ref, sin_ref, qkv_ref):
    rows = tok_ref[...].astype(F32)
    factor = lax.rsqrt(jnp.mean(rows * rows, -1, keepdims=True) + EPSILON)
    normed = (rows * factor * gain_ref[...]).astype(BF16)
    cosine, sine = cos_ref[...], sin_ref[...]
    for part in range(3):
        for head in range(heads):
            columns = slice((part * heads + head) * HEAD_DIM, (part * heads + head + 1) * HEAD_DIM)
            value = dot(normed, w_ref[:, columns])
            if part < 2:
                value = value * cosine + pltpu.roll(value, HEAD_DIM // 2, 1) * sine
            qkv_ref[:, columns] = value.astype(BF16)


def project_qkv(tokens_all, gain, w_qkv, cosine, sine, heads):
    length, width = tokens_all.shape
    columns = w_qkv.shape[1]
    block = QBLK
    return pl.pallas_call(
        functools.partial(qkv_kernel, heads),
        grid=(length // block,),
        in_specs=[
            pl.BlockSpec((block, width), lambda i: (i, 0)),
            pl.BlockSpec((1, width), lambda i: (0, 0)),
            pl.BlockSpec((width, columns), lambda i: (0, 0)),
            pl.BlockSpec((block, HEAD_DIM), lambda i: (i, 0)),
            pl.BlockSpec((block, HEAD_DIM), lambda i: (i, 0)),
        ],
        out_specs=pl.BlockSpec((block, columns), lambda i: (i, 0)),
        out_shape=jax.ShapeDtypeStruct((length, columns), BF16),
        compiler_params=pltpu.CompilerParams(vmem_limit_bytes=48 * MIB),
        cost_estimate=pl.CostEstimate(
            flops=2 * length * width * columns, bytes_accessed=4 * length * (width + columns), transcendentals=0
        ),
        name="project_qkv",
    )(tokens_all, gain, w_qkv, cosine, sine)


def memory_bias(counts_ref, base, top, axis):
    shape = (1, top * MBLK) if axis == 1 else (top * MBLK, 1)
    column = lax.broadcasted_iota(jnp.int32, shape, axis)
    limit = jnp.zeros(shape, jnp.int32)
    for entry in range(top):
        inside = (column >= entry * MBLK) & (column < entry * MBLK + counts_ref[base + entry])
        limit = jnp.where(inside, 1, limit)
    return jnp.where(limit > 0, 0.0, NEGATIVE)


def pick_memory(ref, chosen_ref, base, top, columns):
    rows = [
        ref[pl.ds(pl.multiple_of(chosen_ref[base + entry] * MBLK, MBLK), MBLK), columns]
        for entry in range(top)
    ]
    return jnp.concatenate(rows, 0)


def forward_kernel(heads, top, chosen_ref, counts_ref, q_ref, k_ref, v_ref, mk_ref, mv_ref, out_ref, lse_ref):
    block = pl.program_id(0)
    base = block * top
    bias = memory_bias(counts_ref, base, top, 1)
    row = lax.broadcasted_iota(jnp.int32, (QBLK, QBLK), 0)
    column = lax.broadcasted_iota(jnp.int32, (QBLK, QBLK), 1)
    causal = row >= column
    own = pl.ds(pl.multiple_of(block * QBLK, QBLK), QBLK)
    unit = SCALE * LOG2E
    states = []
    for head in range(heads):
        columns = slice(head * HEAD_DIM, (head + 1) * HEAD_DIM)
        query = q_ref[:, columns]
        remote = dot(query, pick_memory(mk_ref, chosen_ref, base, top, columns), NT) * unit + bias
        local = jnp.where(causal, dot(query, k_ref[own, columns], NT) * unit, NEGATIVE)
        peak = jnp.maximum(jnp.max(remote, -1, keepdims=True), jnp.max(local, -1, keepdims=True))
        remote = jnp.exp2(remote - peak)
        local = jnp.exp2(local - peak)
        total = jnp.sum(remote, -1, keepdims=True) + jnp.sum(local, -1, keepdims=True)
        acc = dot(remote.astype(BF16), pick_memory(mv_ref, chosen_ref, base, top, columns))
        acc = acc + dot(local.astype(BF16), v_ref[own, columns])
        states.append((peak, total, acc))

    def step(index, states):
        rows = pl.ds(pl.multiple_of(index * QBLK, QBLK), QBLK)
        after = []
        for head in range(heads):
            columns = slice(head * HEAD_DIM, (head + 1) * HEAD_DIM)
            peak, total, acc = states[head]
            scores = dot(q_ref[:, columns], k_ref[rows, columns], NT) * unit
            higher = jnp.maximum(peak, jnp.max(scores, -1, keepdims=True))
            shrink = jnp.exp2(peak - higher)
            weights = jnp.exp2(scores - higher)
            total = total * shrink + jnp.sum(weights, -1, keepdims=True)
            acc = acc * shrink + dot(weights.astype(BF16), v_ref[rows, columns])
            after.append((higher, total, acc))
        return tuple(after)

    states = lax.fori_loop(0, block, step, tuple(states))
    for head in range(heads):
        columns = slice(head * HEAD_DIM, (head + 1) * HEAD_DIM)
        peak, total, acc = states[head]
        out_ref[:, columns] = (acc / total).astype(BF16)
        lse_ref[:, head : head + 1] = peak + jnp.log2(total)


def attend_forward(chosen, counts, qkv, memory, heads, top):
    length = qkv.shape[0]
    wide = heads * HEAD_DIM
    blocks = length // QBLK
    mem_rows = memory.shape[0]
    return pl.pallas_call(
        functools.partial(forward_kernel, heads, top),
        grid_spec=pltpu.PrefetchScalarGridSpec(
            num_scalar_prefetch=2,
            grid=(blocks,),
            in_specs=[
                pl.BlockSpec((QBLK, wide), lambda i, *_: (i, 0)),
                pl.BlockSpec((length, wide), lambda i, *_: (0, 1)),
                pl.BlockSpec((length, wide), lambda i, *_: (0, 2)),
                pl.BlockSpec((mem_rows, wide), lambda i, *_: (0, 0)),
                pl.BlockSpec((mem_rows, wide), lambda i, *_: (0, 1)),
            ],
            out_specs=[
                pl.BlockSpec((QBLK, wide), lambda i, *_: (i, 0)),
                pl.BlockSpec((QBLK, heads), lambda i, *_: (i, 0)),
            ],
        ),
        out_shape=[
            jax.ShapeDtypeStruct((length, wide), BF16),
            jax.ShapeDtypeStruct((length, heads), F32),
        ],
        compiler_params=pltpu.CompilerParams(vmem_limit_bytes=48 * MIB),
        cost_estimate=pl.CostEstimate(
            flops=4 * heads * length * HEAD_DIM * (length // 2 + top * MBLK),
            bytes_accessed=8 * length * wide,
            transcendentals=heads * length * (length // 2 + top * MBLK),
        ),
        name="attend_forward",
    )(chosen, counts, qkv, qkv, qkv, memory, memory)


def backward_kernel(
    heads, top, blocks, chosen_ref, counts_ref, q_ref, k_ref, v_ref, mk_ref, mv_ref, go_ref, out_ref, lse_ref,
    cos_ref, sin_ref, tok_ref, gain_ref, w_ref, partial_ref, grad_w_ref, gain_grad_ref, gk_ref, gv_ref, grad_s, gw_s,
):
    block = blocks - 1 - pl.program_id(0)
    base = block * top
    unit = SCALE * LOG2E
    bias = memory_bias(counts_ref, base, top, 0)
    key_at = lax.broadcasted_iota(jnp.int32, (QBLK, QBLK), 0)
    query_at = lax.broadcasted_iota(jnp.int32, (QBLK, QBLK), 1)
    causal = query_at >= key_at
    own = pl.ds(pl.multiple_of(block * QBLK, QBLK), QBLK)

    @pl.when(pl.program_id(0) == 0)
    def _():
        gk_ref[...] = jnp.zeros_like(gk_ref)
        gv_ref[...] = jnp.zeros_like(gv_ref)
        gw_s[...] = jnp.zeros_like(gw_s)
        gain_grad_ref[...] = jnp.zeros_like(gain_grad_ref)

    def spread(column):
        return jnp.transpose(jnp.broadcast_to(column, (QBLK, HEAD_DIM)))[:1]

    stats = []
    for head in range(heads):
        columns = slice(head * HEAD_DIM, (head + 1) * HEAD_DIM)
        grad = go_ref[:, columns]
        delta = jnp.sum(grad.astype(F32) * out_ref[:, columns].astype(F32), -1, keepdims=True)
        stats.append((spread(lse_ref[:, head : head + 1]), spread(delta)))

    def pair(head, keys, values, mask):
        columns = slice(head * HEAD_DIM, (head + 1) * HEAD_DIM)
        lse, delta = stats[head]
        scores = mask(dot(keys, q_ref[:, columns], NT) * unit)
        weights = jnp.exp2(scores - lse)
        grad_weights = dot(values, go_ref[:, columns], NT)
        grad_scores = (weights * (grad_weights - delta)).astype(BF16)
        return weights.astype(BF16), grad_scores

    def update(head, rows, weights, grad_scores):
        columns = slice(head * HEAD_DIM, (head + 1) * HEAD_DIM)
        gk_ref[rows, columns] += dot(grad_scores, q_ref[:, columns])
        gv_ref[rows, columns] += dot(weights, go_ref[:, columns])

    totals = []
    for head in range(heads):
        columns = slice(head * HEAD_DIM, (head + 1) * HEAD_DIM)
        keys = pick_memory(mk_ref, chosen_ref, base, top, columns)
        values = pick_memory(mv_ref, chosen_ref, base, top, columns)
        _, grad_scores = pair(head, keys, values, lambda scores: scores + bias)
        total = dot(grad_scores, keys, TN)
        keys = k_ref[own, columns]
        weights, grad_scores = pair(
            head, keys, v_ref[own, columns], lambda scores: jnp.where(causal, scores, NEGATIVE)
        )
        update(head, own, weights, grad_scores)
        totals.append(total + dot(grad_scores, keys, TN))

    def step(index, totals):
        rows = pl.ds(pl.multiple_of(index * QBLK, QBLK), QBLK)
        after = []
        for head in range(heads):
            columns = slice(head * HEAD_DIM, (head + 1) * HEAD_DIM)
            keys = k_ref[rows, columns]
            weights, grad_scores = pair(head, keys, v_ref[rows, columns], lambda scores: scores)
            update(head, rows, weights, grad_scores)
            after.append(totals[head] + dot(grad_scores, keys, TN))
        return tuple(after)

    totals = lax.fori_loop(0, block, step, tuple(totals))
    cosine, sine = cos_ref[...], sin_ref[...]

    def unturn(value):
        return value * cosine - pltpu.roll(value, HEAD_DIM // 2, 1) * sine

    wide = heads * HEAD_DIM
    for head in range(heads):
        columns = slice(head * HEAD_DIM, (head + 1) * HEAD_DIM)
        at = head * HEAD_DIM
        grad_s[:, at : at + HEAD_DIM] = unturn(totals[head] * SCALE).astype(BF16)
        grad_key = gk_ref[own, columns] * SCALE
        grad_s[:, wide + at : wide + at + HEAD_DIM] = unturn(grad_key).astype(BF16)
        grad_s[:, 2 * wide + at : 2 * wide + at + HEAD_DIM] = gv_ref[own, columns].astype(BF16)

    rows = tok_ref[...].astype(F32)
    rows = rows * lax.rsqrt(jnp.mean(rows * rows, -1, keepdims=True) + EPSILON)
    normed = (rows * gain_ref[...]).astype(BF16)
    grad = grad_s[...]
    partial = dot(grad, w_ref[...], NT)
    partial_ref[...] = partial.astype(BF16)
    gain_grad_ref[...] += jnp.sum(partial * rows, 0, keepdims=True)
    gw_s[...] += dot(normed, grad, TN)

    @pl.when(block == 0)
    def _():
        grad_w_ref[...] = gw_s[...].astype(BF16)


def attend_backward(
    chosen, counts, qkv, memory, grad_out, out, lse, cosine, sine, tokens_all, gain, w_qkv, heads, top
):
    length = qkv.shape[0]
    width = tokens_all.shape[1]
    wide = heads * HEAD_DIM
    blocks = length // QBLK
    mem_rows = memory.shape[0]
    last = blocks - 1
    return pl.pallas_call(
        functools.partial(backward_kernel, heads, top, blocks),
        grid_spec=pltpu.PrefetchScalarGridSpec(
            num_scalar_prefetch=2,
            grid=(blocks,),
            in_specs=[
                pl.BlockSpec((QBLK, wide), lambda i, *_: (last - i, 0)),
                pl.BlockSpec((length, wide), lambda i, *_: (0, 1)),
                pl.BlockSpec((length, wide), lambda i, *_: (0, 2)),
                pl.BlockSpec((mem_rows, wide), lambda i, *_: (0, 0)),
                pl.BlockSpec((mem_rows, wide), lambda i, *_: (0, 1)),
                pl.BlockSpec((QBLK, wide), lambda i, *_: (last - i, 0)),
                pl.BlockSpec((QBLK, wide), lambda i, *_: (last - i, 0)),
                pl.BlockSpec((QBLK, heads), lambda i, *_: (last - i, 0)),
                pl.BlockSpec((QBLK, HEAD_DIM), lambda i, *_: (last - i, 0)),
                pl.BlockSpec((QBLK, HEAD_DIM), lambda i, *_: (last - i, 0)),
                pl.BlockSpec((QBLK, width), lambda i, *_: (last - i, 0)),
                pl.BlockSpec((1, width), lambda i, *_: (0, 0)),
                pl.BlockSpec((width, 3 * wide), lambda i, *_: (0, 0)),
            ],
            out_specs=[
                pl.BlockSpec((QBLK, width), lambda i, *_: (last - i, 0)),
                pl.BlockSpec((width, 3 * wide), lambda i, *_: (0, 0)),
                pl.BlockSpec((1, width), lambda i, *_: (0, 0)),
            ],
            scratch_shapes=[
                pltpu.VMEM((length, wide), F32),
                pltpu.VMEM((length, wide), F32),
                pltpu.VMEM((QBLK, 3 * wide), BF16),
                pltpu.VMEM((width, 3 * wide), F32),
            ],
        ),
        out_shape=[
            jax.ShapeDtypeStruct((length, width), BF16),
            jax.ShapeDtypeStruct((width, 3 * wide), BF16),
            jax.ShapeDtypeStruct((1, width), F32),
        ],
        compiler_params=pltpu.CompilerParams(vmem_limit_bytes=48 * MIB),
        cost_estimate=pl.CostEstimate(
            flops=10 * heads * length * HEAD_DIM * (length // 2 + top * MBLK),
            bytes_accessed=16 * length * wide,
            transcendentals=heads * length * (length // 2 + top * MBLK),
        ),
        name="attend_backward",
    )(
        chosen, counts, qkv, qkv, qkv, memory, memory, grad_out, out, lse, cosine, sine, tokens_all, gain, w_qkv
    )


def ffn_kernel(
    span, merged, tok_ref, att_ref, cot_ref, gain_ref, out_w, gate_w, up_w, down_w,
    mixed_ref, grad_mid_ref, grad_att_ref, gain_grad_ref, grads_ref, *rest,
):
    if not merged:
        down_grads_ref, rest = rest[0], rest[1:]
    middle_s, normed_s, turned_s, mixed_s, upstream_s, gate_s, up_s, down_s, out_s, sems, late_sems = rest
    step, steps = pl.program_id(0), pl.num_programs(0)
    width = tok_ref.shape[1]
    share = width // span
    wide = gate_w.shape[1]
    hidden_width = down_s.shape[0]
    tall = hidden_width // span
    lanes = width // wide
    first = tall * lanes if merged else 0
    slot = step % 2

    @pl.when(step == 0)
    def _():
        middle = tok_ref[...].astype(F32) + dot(att_ref[...], out_w[...])
        middle_s[...] = middle
        factor = lax.rsqrt(jnp.mean(middle * middle, -1, keepdims=True) + EPSILON)
        normed = (middle * factor * gain_ref[...]).astype(BF16)
        normed_s[...] = normed
        turned_s[...] = jnp.transpose(normed)
        mixed_s[...] = middle
        upstream_s[...] = jnp.zeros_like(upstream_s)

    def copy_out(kind, which, index):
        source = (gate_s, up_s)[kind].at[which]
        start = first + (lanes + kind * steps + index) * share
        target = grads_ref.at[:, pl.ds(start, share), :]
        return pltpu.make_async_copy(source, target, sems.at[kind, which])

    normed = normed_s[...]
    upstream = cot_ref[...]
    gate_act = dot(normed, gate_w[...])
    up_act = dot(normed, up_w[...])
    grad_hidden = dot(upstream, down_w[...], NT)
    sigmoid = jax.nn.sigmoid(gate_act)
    silu = gate_act * sigmoid
    hidden = (silu * up_act).astype(BF16)
    grad_gate = (grad_hidden * up_act * sigmoid * (1.0 + gate_act * (1.0 - sigmoid))).astype(BF16)
    grad_up = (grad_hidden * silu).astype(BF16)
    mixed_s[...] += dot(hidden, down_w[...])
    upstream_s[...] += dot(grad_gate, gate_w[...], NT) + dot(grad_up, up_w[...], NT)
    down_s[pl.ds(pl.multiple_of(step * wide, wide), wide), :] = dot(hidden, upstream, TN).astype(BF16)

    @pl.when(step >= 2)
    def _():
        copy_out(0, slot, step - 2).wait()
        copy_out(1, slot, step - 2).wait()

    turned = turned_s[...]
    gate_s[slot] = dot(turned, grad_gate).astype(BF16).reshape(span, share, wide)
    up_s[slot] = dot(turned, grad_up).astype(BF16).reshape(span, share, wide)
    copy_out(0, slot, step).start()
    copy_out(1, slot, step).start()

    @pl.when(step == steps - 1)
    def _():
        copies = []
        if merged:
            for place in range(span):
                for lane in range(lanes):
                    copies.append(
                        pltpu.make_async_copy(
                            down_s.at[pl.ds(place * tall, tall), pl.ds(lane * wide, wide)],
                            grads_ref.at[place, pl.ds(lane * tall, tall), :],
                            late_sems.at[len(copies)],
                        )
                    )
        else:
            copies.append(pltpu.make_async_copy(down_s, down_grads_ref, late_sems.at[0]))
        for copy in copies:
            copy.start()
        mixed_ref[...] = mixed_s[...].astype(BF16)
        middle = middle_s[...]
        grad = upstream_s[...]
        factor = lax.rsqrt(jnp.mean(middle * middle, -1, keepdims=True) + EPSILON)
        gain_grad_ref[...] = jnp.sum(grad * middle * factor, 0, keepdims=True)
        scaled = grad * gain_ref[...]
        inner = jnp.mean(scaled * middle, -1, keepdims=True)
        grad_middle = cot_ref[...].astype(F32) + factor * scaled - middle * (factor * factor * factor * inner)
        grad_mid_ref[...] = grad_middle
        branch = grad_middle.astype(BF16)
        grad_att_ref[...] = dot(branch, out_w[...], NT).astype(BF16)
        turned_att = jnp.transpose(att_ref[...])
        for lane in range(lanes):
            columns = slice(lane * wide, (lane + 1) * wide)
            out_s[lane] = dot(turned_att, branch[:, columns]).astype(BF16).reshape(span, share, wide)
            more = pltpu.make_async_copy(
                out_s.at[lane],
                grads_ref.at[:, pl.ds(first + lane * share, share), :],
                late_sems.at[len(copies)],
            )
            more.start()
            copies.append(more)
        for copy in copies:
            copy.wait()
        copy_out(0, 1 - slot, step - 1).wait()
        copy_out(1, 1 - slot, step - 1).wait()
        copy_out(0, slot, step).wait()
        copy_out(1, slot, step).wait()


def feed_forward(tokens, attended, upstream, gain, weights, w_down, span):
    rows, width = tokens.shape
    hidden_width = w_down.shape[0]
    wide = 2 * HEAD_DIM
    steps = hidden_width // wide
    lanes = width // wide
    share = width // span
    tall = hidden_width // span
    merged = tall % 16 == 0
    total = (lanes + 2 * steps) * share + (lanes * tall if merged else 0)
    shapes = [
        jax.ShapeDtypeStruct((rows, width), BF16),
        jax.ShapeDtypeStruct((rows, width), F32),
        jax.ShapeDtypeStruct((rows, width), BF16),
        jax.ShapeDtypeStruct((1, width), F32),
        jax.ShapeDtypeStruct((span, total, wide), BF16),
    ]
    specs = [
        pl.BlockSpec((rows, width), lambda i: (0, 0)),
        pl.BlockSpec((rows, width), lambda i: (0, 0)),
        pl.BlockSpec((rows, width), lambda i: (0, 0)),
        pl.BlockSpec((1, width), lambda i: (0, 0)),
        pl.BlockSpec(memory_space=pl.ANY),
    ]
    if not merged:
        shapes.append(jax.ShapeDtypeStruct((hidden_width, width), BF16))
        specs.append(pl.BlockSpec(memory_space=pl.ANY))
    return pl.pallas_call(
        functools.partial(ffn_kernel, span, merged),
        grid=(steps,),
        in_specs=[
            pl.BlockSpec((rows, width), lambda i: (0, 0)),
            pl.BlockSpec((rows, width), lambda i: (0, 0)),
            pl.BlockSpec((rows, width), lambda i: (0, 0)),
            pl.BlockSpec((1, width), lambda i: (0, 0)),
            pl.BlockSpec((width, width), lambda i: (0, 0)),
            pl.BlockSpec((width, wide), lambda i: (0, lanes + i)),
            pl.BlockSpec((width, wide), lambda i: (0, lanes + steps + i)),
            pl.BlockSpec((wide, width), lambda i: (i, 0)),
        ],
        out_specs=specs,
        out_shape=shapes,
        scratch_shapes=[
            pltpu.VMEM((rows, width), F32),
            pltpu.VMEM((rows, width), BF16),
            pltpu.VMEM((width, rows), BF16),
            pltpu.VMEM((rows, width), F32),
            pltpu.VMEM((rows, width), F32),
            pltpu.VMEM((2, span, share, wide), BF16),
            pltpu.VMEM((2, span, share, wide), BF16),
            pltpu.VMEM((hidden_width, width), BF16),
            pltpu.VMEM((lanes, span, share, wide), BF16),
            pltpu.SemaphoreType.DMA((2, 2)),
            pltpu.SemaphoreType.DMA(((span * lanes if merged else 1) + lanes,)),
        ],
        compiler_params=pltpu.CompilerParams(vmem_limit_bytes=56 * MIB),
        cost_estimate=pl.CostEstimate(
            flops=6 * rows * width * (3 * hidden_width + width),
            bytes_accessed=4 * width * (3 * hidden_width + width),
            transcendentals=rows * hidden_width,
        ),
        name="feed_forward",
    )(tokens, attended, upstream, gain, weights, weights, weights, w_down)


def after(value, earlier):
    return lax.optimization_barrier((value, earlier))[0]


def chain_gather(block, axis):
    size = lax.axis_size(axis)
    place = lax.axis_index(axis)
    from_below, from_above = [], []
    rising = falling = block
    for step in range(size - 1):
        rising = lax.ppermute(rising, axis, [(i, i + 1) for i in range(step, size - 1)])
        falling = lax.ppermute(falling, axis, [(i + 1, i) for i in range(size - 1 - step)])
        from_below.append(rising)
        from_above.append(falling)
    ordered = []
    for index in range(size):
        cases = []
        for mine in range(size):
            if mine == index:
                cases.append(block)
            elif mine > index:
                cases.append(from_below[mine - index - 1])
            else:
                cases.append(from_above[index - mine - 1])
        ordered.append(lax.select_n(place, *cases) if size > 2 else lax.select_n(place > 0, *cases))
    return ordered, list(zip(from_below, from_above))


def chain_scatter(partial, axis):
    size = lax.axis_size(axis)
    place = lax.axis_index(axis)
    rows = partial.shape[0] // size

    def block(index):
        return lax.dynamic_slice_in_dim(partial, jnp.clip(index, 0, size - 1) * rows, rows, 0).astype(F32)

    rising = falling = None
    for step in range(size - 1):
        up, down = block(size - 1 - step + place), block(step - size + 1 + place)
        if step:
            up, down = up + rising.astype(F32), down + falling.astype(F32)
        rising = lax.ppermute(up.astype(BF16), axis, [(i, i + 1) for i in range(step + 1)])
        falling = lax.ppermute(
            down.astype(BF16), axis, [(i, i - 1) for i in range(size - 1 - step, size)]
        )
    return block(place) + rising.astype(F32) + falling.astype(F32)


def body(
    tokens, memory_keys, memory_values, chosen, counts, w_query, w_key, w_value, w_out, w_gate, w_up, w_down,
    gain_attn, gain_ffn, cotangent,
):
    ring, span = lax.axis_size("fsdp"), lax.axis_size("dp")
    rows, width = tokens.shape[1:]
    heads = width // HEAD_DIM // ring
    wide = heads * HEAD_DIM
    length = rows * ring
    top = chosen.shape[2]
    hidden_width = w_gate.shape[1]
    share = w_query.shape[0]
    mine = tokens[0]

    extra = 8 if share % 8 == 0 else 8 - share % 8
    parts = [w.reshape(share, ring, wide).transpose(1, 0, 2) for w in (w_query, w_key, w_value)]
    choices = jnp.concatenate([chosen[0].reshape(-1), counts[0].reshape(-1)]).astype(BF16)
    notes = jnp.stack(
        [
            jnp.pad(row, (0, 3 * wide - row.shape[0]))
            for row in (jnp.concatenate([gain_attn, gain_ffn]), choices)
        ]
    )
    notes = jnp.broadcast_to(jnp.pad(notes, ((0, extra - 2), (0, 0))), (ring, extra, 3 * wide))
    parcel = jnp.concatenate([jnp.concatenate(parts, 2), notes], 1)
    parcel = lax.all_to_all(parcel, "fsdp", 0, 0, tiled=True)
    picks = parcel[:, share + 1, : choices.shape[0]].astype(jnp.int32).reshape(ring, 2, -1)
    chosen_all, counts_all = picks[:, 0].reshape(-1), picks[:, 1].reshape(-1)
    shards = jnp.concatenate([w_out, w_gate, w_up], 1)
    near, steps = chain_gather(shards, "fsdp")
    near_down, down_steps = chain_gather(after(w_down, steps[0]), "fsdp")
    gathered, token_steps = chain_gather(after(mine, down_steps[-2]), "fsdp")
    parcel = lax.all_gather(parcel, "dp", axis=0, tiled=True)
    w_qkv = parcel[:, :share].reshape(width, 3 * wide)
    gain_one = parcel[:, share, :share].reshape(1, width).astype(F32)
    gain_two = parcel[:, share, share : 2 * share].reshape(1, width).astype(F32)
    first = lax.all_gather(after(jnp.concatenate(near, 0), w_qkv), "dp", axis=0, tiled=True)
    gathered = jnp.concatenate(gathered, 0)

    memory = jnp.concatenate(
        [m[0].reshape(-1, ring, wide).transpose(1, 0, 2) for m in (memory_keys, memory_values)], 2
    )
    memory = lax.all_to_all(after(memory, token_steps[-2]), "fsdp", 0, 0, tiled=True).reshape(-1, 2 * wide)
    down_full = lax.all_gather(after(jnp.concatenate(near_down, 0), first), "dp", axis=0, tiled=True)

    cosine, sine = rotary_tables(length)
    qkv = project_qkv(gathered, gain_one, w_qkv, cosine, sine, heads)
    attended_heads, lse = attend_forward(chosen_all, counts_all, qkv, memory, heads, top)
    attended = lax.all_to_all(attended_heads, "fsdp", 0, 1, tiled=True)

    upstream = cotangent[0]
    mixed, grad_middle, grad_attended, gain_two_grad, grads, *grad_down = feed_forward(
        mine, attended, upstream, gain_two, first, down_full, span
    )
    grad_heads = lax.all_to_all(grad_attended, "fsdp", 1, 0, tiled=True)
    grads = lax.psum_scatter(grads, "dp", scatter_dimension=0, tiled=True)[0]

    partial, grad_w_qkv, gain_one_grad = attend_backward(
        chosen_all, counts_all, qkv, memory, grad_heads, attended_heads, lse, cosine, sine, gathered, gain_one,
        w_qkv, heads, top,
    )
    grad_normed = chain_scatter(partial, "fsdp")
    own = mine.astype(F32)
    factor = lax.rsqrt(jnp.mean(own * own, -1, keepdims=True) + EPSILON)
    scaled = grad_normed * gain_one
    inner = jnp.mean(scaled * own, -1, keepdims=True)
    tokens_grad = (grad_middle + factor * scaled - own * (factor * factor * factor * inner)).astype(BF16)

    def along_z(pieces):
        return jnp.sum(lax.all_to_all(pieces, "fsdp", 0, 0, tiled=True).astype(F32), 0)

    gains = jnp.concatenate([gain_one_grad, gain_two_grad], 0).reshape(2, span, -1).transpose(1, 0, 2)
    gains = jnp.pad(gains.astype(BF16), ((0, 0), (0, extra - 2), (0, 3 * wide - gains.shape[2])))
    late = jnp.concatenate([grad_w_qkv.reshape(span, -1, 3 * wide), gains], 1)
    late = jnp.sum(lax.all_to_all(late, "dp", 0, 0, tiled=True).astype(F32), 0).astype(BF16)
    gains = late[-extra : 2 - extra, : ring * share].reshape(2, ring, share).transpose(1, 0, 2)
    gains = jnp.pad(gains, ((0, 0), (0, extra - 2), (0, 3 * wide - share)))
    late = jnp.concatenate([late[:-extra].reshape(ring, share, 3 * wide), gains], 1)
    late = lax.all_to_all(late, "fsdp", 0, 0, tiled=True).astype(F32)
    projections = [
        late[:, :share, part * wide : (part + 1) * wide].transpose(1, 0, 2).reshape(share, width)
        for part in range(3)
    ]
    gain_shares = jnp.sum(late[:, share : share + 2, :share], 0)

    strip = grads.shape[1]
    lanes = width // strip
    tall = w_down.shape[0]
    if grad_down:
        down = lax.psum_scatter(grad_down[0], "dp", scatter_dimension=0, tiled=True)
        down = down.reshape(ring, tall, lanes, strip).transpose(0, 2, 1, 3)
    else:
        down = grads[: ring * tall * lanes].reshape(lanes, ring, tall, strip).transpose(1, 0, 2, 3)
        grads = grads[ring * tall * lanes :]
    grads = grads.reshape(-1, ring, share, strip).transpose(1, 0, 2, 3)
    pieces = along_z(
        jnp.concatenate([down.reshape(ring, -1, strip), grads.reshape(ring, -1, strip)], 1)
    )
    down_share = pieces[: lanes * tall].reshape(lanes, tall, strip).transpose(1, 0, 2).reshape(tall, width)
    others = pieces[lanes * tall :].reshape(-1, share, strip).transpose(1, 0, 2).reshape(share, -1)
    return (
        mixed[None],
        tokens_grad[None],
        *projections,
        others[:, :width],
        others[:, width : width + hidden_width],
        others[:, width + hidden_width :],
        down_share,
        gain_shares[0],
        gain_shares[1],
    )


def solution(mesh):
    both = ("dp", "fsdp")
    rows, matrix, vector = P("dp", "fsdp", None), P(both, None), P(both)
    in_specs = (rows,) * 5 + (matrix,) * 7 + (vector,) * 2 + (rows,)
    out_specs = (rows,) * 2 + (matrix,) * 7 + (vector,) * 2
    return jax.shard_map(body, mesh=mesh, in_specs=in_specs, out_specs=out_specs, check_vma=False)
```

```python
import functools
import math

import jax
import jax.numpy as jnp
import numpy as np
from jax import lax
from jax.experimental import pallas as pl
from jax.experimental.pallas import tpu as pltpu
from jax.sharding import PartitionSpec as P

HEAD_DIM = 128
QBLK = 256
MBLK = 128
EPSILON = 1e-06
NEGATIVE = -1e30
SCALE = 1.0 / math.sqrt(HEAD_DIM)
LOG2E = math.log2(math.e)
MIB = 1 << 20
F32 = jnp.float32
BF16 = jnp.bfloat16
NT = (((1,), (1,)), ((), ()))
TN = (((0,), (0,)), ((), ()))


def dot(left, right, dims=(((1,), (0,)), ((), ()))):
    return lax.dot_general(left, right, dims, preferred_element_type=F32)


def rotary_tables(length):
    half_dim = HEAD_DIM // 2
    frequency = 10000.0 ** (-jnp.arange(half_dim, dtype=F32) / half_dim)
    angles = jnp.arange(length, dtype=jnp.int32).astype(F32)[:, None] * frequency[None, :]
    cosine, sine = jnp.cos(angles), jnp.sin(angles)
    return jnp.concatenate([cosine, cosine], 1), jnp.concatenate([-sine, sine], 1)


def qkv_kernel(heads, tok_ref, gain_ref, w_ref, cos_ref, sin_ref, qkv_ref):
    rows = tok_ref[...].astype(F32)
    factor = lax.rsqrt(jnp.mean(rows * rows, -1, keepdims=True) + EPSILON)
    normed = (rows * factor * gain_ref[...]).astype(BF16)
    cosine, sine = cos_ref[...], sin_ref[...]
    for part in range(3):
        for head in range(heads):
            columns = slice((part * heads + head) * HEAD_DIM, (part * heads + head + 1) * HEAD_DIM)
            value = dot(normed, w_ref[:, columns])
            if part < 2:
                value = value * cosine + pltpu.roll(value, HEAD_DIM // 2, 1) * sine
            qkv_ref[:, columns] = value.astype(BF16)


def project_qkv(tokens_all, gain, w_qkv, cosine, sine, heads):
    length, width = tokens_all.shape
    columns = w_qkv.shape[1]
    block = QBLK
    return pl.pallas_call(
        functools.partial(qkv_kernel, heads),
        grid=(length // block,),
        in_specs=[
            pl.BlockSpec((block, width), lambda i: (i, 0)),
            pl.BlockSpec((1, width), lambda i: (0, 0)),
            pl.BlockSpec((width, columns), lambda i: (0, 0)),
            pl.BlockSpec((block, HEAD_DIM), lambda i: (i, 0)),
            pl.BlockSpec((block, HEAD_DIM), lambda i: (i, 0)),
        ],
        out_specs=pl.BlockSpec((block, columns), lambda i: (i, 0)),
        out_shape=jax.ShapeDtypeStruct((length, columns), BF16),
        compiler_params=pltpu.CompilerParams(vmem_limit_bytes=48 * MIB),
        cost_estimate=pl.CostEstimate(
            flops=2 * length * width * columns, bytes_accessed=4 * length * (width + columns), transcendentals=0
        ),
        name="project_qkv",
    )(tokens_all, gain, w_qkv, cosine, sine)


def memory_bias(counts_ref, base, top, axis):
    shape = (1, top * MBLK) if axis == 1 else (top * MBLK, 1)
    column = lax.broadcasted_iota(jnp.int32, shape, axis)
    limit = jnp.zeros(shape, jnp.int32)
    for entry in range(top):
        inside = (column >= entry * MBLK) & (column < entry * MBLK + counts_ref[base + entry])
        limit = jnp.where(inside, 1, limit)
    return jnp.where(limit > 0, 0.0, NEGATIVE)


def pick_memory(ref, chosen_ref, base, top, columns):
    rows = [
        ref[pl.ds(pl.multiple_of(chosen_ref[base + entry] * MBLK, MBLK), MBLK), columns]
        for entry in range(top)
    ]
    return jnp.concatenate(rows, 0)


def forward_kernel(heads, top, chosen_ref, counts_ref, q_ref, k_ref, v_ref, mk_ref, mv_ref, out_ref, lse_ref):
    block = pl.program_id(0)
    base = block * top
    bias = memory_bias(counts_ref, base, top, 1)
    row = lax.broadcasted_iota(jnp.int32, (QBLK, QBLK), 0)
    column = lax.broadcasted_iota(jnp.int32, (QBLK, QBLK), 1)
    causal = row >= column
    own = pl.ds(pl.multiple_of(block * QBLK, QBLK), QBLK)
    unit = SCALE * LOG2E
    states = []
    for head in range(heads):
        columns = slice(head * HEAD_DIM, (head + 1) * HEAD_DIM)
        query = q_ref[:, columns]
        remote = dot(query, pick_memory(mk_ref, chosen_ref, base, top, columns), NT) * unit + bias
        local = jnp.where(causal, dot(query, k_ref[own, columns], NT) * unit, NEGATIVE)
        peak = jnp.maximum(jnp.max(remote, -1, keepdims=True), jnp.max(local, -1, keepdims=True))
        remote = jnp.exp2(remote - peak)
        local = jnp.exp2(local - peak)
        total = jnp.sum(remote, -1, keepdims=True) + jnp.sum(local, -1, keepdims=True)
        acc = dot(remote.astype(BF16), pick_memory(mv_ref, chosen_ref, base, top, columns))
        acc = acc + dot(local.astype(BF16), v_ref[own, columns])
        states.append((peak, total, acc))

    def step(index, states):
        rows = pl.ds(pl.multiple_of(index * QBLK, QBLK), QBLK)
        after = []
        for head in range(heads):
            columns = slice(head * HEAD_DIM, (head + 1) * HEAD_DIM)
            peak, total, acc = states[head]
            scores = dot(q_ref[:, columns], k_ref[rows, columns], NT) * unit
            higher = jnp.maximum(peak, jnp.max(scores, -1, keepdims=True))
            shrink = jnp.exp2(peak - higher)
            weights = jnp.exp2(scores - higher)
            total = total * shrink + jnp.sum(weights, -1, keepdims=True)
            acc = acc * shrink + dot(weights.astype(BF16), v_ref[rows, columns])
            after.append((higher, total, acc))
        return tuple(after)

    states = lax.fori_loop(0, block, step, tuple(states))
    for head in range(heads):
        columns = slice(head * HEAD_DIM, (head + 1) * HEAD_DIM)
        peak, total, acc = states[head]
        out_ref[:, columns] = (acc / total).astype(BF16)
        lse_ref[:, head : head + 1] = peak + jnp.log2(total)


def attend_forward(chosen, counts, qkv, memory, heads, top):
    length = qkv.shape[0]
    wide = heads * HEAD_DIM
    blocks = length // QBLK
    mem_rows = memory.shape[0]
    return pl.pallas_call(
        functools.partial(forward_kernel, heads, top),
        grid_spec=pltpu.PrefetchScalarGridSpec(
            num_scalar_prefetch=2,
            grid=(blocks,),
            in_specs=[
                pl.BlockSpec((QBLK, wide), lambda i, *_: (i, 0)),
                pl.BlockSpec((length, wide), lambda i, *_: (0, 1)),
                pl.BlockSpec((length, wide), lambda i, *_: (0, 2)),
                pl.BlockSpec((mem_rows, wide), lambda i, *_: (0, 0)),
                pl.BlockSpec((mem_rows, wide), lambda i, *_: (0, 1)),
            ],
            out_specs=[
                pl.BlockSpec((QBLK, wide), lambda i, *_: (i, 0)),
                pl.BlockSpec((QBLK, heads), lambda i, *_: (i, 0)),
            ],
        ),
        out_shape=[
            jax.ShapeDtypeStruct((length, wide), BF16),
            jax.ShapeDtypeStruct((length, heads), F32),
        ],
        compiler_params=pltpu.CompilerParams(vmem_limit_bytes=48 * MIB),
        cost_estimate=pl.CostEstimate(
            flops=4 * heads * length * HEAD_DIM * (length // 2 + top * MBLK),
            bytes_accessed=8 * length * wide,
            transcendentals=heads * length * (length // 2 + top * MBLK),
        ),
        name="attend_forward",
    )(chosen, counts, qkv, qkv, qkv, memory, memory)


def backward_kernel(
    heads, top, blocks, chosen_ref, counts_ref, q_ref, k_ref, v_ref, mk_ref, mv_ref, go_ref, out_ref, lse_ref,
    cos_ref, sin_ref, tok_ref, gain_ref, w_ref, partial_ref, grad_w_ref, gain_grad_ref, gk_ref, gv_ref, grad_s, gw_s,
):
    block = blocks - 1 - pl.program_id(0)
    base = block * top
    unit = SCALE * LOG2E
    bias = memory_bias(counts_ref, base, top, 0)
    key_at = lax.broadcasted_iota(jnp.int32, (QBLK, QBLK), 0)
    query_at = lax.broadcasted_iota(jnp.int32, (QBLK, QBLK), 1)
    causal = query_at >= key_at
    own = pl.ds(pl.multiple_of(block * QBLK, QBLK), QBLK)

    @pl.when(pl.program_id(0) == 0)
    def _():
        gk_ref[...] = jnp.zeros_like(gk_ref)
        gv_ref[...] = jnp.zeros_like(gv_ref)
        gw_s[...] = jnp.zeros_like(gw_s)
        gain_grad_ref[...] = jnp.zeros_like(gain_grad_ref)

    def spread(column):
        return jnp.transpose(jnp.broadcast_to(column, (QBLK, HEAD_DIM)))[:1]

    stats = []
    for head in range(heads):
        columns = slice(head * HEAD_DIM, (head + 1) * HEAD_DIM)
        grad = go_ref[:, columns]
        delta = jnp.sum(grad.astype(F32) * out_ref[:, columns].astype(F32), -1, keepdims=True)
        stats.append((spread(lse_ref[:, head : head + 1]), spread(delta)))

    def pair(head, keys, values, mask):
        columns = slice(head * HEAD_DIM, (head + 1) * HEAD_DIM)
        lse, delta = stats[head]
        scores = mask(dot(keys, q_ref[:, columns], NT) * unit)
        weights = jnp.exp2(scores - lse)
        grad_weights = dot(values, go_ref[:, columns], NT)
        grad_scores = (weights * (grad_weights - delta)).astype(BF16)
        return weights.astype(BF16), grad_scores

    def update(head, rows, weights, grad_scores):
        columns = slice(head * HEAD_DIM, (head + 1) * HEAD_DIM)
        gk_ref[rows, columns] += dot(grad_scores, q_ref[:, columns])
        gv_ref[rows, columns] += dot(weights, go_ref[:, columns])

    totals = []
    for head in range(heads):
        columns = slice(head * HEAD_DIM, (head + 1) * HEAD_DIM)
        keys = pick_memory(mk_ref, chosen_ref, base, top, columns)
        values = pick_memory(mv_ref, chosen_ref, base, top, columns)
        _, grad_scores = pair(head, keys, values, lambda scores: scores + bias)
        total = dot(grad_scores, keys, TN)
        keys = k_ref[own, columns]
        weights, grad_scores = pair(
            head, keys, v_ref[own, columns], lambda scores: jnp.where(causal, scores, NEGATIVE)
        )
        update(head, own, weights, grad_scores)
        totals.append(total + dot(grad_scores, keys, TN))

    def step(index, totals):
        rows = pl.ds(pl.multiple_of(index * QBLK, QBLK), QBLK)
        after = []
        for head in range(heads):
            columns = slice(head * HEAD_DIM, (head + 1) * HEAD_DIM)
            keys = k_ref[rows, columns]
            weights, grad_scores = pair(head, keys, v_ref[rows, columns], lambda scores: scores)
            update(head, rows, weights, grad_scores)
            after.append(totals[head] + dot(grad_scores, keys, TN))
        return tuple(after)

    totals = lax.fori_loop(0, block, step, tuple(totals))
    cosine, sine = cos_ref[...], sin_ref[...]

    def unturn(value):
        return value * cosine - pltpu.roll(value, HEAD_DIM // 2, 1) * sine

    wide = heads * HEAD_DIM
    for head in range(heads):
        columns = slice(head * HEAD_DIM, (head + 1) * HEAD_DIM)
        at = head * HEAD_DIM
        grad_s[:, at : at + HEAD_DIM] = unturn(totals[head] * SCALE).astype(BF16)
        grad_key = gk_ref[own, columns] * SCALE
        grad_s[:, wide + at : wide + at + HEAD_DIM] = unturn(grad_key).astype(BF16)
        grad_s[:, 2 * wide + at : 2 * wide + at + HEAD_DIM] = gv_ref[own, columns].astype(BF16)

    rows = tok_ref[...].astype(F32)
    rows = rows * lax.rsqrt(jnp.mean(rows * rows, -1, keepdims=True) + EPSILON)
    normed = (rows * gain_ref[...]).astype(BF16)
    grad = grad_s[...]
    partial = dot(grad, w_ref[...], NT)
    partial_ref[...] = partial.astype(BF16)
    gain_grad_ref[...] += jnp.sum(partial * rows, 0, keepdims=True)
    gw_s[...] += dot(normed, grad, TN)

    @pl.when(block == 0)
    def _():
        grad_w_ref[...] = gw_s[...].astype(BF16)


def attend_backward(
    chosen, counts, qkv, memory, grad_out, out, lse, cosine, sine, tokens_all, gain, w_qkv, heads, top
):
    length = qkv.shape[0]
    width = tokens_all.shape[1]
    wide = heads * HEAD_DIM
    blocks = length // QBLK
    mem_rows = memory.shape[0]
    last = blocks - 1
    return pl.pallas_call(
        functools.partial(backward_kernel, heads, top, blocks),
        grid_spec=pltpu.PrefetchScalarGridSpec(
            num_scalar_prefetch=2,
            grid=(blocks,),
            in_specs=[
                pl.BlockSpec((QBLK, wide), lambda i, *_: (last - i, 0)),
                pl.BlockSpec((length, wide), lambda i, *_: (0, 1)),
                pl.BlockSpec((length, wide), lambda i, *_: (0, 2)),
                pl.BlockSpec((mem_rows, wide), lambda i, *_: (0, 0)),
                pl.BlockSpec((mem_rows, wide), lambda i, *_: (0, 1)),
                pl.BlockSpec((QBLK, wide), lambda i, *_: (last - i, 0)),
                pl.BlockSpec((QBLK, wide), lambda i, *_: (last - i, 0)),
                pl.BlockSpec((QBLK, heads), lambda i, *_: (last - i, 0)),
                pl.BlockSpec((QBLK, HEAD_DIM), lambda i, *_: (last - i, 0)),
                pl.BlockSpec((QBLK, HEAD_DIM), lambda i, *_: (last - i, 0)),
                pl.BlockSpec((QBLK, width), lambda i, *_: (last - i, 0)),
                pl.BlockSpec((1, width), lambda i, *_: (0, 0)),
                pl.BlockSpec((width, 3 * wide), lambda i, *_: (0, 0)),
            ],
            out_specs=[
                pl.BlockSpec((QBLK, width), lambda i, *_: (last - i, 0)),
                pl.BlockSpec((width, 3 * wide), lambda i, *_: (0, 0)),
                pl.BlockSpec((1, width), lambda i, *_: (0, 0)),
            ],
            scratch_shapes=[
                pltpu.VMEM((length, wide), F32),
                pltpu.VMEM((length, wide), F32),
                pltpu.VMEM((QBLK, 3 * wide), BF16),
                pltpu.VMEM((width, 3 * wide), F32),
            ],
        ),
        out_shape=[
            jax.ShapeDtypeStruct((length, width), BF16),
            jax.ShapeDtypeStruct((width, 3 * wide), BF16),
            jax.ShapeDtypeStruct((1, width), F32),
        ],
        compiler_params=pltpu.CompilerParams(vmem_limit_bytes=48 * MIB),
        cost_estimate=pl.CostEstimate(
            flops=10 * heads * length * HEAD_DIM * (length // 2 + top * MBLK),
            bytes_accessed=16 * length * wide,
            transcendentals=heads * length * (length // 2 + top * MBLK),
        ),
        name="attend_backward",
    )(
        chosen, counts, qkv, qkv, qkv, memory, memory, grad_out, out, lse, cosine, sine, tokens_all, gain, w_qkv
    )


def ffn_kernel(
    span, merged, tok_ref, att_ref, cot_ref, gain_ref, out_w, gate_w, up_w, down_w,
    mixed_ref, grad_mid_ref, grad_att_ref, gain_grad_ref, grads_ref, *rest,
):
    if not merged:
        down_grads_ref, rest = rest[0], rest[1:]
    middle_s, normed_s, turned_s, mixed_s, upstream_s, gate_s, up_s, down_s, out_s, sems, late_sems = rest
    step, steps = pl.program_id(0), pl.num_programs(0)
    width = tok_ref.shape[1]
    share = width // span
    wide = gate_w.shape[1]
    hidden_width = down_s.shape[0]
    tall = hidden_width // span
    lanes = width // wide
    first = tall * lanes if merged else 0
    slot = step % 2

    @pl.when(step == 0)
    def _():
        middle = tok_ref[...].astype(F32) + dot(att_ref[...], out_w[...])
        middle_s[...] = middle
        factor = lax.rsqrt(jnp.mean(middle * middle, -1, keepdims=True) + EPSILON)
        normed = (middle * factor * gain_ref[...]).astype(BF16)
        normed_s[...] = normed
        turned_s[...] = jnp.transpose(normed)
        mixed_s[...] = middle
        upstream_s[...] = jnp.zeros_like(upstream_s)

    def copy_out(kind, which, index):
        source = (gate_s, up_s)[kind].at[which]
        start = first + (lanes + kind * steps + index) * share
        target = grads_ref.at[:, pl.ds(start, share), :]
        return pltpu.make_async_copy(source, target, sems.at[kind, which])

    normed = normed_s[...]
    upstream = cot_ref[...]
    gate_act = dot(normed, gate_w[...])
    up_act = dot(normed, up_w[...])
    grad_hidden = dot(upstream, down_w[...], NT)
    sigmoid = jax.nn.sigmoid(gate_act)
    silu = gate_act * sigmoid
    hidden = (silu * up_act).astype(BF16)
    grad_gate = (grad_hidden * up_act * sigmoid * (1.0 + gate_act * (1.0 - sigmoid))).astype(BF16)
    grad_up = (grad_hidden * silu).astype(BF16)
    mixed_s[...] += dot(hidden, down_w[...])
    upstream_s[...] += dot(grad_gate, gate_w[...], NT) + dot(grad_up, up_w[...], NT)
    down_s[pl.ds(pl.multiple_of(step * wide, wide), wide), :] = dot(hidden, upstream, TN).astype(BF16)

    @pl.when(step >= 2)
    def _():
        copy_out(0, slot, step - 2).wait()
        copy_out(1, slot, step - 2).wait()

    turned = turned_s[...]
    gate_s[slot] = dot(turned, grad_gate).astype(BF16).reshape(span, share, wide)
    up_s[slot] = dot(turned, grad_up).astype(BF16).reshape(span, share, wide)
    copy_out(0, slot, step).start()
    copy_out(1, slot, step).start()

    @pl.when(step == steps - 1)
    def _():
        copies = []
        if merged:
            for place in range(span):
                for lane in range(lanes):
                    copies.append(
                        pltpu.make_async_copy(
                            down_s.at[pl.ds(place * tall, tall), pl.ds(lane * wide, wide)],
                            grads_ref.at[place, pl.ds(lane * tall, tall), :],
                            late_sems.at[len(copies)],
                        )
                    )
        else:
            copies.append(pltpu.make_async_copy(down_s, down_grads_ref, late_sems.at[0]))
        for copy in copies:
            copy.start()
        mixed_ref[...] = mixed_s[...].astype(BF16)
        middle = middle_s[...]
        grad = upstream_s[...]
        factor = lax.rsqrt(jnp.mean(middle * middle, -1, keepdims=True) + EPSILON)
        gain_grad_ref[...] = jnp.sum(grad * middle * factor, 0, keepdims=True)
        scaled = grad * gain_ref[...]
        inner = jnp.mean(scaled * middle, -1, keepdims=True)
        grad_middle = cot_ref[...].astype(F32) + factor * scaled - middle * (factor * factor * factor * inner)
        grad_mid_ref[...] = grad_middle
        branch = grad_middle.astype(BF16)
        grad_att_ref[...] = dot(branch, out_w[...], NT).astype(BF16)
        turned_att = jnp.transpose(att_ref[...])
        for lane in range(lanes):
            columns = slice(lane * wide, (lane + 1) * wide)
            out_s[lane] = dot(turned_att, branch[:, columns]).astype(BF16).reshape(span, share, wide)
            more = pltpu.make_async_copy(
                out_s.at[lane],
                grads_ref.at[:, pl.ds(first + lane * share, share), :],
                late_sems.at[len(copies)],
            )
            more.start()
            copies.append(more)
        for copy in copies:
            copy.wait()
        copy_out(0, 1 - slot, step - 1).wait()
        copy_out(1, 1 - slot, step - 1).wait()
        copy_out(0, slot, step).wait()
        copy_out(1, slot, step).wait()


def feed_forward(tokens, attended, upstream, gain, weights, w_down, span):
    rows, width = tokens.shape
    hidden_width = w_down.shape[0]
    wide = 2 * HEAD_DIM
    steps = hidden_width // wide
    lanes = width // wide
    share = width // span
    tall = hidden_width // span
    merged = tall % 16 == 0
    total = (lanes + 2 * steps) * share + (lanes * tall if merged else 0)
    shapes = [
        jax.ShapeDtypeStruct((rows, width), BF16),
        jax.ShapeDtypeStruct((rows, width), F32),
        jax.ShapeDtypeStruct((rows, width), BF16),
        jax.ShapeDtypeStruct((1, width), F32),
        jax.ShapeDtypeStruct((span, total, wide), BF16),
    ]
    specs = [
        pl.BlockSpec((rows, width), lambda i: (0, 0)),
        pl.BlockSpec((rows, width), lambda i: (0, 0)),
        pl.BlockSpec((rows, width), lambda i: (0, 0)),
        pl.BlockSpec((1, width), lambda i: (0, 0)),
        pl.BlockSpec(memory_space=pl.ANY),
    ]
    if not merged:
        shapes.append(jax.ShapeDtypeStruct((hidden_width, width), BF16))
        specs.append(pl.BlockSpec(memory_space=pl.ANY))
    return pl.pallas_call(
        functools.partial(ffn_kernel, span, merged),
        grid=(steps,),
        in_specs=[
            pl.BlockSpec((rows, width), lambda i: (0, 0)),
            pl.BlockSpec((rows, width), lambda i: (0, 0)),
            pl.BlockSpec((rows, width), lambda i: (0, 0)),
            pl.BlockSpec((1, width), lambda i: (0, 0)),
            pl.BlockSpec((width, width), lambda i: (0, 0)),
            pl.BlockSpec((width, wide), lambda i: (0, lanes + i)),
            pl.BlockSpec((width, wide), lambda i: (0, lanes + steps + i)),
            pl.BlockSpec((wide, width), lambda i: (i, 0)),
        ],
        out_specs=specs,
        out_shape=shapes,
        scratch_shapes=[
            pltpu.VMEM((rows, width), F32),
            pltpu.VMEM((rows, width), BF16),
            pltpu.VMEM((width, rows), BF16),
            pltpu.VMEM((rows, width), F32),
            pltpu.VMEM((rows, width), F32),
            pltpu.VMEM((2, span, share, wide), BF16),
            pltpu.VMEM((2, span, share, wide), BF16),
            pltpu.VMEM((hidden_width, width), BF16),
            pltpu.VMEM((lanes, span, share, wide), BF16),
            pltpu.SemaphoreType.DMA((2, 2)),
            pltpu.SemaphoreType.DMA(((span * lanes if merged else 1) + lanes,)),
        ],
        compiler_params=pltpu.CompilerParams(vmem_limit_bytes=56 * MIB),
        cost_estimate=pl.CostEstimate(
            flops=6 * rows * width * (3 * hidden_width + width),
            bytes_accessed=4 * width * (3 * hidden_width + width),
            transcendentals=rows * hidden_width,
        ),
        name="feed_forward",
    )(tokens, attended, upstream, gain, weights, weights, weights, w_down)


def after(value, earlier):
    return lax.optimization_barrier((value, earlier))[0]


def chain_gather(blocks, axis):
    size = lax.axis_size(axis)
    place = lax.axis_index(axis)
    steps = []
    rising = falling = tuple(blocks)
    for step in range(size - 1):
        up = [(i, i + 1) for i in range(step, size - 1)]
        down = [(i + 1, i) for i in range(size - 1 - step)]
        rising = tuple(lax.ppermute(block, axis, up) for block in rising)
        falling = tuple(lax.ppermute(block, axis, down) for block in falling)
        if len(blocks) > 1:
            rising, falling = lax.optimization_barrier((rising, falling))
        steps.append((rising, falling))
    results = []
    for number, block in enumerate(blocks):
        ordered = []
        for index in range(size):
            cases = []
            for mine in range(size):
                if mine == index:
                    cases.append(block)
                elif mine > index:
                    cases.append(steps[mine - index - 1][0][number])
                else:
                    cases.append(steps[index - mine - 1][1][number])
            ordered.append(lax.select_n(place, *cases) if size > 2 else lax.select_n(place > 0, *cases))
        results.append(ordered)
    return results, steps


def chain_scatter(partial, axis):
    size = lax.axis_size(axis)
    place = lax.axis_index(axis)
    rows = partial.shape[0] // size

    def block(index):
        return lax.dynamic_slice_in_dim(partial, jnp.clip(index, 0, size - 1) * rows, rows, 0).astype(F32)

    rising = falling = None
    for step in range(size - 1):
        up, down = block(size - 1 - step + place), block(step - size + 1 + place)
        if step:
            up, down = up + rising.astype(F32), down + falling.astype(F32)
        rising = lax.ppermute(up.astype(BF16), axis, [(i, i + 1) for i in range(step + 1)])
        falling = lax.ppermute(
            down.astype(BF16), axis, [(i, i - 1) for i in range(size - 1 - step, size)]
        )
    return block(place) + rising.astype(F32) + falling.astype(F32), (rising, falling)


def body(
    tokens, memory_keys, memory_values, chosen, counts, w_query, w_key, w_value, w_out, w_gate, w_up, w_down,
    gain_attn, gain_ffn, cotangent,
):
    ring, span = lax.axis_size("fsdp"), lax.axis_size("dp")
    rows, width = tokens.shape[1:]
    heads = width // HEAD_DIM // ring
    wide = heads * HEAD_DIM
    length = rows * ring
    top = chosen.shape[2]
    hidden_width = w_gate.shape[1]
    share = w_query.shape[0]
    mine = tokens[0]

    extra = 8 if share % 8 == 0 else 8 - share % 8
    parts = [w.reshape(share, ring, wide).transpose(1, 0, 2) for w in (w_query, w_key, w_value)]
    choices = jnp.concatenate([chosen[0].reshape(-1), counts[0].reshape(-1)]).astype(BF16)
    notes = jnp.stack(
        [
            jnp.pad(row, (0, 3 * wide - row.shape[0]))
            for row in (jnp.concatenate([gain_attn, gain_ffn]), choices)
        ]
    )
    notes = jnp.broadcast_to(jnp.pad(notes, ((0, extra - 2), (0, 0))), (ring, extra, 3 * wide))
    parcel = jnp.concatenate([jnp.concatenate(parts, 2), notes], 1)
    parcel = lax.all_to_all(parcel, "fsdp", 0, 0, tiled=True)
    picks = parcel[:, share + 1, : choices.shape[0]].astype(jnp.int32).reshape(ring, 2, -1)
    chosen_all, counts_all = picks[:, 0].reshape(-1), picks[:, 1].reshape(-1)
    shards = jnp.concatenate([w_out, w_gate, w_up], 1)
    (near, near_down), steps = chain_gather((shards, w_down), "fsdp")
    (gathered,), token_steps = chain_gather((after(mine, steps[-2]),), "fsdp")
    parcel = lax.all_gather(parcel, "dp", axis=0, tiled=True)
    w_qkv = parcel[:, :share].reshape(width, 3 * wide)
    gain_one = parcel[:, share, :share].reshape(1, width).astype(F32)
    gain_two = parcel[:, share, share : 2 * share].reshape(1, width).astype(F32)
    first = lax.all_gather(jnp.concatenate(near, 0), "dp", axis=0, tiled=True)
    gathered = jnp.concatenate(gathered, 0)

    memory = jnp.concatenate(
        [m[0].reshape(-1, ring, wide).transpose(1, 0, 2) for m in (memory_keys, memory_values)], 2
    )
    memory = lax.all_to_all(after(memory, token_steps[-2]), "fsdp", 0, 0, tiled=True).reshape(-1, 2 * wide)
    down_full = lax.all_gather(jnp.concatenate(near_down, 0), "dp", axis=0, tiled=True)

    cosine, sine = rotary_tables(length)
    qkv = project_qkv(gathered, gain_one, w_qkv, cosine, sine, heads)
    attended_heads, lse = attend_forward(chosen_all, counts_all, qkv, memory, heads, top)
    attended = lax.all_to_all(attended_heads, "fsdp", 0, 1, tiled=True)

    upstream = cotangent[0]
    mixed, grad_middle, grad_attended, gain_two_grad, grads, *grad_down = feed_forward(
        mine, attended, upstream, gain_two, first, down_full, span
    )
    grad_heads = lax.all_to_all(grad_attended, "fsdp", 1, 0, tiled=True)
    grads = lax.psum_scatter(grads, "dp", scatter_dimension=0, tiled=True)[0]

    partial, grad_w_qkv, gain_one_grad = attend_backward(
        chosen_all, counts_all, qkv, memory, grad_heads, attended_heads, lse, cosine, sine, gathered, gain_one,
        w_qkv, heads, top,
    )
    grad_normed, last_step = chain_scatter(partial, "fsdp")
    grads = after(grads, last_step)
    own = mine.astype(F32)
    factor = lax.rsqrt(jnp.mean(own * own, -1, keepdims=True) + EPSILON)
    scaled = grad_normed * gain_one
    inner = jnp.mean(scaled * own, -1, keepdims=True)
    tokens_grad = (grad_middle + factor * scaled - own * (factor * factor * factor * inner)).astype(BF16)

    def along_z(pieces):
        return jnp.sum(lax.all_to_all(pieces, "fsdp", 0, 0, tiled=True).astype(F32), 0)

    gains = jnp.concatenate([gain_one_grad, gain_two_grad], 0).reshape(2, span, -1).transpose(1, 0, 2)
    gains = jnp.pad(gains.astype(BF16), ((0, 0), (0, extra - 2), (0, 3 * wide - gains.shape[2])))
    late = jnp.concatenate([grad_w_qkv.reshape(span, -1, 3 * wide), gains], 1)
    late = jnp.sum(lax.all_to_all(late, "dp", 0, 0, tiled=True).astype(F32), 0).astype(BF16)
    gains = late[-extra : 2 - extra, : ring * share].reshape(2, ring, share).transpose(1, 0, 2)
    gains = jnp.pad(gains, ((0, 0), (0, extra - 2), (0, 3 * wide - share)))
    late = jnp.concatenate([late[:-extra].reshape(ring, share, 3 * wide), gains], 1)
    late = lax.all_to_all(late, "fsdp", 0, 0, tiled=True).astype(F32)
    projections = [
        late[:, :share, part * wide : (part + 1) * wide].transpose(1, 0, 2).reshape(share, width)
        for part in range(3)
    ]
    gain_shares = jnp.sum(late[:, share : share + 2, :share], 0)

    strip = grads.shape[1]
    lanes = width // strip
    tall = w_down.shape[0]
    if grad_down:
        down = lax.psum_scatter(grad_down[0], "dp", scatter_dimension=0, tiled=True)
        down = down.reshape(ring, tall, lanes, strip).transpose(0, 2, 1, 3)
    else:
        down = grads[: ring * tall * lanes].reshape(lanes, ring, tall, strip).transpose(1, 0, 2, 3)
        grads = grads[ring * tall * lanes :]
    grads = grads.reshape(-1, ring, share, strip).transpose(1, 0, 2, 3)
    pieces = along_z(
        jnp.concatenate([down.reshape(ring, -1, strip), grads.reshape(ring, -1, strip)], 1)
    )
    down_share = pieces[: lanes * tall].reshape(lanes, tall, strip).transpose(1, 0, 2).reshape(tall, width)
    others = pieces[lanes * tall :].reshape(-1, share, strip).transpose(1, 0, 2).reshape(share, -1)
    return (
        mixed[None],
        tokens_grad[None],
        *projections,
        others[:, :width],
        others[:, width : width + hidden_width],
        others[:, width + hidden_width :],
        down_share,
        gain_shares[0],
        gain_shares[1],
    )


def solution(mesh):
    both = ("dp", "fsdp")
    rows, matrix, vector = P("dp", "fsdp", None), P(both, None), P(both)
    in_specs = (rows,) * 5 + (matrix,) * 7 + (vector,) * 2 + (rows,)
    out_specs = (rows,) * 2 + (matrix,) * 7 + (vector,) * 2
    return jax.shard_map(body, mesh=mesh, in_specs=in_specs, out_specs=out_specs, check_vma=False)
```

```python
import functools
import math

import jax
import jax.numpy as jnp
import numpy as np
from jax import lax
from jax.experimental import pallas as pl
from jax.experimental.pallas import tpu as pltpu
from jax.sharding import PartitionSpec as P

HEAD_DIM = 128
QBLK = 256
MBLK = 128
EPSILON = 1e-06
NEGATIVE = -1e30
SCALE = 1.0 / math.sqrt(HEAD_DIM)
LOG2E = math.log2(math.e)
MIB = 1 << 20
F32 = jnp.float32
BF16 = jnp.bfloat16
NT = (((1,), (1,)), ((), ()))
TN = (((0,), (0,)), ((), ()))


def dot(left, right, dims=(((1,), (0,)), ((), ()))):
    return lax.dot_general(left, right, dims, preferred_element_type=F32)


def rotary_tables(length):
    half_dim = HEAD_DIM // 2
    frequency = 10000.0 ** (-jnp.arange(half_dim, dtype=F32) / half_dim)
    angles = jnp.arange(length, dtype=jnp.int32).astype(F32)[:, None] * frequency[None, :]
    cosine, sine = jnp.cos(angles), jnp.sin(angles)
    return jnp.concatenate([cosine, cosine], 1), jnp.concatenate([-sine, sine], 1)


def qkv_kernel(heads, tok_ref, gain_ref, w_ref, cos_ref, sin_ref, qkv_ref):
    rows = tok_ref[...].astype(F32)
    factor = lax.rsqrt(jnp.mean(rows * rows, -1, keepdims=True) + EPSILON)
    normed = (rows * factor * gain_ref[...]).astype(BF16)
    cosine, sine = cos_ref[...], sin_ref[...]
    wide = heads * HEAD_DIM
    for part in range(3):
        values = dot(normed, w_ref[:, part * wide : (part + 1) * wide])
        for head in range(heads):
            value = values[:, head * HEAD_DIM : (head + 1) * HEAD_DIM]
            if part < 2:
                value = value * cosine + pltpu.roll(value, HEAD_DIM // 2, 1) * sine
            if part == 0:
                value = value * (SCALE * LOG2E)
            at = part * wide + head * HEAD_DIM
            qkv_ref[:, at : at + HEAD_DIM] = value.astype(BF16)


def project_qkv(tokens_all, gain, w_qkv, cosine, sine, heads):
    length, width = tokens_all.shape
    columns = w_qkv.shape[1]
    block = 2 * QBLK
    return pl.pallas_call(
        functools.partial(qkv_kernel, heads),
        grid=(length // block,),
        in_specs=[
            pl.BlockSpec((block, width), lambda i: (i, 0)),
            pl.BlockSpec((1, width), lambda i: (0, 0)),
            pl.BlockSpec((width, columns), lambda i: (0, 0)),
            pl.BlockSpec((block, HEAD_DIM), lambda i: (i, 0)),
            pl.BlockSpec((block, HEAD_DIM), lambda i: (i, 0)),
        ],
        out_specs=pl.BlockSpec((block, columns), lambda i: (i, 0)),
        out_shape=jax.ShapeDtypeStruct((length, columns), BF16),
        compiler_params=pltpu.CompilerParams(vmem_limit_bytes=48 * MIB),
        cost_estimate=pl.CostEstimate(
            flops=2 * length * width * columns, bytes_accessed=4 * length * (width + columns), transcendentals=0
        ),
        name="project_qkv",
    )(tokens_all, gain, w_qkv, cosine, sine)


def memory_bias(counts_ref, base, top, axis):
    shape = (1, top * MBLK) if axis == 1 else (top * MBLK, 1)
    column = lax.broadcasted_iota(jnp.int32, shape, axis)
    limit = jnp.zeros(shape, jnp.int32)
    for entry in range(top):
        inside = (column >= entry * MBLK) & (column < entry * MBLK + counts_ref[base + entry])
        limit = jnp.where(inside, 1, limit)
    return jnp.where(limit > 0, 0.0, NEGATIVE)


def pick_memory(ref, chosen_ref, base, top, columns):
    rows = [
        ref[pl.ds(pl.multiple_of(chosen_ref[base + entry] * MBLK, MBLK), MBLK), columns]
        for entry in range(top)
    ]
    return jnp.concatenate(rows, 0)


def forward_kernel(
    heads, top, chosen_ref, counts_ref, q_ref, k_ref, v_ref, mk_ref, mv_ref, out_ref, lse_ref, acc_s, peak_s
):
    block = pl.program_id(0)
    rows = q_ref.shape[0]
    subs = rows // QBLK
    own = pl.ds(pl.multiple_of(block * rows, rows), rows)
    causal = lax.broadcasted_iota(jnp.int32, (rows, rows), 0) >= lax.broadcasted_iota(jnp.int32, (rows, rows), 1)
    ones = jnp.ones((rows, HEAD_DIM), BF16)
    mem_ones = jnp.ones((top * MBLK, HEAD_DIM), BF16)
    biases = [memory_bias(counts_ref, (block * subs + sub) * top, top, 1) for sub in range(subs)]
    for head in range(heads):
        columns = slice(head * HEAD_DIM, (head + 1) * HEAD_DIM)
        remote = []
        for sub in range(subs):
            keys = pick_memory(mk_ref, chosen_ref, (block * subs + sub) * top, top, columns)
            query = q_ref[sub * QBLK : (sub + 1) * QBLK, columns]
            remote.append(dot(query, keys, NT) + biases[sub])
        local = jnp.where(causal, dot(q_ref[:, columns], k_ref[own, columns], NT), NEGATIVE)
        peak = jnp.max(local, -1, keepdims=True)
        peak = jnp.maximum(peak, jnp.concatenate([jnp.max(r, -1, keepdims=True) for r in remote], 0))
        values = jnp.concatenate([v_ref[own, columns], ones], 1)
        acc = dot(jnp.exp2(local - peak).astype(BF16), values)
        more = []
        for sub in range(subs):
            values = pick_memory(mv_ref, chosen_ref, (block * subs + sub) * top, top, columns)
            weights = jnp.exp2(remote[sub] - peak[sub * QBLK : (sub + 1) * QBLK]).astype(BF16)
            more.append(dot(weights, jnp.concatenate([values, mem_ones], 1)))
        acc_s[head] = acc + jnp.concatenate(more, 0)
        peak_s[head] = jnp.broadcast_to(peak, (rows, HEAD_DIM))

    def step(index, carry):
        there = pl.ds(pl.multiple_of(index * rows, rows), rows)
        for head in range(heads):
            columns = slice(head * HEAD_DIM, (head + 1) * HEAD_DIM)
            peak = peak_s[head][:, :1]
            scores = dot(q_ref[:, columns], k_ref[there, columns], NT)
            higher = jnp.maximum(peak, jnp.max(scores, -1, keepdims=True))
            weights = jnp.exp2(scores - higher).astype(BF16)
            values = jnp.concatenate([v_ref[there, columns], ones], 1)
            acc_s[head] = acc_s[head] * jnp.exp2(peak - higher) + dot(weights, values)
            peak_s[head] = jnp.broadcast_to(higher, (rows, HEAD_DIM))
        return carry

    lax.fori_loop(0, block, step, 0)
    for head in range(heads):
        columns = slice(head * HEAD_DIM, (head + 1) * HEAD_DIM)
        total = acc_s[head][:, HEAD_DIM:]
        out_ref[:, columns] = (acc_s[head][:, :HEAD_DIM] / total).astype(BF16)
        lse_ref[:, head : head + 1] = peak_s[head][:, :1] + jnp.log2(total[:, :1])


def attend_forward(chosen, counts, qkv, memory, heads, top):
    length = qkv.shape[0]
    wide = heads * HEAD_DIM
    rows = min(2 * QBLK, length)
    mem_rows = memory.shape[0]
    return pl.pallas_call(
        functools.partial(forward_kernel, heads, top),
        grid_spec=pltpu.PrefetchScalarGridSpec(
            num_scalar_prefetch=2,
            grid=(length // rows,),
            in_specs=[
                pl.BlockSpec((rows, wide), lambda i, *_: (i, 0)),
                pl.BlockSpec((length, wide), lambda i, *_: (0, 1)),
                pl.BlockSpec((length, wide), lambda i, *_: (0, 2)),
                pl.BlockSpec((mem_rows, wide), lambda i, *_: (0, 0)),
                pl.BlockSpec((mem_rows, wide), lambda i, *_: (0, 1)),
            ],
            out_specs=[
                pl.BlockSpec((rows, wide), lambda i, *_: (i, 0)),
                pl.BlockSpec((rows, heads), lambda i, *_: (i, 0)),
            ],
            scratch_shapes=[
                pltpu.VMEM((heads, rows, 2 * HEAD_DIM), F32),
                pltpu.VMEM((heads, rows, HEAD_DIM), F32),
            ],
        ),
        out_shape=[
            jax.ShapeDtypeStruct((length, wide), BF16),
            jax.ShapeDtypeStruct((length, heads), F32),
        ],
        compiler_params=pltpu.CompilerParams(vmem_limit_bytes=48 * MIB),
        cost_estimate=pl.CostEstimate(
            flops=4 * heads * length * HEAD_DIM * (length // 2 + top * MBLK),
            bytes_accessed=8 * length * wide,
            transcendentals=heads * length * (length // 2 + top * MBLK),
        ),
        name="attend_forward",
    )(chosen, counts, qkv, qkv, qkv, memory, memory)


def backward_kernel(
    heads, top, chosen_ref, counts_ref, q_ref, k_ref, v_ref, mk_ref, mv_ref, go_ref, out_ref, lse_ref,
    cos_ref, sin_ref, tok_ref, gain_ref, w_ref, partial_ref, grad_w_ref, gain_grad_ref,
    gk_s, gv_s, gq_s, grad_s, gw_s,
):
    block = pl.num_programs(0) - 1 - pl.program_id(0)
    rows = q_ref.shape[0]
    subs = rows // QBLK
    wide = heads * HEAD_DIM
    own = pl.ds(pl.multiple_of(block * rows, rows), rows)
    key_at = lax.broadcasted_iota(jnp.int32, (rows, rows), 0)
    query_at = lax.broadcasted_iota(jnp.int32, (rows, rows), 1)
    causal = query_at >= key_at

    @pl.when(pl.program_id(0) == 0)
    def _():
        gk_s[...] = jnp.zeros_like(gk_s)
        gv_s[...] = jnp.zeros_like(gv_s)
        gw_s[...] = jnp.zeros_like(gw_s)
        gain_grad_ref[...] = jnp.zeros_like(gain_grad_ref)

    def spread(column):
        return jnp.transpose(jnp.broadcast_to(column, (rows, HEAD_DIM)))[:1]

    stats = []
    for head in range(heads):
        columns = slice(head * HEAD_DIM, (head + 1) * HEAD_DIM)
        delta = jnp.sum(go_ref[:, columns].astype(F32) * out_ref[:, columns].astype(F32), -1, keepdims=True)
        stats.append((spread(lse_ref[:, head : head + 1]), spread(delta)))

    def pair(head, queries, keys, values, mask):
        columns = slice(head * HEAD_DIM, (head + 1) * HEAD_DIM)
        lse, delta = stats[head]
        scores = mask(dot(keys, q_ref[queries, columns], NT))
        weights = jnp.exp2(scores - lse[:, queries])
        grad_weights = dot(values, go_ref[queries, columns], NT)
        return weights.astype(BF16), (weights * (grad_weights - delta[:, queries])).astype(BF16)

    every = slice(0, rows)
    for head in range(heads):
        columns = slice(head * HEAD_DIM, (head + 1) * HEAD_DIM)
        for sub in range(subs):
            base = (block * subs + sub) * top
            queries = slice(sub * QBLK, (sub + 1) * QBLK)
            keys = pick_memory(mk_ref, chosen_ref, base, top, columns)
            values = pick_memory(mv_ref, chosen_ref, base, top, columns)
            bias = memory_bias(counts_ref, base, top, 0)
            _, grad_scores = pair(head, queries, keys, values, lambda scores: scores + bias)
            gq_s[queries, columns] = dot(grad_scores, keys, TN)

    def local(head, there, mask):
        columns = slice(head * HEAD_DIM, (head + 1) * HEAD_DIM)
        keys = k_ref[there, columns]
        weights, grad_scores = pair(head, every, keys, v_ref[there, columns], mask)
        gk_s[there, columns] += dot(grad_scores, q_ref[:, columns])
        gv_s[there, columns] += dot(weights, go_ref[:, columns])
        gq_s[:, columns] += dot(grad_scores, keys, TN)

    for head in range(heads):
        local(head, own, lambda scores: jnp.where(causal, scores, NEGATIVE))

    def step(index, carry):
        for head in range(heads):
            local(head, pl.ds(pl.multiple_of(index * rows, rows), rows), lambda scores: scores)
        return carry

    lax.fori_loop(0, block, step, 0)
    cosine, sine = cos_ref[...], sin_ref[...]

    def unturn(value):
        return value * cosine - pltpu.roll(value, HEAD_DIM // 2, 1) * sine

    for head in range(heads):
        columns = slice(head * HEAD_DIM, (head + 1) * HEAD_DIM)
        at = head * HEAD_DIM
        grad_s[:, at : at + HEAD_DIM] = unturn(gq_s[:, columns] * SCALE).astype(BF16)
        grad_key = gk_s[own, columns] * (1.0 / LOG2E)
        grad_s[:, wide + at : wide + at + HEAD_DIM] = unturn(grad_key).astype(BF16)
        grad_s[:, 2 * wide + at : 2 * wide + at + HEAD_DIM] = gv_s[own, columns].astype(BF16)

    tokens = tok_ref[...].astype(F32)
    tokens = tokens * lax.rsqrt(jnp.mean(tokens * tokens, -1, keepdims=True) + EPSILON)
    normed = (tokens * gain_ref[...]).astype(BF16)
    grad = grad_s[...]
    partial = dot(grad, w_ref[...], NT)
    partial_ref[...] = partial.astype(BF16)
    gain_grad_ref[...] += jnp.sum(partial * tokens, 0, keepdims=True)
    gw_s[...] += dot(normed, grad, TN)

    @pl.when(block == 0)
    def _():
        grad_w_ref[...] = gw_s[...].astype(BF16)


def attend_backward(
    chosen, counts, qkv, memory, grad_out, out, lse, cosine, sine, tokens_all, gain, w_qkv, heads, top
):
    length = qkv.shape[0]
    width = tokens_all.shape[1]
    wide = heads * HEAD_DIM
    rows = min(2 * QBLK, length)
    mem_rows = memory.shape[0]
    last = length // rows - 1
    return pl.pallas_call(
        functools.partial(backward_kernel, heads, top),
        grid_spec=pltpu.PrefetchScalarGridSpec(
            num_scalar_prefetch=2,
            grid=(last + 1,),
            in_specs=[
                pl.BlockSpec((rows, wide), lambda i, *_: (last - i, 0)),
                pl.BlockSpec((length, wide), lambda i, *_: (0, 1)),
                pl.BlockSpec((length, wide), lambda i, *_: (0, 2)),
                pl.BlockSpec((mem_rows, wide), lambda i, *_: (0, 0)),
                pl.BlockSpec((mem_rows, wide), lambda i, *_: (0, 1)),
                pl.BlockSpec((rows, wide), lambda i, *_: (last - i, 0)),
                pl.BlockSpec((rows, wide), lambda i, *_: (last - i, 0)),
                pl.BlockSpec((rows, heads), lambda i, *_: (last - i, 0)),
                pl.BlockSpec((rows, HEAD_DIM), lambda i, *_: (last - i, 0)),
                pl.BlockSpec((rows, HEAD_DIM), lambda i, *_: (last - i, 0)),
                pl.BlockSpec((rows, width), lambda i, *_: (last - i, 0)),
                pl.BlockSpec((1, width), lambda i, *_: (0, 0)),
                pl.BlockSpec((width, 3 * wide), lambda i, *_: (0, 0)),
            ],
            out_specs=[
                pl.BlockSpec((rows, width), lambda i, *_: (last - i, 0)),
                pl.BlockSpec((width, 3 * wide), lambda i, *_: (0, 0)),
                pl.BlockSpec((1, width), lambda i, *_: (0, 0)),
            ],
            scratch_shapes=[
                pltpu.VMEM((length, wide), F32),
                pltpu.VMEM((length, wide), F32),
                pltpu.VMEM((rows, wide), F32),
                pltpu.VMEM((rows, 3 * wide), BF16),
                pltpu.VMEM((width, 3 * wide), F32),
            ],
        ),
        out_shape=[
            jax.ShapeDtypeStruct((length, width), BF16),
            jax.ShapeDtypeStruct((width, 3 * wide), BF16),
            jax.ShapeDtypeStruct((1, width), F32),
        ],
        compiler_params=pltpu.CompilerParams(vmem_limit_bytes=48 * MIB),
        cost_estimate=pl.CostEstimate(
            flops=10 * heads * length * HEAD_DIM * (length // 2 + top * MBLK),
            bytes_accessed=16 * length * wide,
            transcendentals=heads * length * (length // 2 + top * MBLK),
        ),
        name="attend_backward",
    )(
        chosen, counts, qkv, qkv, qkv, memory, memory, grad_out, out, lse, cosine, sine, tokens_all, gain, w_qkv
    )


def ffn_kernel(
    span, merged, tok_ref, att_ref, cot_ref, gain_ref, out_w, gate_w, up_w, down_w,
    mixed_ref, grad_mid_ref, grad_att_ref, gain_grad_ref, grads_ref, *rest,
):
    if not merged:
        down_grads_ref, rest = rest[0], rest[1:]
    middle_s, normed_s, turned_s, mixed_s, upstream_s, gate_s, up_s, down_s, out_s, sems, late_sems = rest
    step, steps = pl.program_id(0), pl.num_programs(0)
    width = tok_ref.shape[1]
    share = width // span
    wide = gate_w.shape[1]
    hidden_width = down_s.shape[0]
    tall = hidden_width // span
    lanes = width // wide
    first = tall * lanes if merged else 0
    slot = step % 2

    @pl.when(step == 0)
    def _():
        middle = tok_ref[...].astype(F32) + dot(att_ref[...], out_w[...])
        middle_s[...] = middle
        factor = lax.rsqrt(jnp.mean(middle * middle, -1, keepdims=True) + EPSILON)
        normed = (middle * factor * gain_ref[...]).astype(BF16)
        normed_s[...] = normed
        turned_s[...] = jnp.transpose(normed)
        mixed_s[...] = middle
        upstream_s[...] = jnp.zeros_like(upstream_s)

    def copy_out(kind, which, index):
        source = (gate_s, up_s)[kind].at[which]
        start = first + (lanes + kind * steps + index) * share
        target = grads_ref.at[:, pl.ds(start, share), :]
        return pltpu.make_async_copy(source, target, sems.at[kind, which])

    normed = normed_s[...]
    upstream = cot_ref[...]
    both = jnp.concatenate([gate_w[...], up_w[...]], 1)
    acts = dot(normed, both)
    gate_act, up_act = acts[:, :wide], acts[:, wide:]
    grad_hidden = dot(upstream, down_w[...], NT)
    sigmoid = jax.nn.sigmoid(gate_act)
    silu = gate_act * sigmoid
    hidden = (silu * up_act).astype(BF16)
    grad_gate = (grad_hidden * up_act * sigmoid * (1.0 + gate_act * (1.0 - sigmoid))).astype(BF16)
    grad_up = (grad_hidden * silu).astype(BF16)
    mixed_s[...] += dot(hidden, down_w[...])
    grad_acts = jnp.concatenate([grad_gate, grad_up], 1)
    upstream_s[...] += dot(grad_acts, both, NT)
    down_s[pl.ds(pl.multiple_of(step * wide, wide), wide), :] = dot(hidden, upstream, TN).astype(BF16)

    @pl.when(step >= 2)
    def _():
        copy_out(0, slot, step - 2).wait()
        copy_out(1, slot, step - 2).wait()

    weight_grads = dot(turned_s[...], grad_acts).astype(BF16)
    gate_s[slot] = weight_grads[:, :wide].reshape(span, share, wide)
    up_s[slot] = weight_grads[:, wide:].reshape(span, share, wide)
    copy_out(0, slot, step).start()
    copy_out(1, slot, step).start()

    @pl.when(step == steps - 1)
    def _():
        copies = []
        if merged:
            for place in range(span):
                for lane in range(lanes):
                    copies.append(
                        pltpu.make_async_copy(
                            down_s.at[pl.ds(place * tall, tall), pl.ds(lane * wide, wide)],
                            grads_ref.at[place, pl.ds(lane * tall, tall), :],
                            late_sems.at[len(copies)],
                        )
                    )
        else:
            copies.append(pltpu.make_async_copy(down_s, down_grads_ref, late_sems.at[0]))
        for copy in copies:
            copy.start()
        mixed_ref[...] = mixed_s[...].astype(BF16)
        middle = middle_s[...]
        grad = upstream_s[...]
        factor = lax.rsqrt(jnp.mean(middle * middle, -1, keepdims=True) + EPSILON)
        gain_grad_ref[...] = jnp.sum(grad * middle * factor, 0, keepdims=True)
        scaled = grad * gain_ref[...]
        inner = jnp.mean(scaled * middle, -1, keepdims=True)
        grad_middle = cot_ref[...].astype(F32) + factor * scaled - middle * (factor * factor * factor * inner)
        grad_mid_ref[...] = grad_middle
        branch = grad_middle.astype(BF16)
        grad_att_ref[...] = dot(branch, out_w[...], NT).astype(BF16)
        turned_att = jnp.transpose(att_ref[...])
        for lane in range(lanes):
            columns = slice(lane * wide, (lane + 1) * wide)
            out_s[lane] = dot(turned_att, branch[:, columns]).astype(BF16).reshape(span, share, wide)
            more = pltpu.make_async_copy(
                out_s.at[lane],
                grads_ref.at[:, pl.ds(first + lane * share, share), :],
                late_sems.at[len(copies)],
            )
            more.start()
            copies.append(more)
        for copy in copies:
            copy.wait()
        copy_out(0, 1 - slot, step - 1).wait()
        copy_out(1, 1 - slot, step - 1).wait()
        copy_out(0, slot, step).wait()
        copy_out(1, slot, step).wait()


def feed_forward(tokens, attended, upstream, gain, weights, w_down, span):
    rows, width = tokens.shape
    hidden_width = w_down.shape[0]
    wide = 2 * HEAD_DIM
    steps = hidden_width // wide
    lanes = width // wide
    share = width // span
    tall = hidden_width // span
    merged = tall % 16 == 0
    total = (lanes + 2 * steps) * share + (lanes * tall if merged else 0)
    shapes = [
        jax.ShapeDtypeStruct((rows, width), BF16),
        jax.ShapeDtypeStruct((rows, width), F32),
        jax.ShapeDtypeStruct((rows, width), BF16),
        jax.ShapeDtypeStruct((1, width), F32),
        jax.ShapeDtypeStruct((span, total, wide), BF16),
    ]
    specs = [
        pl.BlockSpec((rows, width), lambda i: (0, 0)),
        pl.BlockSpec((rows, width), lambda i: (0, 0)),
        pl.BlockSpec((rows, width), lambda i: (0, 0)),
        pl.BlockSpec((1, width), lambda i: (0, 0)),
        pl.BlockSpec(memory_space=pl.ANY),
    ]
    if not merged:
        shapes.append(jax.ShapeDtypeStruct((hidden_width, width), BF16))
        specs.append(pl.BlockSpec(memory_space=pl.ANY))
    return pl.pallas_call(
        functools.partial(ffn_kernel, span, merged),
        grid=(steps,),
        in_specs=[
            pl.BlockSpec((rows, width), lambda i: (0, 0)),
            pl.BlockSpec((rows, width), lambda i: (0, 0)),
            pl.BlockSpec((rows, width), lambda i: (0, 0)),
            pl.BlockSpec((1, width), lambda i: (0, 0)),
            pl.BlockSpec((width, width), lambda i: (0, 0)),
            pl.BlockSpec((width, wide), lambda i: (0, lanes + i)),
            pl.BlockSpec((width, wide), lambda i: (0, lanes + steps + i)),
            pl.BlockSpec((wide, width), lambda i: (i, 0)),
        ],
        out_specs=specs,
        out_shape=shapes,
        scratch_shapes=[
            pltpu.VMEM((rows, width), F32),
            pltpu.VMEM((rows, width), BF16),
            pltpu.VMEM((width, rows), BF16),
            pltpu.VMEM((rows, width), F32),
            pltpu.VMEM((rows, width), F32),
            pltpu.VMEM((2, span, share, wide), BF16),
            pltpu.VMEM((2, span, share, wide), BF16),
            pltpu.VMEM((hidden_width, width), BF16),
            pltpu.VMEM((lanes, span, share, wide), BF16),
            pltpu.SemaphoreType.DMA((2, 2)),
            pltpu.SemaphoreType.DMA(((span * lanes if merged else 1) + lanes,)),
        ],
        compiler_params=pltpu.CompilerParams(vmem_limit_bytes=56 * MIB),
        cost_estimate=pl.CostEstimate(
            flops=6 * rows * width * (3 * hidden_width + width),
            bytes_accessed=4 * width * (3 * hidden_width + width),
            transcendentals=rows * hidden_width,
        ),
        name="feed_forward",
    )(tokens, attended, upstream, gain, weights, weights, weights, w_down)


def after(value, earlier):
    return lax.optimization_barrier((value, earlier))[0]


def chain_gather(blocks, axis):
    size = lax.axis_size(axis)
    place = lax.axis_index(axis)
    steps = []
    rising = falling = tuple(blocks)
    for step in range(size - 1):
        up = [(i, i + 1) for i in range(step, size - 1)]
        down = [(i + 1, i) for i in range(size - 1 - step)]
        rising = tuple(lax.ppermute(block, axis, up) for block in rising)
        falling = tuple(lax.ppermute(block, axis, down) for block in falling)
        if len(blocks) > 1:
            rising, falling = lax.optimization_barrier((rising, falling))
        steps.append((rising, falling))
    results = []
    for number, block in enumerate(blocks):
        ordered = []
        for index in range(size):
            cases = []
            for mine in range(size):
                if mine == index:
                    cases.append(block)
                elif mine > index:
                    cases.append(steps[mine - index - 1][0][number])
                else:
                    cases.append(steps[index - mine - 1][1][number])
            ordered.append(lax.select_n(place, *cases) if size > 2 else lax.select_n(place > 0, *cases))
        results.append(ordered)
    return results, steps


def chain_scatter(partial, axis):
    size = lax.axis_size(axis)
    place = lax.axis_index(axis)
    rows = partial.shape[0] // size

    def block(index):
        return lax.dynamic_slice_in_dim(partial, jnp.clip(index, 0, size - 1) * rows, rows, 0).astype(F32)

    rising = falling = None
    steps = []
    for step in range(size - 1):
        up, down = block(size - 1 - step + place), block(step - size + 1 + place)
        if step:
            up, down = up + rising.astype(F32), down + falling.astype(F32)
        rising = lax.ppermute(up.astype(BF16), axis, [(i, i + 1) for i in range(step + 1)])
        falling = lax.ppermute(
            down.astype(BF16), axis, [(i, i - 1) for i in range(size - 1 - step, size)]
        )
        steps.append((rising, falling))
    return block(place), steps


def body(
    tokens, memory_keys, memory_values, chosen, counts, w_query, w_key, w_value, w_out, w_gate, w_up, w_down,
    gain_attn, gain_ffn, cotangent,
):
    ring, span = lax.axis_size("fsdp"), lax.axis_size("dp")
    rows, width = tokens.shape[1:]
    heads = width // HEAD_DIM // ring
    wide = heads * HEAD_DIM
    length = rows * ring
    top = chosen.shape[2]
    hidden_width = w_gate.shape[1]
    share = w_query.shape[0]
    mine = tokens[0]

    extra = 8 if share % 8 == 0 else 8 - share % 8
    parts = [w.reshape(share, ring, wide).transpose(1, 0, 2) for w in (w_query, w_key, w_value)]
    choices = jnp.concatenate([chosen[0].reshape(-1), counts[0].reshape(-1)]).astype(BF16)
    notes = jnp.stack(
        [
            jnp.pad(row, (0, 3 * wide - row.shape[0]))
            for row in (jnp.concatenate([gain_attn, gain_ffn]), choices)
        ]
    )
    notes = jnp.broadcast_to(jnp.pad(notes, ((0, extra - 2), (0, 0))), (ring, extra, 3 * wide))
    parcel = jnp.concatenate([jnp.concatenate(parts, 2), notes], 1)
    parcel = lax.all_to_all(parcel, "fsdp", 0, 0, tiled=True)
    picks = parcel[:, share + 1, : choices.shape[0]].astype(jnp.int32).reshape(ring, 2, -1)
    chosen_all, counts_all = picks[:, 0].reshape(-1), picks[:, 1].reshape(-1)
    shards = jnp.concatenate([w_out, w_gate, w_up], 1)
    (near, near_down), steps = chain_gather((shards, w_down), "fsdp")
    (gathered,), token_steps = chain_gather((after(mine, steps[-2]),), "fsdp")
    parcel = lax.all_gather(parcel, "dp", axis=0, tiled=True)
    w_qkv = parcel[:, :share].reshape(width, 3 * wide)
    gain_one = parcel[:, share, :share].reshape(1, width).astype(F32)
    gain_two = parcel[:, share, share : 2 * share].reshape(1, width).astype(F32)
    first = lax.all_gather(jnp.concatenate(near, 0), "dp", axis=0, tiled=True)
    gathered = jnp.concatenate(gathered, 0)

    memory = jnp.concatenate(
        [m[0].reshape(-1, ring, wide).transpose(1, 0, 2) for m in (memory_keys, memory_values)], 2
    )
    memory = lax.all_to_all(after(memory, token_steps[-2]), "fsdp", 0, 0, tiled=True).reshape(-1, 2 * wide)
    down_full = lax.all_gather(jnp.concatenate(near_down, 0), "dp", axis=0, tiled=True)

    cosine, sine = rotary_tables(length)
    qkv = project_qkv(gathered, gain_one, w_qkv, cosine, sine, heads)
    attended_heads, lse = attend_forward(chosen_all, counts_all, qkv, memory, heads, top)
    attended = lax.all_to_all(attended_heads, "fsdp", 0, 1, tiled=True)

    upstream = cotangent[0]
    mixed, grad_middle, grad_attended, gain_two_grad, grads, *grad_down = feed_forward(
        mine, attended, upstream, gain_two, first, down_full, span
    )
    grad_heads = lax.all_to_all(grad_attended, "fsdp", 1, 0, tiled=True)
    grads = lax.psum_scatter(grads, "dp", scatter_dimension=0, tiled=True)[0]

    partial, grad_w_qkv, gain_one_grad = attend_backward(
        chosen_all, counts_all, qkv, memory, grad_heads, attended_heads, lse, cosine, sine, gathered, gain_one,
        w_qkv, heads, top,
    )
    own_term, steps = chain_scatter(partial, "fsdp")
    grads = after(grads, steps[-2])

    gains = jnp.concatenate([gain_one_grad, gain_two_grad], 0).reshape(2, span, -1).transpose(1, 0, 2)
    gains = jnp.pad(gains.astype(BF16), ((0, 0), (0, extra - 2), (0, 3 * wide - gains.shape[2])))
    late = jnp.concatenate([grad_w_qkv.reshape(span, -1, 3 * wide), gains], 1)
    late = jnp.sum(lax.all_to_all(late, "dp", 0, 0, tiled=True).astype(F32), 0).astype(BF16)
    gains = late[-extra : 2 - extra, : ring * share].reshape(2, ring, share).transpose(1, 0, 2)
    gains = jnp.pad(gains, ((0, 0), (0, extra - 2), (0, 3 * wide - share)))
    late = jnp.concatenate([late[:-extra].reshape(ring, share, 3 * wide), gains], 1)
    late = lax.all_to_all(late, "fsdp", 0, 0, tiled=True).astype(F32)
    projections = [
        late[:, :share, part * wide : (part + 1) * wide].transpose(1, 0, 2).reshape(share, width)
        for part in range(3)
    ]
    gain_shares = jnp.sum(late[:, share : share + 2, :share], 0)

    strip = grads.shape[1]
    lanes = width // strip
    tall = w_down.shape[0]
    if grad_down:
        down = lax.psum_scatter(grad_down[0], "dp", scatter_dimension=0, tiled=True)
        down = down.reshape(ring, tall, lanes, strip).transpose(0, 2, 1, 3)
    else:
        down = grads[: ring * tall * lanes].reshape(lanes, ring, tall, strip).transpose(1, 0, 2, 3)
        grads = grads[ring * tall * lanes :]
    grads = grads.reshape(-1, ring, share, strip).transpose(1, 0, 2, 3)
    pieces = jnp.concatenate([down.reshape(ring, -1, strip), grads.reshape(ring, -1, strip)], 1)
    rising, falling = after(steps[-1], pieces)
    grad_normed = own_term + rising.astype(F32) + falling.astype(F32)
    own = mine.astype(F32)
    factor = lax.rsqrt(jnp.mean(own * own, -1, keepdims=True) + EPSILON)
    scaled = grad_normed * gain_one
    inner = jnp.mean(scaled * own, -1, keepdims=True)
    tokens_grad = (grad_middle + factor * scaled - own * (factor * factor * factor * inner)).astype(BF16)

    pieces = jnp.sum(lax.all_to_all(pieces, "fsdp", 0, 0, tiled=True).astype(F32), 0)
    down_share = pieces[: lanes * tall].reshape(lanes, tall, strip).transpose(1, 0, 2).reshape(tall, width)
    others = pieces[lanes * tall :].reshape(-1, share, strip).transpose(1, 0, 2).reshape(share, -1)
    return (
        mixed[None],
        tokens_grad[None],
        *projections,
        others[:, :width],
        others[:, width : width + hidden_width],
        others[:, width + hidden_width :],
        down_share,
        gain_shares[0],
        gain_shares[1],
    )


def solution(mesh):
    both = ("dp", "fsdp")
    rows, matrix, vector = P("dp", "fsdp", None), P(both, None), P(both)
    in_specs = (rows,) * 5 + (matrix,) * 7 + (vector,) * 2 + (rows,)
    out_specs = (rows,) * 2 + (matrix,) * 7 + (vector,) * 2
    return jax.shard_map(body, mesh=mesh, in_specs=in_specs, out_specs=out_specs, check_vma=False)
```

```python
import functools
import math

import jax
import jax.numpy as jnp
import numpy as np
from jax import lax
from jax.experimental import pallas as pl
from jax.experimental.pallas import tpu as pltpu
from jax.sharding import Mesh
from jax.sharding import PartitionSpec as P

HEAD_DIM = 128
QBLK = 256
MBLK = 128
EPSILON = 1e-06
NEGATIVE = -1e30
SCALE = 1.0 / math.sqrt(HEAD_DIM)
LOG2E = math.log2(math.e)
MIB = 1 << 20
F32 = jnp.float32
BF16 = jnp.bfloat16
DP = ("chip", "core")
NT = (((1,), (1,)), ((), ()))
TN = (((0,), (0,)), ((), ()))


def dot(left, right, dims=(((1,), (0,)), ((), ()))):
    return lax.dot_general(left, right, dims, preferred_element_type=F32)


def rotary_tables(length):
    half_dim = HEAD_DIM // 2
    frequency = 10000.0 ** (-jnp.arange(half_dim, dtype=F32) / half_dim)
    angles = jnp.arange(length, dtype=jnp.int32).astype(F32)[:, None] * frequency[None, :]
    cosine, sine = jnp.cos(angles), jnp.sin(angles)
    return jnp.concatenate([cosine, cosine], 1), jnp.concatenate([-sine, sine], 1)


def qkv_kernel(heads, tok_ref, gain_ref, w_ref, cos_ref, sin_ref, qkv_ref):
    rows = tok_ref[...].astype(F32)
    factor = lax.rsqrt(jnp.mean(rows * rows, -1, keepdims=True) + EPSILON)
    normed = (rows * factor * gain_ref[...]).astype(BF16)
    cosine, sine = cos_ref[...], sin_ref[...]
    wide = heads * HEAD_DIM
    for part in range(3):
        values = dot(normed, w_ref[:, part * wide : (part + 1) * wide])
        for head in range(heads):
            value = values[:, head * HEAD_DIM : (head + 1) * HEAD_DIM]
            if part < 2:
                value = value * cosine + pltpu.roll(value, HEAD_DIM // 2, 1) * sine
            if part == 0:
                value = value * (SCALE * LOG2E)
            at = part * wide + head * HEAD_DIM
            qkv_ref[:, at : at + HEAD_DIM] = value.astype(BF16)


def project_qkv(tokens_all, gain, w_qkv, cosine, sine, heads):
    length, width = tokens_all.shape
    columns = w_qkv.shape[1]
    block = 2 * QBLK
    return pl.pallas_call(
        functools.partial(qkv_kernel, heads),
        grid=(length // block,),
        in_specs=[
            pl.BlockSpec((block, width), lambda i: (i, 0)),
            pl.BlockSpec((1, width), lambda i: (0, 0)),
            pl.BlockSpec((width, columns), lambda i: (0, 0)),
            pl.BlockSpec((block, HEAD_DIM), lambda i: (i, 0)),
            pl.BlockSpec((block, HEAD_DIM), lambda i: (i, 0)),
        ],
        out_specs=pl.BlockSpec((block, columns), lambda i: (i, 0)),
        out_shape=jax.ShapeDtypeStruct((length, columns), BF16),
        compiler_params=pltpu.CompilerParams(vmem_limit_bytes=48 * MIB),
        cost_estimate=pl.CostEstimate(
            flops=2 * length * width * columns, bytes_accessed=4 * length * (width + columns), transcendentals=0
        ),
        name="project_qkv",
    )(tokens_all, gain, w_qkv, cosine, sine)


def memory_bias(counts_ref, base, top, axis):
    shape = (1, top * MBLK) if axis == 1 else (top * MBLK, 1)
    column = lax.broadcasted_iota(jnp.int32, shape, axis)
    limit = jnp.zeros(shape, jnp.int32)
    for entry in range(top):
        inside = (column >= entry * MBLK) & (column < entry * MBLK + counts_ref[base + entry])
        limit = jnp.where(inside, 1, limit)
    return jnp.where(limit > 0, 0.0, NEGATIVE)


def pick_memory(ref, chosen_ref, base, top, columns):
    rows = [
        ref[pl.ds(pl.multiple_of(chosen_ref[base + entry] * MBLK, MBLK), MBLK), columns]
        for entry in range(top)
    ]
    return jnp.concatenate(rows, 0)


def forward_kernel(
    heads, top, chosen_ref, counts_ref, q_ref, k_ref, v_ref, mk_ref, mv_ref, out_ref, lse_ref, acc_s, peak_s
):
    block = pl.program_id(0)
    rows = q_ref.shape[0]
    subs = rows // QBLK
    own = pl.ds(pl.multiple_of(block * rows, rows), rows)
    causal = lax.broadcasted_iota(jnp.int32, (rows, rows), 0) >= lax.broadcasted_iota(jnp.int32, (rows, rows), 1)
    ones = jnp.ones((rows, HEAD_DIM), BF16)
    mem_ones = jnp.ones((top * MBLK, HEAD_DIM), BF16)
    biases = [memory_bias(counts_ref, (block * subs + sub) * top, top, 1) for sub in range(subs)]
    for head in range(heads):
        columns = slice(head * HEAD_DIM, (head + 1) * HEAD_DIM)
        remote = []
        for sub in range(subs):
            keys = pick_memory(mk_ref, chosen_ref, (block * subs + sub) * top, top, columns)
            query = q_ref[sub * QBLK : (sub + 1) * QBLK, columns]
            remote.append(dot(query, keys, NT) + biases[sub])
        local = jnp.where(causal, dot(q_ref[:, columns], k_ref[own, columns], NT), NEGATIVE)
        peak = jnp.max(local, -1, keepdims=True)
        peak = jnp.maximum(peak, jnp.concatenate([jnp.max(r, -1, keepdims=True) for r in remote], 0))
        values = jnp.concatenate([v_ref[own, columns], ones], 1)
        acc = dot(jnp.exp2(local - peak).astype(BF16), values)
        more = []
        for sub in range(subs):
            values = pick_memory(mv_ref, chosen_ref, (block * subs + sub) * top, top, columns)
            weights = jnp.exp2(remote[sub] - peak[sub * QBLK : (sub + 1) * QBLK]).astype(BF16)
            more.append(dot(weights, jnp.concatenate([values, mem_ones], 1)))
        acc_s[head] = acc + jnp.concatenate(more, 0)
        peak_s[head] = jnp.broadcast_to(peak, (rows, HEAD_DIM))

    def step(index, carry):
        there = pl.ds(pl.multiple_of(index * rows, rows), rows)
        for head in range(heads):
            columns = slice(head * HEAD_DIM, (head + 1) * HEAD_DIM)
            peak = peak_s[head][:, :1]
            scores = dot(q_ref[:, columns], k_ref[there, columns], NT)
            higher = jnp.maximum(peak, jnp.max(scores, -1, keepdims=True))
            weights = jnp.exp2(scores - higher).astype(BF16)
            values = jnp.concatenate([v_ref[there, columns], ones], 1)
            acc_s[head] = acc_s[head] * jnp.exp2(peak - higher) + dot(weights, values)
            peak_s[head] = jnp.broadcast_to(higher, (rows, HEAD_DIM))
        return carry

    lax.fori_loop(0, block, step, 0)
    for head in range(heads):
        columns = slice(head * HEAD_DIM, (head + 1) * HEAD_DIM)
        total = acc_s[head][:, HEAD_DIM:]
        out_ref[:, columns] = (acc_s[head][:, :HEAD_DIM] / total).astype(BF16)
        lse_ref[:, head : head + 1] = peak_s[head][:, :1] + jnp.log2(total[:, :1])


def attend_forward(chosen, counts, qkv, memory, heads, top):
    length = qkv.shape[0]
    wide = heads * HEAD_DIM
    rows = min(2 * QBLK, length)
    mem_rows = memory.shape[0]
    return pl.pallas_call(
        functools.partial(forward_kernel, heads, top),
        grid_spec=pltpu.PrefetchScalarGridSpec(
            num_scalar_prefetch=2,
            grid=(length // rows,),
            in_specs=[
                pl.BlockSpec((rows, wide), lambda i, *_: (i, 0)),
                pl.BlockSpec((length, wide), lambda i, *_: (0, 1)),
                pl.BlockSpec((length, wide), lambda i, *_: (0, 2)),
                pl.BlockSpec((mem_rows, wide), lambda i, *_: (0, 0)),
                pl.BlockSpec((mem_rows, wide), lambda i, *_: (0, 1)),
            ],
            out_specs=[
                pl.BlockSpec((rows, wide), lambda i, *_: (i, 0)),
                pl.BlockSpec((rows, heads), lambda i, *_: (i, 0)),
            ],
            scratch_shapes=[
                pltpu.VMEM((heads, rows, 2 * HEAD_DIM), F32),
                pltpu.VMEM((heads, rows, HEAD_DIM), F32),
            ],
        ),
        out_shape=[
            jax.ShapeDtypeStruct((length, wide), BF16),
            jax.ShapeDtypeStruct((length, heads), F32),
        ],
        compiler_params=pltpu.CompilerParams(vmem_limit_bytes=48 * MIB),
        cost_estimate=pl.CostEstimate(
            flops=4 * heads * length * HEAD_DIM * (length // 2 + top * MBLK),
            bytes_accessed=8 * length * wide,
            transcendentals=heads * length * (length // 2 + top * MBLK),
        ),
        name="attend_forward",
    )(chosen, counts, qkv, qkv, qkv, memory, memory)


def backward_kernel(
    heads, top, chosen_ref, counts_ref, q_ref, k_ref, v_ref, mk_ref, mv_ref, go_ref, out_ref, lse_ref,
    cos_ref, sin_ref, tok_ref, gain_ref, w_ref, partial_ref, grad_w_ref, gain_grad_ref,
    gk_s, gv_s, gq_s, grad_s, gw_s,
):
    block = pl.num_programs(0) - 1 - pl.program_id(0)
    rows = q_ref.shape[0]
    subs = rows // QBLK
    wide = heads * HEAD_DIM
    own = pl.ds(pl.multiple_of(block * rows, rows), rows)
    key_at = lax.broadcasted_iota(jnp.int32, (rows, rows), 0)
    query_at = lax.broadcasted_iota(jnp.int32, (rows, rows), 1)
    causal = query_at >= key_at

    @pl.when(pl.program_id(0) == 0)
    def _():
        gk_s[...] = jnp.zeros_like(gk_s)
        gv_s[...] = jnp.zeros_like(gv_s)
        gw_s[...] = jnp.zeros_like(gw_s)
        gain_grad_ref[...] = jnp.zeros_like(gain_grad_ref)

    def spread(column):
        return jnp.transpose(jnp.broadcast_to(column, (rows, HEAD_DIM)))[:1]

    stats = []
    for head in range(heads):
        columns = slice(head * HEAD_DIM, (head + 1) * HEAD_DIM)
        delta = jnp.sum(go_ref[:, columns].astype(F32) * out_ref[:, columns].astype(F32), -1, keepdims=True)
        stats.append((spread(lse_ref[:, head : head + 1]), spread(delta)))

    def pair(head, queries, keys, values, mask):
        columns = slice(head * HEAD_DIM, (head + 1) * HEAD_DIM)
        lse, delta = stats[head]
        scores = mask(dot(keys, q_ref[queries, columns], NT))
        weights = jnp.exp2(scores - lse[:, queries])
        grad_weights = dot(values, go_ref[queries, columns], NT)
        return weights.astype(BF16), (weights * (grad_weights - delta[:, queries])).astype(BF16)

    every = slice(0, rows)
    for head in range(heads):
        columns = slice(head * HEAD_DIM, (head + 1) * HEAD_DIM)
        for sub in range(subs):
            base = (block * subs + sub) * top
            queries = slice(sub * QBLK, (sub + 1) * QBLK)
            keys = pick_memory(mk_ref, chosen_ref, base, top, columns)
            values = pick_memory(mv_ref, chosen_ref, base, top, columns)
            bias = memory_bias(counts_ref, base, top, 0)
            _, grad_scores = pair(head, queries, keys, values, lambda scores: scores + bias)
            gq_s[queries, columns] = dot(grad_scores, keys, TN)

    def local(head, there, mask):
        columns = slice(head * HEAD_DIM, (head + 1) * HEAD_DIM)
        keys = k_ref[there, columns]
        weights, grad_scores = pair(head, every, keys, v_ref[there, columns], mask)
        gk_s[there, columns] += dot(grad_scores, q_ref[:, columns])
        gv_s[there, columns] += dot(weights, go_ref[:, columns])
        gq_s[:, columns] += dot(grad_scores, keys, TN)

    for head in range(heads):
        local(head, own, lambda scores: jnp.where(causal, scores, NEGATIVE))

    def step(index, carry):
        for head in range(heads):
            local(head, pl.ds(pl.multiple_of(index * rows, rows), rows), lambda scores: scores)
        return carry

    lax.fori_loop(0, block, step, 0)
    cosine, sine = cos_ref[...], sin_ref[...]

    def unturn(value):
        return value * cosine - pltpu.roll(value, HEAD_DIM // 2, 1) * sine

    for head in range(heads):
        columns = slice(head * HEAD_DIM, (head + 1) * HEAD_DIM)
        at = head * HEAD_DIM
        grad_s[:, at : at + HEAD_DIM] = unturn(gq_s[:, columns] * SCALE).astype(BF16)
        grad_key = gk_s[own, columns] * (1.0 / LOG2E)
        grad_s[:, wide + at : wide + at + HEAD_DIM] = unturn(grad_key).astype(BF16)
        grad_s[:, 2 * wide + at : 2 * wide + at + HEAD_DIM] = gv_s[own, columns].astype(BF16)

    tokens = tok_ref[...].astype(F32)
    tokens = tokens * lax.rsqrt(jnp.mean(tokens * tokens, -1, keepdims=True) + EPSILON)
    normed = (tokens * gain_ref[...]).astype(BF16)
    grad = grad_s[...]
    partial = dot(grad, w_ref[...], NT)
    partial_ref[...] = partial.astype(BF16)
    gain_grad_ref[...] += jnp.sum(partial * tokens, 0, keepdims=True)
    gw_s[...] += dot(normed, grad, TN)

    @pl.when(block == 0)
    def _():
        grad_w_ref[...] = gw_s[...].astype(BF16)


def attend_backward(
    chosen, counts, qkv, memory, grad_out, out, lse, cosine, sine, tokens_all, gain, w_qkv, heads, top
):
    length = qkv.shape[0]
    width = tokens_all.shape[1]
    wide = heads * HEAD_DIM
    rows = min(2 * QBLK, length)
    mem_rows = memory.shape[0]
    last = length // rows - 1
    return pl.pallas_call(
        functools.partial(backward_kernel, heads, top),
        grid_spec=pltpu.PrefetchScalarGridSpec(
            num_scalar_prefetch=2,
            grid=(last + 1,),
            in_specs=[
                pl.BlockSpec((rows, wide), lambda i, *_: (last - i, 0)),
                pl.BlockSpec((length, wide), lambda i, *_: (0, 1)),
                pl.BlockSpec((length, wide), lambda i, *_: (0, 2)),
                pl.BlockSpec((mem_rows, wide), lambda i, *_: (0, 0)),
                pl.BlockSpec((mem_rows, wide), lambda i, *_: (0, 1)),
                pl.BlockSpec((rows, wide), lambda i, *_: (last - i, 0)),
                pl.BlockSpec((rows, wide), lambda i, *_: (last - i, 0)),
                pl.BlockSpec((rows, heads), lambda i, *_: (last - i, 0)),
                pl.BlockSpec((rows, HEAD_DIM), lambda i, *_: (last - i, 0)),
                pl.BlockSpec((rows, HEAD_DIM), lambda i, *_: (last - i, 0)),
                pl.BlockSpec((rows, width), lambda i, *_: (last - i, 0)),
                pl.BlockSpec((1, width), lambda i, *_: (0, 0)),
                pl.BlockSpec((width, 3 * wide), lambda i, *_: (0, 0)),
            ],
            out_specs=[
                pl.BlockSpec((rows, width), lambda i, *_: (last - i, 0)),
                pl.BlockSpec((width, 3 * wide), lambda i, *_: (0, 0)),
                pl.BlockSpec((1, width), lambda i, *_: (0, 0)),
            ],
            scratch_shapes=[
                pltpu.VMEM((length, wide), F32),
                pltpu.VMEM((length, wide), F32),
                pltpu.VMEM((rows, wide), F32),
                pltpu.VMEM((rows, 3 * wide), BF16),
                pltpu.VMEM((width, 3 * wide), F32),
            ],
        ),
        out_shape=[
            jax.ShapeDtypeStruct((length, width), BF16),
            jax.ShapeDtypeStruct((width, 3 * wide), BF16),
            jax.ShapeDtypeStruct((1, width), F32),
        ],
        compiler_params=pltpu.CompilerParams(vmem_limit_bytes=48 * MIB),
        cost_estimate=pl.CostEstimate(
            flops=10 * heads * length * HEAD_DIM * (length // 2 + top * MBLK),
            bytes_accessed=16 * length * wide,
            transcendentals=heads * length * (length // 2 + top * MBLK),
        ),
        name="attend_backward",
    )(
        chosen, counts, qkv, qkv, qkv, memory, memory, grad_out, out, lse, cosine, sine, tokens_all, gain, w_qkv
    )


def ffn_kernel(
    span, merged, tok_ref, att_ref, cot_ref, gain_ref, out_w, gate_w, up_w, down_w,
    mixed_ref, grad_mid_ref, grad_att_ref, gain_grad_ref, grads_ref, *rest,
):
    if not merged:
        down_grads_ref, rest = rest[0], rest[1:]
    middle_s, normed_s, turned_s, mixed_s, upstream_s, gate_s, up_s, down_s, out_s, sems, late_sems = rest
    step, steps = pl.program_id(0), pl.num_programs(0)
    width = tok_ref.shape[1]
    share = width // span
    wide = gate_w.shape[1]
    hidden_width = down_s.shape[0]
    tall = hidden_width // span
    lanes = width // wide
    first = tall * lanes if merged else 0
    slot = step % 2

    @pl.when(step == 0)
    def _():
        middle = tok_ref[...].astype(F32) + dot(att_ref[...], out_w[...])
        middle_s[...] = middle
        factor = lax.rsqrt(jnp.mean(middle * middle, -1, keepdims=True) + EPSILON)
        normed = (middle * factor * gain_ref[...]).astype(BF16)
        normed_s[...] = normed
        turned_s[...] = jnp.transpose(normed)
        mixed_s[...] = middle
        upstream_s[...] = jnp.zeros_like(upstream_s)

    def copy_out(kind, which, index):
        source = (gate_s, up_s)[kind].at[which]
        start = first + (lanes + kind * steps + index) * share
        target = grads_ref.at[:, pl.ds(start, share), :]
        return pltpu.make_async_copy(source, target, sems.at[kind, which])

    normed = normed_s[...]
    upstream = cot_ref[...]
    both = jnp.concatenate([gate_w[...], up_w[...]], 1)
    acts = dot(normed, both)
    gate_act, up_act = acts[:, :wide], acts[:, wide:]
    grad_hidden = dot(upstream, down_w[...], NT)
    sigmoid = jax.nn.sigmoid(gate_act)
    silu = gate_act * sigmoid
    hidden = (silu * up_act).astype(BF16)
    grad_gate = (grad_hidden * up_act * sigmoid * (1.0 + gate_act * (1.0 - sigmoid))).astype(BF16)
    grad_up = (grad_hidden * silu).astype(BF16)
    mixed_s[...] += dot(hidden, down_w[...])
    grad_acts = jnp.concatenate([grad_gate, grad_up], 1)
    upstream_s[...] += dot(grad_acts, both, NT)
    down_s[pl.ds(pl.multiple_of(step * wide, wide), wide), :] = dot(hidden, upstream, TN).astype(BF16)

    @pl.when(step >= 2)
    def _():
        copy_out(0, slot, step - 2).wait()
        copy_out(1, slot, step - 2).wait()

    weight_grads = dot(turned_s[...], grad_acts).astype(BF16)
    gate_s[slot] = weight_grads[:, :wide].reshape(span, share, wide)
    up_s[slot] = weight_grads[:, wide:].reshape(span, share, wide)
    copy_out(0, slot, step).start()
    copy_out(1, slot, step).start()

    @pl.when(step == steps - 1)
    def _():
        copies = []
        if merged:
            for place in range(span):
                for lane in range(lanes):
                    copies.append(
                        pltpu.make_async_copy(
                            down_s.at[pl.ds(place * tall, tall), pl.ds(lane * wide, wide)],
                            grads_ref.at[place, pl.ds(lane * tall, tall), :],
                            late_sems.at[len(copies)],
                        )
                    )
        else:
            copies.append(pltpu.make_async_copy(down_s, down_grads_ref, late_sems.at[0]))
        for copy in copies:
            copy.start()
        mixed_ref[...] = mixed_s[...].astype(BF16)
        middle = middle_s[...]
        grad = upstream_s[...]
        factor = lax.rsqrt(jnp.mean(middle * middle, -1, keepdims=True) + EPSILON)
        gain_grad_ref[...] = jnp.sum(grad * middle * factor, 0, keepdims=True)
        scaled = grad * gain_ref[...]
        inner = jnp.mean(scaled * middle, -1, keepdims=True)
        grad_middle = cot_ref[...].astype(F32) + factor * scaled - middle * (factor * factor * factor * inner)
        grad_mid_ref[...] = grad_middle
        branch = grad_middle.astype(BF16)
        grad_att_ref[...] = dot(branch, out_w[...], NT).astype(BF16)
        turned_att = jnp.transpose(att_ref[...])
        for lane in range(lanes):
            columns = slice(lane * wide, (lane + 1) * wide)
            out_s[lane] = dot(turned_att, branch[:, columns]).astype(BF16).reshape(span, share, wide)
            more = pltpu.make_async_copy(
                out_s.at[lane],
                grads_ref.at[:, pl.ds(first + lane * share, share), :],
                late_sems.at[len(copies)],
            )
            more.start()
            copies.append(more)
        for copy in copies:
            copy.wait()
        copy_out(0, 1 - slot, step - 1).wait()
        copy_out(1, 1 - slot, step - 1).wait()
        copy_out(0, slot, step).wait()
        copy_out(1, slot, step).wait()


def feed_forward(tokens, attended, upstream, gain, weights, w_down, span):
    rows, width = tokens.shape
    hidden_width = w_down.shape[0]
    wide = 2 * HEAD_DIM
    steps = hidden_width // wide
    lanes = width // wide
    share = width // span
    tall = hidden_width // span
    merged = tall % 16 == 0
    total = (lanes + 2 * steps) * share + (lanes * tall if merged else 0)
    shapes = [
        jax.ShapeDtypeStruct((rows, width), BF16),
        jax.ShapeDtypeStruct((rows, width), F32),
        jax.ShapeDtypeStruct((rows, width), BF16),
        jax.ShapeDtypeStruct((1, width), F32),
        jax.ShapeDtypeStruct((span, total, wide), BF16),
    ]
    specs = [
        pl.BlockSpec((rows, width), lambda i: (0, 0)),
        pl.BlockSpec((rows, width), lambda i: (0, 0)),
        pl.BlockSpec((rows, width), lambda i: (0, 0)),
        pl.BlockSpec((1, width), lambda i: (0, 0)),
        pl.BlockSpec(memory_space=pl.ANY),
    ]
    if not merged:
        shapes.append(jax.ShapeDtypeStruct((hidden_width, width), BF16))
        specs.append(pl.BlockSpec(memory_space=pl.ANY))
    return pl.pallas_call(
        functools.partial(ffn_kernel, span, merged),
        grid=(steps,),
        in_specs=[
            pl.BlockSpec((rows, width), lambda i: (0, 0)),
            pl.BlockSpec((rows, width), lambda i: (0, 0)),
            pl.BlockSpec((rows, width), lambda i: (0, 0)),
            pl.BlockSpec((1, width), lambda i: (0, 0)),
            pl.BlockSpec((width, width), lambda i: (0, 0)),
            pl.BlockSpec((width, wide), lambda i: (0, lanes + i)),
            pl.BlockSpec((width, wide), lambda i: (0, lanes + steps + i)),
            pl.BlockSpec((wide, width), lambda i: (i, 0)),
        ],
        out_specs=specs,
        out_shape=shapes,
        scratch_shapes=[
            pltpu.VMEM((rows, width), F32),
            pltpu.VMEM((rows, width), BF16),
            pltpu.VMEM((width, rows), BF16),
            pltpu.VMEM((rows, width), F32),
            pltpu.VMEM((rows, width), F32),
            pltpu.VMEM((2, span, share, wide), BF16),
            pltpu.VMEM((2, span, share, wide), BF16),
            pltpu.VMEM((hidden_width, width), BF16),
            pltpu.VMEM((lanes, span, share, wide), BF16),
            pltpu.SemaphoreType.DMA((2, 2)),
            pltpu.SemaphoreType.DMA(((span * lanes if merged else 1) + lanes,)),
        ],
        compiler_params=pltpu.CompilerParams(vmem_limit_bytes=56 * MIB),
        cost_estimate=pl.CostEstimate(
            flops=6 * rows * width * (3 * hidden_width + width),
            bytes_accessed=4 * width * (3 * hidden_width + width),
            transcendentals=rows * hidden_width,
        ),
        name="feed_forward",
    )(tokens, attended, upstream, gain, weights, weights, weights, w_down)


def after(value, earlier):
    return lax.optimization_barrier((value, earlier))[0]


def chain_gather(blocks, axis):
    size = lax.axis_size(axis)
    place = lax.axis_index(axis)
    steps = []
    rising = falling = tuple(blocks)
    for step in range(size - 1):
        up = [(i, i + 1) for i in range(step, size - 1)]
        down = [(i + 1, i) for i in range(size - 1 - step)]
        rising = tuple(lax.ppermute(block, axis, up) for block in rising)
        falling = tuple(lax.ppermute(block, axis, down) for block in falling)
        if len(blocks) > 1:
            rising, falling = lax.optimization_barrier((rising, falling))
        steps.append((rising, falling))
    results = []
    for number, block in enumerate(blocks):
        ordered = []
        for index in range(size):
            cases = []
            for mine in range(size):
                if mine == index:
                    cases.append(block)
                elif mine > index:
                    cases.append(steps[mine - index - 1][0][number])
                else:
                    cases.append(steps[index - mine - 1][1][number])
            ordered.append(lax.select_n(place, *cases) if size > 2 else lax.select_n(place > 0, *cases))
        results.append(ordered)
    return results, steps


def chain_scatter(partial, axis):
    size = lax.axis_size(axis)
    place = lax.axis_index(axis)
    rows = partial.shape[0] // size

    def block(index):
        return lax.dynamic_slice_in_dim(partial, jnp.clip(index, 0, size - 1) * rows, rows, 0).astype(F32)

    rising = falling = None
    steps = []
    for step in range(size - 1):
        up, down = block(size - 1 - step + place), block(step - size + 1 + place)
        if step:
            up, down = up + rising.astype(F32), down + falling.astype(F32)
        up, down = lax.optimization_barrier((up.astype(BF16), down.astype(BF16)))
        rising = lax.ppermute(up, axis, [(i, i + 1) for i in range(step + 1)])
        falling = lax.ppermute(down, axis, [(i, i - 1) for i in range(size - 1 - step, size)])
        rising, falling = lax.optimization_barrier((rising, falling))
        steps.append((rising, falling))
    return block(place), steps


def body(
    tokens, memory_keys, memory_values, chosen, counts, w_query, w_key, w_value, w_out, w_gate, w_up, w_down,
    gain_attn, gain_ffn, cotangent,
):
    ring, span = lax.axis_size("fsdp"), lax.axis_size(DP)
    rows, width = tokens.shape[1:]
    heads = width // HEAD_DIM // ring
    wide = heads * HEAD_DIM
    length = rows * ring
    top = chosen.shape[2]
    hidden_width = w_gate.shape[1]
    share = w_query.shape[0]
    mine = tokens[0]

    extra = 8 if share % 8 == 0 else 8 - share % 8
    parts = [w.reshape(share, ring, wide).transpose(1, 0, 2) for w in (w_query, w_key, w_value)]
    choices = jnp.concatenate([chosen[0].reshape(-1), counts[0].reshape(-1)]).astype(BF16)
    notes = jnp.stack(
        [
            jnp.pad(row, (0, 3 * wide - row.shape[0]))
            for row in (jnp.concatenate([gain_attn, gain_ffn]), choices)
        ]
    )
    notes = jnp.broadcast_to(jnp.pad(notes, ((0, extra - 2), (0, 0))), (ring, extra, 3 * wide))
    parcel = jnp.concatenate([jnp.concatenate(parts, 2), notes], 1)
    parcel = lax.all_to_all(parcel, "fsdp", 0, 0, tiled=True)
    picks = parcel[:, share + 1, : choices.shape[0]].astype(jnp.int32).reshape(ring, 2, -1)
    chosen_all, counts_all = picks[:, 0].reshape(-1), picks[:, 1].reshape(-1)
    shards = jnp.concatenate([w_out, w_gate, w_up], 1)
    (near, near_down), steps = chain_gather((shards, w_down), "fsdp")
    (gathered,), token_steps = chain_gather((after(mine, steps[-2]),), "fsdp")
    parcel = lax.all_gather(parcel, DP, axis=0, tiled=True)
    w_qkv = parcel[:, :share].reshape(width, 3 * wide)
    gain_one = parcel[:, share, :share].reshape(1, width).astype(F32)
    gain_two = parcel[:, share, share : 2 * share].reshape(1, width).astype(F32)
    first = lax.all_gather(jnp.concatenate(near, 0), DP, axis=0, tiled=True)
    gathered = jnp.concatenate(gathered, 0)

    memory = jnp.concatenate(
        [m[0].reshape(-1, ring, wide).transpose(1, 0, 2) for m in (memory_keys, memory_values)], 2
    )
    memory = lax.all_to_all(after(memory, token_steps[-2]), "fsdp", 0, 0, tiled=True).reshape(-1, 2 * wide)
    down_full = lax.all_gather(jnp.concatenate(near_down, 0), DP, axis=0, tiled=True)

    cosine, sine = rotary_tables(length)
    qkv = project_qkv(gathered, gain_one, w_qkv, cosine, sine, heads)
    attended_heads, lse = attend_forward(chosen_all, counts_all, qkv, memory, heads, top)
    attended = lax.all_to_all(attended_heads, "fsdp", 0, 1, tiled=True)

    upstream = cotangent[0]
    mixed, grad_middle, grad_attended, gain_two_grad, grads, *grad_down = feed_forward(
        mine, attended, upstream, gain_two, first, down_full, span
    )
    grad_heads = lax.all_to_all(grad_attended, "fsdp", 1, 0, tiled=True)
    grads = lax.psum_scatter(grads, DP, scatter_dimension=0, tiled=True)[0]

    partial, grad_w_qkv, gain_one_grad = attend_backward(
        chosen_all, counts_all, qkv, memory, grad_heads, attended_heads, lse, cosine, sine, gathered, gain_one,
        w_qkv, heads, top,
    )
    own_term, steps = chain_scatter(partial, "fsdp")
    grads = after(grads, steps[-1])

    gains = jnp.concatenate([gain_one_grad, gain_two_grad], 0).reshape(2, span, -1).transpose(1, 0, 2)
    gains = jnp.pad(gains.astype(BF16), ((0, 0), (0, extra - 2), (0, 3 * wide - gains.shape[2])))
    late = jnp.concatenate([grad_w_qkv.reshape(span, -1, 3 * wide), gains], 1)
    late = late.reshape(span // 2, 2, late.shape[1], 3 * wide)
    core = lax.axis_index("core")
    taken = lax.ppermute(lax.dynamic_index_in_dim(late, 1 - core, 1, keepdims=False), "core", [(0, 1), (1, 0)])
    late = lax.dynamic_index_in_dim(late, core, 1, keepdims=False).astype(F32) + taken.astype(F32)
    late = after(late.astype(BF16), steps[0])
    late = jnp.sum(lax.all_to_all(late, "chip", 0, 0, tiled=True).astype(F32), 0).astype(BF16)
    gains = late[-extra : 2 - extra, : ring * share].reshape(2, ring, share).transpose(1, 0, 2)
    gains = jnp.pad(gains, ((0, 0), (0, extra - 2), (0, 3 * wide - share)))
    late = jnp.concatenate([late[:-extra].reshape(ring, share, 3 * wide), gains], 1)
    late = lax.all_to_all(late, "fsdp", 0, 0, tiled=True).astype(F32)
    projections = [
        late[:, :share, part * wide : (part + 1) * wide].transpose(1, 0, 2).reshape(share, width)
        for part in range(3)
    ]
    gain_shares = jnp.sum(late[:, share : share + 2, :share], 0)

    strip = grads.shape[1]
    lanes = width // strip
    tall = w_down.shape[0]
    if grad_down:
        down = lax.psum_scatter(grad_down[0], DP, scatter_dimension=0, tiled=True)
        down = down.reshape(ring, tall, lanes, strip).transpose(0, 2, 1, 3)
    else:
        down = grads[: ring * tall * lanes].reshape(lanes, ring, tall, strip).transpose(1, 0, 2, 3)
        grads = grads[ring * tall * lanes :]
    grads = grads.reshape(-1, ring, share, strip).transpose(1, 0, 2, 3)
    pieces = jnp.concatenate([down.reshape(ring, -1, strip), grads.reshape(ring, -1, strip)], 1)
    rising, falling = steps[-1]
    grad_normed = own_term + rising.astype(F32) + falling.astype(F32)
    own = mine.astype(F32)
    factor = lax.rsqrt(jnp.mean(own * own, -1, keepdims=True) + EPSILON)
    scaled = grad_normed * gain_one
    inner = jnp.mean(scaled * own, -1, keepdims=True)
    tokens_grad = (grad_middle + factor * scaled - own * (factor * factor * factor * inner)).astype(BF16)

    pieces = lax.psum_scatter(pieces, "fsdp", scatter_dimension=0, tiled=True)[0].astype(F32)
    down_share = pieces[: lanes * tall].reshape(lanes, tall, strip).transpose(1, 0, 2).reshape(tall, width)
    others = pieces[lanes * tall :].reshape(-1, share, strip).transpose(1, 0, 2).reshape(share, -1)
    return (
        mixed[None],
        tokens_grad[None],
        *projections,
        others[:, :width],
        others[:, width : width + hidden_width],
        others[:, width + hidden_width :],
        down_share,
        gain_shares[0],
        gain_shares[1],
    )


def solution(mesh):
    span, ring = mesh.shape["dp"], mesh.shape["fsdp"]
    fine = Mesh(mesh.devices.reshape(span // 2, 2, ring), DP + ("fsdp",))
    every = DP + ("fsdp",)
    rows, matrix, vector = P(DP, "fsdp", None), P(every, None), P(every)
    in_specs = (rows,) * 5 + (matrix,) * 7 + (vector,) * 2 + (rows,)
    out_specs = (rows,) * 2 + (matrix,) * 7 + (vector,) * 2
    return jax.shard_map(body, mesh=fine, in_specs=in_specs, out_specs=out_specs, check_vma=False)
```

```python
import functools
import math

import jax
import jax.numpy as jnp
import numpy as np
from jax import lax
from jax.experimental import pallas as pl
from jax.experimental.pallas import tpu as pltpu
from jax.sharding import Mesh
from jax.sharding import PartitionSpec as P

HEAD_DIM = 128
QBLK = 256
MBLK = 128
EPSILON = 1e-06
NEGATIVE = -1e30
SCALE = 1.0 / math.sqrt(HEAD_DIM)
LOG2E = math.log2(math.e)
MIB = 1 << 20
F32 = jnp.float32
BF16 = jnp.bfloat16
DP = ("chip", "core")
NT = (((1,), (1,)), ((), ()))
TN = (((0,), (0,)), ((), ()))


def dot(left, right, dims=(((1,), (0,)), ((), ()))):
    return lax.dot_general(left, right, dims, preferred_element_type=F32)


def rotary_tables(length):
    half_dim = HEAD_DIM // 2
    frequency = 10000.0 ** (-jnp.arange(half_dim, dtype=F32) / half_dim)
    angles = jnp.arange(length, dtype=jnp.int32).astype(F32)[:, None] * frequency[None, :]
    cosine, sine = jnp.cos(angles), jnp.sin(angles)
    return jnp.concatenate([cosine, cosine], 1), jnp.concatenate([-sine, sine], 1)


def qkv_kernel(heads, place_ref, tok_ref, gain_ref, wq_ref, wk_ref, wv_ref, cos_ref, sin_ref, qkv_ref):
    rows = tok_ref[...].astype(F32)
    factor = lax.rsqrt(jnp.mean(rows * rows, -1, keepdims=True) + EPSILON)
    normed = (rows * factor * gain_ref[...]).astype(BF16)
    cosine, sine = cos_ref[...], sin_ref[...]
    for part, w_ref in enumerate((wq_ref, wk_ref, wv_ref)):
        values = dot(normed, w_ref[...])
        for head in range(heads):
            value = values[:, head * HEAD_DIM : (head + 1) * HEAD_DIM]
            if part < 2:
                value = value * cosine + pltpu.roll(value, HEAD_DIM // 2, 1) * sine
            if part == 0:
                value = value * (SCALE * LOG2E)
            at = (part * heads + head) * HEAD_DIM
            qkv_ref[:, at : at + HEAD_DIM] = value.astype(BF16)


def project_qkv(place, tokens_all, gain, w_qkv, cosine, sine, heads, ring):
    length, width = tokens_all.shape
    wide = heads * HEAD_DIM
    block = 2 * QBLK
    part = [pl.BlockSpec((width, wide), lambda i, place, p=p: (0, p * ring + place[0])) for p in range(3)]
    return pl.pallas_call(
        functools.partial(qkv_kernel, heads),
        grid_spec=pltpu.PrefetchScalarGridSpec(
            num_scalar_prefetch=1,
            grid=(length // block,),
            in_specs=[
                pl.BlockSpec((block, width), lambda i, _: (i, 0)),
                pl.BlockSpec((1, width), lambda i, _: (0, 0)),
                *part,
                pl.BlockSpec((block, HEAD_DIM), lambda i, _: (i, 0)),
                pl.BlockSpec((block, HEAD_DIM), lambda i, _: (i, 0)),
            ],
            out_specs=pl.BlockSpec((block, 3 * wide), lambda i, _: (i, 0)),
        ),
        out_shape=jax.ShapeDtypeStruct((length, 3 * wide), BF16),
        compiler_params=pltpu.CompilerParams(vmem_limit_bytes=48 * MIB),
        cost_estimate=pl.CostEstimate(
            flops=6 * length * width * wide, bytes_accessed=4 * length * (width + 3 * wide), transcendentals=0
        ),
        name="project_qkv",
    )(place, tokens_all, gain, w_qkv, w_qkv, w_qkv, cosine, sine)


def memory_bias(counts_ref, base, top, axis):
    shape = (1, top * MBLK) if axis == 1 else (top * MBLK, 1)
    column = lax.broadcasted_iota(jnp.int32, shape, axis)
    limit = jnp.zeros(shape, jnp.int32)
    for entry in range(top):
        inside = (column >= entry * MBLK) & (column < entry * MBLK + counts_ref[base + entry])
        limit = jnp.where(inside, 1, limit)
    return jnp.where(limit > 0, 0.0, NEGATIVE)


def pick_memory(ref, chosen_ref, base, top):
    rows = [
        ref[pl.ds(pl.multiple_of(chosen_ref[base + entry] * MBLK, MBLK), MBLK), :]
        for entry in range(top)
    ]
    return jnp.concatenate(rows, 0)


def forward_kernel(
    top, chosen_ref, counts_ref, q_ref, k_ref, v_ref, mk_ref, mv_ref, out_ref, lse_ref, acc_s, peak_s
):
    block = pl.program_id(0)
    rows = q_ref.shape[0]
    subs = rows // QBLK
    own = pl.ds(pl.multiple_of(block * rows, rows), rows)
    causal = lax.broadcasted_iota(jnp.int32, (rows, rows), 0) >= lax.broadcasted_iota(jnp.int32, (rows, rows), 1)
    ones = jnp.ones((rows, HEAD_DIM), BF16)
    mem_ones = jnp.ones((top * MBLK, HEAD_DIM), BF16)
    remote = []
    for sub in range(subs):
        base = (block * subs + sub) * top
        keys = pick_memory(mk_ref, chosen_ref, base, top)
        query = q_ref[sub * QBLK : (sub + 1) * QBLK, :]
        remote.append(dot(query, keys, NT) + memory_bias(counts_ref, base, top, 1))
    local = jnp.where(causal, dot(q_ref[...], k_ref[own, :], NT), NEGATIVE)
    peak = jnp.max(local, -1, keepdims=True)
    peak = jnp.maximum(peak, jnp.concatenate([jnp.max(r, -1, keepdims=True) for r in remote], 0))
    acc = dot(jnp.exp2(local - peak).astype(BF16), jnp.concatenate([v_ref[own, :], ones], 1))
    more = []
    for sub in range(subs):
        values = pick_memory(mv_ref, chosen_ref, (block * subs + sub) * top, top)
        weights = jnp.exp2(remote[sub] - peak[sub * QBLK : (sub + 1) * QBLK]).astype(BF16)
        more.append(dot(weights, jnp.concatenate([values, mem_ones], 1)))
    acc_s[...] = acc + jnp.concatenate(more, 0)
    peak_s[...] = jnp.broadcast_to(peak, (rows, HEAD_DIM))

    def step(index, carry):
        there = pl.ds(pl.multiple_of(index * rows, rows), rows)
        peak = peak_s[:, :1]
        scores = dot(q_ref[...], k_ref[there, :], NT)
        higher = jnp.maximum(peak, jnp.max(scores, -1, keepdims=True))
        weights = jnp.exp2(scores - higher).astype(BF16)
        values = jnp.concatenate([v_ref[there, :], ones], 1)
        acc_s[...] = acc_s[...] * jnp.exp2(peak - higher) + dot(weights, values)
        peak_s[...] = jnp.broadcast_to(higher, (rows, HEAD_DIM))
        return carry

    lax.fori_loop(0, block, step, 0)
    total = acc_s[:, HEAD_DIM:]
    out_ref[...] = (acc_s[:, :HEAD_DIM] / total).astype(BF16)
    lse_ref[...] = peak_s[:, :1] + jnp.log2(total[:, :1])


def attend_forward(chosen, counts, qkv, memory, head, heads, top):
    length = qkv.shape[0]
    rows = min(2 * QBLK, length)
    mem_rows = memory.shape[0]
    return pl.pallas_call(
        functools.partial(forward_kernel, top),
        grid_spec=pltpu.PrefetchScalarGridSpec(
            num_scalar_prefetch=2,
            grid=(length // rows,),
            in_specs=[
                pl.BlockSpec((rows, HEAD_DIM), lambda i, *_: (i, head)),
                pl.BlockSpec((length, HEAD_DIM), lambda i, *_: (0, heads + head)),
                pl.BlockSpec((length, HEAD_DIM), lambda i, *_: (0, 2 * heads + head)),
                pl.BlockSpec((mem_rows, HEAD_DIM), lambda i, *_: (0, head)),
                pl.BlockSpec((mem_rows, HEAD_DIM), lambda i, *_: (0, heads + head)),
            ],
            out_specs=[
                pl.BlockSpec((rows, HEAD_DIM), lambda i, *_: (i, 0)),
                pl.BlockSpec((rows, 1), lambda i, *_: (i, 0)),
            ],
            scratch_shapes=[
                pltpu.VMEM((rows, 2 * HEAD_DIM), F32),
                pltpu.VMEM((rows, HEAD_DIM), F32),
            ],
        ),
        out_shape=[
            jax.ShapeDtypeStruct((length, HEAD_DIM), BF16),
            jax.ShapeDtypeStruct((length, 1), F32),
        ],
        compiler_params=pltpu.CompilerParams(vmem_limit_bytes=48 * MIB),
        cost_estimate=pl.CostEstimate(
            flops=4 * length * HEAD_DIM * (length // 2 + top * MBLK),
            bytes_accessed=8 * length * HEAD_DIM,
            transcendentals=length * (length // 2 + top * MBLK),
        ),
        name="attend_forward",
    )(chosen, counts, qkv, qkv, qkv, memory, memory)


def backward_kernel(
    top, chosen_ref, counts_ref, place_ref, q_ref, k_ref, v_ref, mk_ref, mv_ref, go_ref, out_ref, lse_ref,
    cos_ref, sin_ref, tok_ref, gain_ref, wq_ref, wk_ref, wv_ref, grad_ref, grad_w_ref, gain_grad_ref,
    gk_s, gv_s, gq_s, gw_s,
):
    block = pl.num_programs(0) - 1 - pl.program_id(0)
    rows = q_ref.shape[0]
    subs = rows // QBLK
    own = pl.ds(pl.multiple_of(block * rows, rows), rows)
    key_at = lax.broadcasted_iota(jnp.int32, (rows, rows), 0)
    query_at = lax.broadcasted_iota(jnp.int32, (rows, rows), 1)
    causal = query_at >= key_at

    @pl.when(pl.program_id(0) == 0)
    def _():
        gk_s[...] = jnp.zeros_like(gk_s)
        gv_s[...] = jnp.zeros_like(gv_s)
        gw_s[...] = jnp.zeros_like(gw_s)

    def spread(column):
        return jnp.transpose(jnp.broadcast_to(column, (rows, HEAD_DIM)))[:1]

    lse = spread(lse_ref[...])
    delta = spread(jnp.sum(go_ref[...].astype(F32) * out_ref[...].astype(F32), -1, keepdims=True))

    def pair(queries, keys, values, mask):
        scores = mask(dot(keys, q_ref[queries, :], NT))
        weights = jnp.exp2(scores - lse[:, queries])
        grad_weights = dot(values, go_ref[queries, :], NT)
        return weights.astype(BF16), (weights * (grad_weights - delta[:, queries])).astype(BF16)

    for sub in range(subs):
        base = (block * subs + sub) * top
        queries = slice(sub * QBLK, (sub + 1) * QBLK)
        keys = pick_memory(mk_ref, chosen_ref, base, top)
        values = pick_memory(mv_ref, chosen_ref, base, top)
        bias = memory_bias(counts_ref, base, top, 0)
        _, grad_scores = pair(queries, keys, values, lambda scores: scores + bias)
        gq_s[queries, :] = dot(grad_scores, keys, TN)

    def local(there, mask):
        keys = k_ref[there, :]
        weights, grad_scores = pair(slice(0, rows), keys, v_ref[there, :], mask)
        gk_s[there, :] += dot(grad_scores, q_ref[...])
        gv_s[there, :] += dot(weights, go_ref[...])
        gq_s[...] += dot(grad_scores, keys, TN)

    local(own, lambda scores: jnp.where(causal, scores, NEGATIVE))

    def step(index, carry):
        local(pl.ds(pl.multiple_of(index * rows, rows), rows), lambda scores: scores)
        return carry

    lax.fori_loop(0, block, step, 0)
    cosine, sine = cos_ref[...], sin_ref[...]

    def unturn(value):
        return value * cosine - pltpu.roll(value, HEAD_DIM // 2, 1) * sine

    grad = jnp.concatenate(
        [
            unturn(gq_s[...] * SCALE).astype(BF16),
            unturn(gk_s[own, :] * (1.0 / LOG2E)).astype(BF16),
            gv_s[own, :].astype(BF16),
        ],
        1,
    )
    grad_ref[...] = grad
    tokens = tok_ref[...].astype(F32)
    tokens = tokens * lax.rsqrt(jnp.mean(tokens * tokens, -1, keepdims=True) + EPSILON)
    gw_s[...] += dot(tokens.astype(BF16), grad, TN)

    @pl.when(block == 0)
    def _():
        raw = gw_s[...]
        weights = jnp.concatenate([wq_ref[...], wk_ref[...], wv_ref[...]], 1).astype(F32)
        gain_grad_ref[...] = jnp.sum(raw * weights, -1, keepdims=True)
        grad_w_ref[...] = (raw * gain_ref[...]).astype(BF16)


def attend_backward(
    chosen, counts, place, qkv, memory, grad_out, out, lse, cosine, sine, tokens_all, gain, w_qkv, head, heads, top, ring
):
    length = qkv.shape[0]
    width = tokens_all.shape[1]
    rows = min(2 * QBLK, length)
    mem_rows = memory.shape[0]
    last = length // rows - 1
    parts = [
        pl.BlockSpec((width, HEAD_DIM), lambda i, c, n, place, p=p: (0, (p * ring + place[0]) * heads + head))
        for p in range(3)
    ]
    return pl.pallas_call(
        functools.partial(backward_kernel, top),
        grid_spec=pltpu.PrefetchScalarGridSpec(
            num_scalar_prefetch=3,
            grid=(last + 1,),
            in_specs=[
                pl.BlockSpec((rows, HEAD_DIM), lambda i, *_: (last - i, head)),
                pl.BlockSpec((length, HEAD_DIM), lambda i, *_: (0, heads + head)),
                pl.BlockSpec((length, HEAD_DIM), lambda i, *_: (0, 2 * heads + head)),
                pl.BlockSpec((mem_rows, HEAD_DIM), lambda i, *_: (0, head)),
                pl.BlockSpec((mem_rows, HEAD_DIM), lambda i, *_: (0, heads + head)),
                pl.BlockSpec((rows, HEAD_DIM), lambda i, *_: (last - i, 0)),
                pl.BlockSpec((rows, HEAD_DIM), lambda i, *_: (last - i, 0)),
                pl.BlockSpec((rows, 1), lambda i, *_: (last - i, 0)),
                pl.BlockSpec((rows, HEAD_DIM), lambda i, *_: (last - i, 0)),
                pl.BlockSpec((rows, HEAD_DIM), lambda i, *_: (last - i, 0)),
                pl.BlockSpec((rows, width), lambda i, *_: (last - i, 0)),
                pl.BlockSpec((width, 1), lambda i, *_: (0, 0)),
                *parts,
            ],
            out_specs=[
                pl.BlockSpec((rows, 3 * HEAD_DIM), lambda i, *_: (last - i, 0)),
                pl.BlockSpec((width, 3 * HEAD_DIM), lambda i, *_: (0, 0)),
                pl.BlockSpec((width, 1), lambda i, *_: (0, 0)),
            ],
            scratch_shapes=[
                pltpu.VMEM((length, HEAD_DIM), F32),
                pltpu.VMEM((length, HEAD_DIM), F32),
                pltpu.VMEM((rows, HEAD_DIM), F32),
                pltpu.VMEM((width, 3 * HEAD_DIM), F32),
            ],
        ),
        out_shape=[
            jax.ShapeDtypeStruct((length, 3 * HEAD_DIM), BF16),
            jax.ShapeDtypeStruct((width, 3 * HEAD_DIM), BF16),
            jax.ShapeDtypeStruct((width, 1), F32),
        ],
        compiler_params=pltpu.CompilerParams(vmem_limit_bytes=48 * MIB),
        cost_estimate=pl.CostEstimate(
            flops=10 * length * HEAD_DIM * (length // 2 + top * MBLK),
            bytes_accessed=16 * length * HEAD_DIM,
            transcendentals=length * (length // 2 + top * MBLK),
        ),
        name="attend_backward",
    )(
        chosen, counts, place, qkv, qkv, qkv, memory, memory, grad_out, out, lse, cosine, sine, tokens_all, gain,
        w_qkv, w_qkv, w_qkv,
    )


def finish_kernel(heads, tok_ref, gain_ref, mid_ref, w_ref, *refs):
    grads, out_ref = refs[:-1], refs[-1]
    ring = grads[0].shape[0]
    width = tok_ref.shape[1]
    wide = heads * HEAD_DIM
    total = None
    for part in range(3):
        lanes = slice(part * HEAD_DIM, (part + 1) * HEAD_DIM)
        for place in range(ring):
            left = [grad[place, :, lanes] for grad in grads]
            left = jnp.concatenate(left, 1) if heads > 1 else left[0]
            at = (part * ring + place) * wide
            term = dot(left, w_ref[:, at : at + wide], NT)
            total = term if total is None else total + term
    own = tok_ref[...].astype(F32)
    factor = lax.rsqrt(jnp.mean(own * own, -1, keepdims=True) + EPSILON)
    scaled = total * gain_ref[...]
    inner = jnp.mean(scaled * own, -1, keepdims=True)
    out_ref[...] = (mid_ref[...] + factor * scaled - own * (factor * factor * factor * inner)).astype(BF16)


def finish_tokens(tokens, gain, grad_middle, w_qkv, grads):
    rows, width = tokens.shape
    ring = grads[0].shape[0]
    heads = len(grads)
    block = min(rows, QBLK)
    return pl.pallas_call(
        functools.partial(finish_kernel, heads),
        grid=(rows // block,),
        in_specs=[
            pl.BlockSpec((block, width), lambda i: (i, 0)),
            pl.BlockSpec((1, width), lambda i: (0, 0)),
            pl.BlockSpec((block, width), lambda i: (i, 0)),
            pl.BlockSpec(w_qkv.shape, lambda i: (0, 0)),
            *[pl.BlockSpec((ring, block, 3 * HEAD_DIM), lambda i: (0, i, 0)) for _ in grads],
        ],
        out_specs=pl.BlockSpec((block, width), lambda i: (i, 0)),
        out_shape=jax.ShapeDtypeStruct((rows, width), BF16),
        compiler_params=pltpu.CompilerParams(vmem_limit_bytes=48 * MIB),
        cost_estimate=pl.CostEstimate(
            flops=6 * rows * width * width, bytes_accessed=8 * width * width, transcendentals=0
        ),
        name="finish_tokens",
    )(tokens, gain, grad_middle, w_qkv, *grads)


def ffn_kernel(
    span, merged, heads, tok_ref, cot_ref, gain_ref, out_w, gate_w, up_w, down_w, *rest
):
    att_refs, rest = rest[:heads], rest[heads:]
    mixed_ref, grad_mid_ref, gain_grad_ref, grads_ref, *rest = rest
    grad_att_refs, rest = rest[:heads], rest[heads:]
    if not merged:
        down_grads_ref, rest = rest[0], rest[1:]
    att_s, middle_s, normed_s, turned_s, mixed_s, upstream_s, gate_s, up_s, down_s, out_s, sems, late_sems = rest
    step, steps = pl.program_id(0), pl.num_programs(0)
    width = tok_ref.shape[1]
    share = width // span
    wide = gate_w.shape[1]
    hidden_width = down_s.shape[0]
    tall = hidden_width // span
    lanes = width // wide
    first = tall * lanes if merged else 0
    slot = step % 2

    @pl.when(step == 0)
    def _():
        for place in range(att_refs[0].shape[0]):
            for head in range(heads):
                at = (place * heads + head) * HEAD_DIM
                att_s[:, at : at + HEAD_DIM] = att_refs[head][place]
        middle = tok_ref[...].astype(F32) + dot(att_s[...], out_w[...])
        middle_s[...] = middle
        factor = lax.rsqrt(jnp.mean(middle * middle, -1, keepdims=True) + EPSILON)
        normed = (middle * factor * gain_ref[...]).astype(BF16)
        normed_s[...] = normed
        turned_s[...] = jnp.transpose(normed)
        mixed_s[...] = middle
        upstream_s[...] = jnp.zeros_like(upstream_s)

    def copy_out(kind, which, index):
        source = (gate_s, up_s)[kind].at[which]
        start = first + (lanes + kind * steps + index) * share
        target = grads_ref.at[:, pl.ds(start, share), :]
        return pltpu.make_async_copy(source, target, sems.at[kind, which])

    normed = normed_s[...]
    upstream = cot_ref[...]
    both = jnp.concatenate([gate_w[...], up_w[...]], 1)
    acts = dot(normed, both)
    gate_act, up_act = acts[:, :wide], acts[:, wide:]
    grad_hidden = dot(upstream, down_w[...], NT)
    sigmoid = jax.nn.sigmoid(gate_act)
    silu = gate_act * sigmoid
    hidden = (silu * up_act).astype(BF16)
    grad_gate = (grad_hidden * up_act * sigmoid * (1.0 + gate_act * (1.0 - sigmoid))).astype(BF16)
    grad_up = (grad_hidden * silu).astype(BF16)
    mixed_s[...] += dot(hidden, down_w[...])
    grad_acts = jnp.concatenate([grad_gate, grad_up], 1)
    upstream_s[...] += dot(grad_acts, both, NT)
    down_s[pl.ds(pl.multiple_of(step * wide, wide), wide), :] = dot(hidden, upstream, TN).astype(BF16)

    @pl.when(step >= 2)
    def _():
        copy_out(0, slot, step - 2).wait()
        copy_out(1, slot, step - 2).wait()

    weight_grads = dot(turned_s[...], grad_acts).astype(BF16)
    gate_s[slot] = weight_grads[:, :wide].reshape(span, share, wide)
    up_s[slot] = weight_grads[:, wide:].reshape(span, share, wide)
    copy_out(0, slot, step).start()
    copy_out(1, slot, step).start()

    @pl.when(step == steps - 1)
    def _():
        copies = []
        if merged:
            for place in range(span):
                for lane in range(lanes):
                    copies.append(
                        pltpu.make_async_copy(
                            down_s.at[pl.ds(place * tall, tall), pl.ds(lane * wide, wide)],
                            grads_ref.at[place, pl.ds(lane * tall, tall), :],
                            late_sems.at[len(copies)],
                        )
                    )
        else:
            copies.append(pltpu.make_async_copy(down_s, down_grads_ref, late_sems.at[0]))
        for copy in copies:
            copy.start()
        mixed_ref[...] = mixed_s[...].astype(BF16)
        middle = middle_s[...]
        grad = upstream_s[...]
        factor = lax.rsqrt(jnp.mean(middle * middle, -1, keepdims=True) + EPSILON)
        gain_grad_ref[...] = jnp.sum(grad * middle * factor, 0, keepdims=True)
        scaled = grad * gain_ref[...]
        inner = jnp.mean(scaled * middle, -1, keepdims=True)
        grad_middle = cot_ref[...].astype(F32) + factor * scaled - middle * (factor * factor * factor * inner)
        grad_mid_ref[...] = grad_middle
        branch = grad_middle.astype(BF16)
        grad_att = dot(branch, out_w[...], NT).astype(BF16)
        for place in range(att_refs[0].shape[0]):
            for head in range(heads):
                at = (place * heads + head) * HEAD_DIM
                grad_att_refs[head][place] = grad_att[:, at : at + HEAD_DIM]
        turned_att = jnp.transpose(att_s[...])
        for lane in range(lanes):
            columns = slice(lane * wide, (lane + 1) * wide)
            out_s[lane] = dot(turned_att, branch[:, columns]).astype(BF16).reshape(span, share, wide)
            more = pltpu.make_async_copy(
                out_s.at[lane],
                grads_ref.at[:, pl.ds(first + lane * share, share), :],
                late_sems.at[len(copies)],
            )
            more.start()
            copies.append(more)
        for copy in copies:
            copy.wait()
        copy_out(0, 1 - slot, step - 1).wait()
        copy_out(1, 1 - slot, step - 1).wait()
        copy_out(0, slot, step).wait()
        copy_out(1, slot, step).wait()


def feed_forward(tokens, attended, upstream, gain, weights, w_down, span):
    rows, width = tokens.shape
    heads, ring = len(attended), attended[0].shape[0]
    hidden_width = w_down.shape[0]
    wide = 2 * HEAD_DIM
    steps = hidden_width // wide
    lanes = width // wide
    share = width // span
    tall = hidden_width // span
    merged = tall % 16 == 0
    total = (lanes + 2 * steps) * share + (lanes * tall if merged else 0)
    shapes = [
        jax.ShapeDtypeStruct((rows, width), BF16),
        jax.ShapeDtypeStruct((rows, width), F32),
        jax.ShapeDtypeStruct((1, width), F32),
        jax.ShapeDtypeStruct((span, total, wide), BF16),
        *[jax.ShapeDtypeStruct((ring, rows, HEAD_DIM), BF16) for _ in attended],
    ]
    by_head = [pl.BlockSpec((ring, rows, HEAD_DIM), lambda i: (0, 0, 0)) for _ in attended]
    specs = [
        pl.BlockSpec((rows, width), lambda i: (0, 0)),
        pl.BlockSpec((rows, width), lambda i: (0, 0)),
        pl.BlockSpec((1, width), lambda i: (0, 0)),
        pl.BlockSpec(memory_space=pl.ANY),
        *by_head,
    ]
    if not merged:
        shapes.append(jax.ShapeDtypeStruct((hidden_width, width), BF16))
        specs.append(pl.BlockSpec(memory_space=pl.ANY))
    return pl.pallas_call(
        functools.partial(ffn_kernel, span, merged, heads),
        grid=(steps,),
        in_specs=[
            pl.BlockSpec((rows, width), lambda i: (0, 0)),
            pl.BlockSpec((rows, width), lambda i: (0, 0)),
            pl.BlockSpec((1, width), lambda i: (0, 0)),
            pl.BlockSpec((width, width), lambda i: (0, 0)),
            pl.BlockSpec((width, wide), lambda i: (0, lanes + i)),
            pl.BlockSpec((width, wide), lambda i: (0, lanes + steps + i)),
            pl.BlockSpec((wide, width), lambda i: (i, 0)),
            *by_head,
        ],
        out_specs=specs,
        out_shape=shapes,
        scratch_shapes=[
            pltpu.VMEM((rows, width), BF16),
            pltpu.VMEM((rows, width), F32),
            pltpu.VMEM((rows, width), BF16),
            pltpu.VMEM((width, rows), BF16),
            pltpu.VMEM((rows, width), F32),
            pltpu.VMEM((rows, width), F32),
            pltpu.VMEM((2, span, share, wide), BF16),
            pltpu.VMEM((2, span, share, wide), BF16),
            pltpu.VMEM((hidden_width, width), BF16),
            pltpu.VMEM((lanes, span, share, wide), BF16),
            pltpu.SemaphoreType.DMA((2, 2)),
            pltpu.SemaphoreType.DMA(((span * lanes if merged else 1) + lanes,)),
        ],
        compiler_params=pltpu.CompilerParams(vmem_limit_bytes=56 * MIB),
        cost_estimate=pl.CostEstimate(
            flops=6 * rows * width * (3 * hidden_width + width),
            bytes_accessed=4 * width * (3 * hidden_width + width),
            transcendentals=rows * hidden_width,
        ),
        name="feed_forward",
    )(tokens, upstream, gain, weights, weights, weights, w_down, *attended)


def after(value, earlier):
    return lax.optimization_barrier((value, earlier))[0]


def chain_gather(blocks, axis):
    size = lax.axis_size(axis)
    place = lax.axis_index(axis)
    steps = []
    rising = falling = tuple(blocks)
    for step in range(size - 1):
        up = [(i, i + 1) for i in range(step, size - 1)]
        down = [(i + 1, i) for i in range(size - 1 - step)]
        rising = tuple(lax.ppermute(block, axis, up) for block in rising)
        falling = tuple(lax.ppermute(block, axis, down) for block in falling)
        if len(blocks) > 1:
            rising, falling = lax.optimization_barrier((rising, falling))
        steps.append((rising, falling))
    results = []
    for number, block in enumerate(blocks):
        ordered = []
        for index in range(size):
            cases = []
            for mine in range(size):
                if mine == index:
                    cases.append(block)
                elif mine > index:
                    cases.append(steps[mine - index - 1][0][number])
                else:
                    cases.append(steps[index - mine - 1][1][number])
            ordered.append(lax.select_n(place, *cases) if size > 2 else lax.select_n(place > 0, *cases))
        results.append(ordered)
    return results, steps


def shift_gather(block, axis):
    size = lax.axis_size(axis)
    place = lax.axis_index(axis)
    taken = [block]
    for far in range(1, size):
        taken.append(lax.ppermute(block, axis, [(i, (i + far) % size) for i in range(size)]))
    ordered = []
    for index in range(size):
        cases = [taken[(mine - index) % size] for mine in range(size)]
        ordered.append(lax.select_n(place, *cases) if size > 2 else lax.select_n(place > 0, *cases))
    return ordered


def exchange(blocks, axis):
    return lax.all_to_all(blocks, axis, 0, 0, tiled=True)


def body(
    tokens, memory_keys, memory_values, chosen, counts, w_query, w_key, w_value, w_out, w_gate, w_up, w_down,
    gain_attn, gain_ffn, cotangent,
):
    ring, span = lax.axis_size("fsdp"), lax.axis_size(DP)
    rows, width = tokens.shape[1:]
    heads = width // HEAD_DIM // ring
    wide = heads * HEAD_DIM
    length = rows * ring
    top = chosen.shape[2]
    hidden_width = w_gate.shape[1]
    share = w_query.shape[0]
    mine = tokens[0]

    extra = 8 if share % 8 == 0 else 8 - share % 8
    choices = jnp.concatenate([chosen[0].reshape(-1), counts[0].reshape(-1)]).astype(BF16)
    notes = [
        jnp.pad(row, (0, 3 * width - row.shape[0]))[None]
        for row in (jnp.concatenate([gain_attn, gain_ffn]), choices)
    ]
    notes.append(jnp.zeros((extra - 2, 3 * width), BF16))
    parcel = jnp.concatenate([jnp.concatenate([w_query, w_key, w_value], 1), *notes], 0)
    parcel = jnp.stack(shift_gather(parcel, "fsdp"))
    picks = parcel[:, share + 1, : choices.shape[0]].astype(jnp.int32).reshape(ring, 2, -1)
    chosen_all, counts_all = picks[:, 0].reshape(-1), picks[:, 1].reshape(-1)
    parcel = lax.all_gather(parcel, DP, axis=0, tiled=True)
    shards = jnp.concatenate([w_out, w_gate, w_up], 1)
    (near, near_down), steps = chain_gather((shards, w_down), "fsdp")
    (gathered,), token_steps = chain_gather((after(mine, steps[-2]),), "fsdp")
    w_qkv = parcel[:, :share].reshape(width, 3 * width)
    gain_one = parcel[:, share, :share].reshape(1, width).astype(F32)
    gain_two = parcel[:, share, share : 2 * share].reshape(1, width).astype(F32)
    first = lax.all_gather(jnp.concatenate(near, 0), DP, axis=0, tiled=True)
    gathered = jnp.concatenate(gathered, 0)

    memory = jnp.concatenate(
        [m[0].reshape(-1, ring, wide).transpose(1, 0, 2) for m in (memory_keys, memory_values)], 2
    )
    memory = exchange(after(memory, token_steps[-2]), "fsdp").reshape(-1, 2 * wide)
    down_full = lax.all_gather(jnp.concatenate(near_down, 0), DP, axis=0, tiled=True)

    cosine, sine = rotary_tables(length)
    place = lax.axis_index("fsdp").astype(jnp.int32).reshape(1)
    qkv = project_qkv(place, gathered, gain_one, w_qkv, cosine, sine, heads, ring)
    outs, stats, attended = [], [], []
    for head in range(heads):
        out, lse = attend_forward(chosen_all, counts_all, qkv, memory, head, heads, top)
        outs.append(out)
        stats.append(lse)
        attended.append(exchange(out.reshape(ring, rows, HEAD_DIM), "fsdp"))

    mixed, grad_middle, gain_two_grad, grads, *others = feed_forward(
        mine, attended, cotangent[0], gain_two, first, down_full, span
    )
    grad_heads, grad_down = others[:heads], others[heads:]
    grads = lax.psum_scatter(grads, DP, scatter_dimension=0, tiled=True)[0]
    column = gain_one.reshape(width, 1)
    returned, weight_grads, gain_one_grad = [], [], 0.0
    for head in range(heads):
        grad_out = exchange(grad_heads[head], "fsdp").reshape(length, HEAD_DIM)
        if head:
            qkv = after(qkv, weight_grads[-1])
        grad, grad_w, gain_grad = attend_backward(
            chosen_all, counts_all, place, qkv, memory, grad_out, outs[head], stats[head], cosine, sine, gathered,
            column, w_qkv, head, heads, top, ring,
        )
        returned.append(exchange(grad.reshape(ring, rows, 3 * HEAD_DIM), "fsdp"))
        weight_grads.append(grad_w)
        gain_one_grad = gain_one_grad + gain_grad

    gains = jnp.stack([gain_one_grad.reshape(span, -1), gain_two_grad.reshape(span, -1)], 1)
    gains = jnp.pad(gains.astype(BF16), ((0, 0), (0, extra - 2), (0, 3 * wide - gains.shape[2])))
    late = jnp.concatenate(weight_grads, 1).reshape(span, -1, 3 * wide)
    late = jnp.concatenate([late, gains], 1)
    late = late.reshape(span // 2, 2, late.shape[1], 3 * wide)
    core = lax.axis_index("core")
    taken = lax.ppermute(lax.dynamic_index_in_dim(late, 1 - core, 1, keepdims=False), "core", [(0, 1), (1, 0)])
    late = lax.dynamic_index_in_dim(late, core, 1, keepdims=False).astype(F32) + taken.astype(F32)
    late = jnp.sum(exchange(late.astype(BF16), "chip").astype(F32), 0).astype(BF16)
    grads = after(grads, late)
    gains = late[-extra : 2 - extra, : ring * share].reshape(2, ring, share).transpose(1, 0, 2)
    gains = jnp.pad(gains, ((0, 0), (0, extra - 2), (0, 3 * wide - share)))
    late = jnp.concatenate([late[:-extra].reshape(ring, share, 3 * wide), gains], 1)
    late = exchange(late, "fsdp").astype(F32)
    projections = [
        jnp.concatenate(
            [
                late[:, :share, (head * 3 + part) * HEAD_DIM : (head * 3 + part + 1) * HEAD_DIM]
                for head in range(heads)
            ],
            2,
        )
        .transpose(1, 0, 2)
        .reshape(share, width)
        for part in range(3)
    ]
    gain_shares = jnp.sum(late[:, share : share + 2, :share], 0)
    tokens_grad = finish_tokens(mine, gain_one, grad_middle, w_qkv, returned)

    strip = grads.shape[1]
    lanes = width // strip
    tall = w_down.shape[0]
    if grad_down:
        down = lax.psum_scatter(grad_down[0], DP, scatter_dimension=0, tiled=True)
        down = down.reshape(ring, tall, lanes, strip).transpose(0, 2, 1, 3)
    else:
        down = grads[: ring * tall * lanes].reshape(lanes, ring, tall, strip).transpose(1, 0, 2, 3)
        grads = grads[ring * tall * lanes :]
    grads = grads.reshape(-1, ring, share, strip).transpose(1, 0, 2, 3)
    pieces = jnp.concatenate([down.reshape(ring, -1, strip), grads.reshape(ring, -1, strip)], 1)
    pieces = lax.psum_scatter(pieces, "fsdp", scatter_dimension=0, tiled=True)[0].astype(F32)
    down_share = pieces[: lanes * tall].reshape(lanes, tall, strip).transpose(1, 0, 2).reshape(tall, width)
    others = pieces[lanes * tall :].reshape(-1, share, strip).transpose(1, 0, 2).reshape(share, -1)
    return (
        mixed[None],
        tokens_grad[None],
        *projections,
        others[:, :width],
        others[:, width : width + hidden_width],
        others[:, width + hidden_width :],
        down_share,
        gain_shares[0],
        gain_shares[1],
    )


def solution(mesh):
    span, ring = mesh.shape["dp"], mesh.shape["fsdp"]
    fine = Mesh(mesh.devices.reshape(span // 2, 2, ring), DP + ("fsdp",))
    every = DP + ("fsdp",)
    rows, matrix, vector = P(DP, "fsdp", None), P(every, None), P(every)
    in_specs = (rows,) * 5 + (matrix,) * 7 + (vector,) * 2 + (rows,)
    out_specs = (rows,) * 2 + (matrix,) * 7 + (vector,) * 2
    return jax.shard_map(body, mesh=fine, in_specs=in_specs, out_specs=out_specs, check_vma=False)
```

```python
import functools
import math

import jax
import jax.numpy as jnp
import numpy as np
from jax import lax
from jax.experimental import pallas as pl
from jax.experimental.pallas import tpu as pltpu
from jax.sharding import Mesh
from jax.sharding import PartitionSpec as P

HEAD_DIM = 128
QBLK = 256
MBLK = 128
EPSILON = 1e-06
NEGATIVE = -1e30
SCALE = 1.0 / math.sqrt(HEAD_DIM)
LOG2E = math.log2(math.e)
MIB = 1 << 20
F32 = jnp.float32
BF16 = jnp.bfloat16
DP = ("chip", "core")
NT = (((1,), (1,)), ((), ()))
TN = (((0,), (0,)), ((), ()))


def dot(left, right, dims=(((1,), (0,)), ((), ()))):
    return lax.dot_general(left, right, dims, preferred_element_type=F32)


def rotary_tables(length):
    half_dim = HEAD_DIM // 2
    frequency = 10000.0 ** (-jnp.arange(half_dim, dtype=F32) / half_dim)
    angles = jnp.arange(length, dtype=jnp.int32).astype(F32)[:, None] * frequency[None, :]
    cosine, sine = jnp.cos(angles), jnp.sin(angles)
    return jnp.concatenate([cosine, cosine], 1), jnp.concatenate([-sine, sine], 1)


def qkv_kernel(heads, tok_ref, gain_ref, w_ref, cos_ref, sin_ref, qkv_ref):
    rows = tok_ref[...].astype(F32)
    factor = lax.rsqrt(jnp.mean(rows * rows, -1, keepdims=True) + EPSILON)
    normed = (rows * factor * gain_ref[...]).astype(BF16)
    cosine, sine = cos_ref[...], sin_ref[...]
    wide = heads * HEAD_DIM
    for part in range(3):
        values = dot(normed, w_ref[:, part * wide : (part + 1) * wide])
        for head in range(heads):
            value = values[:, head * HEAD_DIM : (head + 1) * HEAD_DIM]
            if part < 2:
                value = value * cosine + pltpu.roll(value, HEAD_DIM // 2, 1) * sine
            if part == 0:
                value = value * (SCALE * LOG2E)
            at = part * wide + head * HEAD_DIM
            qkv_ref[:, at : at + HEAD_DIM] = value.astype(BF16)


def project_qkv(tokens_all, gain, w_qkv, cosine, sine, heads):
    length, width = tokens_all.shape
    columns = w_qkv.shape[1]
    block = 2 * QBLK
    return pl.pallas_call(
        functools.partial(qkv_kernel, heads),
        grid=(length // block,),
        in_specs=[
            pl.BlockSpec((block, width), lambda i: (i, 0)),
            pl.BlockSpec((1, width), lambda i: (0, 0)),
            pl.BlockSpec((width, columns), lambda i: (0, 0)),
            pl.BlockSpec((block, HEAD_DIM), lambda i: (i, 0)),
            pl.BlockSpec((block, HEAD_DIM), lambda i: (i, 0)),
        ],
        out_specs=pl.BlockSpec((block, columns), lambda i: (i, 0)),
        out_shape=jax.ShapeDtypeStruct((length, columns), BF16),
        compiler_params=pltpu.CompilerParams(vmem_limit_bytes=48 * MIB),
        cost_estimate=pl.CostEstimate(
            flops=2 * length * width * columns, bytes_accessed=4 * length * (width + columns), transcendentals=0
        ),
        name="project_qkv",
    )(tokens_all, gain, w_qkv, cosine, sine)


def memory_bias(counts_ref, base, top, axis):
    shape = (1, top * MBLK) if axis == 1 else (top * MBLK, 1)
    column = lax.broadcasted_iota(jnp.int32, shape, axis)
    limit = jnp.zeros(shape, jnp.int32)
    for entry in range(top):
        inside = (column >= entry * MBLK) & (column < entry * MBLK + counts_ref[base + entry])
        limit = jnp.where(inside, 1, limit)
    return jnp.where(limit > 0, 0.0, NEGATIVE)


def pick_memory(ref, chosen_ref, base, top, columns=slice(None)):
    rows = [
        ref[pl.ds(pl.multiple_of(chosen_ref[base + entry] * MBLK, MBLK), MBLK), columns]
        for entry in range(top)
    ]
    return jnp.concatenate(rows, 0)


def forward_kernel(
    heads, top, chosen_ref, counts_ref, q_ref, k_ref, v_ref, mk_ref, mv_ref, out_ref, lse_ref, acc_s, peak_s
):
    block = pl.program_id(0)
    rows = q_ref.shape[0]
    subs = rows // QBLK
    own = pl.ds(pl.multiple_of(block * rows, rows), rows)
    causal = lax.broadcasted_iota(jnp.int32, (rows, rows), 0) >= lax.broadcasted_iota(jnp.int32, (rows, rows), 1)
    ones = jnp.ones((rows, HEAD_DIM), BF16)
    mem_ones = jnp.ones((top * MBLK, HEAD_DIM), BF16)
    biases = [memory_bias(counts_ref, (block * subs + sub) * top, top, 1) for sub in range(subs)]
    for head in range(heads):
        columns = slice(head * HEAD_DIM, (head + 1) * HEAD_DIM)
        remote = []
        for sub in range(subs):
            keys = pick_memory(mk_ref, chosen_ref, (block * subs + sub) * top, top, columns)
            query = q_ref[sub * QBLK : (sub + 1) * QBLK, columns]
            remote.append(dot(query, keys, NT) + biases[sub])
        local = jnp.where(causal, dot(q_ref[:, columns], k_ref[own, columns], NT), NEGATIVE)
        peak = jnp.max(local, -1, keepdims=True)
        peak = jnp.maximum(peak, jnp.concatenate([jnp.max(r, -1, keepdims=True) for r in remote], 0))
        values = jnp.concatenate([v_ref[own, columns], ones], 1)
        acc = dot(jnp.exp2(local - peak).astype(BF16), values)
        more = []
        for sub in range(subs):
            values = pick_memory(mv_ref, chosen_ref, (block * subs + sub) * top, top, columns)
            weights = jnp.exp2(remote[sub] - peak[sub * QBLK : (sub + 1) * QBLK]).astype(BF16)
            more.append(dot(weights, jnp.concatenate([values, mem_ones], 1)))
        acc_s[head] = acc + jnp.concatenate(more, 0)
        peak_s[head] = jnp.broadcast_to(peak, (rows, HEAD_DIM))

    def step(index, carry):
        there = pl.ds(pl.multiple_of(index * rows, rows), rows)
        for head in range(heads):
            columns = slice(head * HEAD_DIM, (head + 1) * HEAD_DIM)
            peak = peak_s[head][:, :1]
            scores = dot(q_ref[:, columns], k_ref[there, columns], NT)
            higher = jnp.maximum(peak, jnp.max(scores, -1, keepdims=True))
            weights = jnp.exp2(scores - higher).astype(BF16)
            values = jnp.concatenate([v_ref[there, columns], ones], 1)
            acc_s[head] = acc_s[head] * jnp.exp2(peak - higher) + dot(weights, values)
            peak_s[head] = jnp.broadcast_to(higher, (rows, HEAD_DIM))
        return carry

    lax.fori_loop(0, block, step, 0)
    for head in range(heads):
        columns = slice(head * HEAD_DIM, (head + 1) * HEAD_DIM)
        total = acc_s[head][:, HEAD_DIM:]
        out_ref[:, columns] = (acc_s[head][:, :HEAD_DIM] / total).astype(BF16)
        lse_ref[:, head : head + 1] = peak_s[head][:, :1] + jnp.log2(total[:, :1])


def attend_forward(chosen, counts, qkv, memory, heads, top):
    length = qkv.shape[0]
    wide = heads * HEAD_DIM
    rows = min(2 * QBLK, length)
    mem_rows = memory.shape[0]
    return pl.pallas_call(
        functools.partial(forward_kernel, heads, top),
        grid_spec=pltpu.PrefetchScalarGridSpec(
            num_scalar_prefetch=2,
            grid=(length // rows,),
            in_specs=[
                pl.BlockSpec((rows, wide), lambda i, *_: (i, 0)),
                pl.BlockSpec((length, wide), lambda i, *_: (0, 1)),
                pl.BlockSpec((length, wide), lambda i, *_: (0, 2)),
                pl.BlockSpec((mem_rows, wide), lambda i, *_: (0, 0)),
                pl.BlockSpec((mem_rows, wide), lambda i, *_: (0, 1)),
            ],
            out_specs=[
                pl.BlockSpec((rows, wide), lambda i, *_: (i, 0)),
                pl.BlockSpec((rows, heads), lambda i, *_: (i, 0)),
            ],
            scratch_shapes=[
                pltpu.VMEM((heads, rows, 2 * HEAD_DIM), F32),
                pltpu.VMEM((heads, rows, HEAD_DIM), F32),
            ],
        ),
        out_shape=[
            jax.ShapeDtypeStruct((length, wide), BF16),
            jax.ShapeDtypeStruct((length, heads), F32),
        ],
        compiler_params=pltpu.CompilerParams(vmem_limit_bytes=48 * MIB),
        cost_estimate=pl.CostEstimate(
            flops=4 * heads * length * HEAD_DIM * (length // 2 + top * MBLK),
            bytes_accessed=8 * length * wide,
            transcendentals=heads * length * (length // 2 + top * MBLK),
        ),
        name="attend_forward",
    )(chosen, counts, qkv, qkv, qkv, memory, memory)


def backward_kernel(
    head, top, chosen_ref, counts_ref, q_ref, k_ref, v_ref, mk_ref, mv_ref, go_ref, out_ref, lse_ref,
    cos_ref, sin_ref, tok_ref, gain_ref, wq_ref, wk_ref, wv_ref, grad_ref, grad_w_ref, gain_grad_ref,
    gk_s, gv_s, gq_s, gw_s,
):
    block = pl.num_programs(0) - 1 - pl.program_id(0)
    rows = q_ref.shape[0]
    subs = rows // QBLK
    own = pl.ds(pl.multiple_of(block * rows, rows), rows)
    key_at = lax.broadcasted_iota(jnp.int32, (rows, rows), 0)
    query_at = lax.broadcasted_iota(jnp.int32, (rows, rows), 1)
    causal = query_at >= key_at

    @pl.when(pl.program_id(0) == 0)
    def _():
        gk_s[...] = jnp.zeros_like(gk_s)
        gv_s[...] = jnp.zeros_like(gv_s)
        gw_s[...] = jnp.zeros_like(gw_s)

    def spread(column):
        return jnp.transpose(jnp.broadcast_to(column, (rows, HEAD_DIM)))[:1]

    lse = spread(lse_ref[:, head : head + 1])
    delta = spread(jnp.sum(go_ref[...].astype(F32) * out_ref[...].astype(F32), -1, keepdims=True))

    def pair(queries, keys, values, mask):
        scores = mask(dot(keys, q_ref[queries, :], NT))
        weights = jnp.exp2(scores - lse[:, queries])
        grad_weights = dot(values, go_ref[queries, :], NT)
        return weights.astype(BF16), (weights * (grad_weights - delta[:, queries])).astype(BF16)

    for sub in range(subs):
        base = (block * subs + sub) * top
        queries = slice(sub * QBLK, (sub + 1) * QBLK)
        keys = pick_memory(mk_ref, chosen_ref, base, top)
        values = pick_memory(mv_ref, chosen_ref, base, top)
        bias = memory_bias(counts_ref, base, top, 0)
        _, grad_scores = pair(queries, keys, values, lambda scores: scores + bias)
        gq_s[queries, :] = dot(grad_scores, keys, TN)

    def local(there, mask):
        keys = k_ref[there, :]
        weights, grad_scores = pair(slice(0, rows), keys, v_ref[there, :], mask)
        gk_s[there, :] += dot(grad_scores, q_ref[...])
        gv_s[there, :] += dot(weights, go_ref[...])
        gq_s[...] += dot(grad_scores, keys, TN)

    local(own, lambda scores: jnp.where(causal, scores, NEGATIVE))

    def step(index, carry):
        local(pl.ds(pl.multiple_of(index * rows, rows), rows), lambda scores: scores)
        return carry

    lax.fori_loop(0, block, step, 0)
    cosine, sine = cos_ref[...], sin_ref[...]

    def unturn(value):
        return value * cosine - pltpu.roll(value, HEAD_DIM // 2, 1) * sine

    grad = jnp.concatenate(
        [
            unturn(gq_s[...] * SCALE).astype(BF16),
            unturn(gk_s[own, :] * (1.0 / LOG2E)).astype(BF16),
            gv_s[own, :].astype(BF16),
        ],
        1,
    )
    grad_ref[...] = grad
    tokens = tok_ref[...].astype(F32)
    tokens = tokens * lax.rsqrt(jnp.mean(tokens * tokens, -1, keepdims=True) + EPSILON)
    gw_s[...] += dot(tokens.astype(BF16), grad, TN)

    @pl.when(block == 0)
    def _():
        raw = gw_s[...]
        weights = jnp.concatenate([wq_ref[...], wk_ref[...], wv_ref[...]], 1).astype(F32)
        gain_grad_ref[...] = jnp.sum(raw * weights, -1, keepdims=True)
        grad_w_ref[...] = (raw * gain_ref[...]).astype(BF16)


def attend_backward(
    chosen, counts, qkv, memory, grad_out, out, lse, cosine, sine, tokens_all, gain, w_qkv, head, heads, top
):
    length = qkv.shape[0]
    width = tokens_all.shape[1]
    rows = min(2 * QBLK, length)
    mem_rows = memory.shape[0]
    last = length // rows - 1
    parts = [
        pl.BlockSpec((width, HEAD_DIM), lambda i, c, n, p=p: (0, p * heads + head)) for p in range(3)
    ]
    return pl.pallas_call(
        functools.partial(backward_kernel, head, top),
        grid_spec=pltpu.PrefetchScalarGridSpec(
            num_scalar_prefetch=2,
            grid=(last + 1,),
            in_specs=[
                pl.BlockSpec((rows, HEAD_DIM), lambda i, *_: (last - i, head)),
                pl.BlockSpec((length, HEAD_DIM), lambda i, *_: (0, heads + head)),
                pl.BlockSpec((length, HEAD_DIM), lambda i, *_: (0, 2 * heads + head)),
                pl.BlockSpec((mem_rows, HEAD_DIM), lambda i, *_: (0, head)),
                pl.BlockSpec((mem_rows, HEAD_DIM), lambda i, *_: (0, heads + head)),
                pl.BlockSpec((rows, HEAD_DIM), lambda i, *_: (last - i, 0)),
                pl.BlockSpec((rows, HEAD_DIM), lambda i, *_: (last - i, head)),
                pl.BlockSpec((rows, heads), lambda i, *_: (last - i, 0)),
                pl.BlockSpec((rows, HEAD_DIM), lambda i, *_: (last - i, 0)),
                pl.BlockSpec((rows, HEAD_DIM), lambda i, *_: (last - i, 0)),
                pl.BlockSpec((rows, width), lambda i, *_: (last - i, 0)),
                pl.BlockSpec((width, 1), lambda i, *_: (0, 0)),
                *parts,
            ],
            out_specs=[
                pl.BlockSpec((rows, 3 * HEAD_DIM), lambda i, *_: (last - i, 0)),
                pl.BlockSpec((width, 3 * HEAD_DIM), lambda i, *_: (0, 0)),
                pl.BlockSpec((width, 1), lambda i, *_: (0, 0)),
            ],
            scratch_shapes=[
                pltpu.VMEM((length, HEAD_DIM), F32),
                pltpu.VMEM((length, HEAD_DIM), F32),
                pltpu.VMEM((rows, HEAD_DIM), F32),
                pltpu.VMEM((width, 3 * HEAD_DIM), F32),
            ],
        ),
        out_shape=[
            jax.ShapeDtypeStruct((length, 3 * HEAD_DIM), BF16),
            jax.ShapeDtypeStruct((width, 3 * HEAD_DIM), BF16),
            jax.ShapeDtypeStruct((width, 1), F32),
        ],
        compiler_params=pltpu.CompilerParams(vmem_limit_bytes=48 * MIB),
        cost_estimate=pl.CostEstimate(
            flops=10 * length * HEAD_DIM * (length // 2 + top * MBLK),
            bytes_accessed=16 * length * HEAD_DIM,
            transcendentals=length * (length // 2 + top * MBLK),
        ),
        name="attend_backward",
    )(
        chosen, counts, qkv, qkv, qkv, memory, memory, grad_out, out, lse, cosine, sine, tokens_all, gain,
        w_qkv, w_qkv, w_qkv,
    )


def finish_kernel(heads, tok_ref, gain_ref, mid_ref, w_ref, *refs):
    grads, out_ref = refs[:-1], refs[-1]
    ring = grads[0].shape[0]
    width = tok_ref.shape[1]
    wide = heads * HEAD_DIM
    total = None
    for part in range(3):
        lanes = slice(part * HEAD_DIM, (part + 1) * HEAD_DIM)
        for place in range(ring):
            left = [grad[place, :, lanes] for grad in grads]
            left = jnp.concatenate(left, 1) if heads > 1 else left[0]
            at = (part * ring + place) * wide
            term = dot(left, w_ref[:, at : at + wide], NT)
            total = term if total is None else total + term
    own = tok_ref[...].astype(F32)
    factor = lax.rsqrt(jnp.mean(own * own, -1, keepdims=True) + EPSILON)
    scaled = total * gain_ref[...]
    inner = jnp.mean(scaled * own, -1, keepdims=True)
    out_ref[...] = (mid_ref[...] + factor * scaled - own * (factor * factor * factor * inner)).astype(BF16)


def finish_tokens(tokens, gain, grad_middle, w_qkv, grads):
    rows, width = tokens.shape
    ring = grads[0].shape[0]
    heads = len(grads)
    block = min(rows, QBLK)
    return pl.pallas_call(
        functools.partial(finish_kernel, heads),
        grid=(rows // block,),
        in_specs=[
            pl.BlockSpec((block, width), lambda i: (i, 0)),
            pl.BlockSpec((1, width), lambda i: (0, 0)),
            pl.BlockSpec((block, width), lambda i: (i, 0)),
            pl.BlockSpec(w_qkv.shape, lambda i: (0, 0)),
            *[pl.BlockSpec((ring, block, 3 * HEAD_DIM), lambda i: (0, i, 0)) for _ in grads],
        ],
        out_specs=pl.BlockSpec((block, width), lambda i: (i, 0)),
        out_shape=jax.ShapeDtypeStruct((rows, width), BF16),
        compiler_params=pltpu.CompilerParams(vmem_limit_bytes=48 * MIB),
        cost_estimate=pl.CostEstimate(
            flops=6 * rows * width * width, bytes_accessed=8 * width * width, transcendentals=0
        ),
        name="finish_tokens",
    )(tokens, gain, grad_middle, w_qkv, *grads)


def ffn_kernel(
    span, merged, heads, tok_ref, cot_ref, gain_ref, out_w, gate_w, up_w, down_w, *rest
):
    att_ref, rest = rest[0], rest[1:]
    mixed_ref, grad_mid_ref, gain_grad_ref, grads_ref, *rest = rest
    grad_att_refs, rest = rest[:heads], rest[heads:]
    if not merged:
        down_grads_ref, rest = rest[0], rest[1:]
    att_s, middle_s, normed_s, turned_s, mixed_s, upstream_s, gate_s, up_s, down_s, out_s, sems, late_sems = rest
    step, steps = pl.program_id(0), pl.num_programs(0)
    width = tok_ref.shape[1]
    share = width // span
    wide = gate_w.shape[1]
    hidden_width = down_s.shape[0]
    tall = hidden_width // span
    lanes = width // wide
    first = tall * lanes if merged else 0
    slot = step % 2

    @pl.when(step == 0)
    def _():
        for place in range(att_ref.shape[0]):
            at = place * heads * HEAD_DIM
            att_s[:, at : at + heads * HEAD_DIM] = att_ref[place]
        middle = tok_ref[...].astype(F32) + dot(att_s[...], out_w[...])
        middle_s[...] = middle
        factor = lax.rsqrt(jnp.mean(middle * middle, -1, keepdims=True) + EPSILON)
        normed = (middle * factor * gain_ref[...]).astype(BF16)
        normed_s[...] = normed
        turned_s[...] = jnp.transpose(normed)
        mixed_s[...] = middle
        upstream_s[...] = jnp.zeros_like(upstream_s)

    def copy_out(kind, which, index):
        source = (gate_s, up_s)[kind].at[which]
        start = first + (lanes + kind * steps + index) * share
        target = grads_ref.at[:, pl.ds(start, share), :]
        return pltpu.make_async_copy(source, target, sems.at[kind, which])

    normed = normed_s[...]
    upstream = cot_ref[...]
    both = jnp.concatenate([gate_w[...], up_w[...]], 1)
    acts = dot(normed, both)
    gate_act, up_act = acts[:, :wide], acts[:, wide:]
    grad_hidden = dot(upstream, down_w[...], NT)
    sigmoid = jax.nn.sigmoid(gate_act)
    silu = gate_act * sigmoid
    hidden = (silu * up_act).astype(BF16)
    grad_gate = (grad_hidden * up_act * sigmoid * (1.0 + gate_act * (1.0 - sigmoid))).astype(BF16)
    grad_up = (grad_hidden * silu).astype(BF16)
    mixed_s[...] += dot(hidden, down_w[...])
    grad_acts = jnp.concatenate([grad_gate, grad_up], 1)
    upstream_s[...] += dot(grad_acts, both, NT)
    down_s[pl.ds(pl.multiple_of(step * wide, wide), wide), :] = dot(hidden, upstream, TN).astype(BF16)

    @pl.when(step >= 2)
    def _():
        copy_out(0, slot, step - 2).wait()
        copy_out(1, slot, step - 2).wait()

    weight_grads = dot(turned_s[...], grad_acts).astype(BF16)
    gate_s[slot] = weight_grads[:, :wide].reshape(span, share, wide)
    up_s[slot] = weight_grads[:, wide:].reshape(span, share, wide)
    copy_out(0, slot, step).start()
    copy_out(1, slot, step).start()

    @pl.when(step == steps - 1)
    def _():
        copies = []
        if merged:
            for place in range(span):
                for lane in range(lanes):
                    copies.append(
                        pltpu.make_async_copy(
                            down_s.at[pl.ds(place * tall, tall), pl.ds(lane * wide, wide)],
                            grads_ref.at[place, pl.ds(lane * tall, tall), :],
                            late_sems.at[len(copies)],
                        )
                    )
        else:
            copies.append(pltpu.make_async_copy(down_s, down_grads_ref, late_sems.at[0]))
        for copy in copies:
            copy.start()
        mixed_ref[...] = mixed_s[...].astype(BF16)
        middle = middle_s[...]
        grad = upstream_s[...]
        factor = lax.rsqrt(jnp.mean(middle * middle, -1, keepdims=True) + EPSILON)
        gain_grad_ref[...] = jnp.sum(grad * middle * factor, 0, keepdims=True)
        scaled = grad * gain_ref[...]
        inner = jnp.mean(scaled * middle, -1, keepdims=True)
        grad_middle = cot_ref[...].astype(F32) + factor * scaled - middle * (factor * factor * factor * inner)
        grad_mid_ref[...] = grad_middle
        branch = grad_middle.astype(BF16)
        grad_att = dot(branch, out_w[...], NT).astype(BF16)
        for place in range(att_ref.shape[0]):
            for head in range(heads):
                at = (place * heads + head) * HEAD_DIM
                grad_att_refs[head][place] = grad_att[:, at : at + HEAD_DIM]
        turned_att = jnp.transpose(att_s[...])
        for lane in range(lanes):
            columns = slice(lane * wide, (lane + 1) * wide)
            out_s[lane] = dot(turned_att, branch[:, columns]).astype(BF16).reshape(span, share, wide)
            more = pltpu.make_async_copy(
                out_s.at[lane],
                grads_ref.at[:, pl.ds(first + lane * share, share), :],
                late_sems.at[len(copies)],
            )
            more.start()
            copies.append(more)
        for copy in copies:
            copy.wait()
        copy_out(0, 1 - slot, step - 1).wait()
        copy_out(1, 1 - slot, step - 1).wait()
        copy_out(0, slot, step).wait()
        copy_out(1, slot, step).wait()


def feed_forward(tokens, attended, upstream, gain, weights, w_down, span):
    rows, width = tokens.shape
    ring = attended.shape[0]
    heads = attended.shape[2] // HEAD_DIM
    hidden_width = w_down.shape[0]
    wide = 2 * HEAD_DIM
    steps = hidden_width // wide
    lanes = width // wide
    share = width // span
    tall = hidden_width // span
    merged = tall % 16 == 0
    total = (lanes + 2 * steps) * share + (lanes * tall if merged else 0)
    shapes = [
        jax.ShapeDtypeStruct((rows, width), BF16),
        jax.ShapeDtypeStruct((rows, width), F32),
        jax.ShapeDtypeStruct((1, width), F32),
        jax.ShapeDtypeStruct((span, total, wide), BF16),
        *[jax.ShapeDtypeStruct((ring, rows, HEAD_DIM), BF16) for _ in range(heads)],
    ]
    by_head = [pl.BlockSpec((ring, rows, HEAD_DIM), lambda i: (0, 0, 0)) for _ in range(heads)]
    specs = [
        pl.BlockSpec((rows, width), lambda i: (0, 0)),
        pl.BlockSpec((rows, width), lambda i: (0, 0)),
        pl.BlockSpec((1, width), lambda i: (0, 0)),
        pl.BlockSpec(memory_space=pl.ANY),
        *by_head,
    ]
    if not merged:
        shapes.append(jax.ShapeDtypeStruct((hidden_width, width), BF16))
        specs.append(pl.BlockSpec(memory_space=pl.ANY))
    return pl.pallas_call(
        functools.partial(ffn_kernel, span, merged, heads),
        grid=(steps,),
        in_specs=[
            pl.BlockSpec((rows, width), lambda i: (0, 0)),
            pl.BlockSpec((rows, width), lambda i: (0, 0)),
            pl.BlockSpec((1, width), lambda i: (0, 0)),
            pl.BlockSpec((width, width), lambda i: (0, 0)),
            pl.BlockSpec((width, wide), lambda i: (0, lanes + i)),
            pl.BlockSpec((width, wide), lambda i: (0, lanes + steps + i)),
            pl.BlockSpec((wide, width), lambda i: (i, 0)),
            pl.BlockSpec(attended.shape, lambda i: (0, 0, 0)),
        ],
        out_specs=specs,
        out_shape=shapes,
        scratch_shapes=[
            pltpu.VMEM((rows, width), BF16),
            pltpu.VMEM((rows, width), F32),
            pltpu.VMEM((rows, width), BF16),
            pltpu.VMEM((width, rows), BF16),
            pltpu.VMEM((rows, width), F32),
            pltpu.VMEM((rows, width), F32),
            pltpu.VMEM((2, span, share, wide), BF16),
            pltpu.VMEM((2, span, share, wide), BF16),
            pltpu.VMEM((hidden_width, width), BF16),
            pltpu.VMEM((lanes, span, share, wide), BF16),
            pltpu.SemaphoreType.DMA((2, 2)),
            pltpu.SemaphoreType.DMA(((span * lanes if merged else 1) + lanes,)),
        ],
        compiler_params=pltpu.CompilerParams(vmem_limit_bytes=56 * MIB),
        cost_estimate=pl.CostEstimate(
            flops=6 * rows * width * (3 * hidden_width + width),
            bytes_accessed=4 * width * (3 * hidden_width + width),
            transcendentals=rows * hidden_width,
        ),
        name="feed_forward",
    )(tokens, upstream, gain, weights, weights, weights, w_down, attended)


def after(value, earlier):
    return lax.optimization_barrier((value, earlier))[0]


def chain_gather(blocks, axis):
    size = lax.axis_size(axis)
    place = lax.axis_index(axis)
    steps = []
    rising = falling = tuple(blocks)
    for step in range(size - 1):
        up = [(i, i + 1) for i in range(step, size - 1)]
        down = [(i + 1, i) for i in range(size - 1 - step)]
        rising = tuple(lax.ppermute(block, axis, up) for block in rising)
        falling = tuple(lax.ppermute(block, axis, down) for block in falling)
        if len(blocks) > 1:
            rising, falling = lax.optimization_barrier((rising, falling))
        steps.append((rising, falling))
    results = []
    for number, block in enumerate(blocks):
        ordered = []
        for index in range(size):
            cases = []
            for mine in range(size):
                if mine == index:
                    cases.append(block)
                elif mine > index:
                    cases.append(steps[mine - index - 1][0][number])
                else:
                    cases.append(steps[index - mine - 1][1][number])
            ordered.append(lax.select_n(place, *cases) if size > 2 else lax.select_n(place > 0, *cases))
        results.append(ordered)
    return results, steps


def shift_gather(block, axis):
    size = lax.axis_size(axis)
    place = lax.axis_index(axis)
    taken = [block]
    for far in range(1, size):
        taken.append(lax.ppermute(block, axis, [(i, (i + far) % size) for i in range(size)]))
    ordered = []
    for index in range(size):
        cases = [taken[(mine - index) % size] for mine in range(size)]
        ordered.append(lax.select_n(place, *cases) if size > 2 else lax.select_n(place > 0, *cases))
    return ordered


def exchange(blocks, axis):
    return lax.all_to_all(blocks, axis, 0, 0, tiled=True)


def body(
    tokens, memory_keys, memory_values, chosen, counts, w_query, w_key, w_value, w_out, w_gate, w_up, w_down,
    gain_attn, gain_ffn, cotangent,
):
    ring, span = lax.axis_size("fsdp"), lax.axis_size(DP)
    rows, width = tokens.shape[1:]
    heads = width // HEAD_DIM // ring
    wide = heads * HEAD_DIM
    length = rows * ring
    top = chosen.shape[2]
    hidden_width = w_gate.shape[1]
    share = w_query.shape[0]
    mine = tokens[0]

    extra = 8 if share % 8 == 0 else 8 - share % 8
    parts = [w.reshape(share, ring, wide).transpose(1, 0, 2) for w in (w_query, w_key, w_value)]
    choices = jnp.concatenate([chosen[0].reshape(-1), counts[0].reshape(-1)]).astype(BF16)
    notes = jnp.stack(
        [
            jnp.pad(row, (0, 3 * wide - row.shape[0]))
            for row in (jnp.concatenate([gain_attn, gain_ffn]), choices)
        ]
    )
    notes = jnp.broadcast_to(jnp.pad(notes, ((0, extra - 2), (0, 0))), (ring, extra, 3 * wide))
    parcel = jnp.concatenate([jnp.concatenate(parts, 2), notes], 1)
    parcel = lax.all_to_all(parcel, "fsdp", 0, 0, tiled=True)
    picks = parcel[:, share + 1, : choices.shape[0]].astype(jnp.int32).reshape(ring, 2, -1)
    chosen_all, counts_all = picks[:, 0].reshape(-1), picks[:, 1].reshape(-1)
    shards = jnp.concatenate([w_out, w_gate, w_up], 1)
    (near, near_down), steps = chain_gather((shards, w_down), "fsdp")
    (gathered,), token_steps = chain_gather((after(mine, steps[-2]),), "fsdp")
    parcel = lax.all_gather(parcel, DP, axis=0, tiled=True)
    w_qkv = parcel[:, :share].reshape(width, 3 * wide)
    gain_one = parcel[:, share, :share].reshape(1, width).astype(F32)
    gain_two = parcel[:, share, share : 2 * share].reshape(1, width).astype(F32)
    first = lax.all_gather(jnp.concatenate(near, 0), DP, axis=0, tiled=True)
    gathered = jnp.concatenate(gathered, 0)

    memory = jnp.concatenate(
        [m[0].reshape(-1, ring, wide).transpose(1, 0, 2) for m in (memory_keys, memory_values)], 2
    )
    memory = exchange(after(memory, token_steps[-2]), "fsdp").reshape(-1, 2 * wide)
    down_full = lax.all_gather(jnp.concatenate(near_down, 0), DP, axis=0, tiled=True)

    cosine, sine = rotary_tables(length)
    qkv = project_qkv(gathered, gain_one, w_qkv, cosine, sine, heads)
    out, lse = attend_forward(chosen_all, counts_all, qkv, memory, heads, top)
    attended = exchange(out.reshape(ring, rows, wide), "fsdp")

    projections = after(jnp.concatenate([w_query, w_key, w_value], 1), qkv)
    projections = jnp.concatenate(shift_gather(projections, "fsdp"), 0)
    projections, attended = lax.optimization_barrier((projections, attended))
    w_all = lax.all_gather(after(projections, down_full), DP, axis=0, tiled=True)

    mixed, grad_middle, gain_two_grad, grads, *others = feed_forward(
        mine, attended, cotangent[0], gain_two, first, down_full, span
    )
    grad_heads, grad_down = others[:heads], others[heads:]
    grads = lax.psum_scatter(after(grads, w_all), DP, scatter_dimension=0, tiled=True)[0]
    column = gain_one.reshape(width, 1)
    returned, weight_grads, gain_one_grad = [], [], 0.0
    for head in range(heads):
        grad_out = exchange(grad_heads[head], "fsdp").reshape(length, HEAD_DIM)
        if head:
            qkv = after(qkv, weight_grads[-1])
        grad, grad_w, gain_grad = attend_backward(
            chosen_all, counts_all, qkv, memory, grad_out, out, lse, cosine, sine, gathered, column, w_qkv, head,
            heads, top,
        )
        returned.append(exchange(grad.reshape(ring, rows, 3 * HEAD_DIM), "fsdp"))
        weight_grads.append(grad_w)
        gain_one_grad = gain_one_grad + gain_grad

    gains = jnp.stack([gain_one_grad.reshape(span, -1), gain_two_grad.reshape(span, -1)], 1)
    gains = jnp.pad(gains.astype(BF16), ((0, 0), (0, extra - 2), (0, 3 * wide - gains.shape[2])))
    late = jnp.concatenate(weight_grads, 1).reshape(span, -1, 3 * wide)
    late = after(jnp.concatenate([late, gains], 1), returned[0])
    late = late.reshape(span // 2, 2, late.shape[1], 3 * wide)
    core = lax.axis_index("core")
    taken = lax.ppermute(lax.dynamic_index_in_dim(late, 1 - core, 1, keepdims=False), "core", [(0, 1), (1, 0)])
    late = lax.dynamic_index_in_dim(late, core, 1, keepdims=False).astype(F32) + taken.astype(F32)
    late = jnp.sum(exchange(late.astype(BF16), "chip").astype(F32), 0).astype(BF16)
    grads = after(grads, (late, returned[-1]))
    gains = late[-extra : 2 - extra, : ring * share].reshape(2, ring, share).transpose(1, 0, 2)
    gains = jnp.pad(gains, ((0, 0), (0, extra - 2), (0, 3 * wide - share)))
    late = jnp.concatenate([late[:-extra].reshape(ring, share, 3 * wide), gains], 1)
    late = exchange(late, "fsdp").astype(F32)
    projections = [
        jnp.concatenate(
            [
                late[:, :share, (head * 3 + part) * HEAD_DIM : (head * 3 + part + 1) * HEAD_DIM]
                for head in range(heads)
            ],
            2,
        )
        .transpose(1, 0, 2)
        .reshape(share, width)
        for part in range(3)
    ]
    gain_shares = jnp.sum(late[:, share : share + 2, :share], 0)
    tokens_grad = finish_tokens(mine, gain_one, grad_middle, w_all, returned)

    strip = grads.shape[1]
    lanes = width // strip
    tall = w_down.shape[0]
    if grad_down:
        down = lax.psum_scatter(grad_down[0], DP, scatter_dimension=0, tiled=True)
        down = down.reshape(ring, tall, lanes, strip).transpose(0, 2, 1, 3)
    else:
        down = grads[: ring * tall * lanes].reshape(lanes, ring, tall, strip).transpose(1, 0, 2, 3)
        grads = grads[ring * tall * lanes :]
    grads = grads.reshape(-1, ring, share, strip).transpose(1, 0, 2, 3)
    pieces = jnp.concatenate([down.reshape(ring, -1, strip), grads.reshape(ring, -1, strip)], 1)
    pieces = lax.psum_scatter(pieces, "fsdp", scatter_dimension=0, tiled=True)[0].astype(F32)
    down_share = pieces[: lanes * tall].reshape(lanes, tall, strip).transpose(1, 0, 2).reshape(tall, width)
    others = pieces[lanes * tall :].reshape(-1, share, strip).transpose(1, 0, 2).reshape(share, -1)
    return (
        mixed[None],
        tokens_grad[None],
        *projections,
        others[:, :width],
        others[:, width : width + hidden_width],
        others[:, width + hidden_width :],
        down_share,
        gain_shares[0],
        gain_shares[1],
    )


def solution(mesh):
    span, ring = mesh.shape["dp"], mesh.shape["fsdp"]
    fine = Mesh(mesh.devices.reshape(span // 2, 2, ring), DP + ("fsdp",))
    every = DP + ("fsdp",)
    rows, matrix, vector = P(DP, "fsdp", None), P(every, None), P(every)
    in_specs = (rows,) * 5 + (matrix,) * 7 + (vector,) * 2 + (rows,)
    out_specs = (rows,) * 2 + (matrix,) * 7 + (vector,) * 2
    return jax.shard_map(body, mesh=fine, in_specs=in_specs, out_specs=out_specs, check_vma=False)
```

```python
import functools
import math

import jax
import jax.numpy as jnp
import numpy as np
from jax import lax
from jax.experimental import pallas as pl
from jax.experimental.pallas import tpu as pltpu
from jax.sharding import Mesh
from jax.sharding import PartitionSpec as P

HEAD_DIM = 128
QBLK = 256
MBLK = 128
EPSILON = 1e-06
NEGATIVE = -1e30
SCALE = 1.0 / math.sqrt(HEAD_DIM)
LOG2E = math.log2(math.e)
MIB = 1 << 20
F32 = jnp.float32
BF16 = jnp.bfloat16
DP = ("chip", "core")
NT = (((1,), (1,)), ((), ()))
TN = (((0,), (0,)), ((), ()))


def dot(left, right, dims=(((1,), (0,)), ((), ()))):
    return lax.dot_general(left, right, dims, preferred_element_type=F32)


def rotary_tables(length):
    half_dim = HEAD_DIM // 2
    frequency = 10000.0 ** (-jnp.arange(half_dim, dtype=F32) / half_dim)
    angles = jnp.arange(length, dtype=jnp.int32).astype(F32)[:, None] * frequency[None, :]
    cosine, sine = jnp.cos(angles), jnp.sin(angles)
    return jnp.concatenate([cosine, cosine], 1), jnp.concatenate([-sine, sine], 1)


def qkv_kernel(heads, tok_ref, gain_ref, w_ref, cos_ref, sin_ref, qkv_ref):
    rows = tok_ref[...].astype(F32)
    factor = lax.rsqrt(jnp.mean(rows * rows, -1, keepdims=True) + EPSILON)
    normed = (rows * factor * gain_ref[...]).astype(BF16)
    cosine, sine = cos_ref[...], sin_ref[...]
    wide = heads * HEAD_DIM
    for part in range(3):
        values = dot(normed, w_ref[:, part * wide : (part + 1) * wide])
        for head in range(heads):
            value = values[:, head * HEAD_DIM : (head + 1) * HEAD_DIM]
            if part < 2:
                value = value * cosine + pltpu.roll(value, HEAD_DIM // 2, 1) * sine
            if part == 0:
                value = value * (SCALE * LOG2E)
            at = part * wide + head * HEAD_DIM
            qkv_ref[:, at : at + HEAD_DIM] = value.astype(BF16)


def project_qkv(tokens_all, gain, w_qkv, cosine, sine, heads):
    length, width = tokens_all.shape
    columns = w_qkv.shape[1]
    block = 2 * QBLK
    return pl.pallas_call(
        functools.partial(qkv_kernel, heads),
        grid=(length // block,),
        in_specs=[
            pl.BlockSpec((block, width), lambda i: (i, 0)),
            pl.BlockSpec((1, width), lambda i: (0, 0)),
            pl.BlockSpec((width, columns), lambda i: (0, 0)),
            pl.BlockSpec((block, HEAD_DIM), lambda i: (i, 0)),
            pl.BlockSpec((block, HEAD_DIM), lambda i: (i, 0)),
        ],
        out_specs=pl.BlockSpec((block, columns), lambda i: (i, 0)),
        out_shape=jax.ShapeDtypeStruct((length, columns), BF16),
        compiler_params=pltpu.CompilerParams(vmem_limit_bytes=48 * MIB),
        cost_estimate=pl.CostEstimate(
            flops=2 * length * width * columns, bytes_accessed=4 * length * (width + columns), transcendentals=0
        ),
        name="project_qkv",
    )(tokens_all, gain, w_qkv, cosine, sine)


def memory_bias(counts_ref, base, top, axis):
    shape = (1, top * MBLK) if axis == 1 else (top * MBLK, 1)
    column = lax.broadcasted_iota(jnp.int32, shape, axis)
    limit = jnp.zeros(shape, jnp.int32)
    for entry in range(top):
        inside = (column >= entry * MBLK) & (column < entry * MBLK + counts_ref[base + entry])
        limit = jnp.where(inside, 1, limit)
    return jnp.where(limit > 0, 0.0, NEGATIVE)


def pick_memory(ref, chosen_ref, base, top, columns):
    rows = [
        ref[pl.ds(pl.multiple_of(chosen_ref[base + entry] * MBLK, MBLK), MBLK), columns]
        for entry in range(top)
    ]
    return jnp.concatenate(rows, 0)


def forward_kernel(
    heads, top, chosen_ref, counts_ref, q_ref, k_ref, v_ref, mk_ref, mv_ref, out_ref, lse_ref, acc_s, peak_s
):
    block = pl.program_id(0)
    rows = q_ref.shape[0]
    subs = rows // QBLK
    own = pl.ds(pl.multiple_of(block * rows, rows), rows)
    causal = lax.broadcasted_iota(jnp.int32, (rows, rows), 0) >= lax.broadcasted_iota(jnp.int32, (rows, rows), 1)
    ones = jnp.ones((rows, HEAD_DIM), BF16)
    mem_ones = jnp.ones((top * MBLK, HEAD_DIM), BF16)
    biases = [memory_bias(counts_ref, (block * subs + sub) * top, top, 1) for sub in range(subs)]
    for head in range(heads):
        columns = slice(head * HEAD_DIM, (head + 1) * HEAD_DIM)
        remote = []
        for sub in range(subs):
            keys = pick_memory(mk_ref, chosen_ref, (block * subs + sub) * top, top, columns)
            query = q_ref[sub * QBLK : (sub + 1) * QBLK, columns]
            remote.append(dot(query, keys, NT) + biases[sub])
        local = jnp.where(causal, dot(q_ref[:, columns], k_ref[own, columns], NT), NEGATIVE)
        peak = jnp.max(local, -1, keepdims=True)
        peak = jnp.maximum(peak, jnp.concatenate([jnp.max(r, -1, keepdims=True) for r in remote], 0))
        values = jnp.concatenate([v_ref[own, columns], ones], 1)
        acc = dot(jnp.exp2(local - peak).astype(BF16), values)
        more = []
        for sub in range(subs):
            values = pick_memory(mv_ref, chosen_ref, (block * subs + sub) * top, top, columns)
            weights = jnp.exp2(remote[sub] - peak[sub * QBLK : (sub + 1) * QBLK]).astype(BF16)
            more.append(dot(weights, jnp.concatenate([values, mem_ones], 1)))
        acc_s[head] = acc + jnp.concatenate(more, 0)
        peak_s[head] = jnp.broadcast_to(peak, (rows, HEAD_DIM))

    def step(index, carry):
        there = pl.ds(pl.multiple_of(index * rows, rows), rows)
        for head in range(heads):
            columns = slice(head * HEAD_DIM, (head + 1) * HEAD_DIM)
            peak = peak_s[head][:, :1]
            scores = dot(q_ref[:, columns], k_ref[there, columns], NT)
            higher = jnp.maximum(peak, jnp.max(scores, -1, keepdims=True))
            weights = jnp.exp2(scores - higher).astype(BF16)
            values = jnp.concatenate([v_ref[there, columns], ones], 1)
            acc_s[head] = acc_s[head] * jnp.exp2(peak - higher) + dot(weights, values)
            peak_s[head] = jnp.broadcast_to(higher, (rows, HEAD_DIM))
        return carry

    lax.fori_loop(0, block, step, 0)
    for head in range(heads):
        columns = slice(head * HEAD_DIM, (head + 1) * HEAD_DIM)
        total = acc_s[head][:, HEAD_DIM:]
        out_ref[:, columns] = (acc_s[head][:, :HEAD_DIM] / total).astype(BF16)
        lse_ref[:, head : head + 1] = peak_s[head][:, :1] + jnp.log2(total[:, :1])


def attend_forward(chosen, counts, qkv, memory, heads, top):
    length = qkv.shape[0]
    wide = heads * HEAD_DIM
    rows = min(2 * QBLK, length)
    mem_rows = memory.shape[0]
    return pl.pallas_call(
        functools.partial(forward_kernel, heads, top),
        grid_spec=pltpu.PrefetchScalarGridSpec(
            num_scalar_prefetch=2,
            grid=(length // rows,),
            in_specs=[
                pl.BlockSpec((rows, wide), lambda i, *_: (i, 0)),
                pl.BlockSpec((length, wide), lambda i, *_: (0, 1)),
                pl.BlockSpec((length, wide), lambda i, *_: (0, 2)),
                pl.BlockSpec((mem_rows, wide), lambda i, *_: (0, 0)),
                pl.BlockSpec((mem_rows, wide), lambda i, *_: (0, 1)),
            ],
            out_specs=[
                pl.BlockSpec((rows, wide), lambda i, *_: (i, 0)),
                pl.BlockSpec((rows, heads), lambda i, *_: (i, 0)),
            ],
            scratch_shapes=[
                pltpu.VMEM((heads, rows, 2 * HEAD_DIM), F32),
                pltpu.VMEM((heads, rows, HEAD_DIM), F32),
            ],
        ),
        out_shape=[
            jax.ShapeDtypeStruct((length, wide), BF16),
            jax.ShapeDtypeStruct((length, heads), F32),
        ],
        compiler_params=pltpu.CompilerParams(vmem_limit_bytes=48 * MIB),
        cost_estimate=pl.CostEstimate(
            flops=4 * heads * length * HEAD_DIM * (length // 2 + top * MBLK),
            bytes_accessed=8 * length * wide,
            transcendentals=heads * length * (length // 2 + top * MBLK),
        ),
        name="attend_forward",
    )(chosen, counts, qkv, qkv, qkv, memory, memory)


def backward_kernel(
    heads, top, chosen_ref, counts_ref, q_ref, k_ref, v_ref, mk_ref, mv_ref, go_ref, out_ref, lse_ref,
    cos_ref, sin_ref, tok_ref, gain_ref, w_ref, partial_ref, grad_w_ref, gain_grad_ref,
    gk_s, gv_s, gq_s, grad_s, gw_s,
):
    block = pl.num_programs(0) - 1 - pl.program_id(0)
    rows = q_ref.shape[0]
    subs = rows // QBLK
    wide = heads * HEAD_DIM
    own = pl.ds(pl.multiple_of(block * rows, rows), rows)
    key_at = lax.broadcasted_iota(jnp.int32, (rows, rows), 0)
    query_at = lax.broadcasted_iota(jnp.int32, (rows, rows), 1)
    causal = query_at >= key_at

    @pl.when(pl.program_id(0) == 0)
    def _():
        gk_s[...] = jnp.zeros_like(gk_s)
        gv_s[...] = jnp.zeros_like(gv_s)
        gw_s[...] = jnp.zeros_like(gw_s)
        gain_grad_ref[...] = jnp.zeros_like(gain_grad_ref)

    def spread(column):
        return jnp.transpose(jnp.broadcast_to(column, (rows, HEAD_DIM)))[:1]

    stats = []
    for head in range(heads):
        columns = slice(head * HEAD_DIM, (head + 1) * HEAD_DIM)
        delta = jnp.sum(go_ref[:, columns].astype(F32) * out_ref[:, columns].astype(F32), -1, keepdims=True)
        stats.append((spread(lse_ref[:, head : head + 1]), spread(delta)))

    def pair(head, queries, keys, values, mask):
        columns = slice(head * HEAD_DIM, (head + 1) * HEAD_DIM)
        lse, delta = stats[head]
        scores = mask(dot(keys, q_ref[queries, columns], NT))
        weights = jnp.exp2(scores - lse[:, queries])
        grad_weights = dot(values, go_ref[queries, columns], NT)
        return weights.astype(BF16), (weights * (grad_weights - delta[:, queries])).astype(BF16)

    every = slice(0, rows)
    for head in range(heads):
        columns = slice(head * HEAD_DIM, (head + 1) * HEAD_DIM)
        for sub in range(subs):
            base = (block * subs + sub) * top
            queries = slice(sub * QBLK, (sub + 1) * QBLK)
            keys = pick_memory(mk_ref, chosen_ref, base, top, columns)
            values = pick_memory(mv_ref, chosen_ref, base, top, columns)
            bias = memory_bias(counts_ref, base, top, 0)
            _, grad_scores = pair(head, queries, keys, values, lambda scores: scores + bias)
            gq_s[queries, columns] = dot(grad_scores, keys, TN)

    def local(head, there, mask):
        columns = slice(head * HEAD_DIM, (head + 1) * HEAD_DIM)
        keys = k_ref[there, columns]
        weights, grad_scores = pair(head, every, keys, v_ref[there, columns], mask)
        gk_s[there, columns] += dot(grad_scores, q_ref[:, columns])
        gv_s[there, columns] += dot(weights, go_ref[:, columns])
        gq_s[:, columns] += dot(grad_scores, keys, TN)

    for head in range(heads):
        local(head, own, lambda scores: jnp.where(causal, scores, NEGATIVE))

    def step(index, carry):
        for head in range(heads):
            local(head, pl.ds(pl.multiple_of(index * rows, rows), rows), lambda scores: scores)
        return carry

    lax.fori_loop(0, block, step, 0)
    cosine, sine = cos_ref[...], sin_ref[...]

    def unturn(value):
        return value * cosine - pltpu.roll(value, HEAD_DIM // 2, 1) * sine

    for head in range(heads):
        columns = slice(head * HEAD_DIM, (head + 1) * HEAD_DIM)
        at = head * HEAD_DIM
        grad_s[:, at : at + HEAD_DIM] = unturn(gq_s[:, columns] * SCALE).astype(BF16)
        grad_key = gk_s[own, columns] * (1.0 / LOG2E)
        grad_s[:, wide + at : wide + at + HEAD_DIM] = unturn(grad_key).astype(BF16)
        grad_s[:, 2 * wide + at : 2 * wide + at + HEAD_DIM] = gv_s[own, columns].astype(BF16)

    tokens = tok_ref[...].astype(F32)
    tokens = tokens * lax.rsqrt(jnp.mean(tokens * tokens, -1, keepdims=True) + EPSILON)
    normed = (tokens * gain_ref[...]).astype(BF16)
    grad = grad_s[...]
    partial = dot(grad, w_ref[...], NT)
    partial_ref[...] = partial.astype(BF16)
    gain_grad_ref[...] += jnp.sum(partial * tokens, 0, keepdims=True)
    gw_s[...] += dot(normed, grad, TN)

    @pl.when(block == 0)
    def _():
        grad_w_ref[...] = gw_s[...].astype(BF16)


def attend_backward(
    chosen, counts, qkv, memory, grad_out, out, lse, cosine, sine, tokens_all, gain, w_qkv, heads, top
):
    length = qkv.shape[0]
    width = tokens_all.shape[1]
    wide = heads * HEAD_DIM
    rows = min(2 * QBLK, length)
    mem_rows = memory.shape[0]
    last = length // rows - 1
    return pl.pallas_call(
        functools.partial(backward_kernel, heads, top),
        grid_spec=pltpu.PrefetchScalarGridSpec(
            num_scalar_prefetch=2,
            grid=(last + 1,),
            in_specs=[
                pl.BlockSpec((rows, wide), lambda i, *_: (last - i, 0)),
                pl.BlockSpec((length, wide), lambda i, *_: (0, 1)),
                pl.BlockSpec((length, wide), lambda i, *_: (0, 2)),
                pl.BlockSpec((mem_rows, wide), lambda i, *_: (0, 0)),
                pl.BlockSpec((mem_rows, wide), lambda i, *_: (0, 1)),
                pl.BlockSpec((rows, wide), lambda i, *_: (last - i, 0)),
                pl.BlockSpec((rows, wide), lambda i, *_: (last - i, 0)),
                pl.BlockSpec((rows, heads), lambda i, *_: (last - i, 0)),
                pl.BlockSpec((rows, HEAD_DIM), lambda i, *_: (last - i, 0)),
                pl.BlockSpec((rows, HEAD_DIM), lambda i, *_: (last - i, 0)),
                pl.BlockSpec((rows, width), lambda i, *_: (last - i, 0)),
                pl.BlockSpec((1, width), lambda i, *_: (0, 0)),
                pl.BlockSpec((width, 3 * wide), lambda i, *_: (0, 0)),
            ],
            out_specs=[
                pl.BlockSpec((rows, width), lambda i, *_: (last - i, 0)),
                pl.BlockSpec((width, 3 * wide), lambda i, *_: (0, 0)),
                pl.BlockSpec((1, width), lambda i, *_: (0, 0)),
            ],
            scratch_shapes=[
                pltpu.VMEM((length, wide), F32),
                pltpu.VMEM((length, wide), F32),
                pltpu.VMEM((rows, wide), F32),
                pltpu.VMEM((rows, 3 * wide), BF16),
                pltpu.VMEM((width, 3 * wide), F32),
            ],
        ),
        out_shape=[
            jax.ShapeDtypeStruct((length, width), BF16),
            jax.ShapeDtypeStruct((width, 3 * wide), BF16),
            jax.ShapeDtypeStruct((1, width), F32),
        ],
        compiler_params=pltpu.CompilerParams(vmem_limit_bytes=48 * MIB),
        cost_estimate=pl.CostEstimate(
            flops=10 * heads * length * HEAD_DIM * (length // 2 + top * MBLK),
            bytes_accessed=16 * length * wide,
            transcendentals=heads * length * (length // 2 + top * MBLK),
        ),
        name="attend_backward",
    )(
        chosen, counts, qkv, qkv, qkv, memory, memory, grad_out, out, lse, cosine, sine, tokens_all, gain, w_qkv
    )


def ffn_kernel(
    span, merged, tok_ref, att_ref, cot_ref, gain_ref, out_w, gate_w, up_w, down_w,
    mixed_ref, grad_mid_ref, grad_att_ref, gain_grad_ref, grads_ref, *rest,
):
    if not merged:
        down_grads_ref, rest = rest[0], rest[1:]
    middle_s, normed_s, turned_s, mixed_s, upstream_s, gate_s, up_s, down_s, out_s, sems, late_sems = rest
    step, steps = pl.program_id(0), pl.num_programs(0)
    width = tok_ref.shape[1]
    share = width // span
    wide = gate_w.shape[1]
    hidden_width = down_s.shape[0]
    tall = hidden_width // span
    lanes = width // wide
    first = tall * lanes if merged else 0
    slot = step % 2

    @pl.when(step == 0)
    def _():
        middle = tok_ref[...].astype(F32) + dot(att_ref[...], out_w[...])
        middle_s[...] = middle
        factor = lax.rsqrt(jnp.mean(middle * middle, -1, keepdims=True) + EPSILON)
        normed = (middle * factor * gain_ref[...]).astype(BF16)
        normed_s[...] = normed
        turned_s[...] = jnp.transpose(normed)
        mixed_s[...] = middle
        upstream_s[...] = jnp.zeros_like(upstream_s)

    def copy_out(kind, which, index):
        source = (gate_s, up_s)[kind].at[which]
        start = first + (lanes + kind * steps + index) * share
        target = grads_ref.at[:, pl.ds(start, share), :]
        return pltpu.make_async_copy(source, target, sems.at[kind, which])

    normed = normed_s[...]
    upstream = cot_ref[...]
    both = jnp.concatenate([gate_w[...], up_w[...]], 1)
    acts = dot(normed, both)
    gate_act, up_act = acts[:, :wide], acts[:, wide:]
    grad_hidden = dot(upstream, down_w[...], NT)
    sigmoid = jax.nn.sigmoid(gate_act)
    silu = gate_act * sigmoid
    hidden = (silu * up_act).astype(BF16)
    grad_gate = (grad_hidden * up_act * sigmoid * (1.0 + gate_act * (1.0 - sigmoid))).astype(BF16)
    grad_up = (grad_hidden * silu).astype(BF16)
    mixed_s[...] += dot(hidden, down_w[...])
    grad_acts = jnp.concatenate([grad_gate, grad_up], 1)
    upstream_s[...] += dot(grad_acts, both, NT)
    down_s[pl.ds(pl.multiple_of(step * wide, wide), wide), :] = dot(hidden, upstream, TN).astype(BF16)

    @pl.when(step >= 2)
    def _():
        copy_out(0, slot, step - 2).wait()
        copy_out(1, slot, step - 2).wait()

    weight_grads = dot(turned_s[...], grad_acts).astype(BF16)
    gate_s[slot] = weight_grads[:, :wide].reshape(span, share, wide)
    up_s[slot] = weight_grads[:, wide:].reshape(span, share, wide)
    copy_out(0, slot, step).start()
    copy_out(1, slot, step).start()

    @pl.when(step == steps - 1)
    def _():
        copies = []
        if merged:
            for place in range(span):
                for lane in range(lanes):
                    copies.append(
                        pltpu.make_async_copy(
                            down_s.at[pl.ds(place * tall, tall), pl.ds(lane * wide, wide)],
                            grads_ref.at[place, pl.ds(lane * tall, tall), :],
                            late_sems.at[len(copies)],
                        )
                    )
        else:
            copies.append(pltpu.make_async_copy(down_s, down_grads_ref, late_sems.at[0]))
        for copy in copies:
            copy.start()
        mixed_ref[...] = mixed_s[...].astype(BF16)
        middle = middle_s[...]
        grad = upstream_s[...]
        factor = lax.rsqrt(jnp.mean(middle * middle, -1, keepdims=True) + EPSILON)
        gain_grad_ref[...] = jnp.sum(grad * middle * factor, 0, keepdims=True)
        scaled = grad * gain_ref[...]
        inner = jnp.mean(scaled * middle, -1, keepdims=True)
        grad_middle = cot_ref[...].astype(F32) + factor * scaled - middle * (factor * factor * factor * inner)
        grad_mid_ref[...] = grad_middle
        branch = grad_middle.astype(BF16)
        grad_att_ref[...] = dot(branch, out_w[...], NT).astype(BF16)
        turned_att = jnp.transpose(att_ref[...])
        for lane in range(lanes):
            columns = slice(lane * wide, (lane + 1) * wide)
            out_s[lane] = dot(turned_att, branch[:, columns]).astype(BF16).reshape(span, share, wide)
            more = pltpu.make_async_copy(
                out_s.at[lane],
                grads_ref.at[:, pl.ds(first + lane * share, share), :],
                late_sems.at[len(copies)],
            )
            more.start()
            copies.append(more)
        for copy in copies:
            copy.wait()
        copy_out(0, 1 - slot, step - 1).wait()
        copy_out(1, 1 - slot, step - 1).wait()
        copy_out(0, slot, step).wait()
        copy_out(1, slot, step).wait()


def feed_forward(tokens, attended, upstream, gain, weights, w_down, span):
    rows, width = tokens.shape
    hidden_width = w_down.shape[0]
    wide = 2 * HEAD_DIM
    steps = hidden_width // wide
    lanes = width // wide
    share = width // span
    tall = hidden_width // span
    merged = tall % 16 == 0
    total = (lanes + 2 * steps) * share + (lanes * tall if merged else 0)
    shapes = [
        jax.ShapeDtypeStruct((rows, width), BF16),
        jax.ShapeDtypeStruct((rows, width), F32),
        jax.ShapeDtypeStruct((rows, width), BF16),
        jax.ShapeDtypeStruct((1, width), F32),
        jax.ShapeDtypeStruct((span, total, wide), BF16),
    ]
    specs = [
        pl.BlockSpec((rows, width), lambda i: (0, 0)),
        pl.BlockSpec((rows, width), lambda i: (0, 0)),
        pl.BlockSpec((rows, width), lambda i: (0, 0)),
        pl.BlockSpec((1, width), lambda i: (0, 0)),
        pl.BlockSpec(memory_space=pl.ANY),
    ]
    if not merged:
        shapes.append(jax.ShapeDtypeStruct((hidden_width, width), BF16))
        specs.append(pl.BlockSpec(memory_space=pl.ANY))
    return pl.pallas_call(
        functools.partial(ffn_kernel, span, merged),
        grid=(steps,),
        in_specs=[
            pl.BlockSpec((rows, width), lambda i: (0, 0)),
            pl.BlockSpec((rows, width), lambda i: (0, 0)),
            pl.BlockSpec((rows, width), lambda i: (0, 0)),
            pl.BlockSpec((1, width), lambda i: (0, 0)),
            pl.BlockSpec((width, width), lambda i: (0, 0)),
            pl.BlockSpec((width, wide), lambda i: (0, lanes + i)),
            pl.BlockSpec((width, wide), lambda i: (0, lanes + steps + i)),
            pl.BlockSpec((wide, width), lambda i: (i, 0)),
        ],
        out_specs=specs,
        out_shape=shapes,
        scratch_shapes=[
            pltpu.VMEM((rows, width), F32),
            pltpu.VMEM((rows, width), BF16),
            pltpu.VMEM((width, rows), BF16),
            pltpu.VMEM((rows, width), F32),
            pltpu.VMEM((rows, width), F32),
            pltpu.VMEM((2, span, share, wide), BF16),
            pltpu.VMEM((2, span, share, wide), BF16),
            pltpu.VMEM((hidden_width, width), BF16),
            pltpu.VMEM((lanes, span, share, wide), BF16),
            pltpu.SemaphoreType.DMA((2, 2)),
            pltpu.SemaphoreType.DMA(((span * lanes if merged else 1) + lanes,)),
        ],
        compiler_params=pltpu.CompilerParams(vmem_limit_bytes=56 * MIB),
        cost_estimate=pl.CostEstimate(
            flops=6 * rows * width * (3 * hidden_width + width),
            bytes_accessed=4 * width * (3 * hidden_width + width),
            transcendentals=rows * hidden_width,
        ),
        name="feed_forward",
    )(tokens, attended, upstream, gain, weights, weights, weights, w_down)


def after(value, earlier):
    return lax.optimization_barrier((value, earlier))[0]


def chain_gather(blocks, axis):
    size = lax.axis_size(axis)
    place = lax.axis_index(axis)
    steps = []
    rising = falling = tuple(blocks)
    for step in range(size - 1):
        up = [(i, i + 1) for i in range(step, size - 1)]
        down = [(i + 1, i) for i in range(size - 1 - step)]
        rising = tuple(lax.ppermute(block, axis, up) for block in rising)
        falling = tuple(lax.ppermute(block, axis, down) for block in falling)
        if len(blocks) > 1:
            rising, falling = lax.optimization_barrier((rising, falling))
        steps.append((rising, falling))
    results = []
    for number, block in enumerate(blocks):
        ordered = []
        for index in range(size):
            cases = []
            for mine in range(size):
                if mine == index:
                    cases.append(block)
                elif mine > index:
                    cases.append(steps[mine - index - 1][0][number])
                else:
                    cases.append(steps[index - mine - 1][1][number])
            ordered.append(lax.select_n(place, *cases) if size > 2 else lax.select_n(place > 0, *cases))
        results.append(ordered)
    return results, steps


def chain_scatter(partial, axis, beside):
    size = lax.axis_size(axis)
    place = lax.axis_index(axis)
    rows = partial.shape[0] // size

    def block(index):
        return lax.dynamic_slice_in_dim(partial, jnp.clip(index, 0, size - 1) * rows, rows, 0).astype(F32)

    rising = falling = None
    for step in range(size - 1):
        up, down = block(size - 1 - step + place), block(step - size + 1 + place)
        extra = None
        if step:
            up, down = up + rising.astype(F32), down + falling.astype(F32)
            extra = beside[step - 1]() if step <= len(beside) else None
        up, down, _ = lax.optimization_barrier((up.astype(BF16), down.astype(BF16), extra))
        rising = lax.ppermute(up, axis, [(i, i + 1) for i in range(step + 1)])
        falling = lax.ppermute(down, axis, [(i, i - 1) for i in range(size - 1 - step, size)])
        rising, falling = lax.optimization_barrier((rising, falling))
    return block(place) + rising.astype(F32) + falling.astype(F32)


def direct_exchange(blocks, axis):
    size = lax.axis_size(axis)
    place = lax.axis_index(axis)
    taken = [lax.dynamic_index_in_dim(blocks, place, 0, keepdims=False)]
    for far in range(1, size):
        give = lax.dynamic_index_in_dim(blocks, (place + far) % size, 0, keepdims=False)
        taken.append(lax.ppermute(give, axis, [(i, (i + far) % size) for i in range(size)]))
    return taken


def body(
    tokens, memory_keys, memory_values, chosen, counts, w_query, w_key, w_value, w_out, w_gate, w_up, w_down,
    gain_attn, gain_ffn, cotangent,
):
    ring, span = lax.axis_size("fsdp"), lax.axis_size(DP)
    rows, width = tokens.shape[1:]
    heads = width // HEAD_DIM // ring
    wide = heads * HEAD_DIM
    length = rows * ring
    top = chosen.shape[2]
    hidden_width = w_gate.shape[1]
    share = w_query.shape[0]
    mine = tokens[0]

    extra = 8 if share % 8 == 0 else 8 - share % 8
    parts = [w.reshape(share, ring, wide).transpose(1, 0, 2) for w in (w_query, w_key, w_value)]
    choices = jnp.concatenate([chosen[0].reshape(-1), counts[0].reshape(-1)]).astype(BF16)
    notes = jnp.stack(
        [
            jnp.pad(row, (0, 3 * wide - row.shape[0]))
            for row in (jnp.concatenate([gain_attn, gain_ffn]), choices)
        ]
    )
    notes = jnp.broadcast_to(jnp.pad(notes, ((0, extra - 2), (0, 0))), (ring, extra, 3 * wide))
    parcel = jnp.concatenate([jnp.concatenate(parts, 2), notes], 1)
    parcel = lax.all_to_all(parcel, "fsdp", 0, 0, tiled=True)
    picks = parcel[:, share + 1, : choices.shape[0]].astype(jnp.int32).reshape(ring, 2, -1)
    chosen_all, counts_all = picks[:, 0].reshape(-1), picks[:, 1].reshape(-1)
    shards = jnp.concatenate([w_out, w_gate, w_up], 1)
    (near, near_down), steps = chain_gather((shards, w_down), "fsdp")
    (gathered,), token_steps = chain_gather((after(mine, steps[-2]),), "fsdp")
    parcel = lax.all_gather(parcel, DP, axis=0, tiled=True)
    w_qkv = parcel[:, :share].reshape(width, 3 * wide)
    gain_one = parcel[:, share, :share].reshape(1, width).astype(F32)
    gain_two = parcel[:, share, share : 2 * share].reshape(1, width).astype(F32)
    first = lax.all_gather(jnp.concatenate(near, 0), DP, axis=0, tiled=True)
    gathered = jnp.concatenate(gathered, 0)

    memory = jnp.concatenate(
        [m[0].reshape(-1, ring, wide).transpose(1, 0, 2) for m in (memory_keys, memory_values)], 2
    )
    memory = lax.all_to_all(after(memory, token_steps[-2]), "fsdp", 0, 0, tiled=True).reshape(-1, 2 * wide)
    down_full = lax.all_gather(jnp.concatenate(near_down, 0), DP, axis=0, tiled=True)

    cosine, sine = rotary_tables(length)
    qkv = project_qkv(gathered, gain_one, w_qkv, cosine, sine, heads)
    attended_heads, lse = attend_forward(chosen_all, counts_all, qkv, memory, heads, top)
    attended = lax.all_to_all(attended_heads, "fsdp", 0, 1, tiled=True)

    upstream = cotangent[0]
    mixed, grad_middle, grad_attended, gain_two_grad, grads, *grad_down = feed_forward(
        mine, attended, upstream, gain_two, first, down_full, span
    )
    grad_heads = lax.all_to_all(grad_attended, "fsdp", 1, 0, tiled=True)
    grads = lax.psum_scatter(grads, DP, scatter_dimension=0, tiled=True)[0]

    partial, grad_w_qkv, gain_one_grad = attend_backward(
        chosen_all, counts_all, qkv, memory, grad_heads, attended_heads, lse, cosine, sine, gathered, gain_one,
        w_qkv, heads, top,
    )
    gains = jnp.concatenate([gain_one_grad, gain_two_grad], 0).reshape(2, span, -1).transpose(1, 0, 2)
    gains = jnp.pad(gains.astype(BF16), ((0, 0), (0, extra - 2), (0, 3 * wide - gains.shape[2])))
    late = jnp.concatenate([grad_w_qkv.reshape(span, -1, 3 * wide), gains], 1)
    late = late.reshape(span // 2, 2, late.shape[1], 3 * wide)
    core = lax.axis_index("core")
    sums = []

    def between_cores():
        give = lax.dynamic_index_in_dim(late, 1 - core, 1, keepdims=False)
        keep = lax.dynamic_index_in_dim(late, core, 1, keepdims=False)
        taken = lax.ppermute(give, "core", [(0, 1), (1, 0)])
        sums.append((keep.astype(F32) + taken.astype(F32)).astype(BF16))
        return sums[-1]

    def between_chips():
        sums.append(sum(piece.astype(F32) for piece in direct_exchange(sums[-1], "chip")).astype(BF16))
        return sums[-1]

    grad_normed = chain_scatter(partial, "fsdp", [between_cores, between_chips])
    late = sums[-1]
    own = mine.astype(F32)
    factor = lax.rsqrt(jnp.mean(own * own, -1, keepdims=True) + EPSILON)
    scaled = grad_normed * gain_one
    inner = jnp.mean(scaled * own, -1, keepdims=True)
    tokens_grad = (grad_middle + factor * scaled - own * (factor * factor * factor * inner)).astype(BF16)

    gains = late[-extra : 2 - extra, : ring * share].reshape(2, ring, share).transpose(1, 0, 2)
    gains = jnp.pad(gains, ((0, 0), (0, extra - 2), (0, 3 * wide - share)))
    late = jnp.concatenate([late[:-extra].reshape(ring, share, 3 * wide), gains], 1)
    grads = after(grads, grad_normed)
    strip = grads.shape[1]
    lanes = width // strip
    tall = w_down.shape[0]
    if grad_down:
        down = lax.psum_scatter(grad_down[0], DP, scatter_dimension=0, tiled=True)
        down = down.reshape(ring, tall, lanes, strip).transpose(0, 2, 1, 3)
    else:
        down = grads[: ring * tall * lanes].reshape(lanes, ring, tall, strip).transpose(1, 0, 2, 3)
        grads = grads[ring * tall * lanes :]
    grads = grads.reshape(-1, ring, share, strip).transpose(1, 0, 2, 3)
    pieces = jnp.concatenate([down.reshape(ring, -1, strip), grads.reshape(ring, -1, strip)], 1)
    pieces = sum(piece.astype(F32) for piece in direct_exchange(pieces, "fsdp"))
    late = direct_exchange(late, "fsdp")
    place = lax.axis_index("fsdp")
    gain_shares = sum(piece.astype(F32) for piece in late)[share : share + 2, :share]
    in_order = [
        lax.select_n(place if ring > 2 else place > 0, *[late[(here - source) % ring] for here in range(ring)])
        for source in range(ring)
    ]
    projections = [
        jnp.concatenate([piece[:share, part * wide : (part + 1) * wide] for piece in in_order], 1).astype(F32)
        for part in range(3)
    ]
    down_share = pieces[: lanes * tall].reshape(lanes, tall, strip).transpose(1, 0, 2).reshape(tall, width)
    others = pieces[lanes * tall :].reshape(-1, share, strip).transpose(1, 0, 2).reshape(share, -1)
    return (
        mixed[None],
        tokens_grad[None],
        *projections,
        others[:, :width],
        others[:, width : width + hidden_width],
        others[:, width + hidden_width :],
        down_share,
        gain_shares[0],
        gain_shares[1],
    )


def solution(mesh):
    span, ring = mesh.shape["dp"], mesh.shape["fsdp"]
    fine = Mesh(mesh.devices.reshape(span // 2, 2, ring), DP + ("fsdp",))
    every = DP + ("fsdp",)
    rows, matrix, vector = P(DP, "fsdp", None), P(every, None), P(every)
    in_specs = (rows,) * 5 + (matrix,) * 7 + (vector,) * 2 + (rows,)
    out_specs = (rows,) * 2 + (matrix,) * 7 + (vector,) * 2
    return jax.shard_map(body, mesh=fine, in_specs=in_specs, out_specs=out_specs, check_vma=False)
```

```python
import functools
import math

import jax
import jax.numpy as jnp
import numpy as np
from jax import lax
from jax.experimental import pallas as pl
from jax.experimental.pallas import tpu as pltpu
from jax.sharding import Mesh
from jax.sharding import PartitionSpec as P

HEAD_DIM = 128
QBLK = 256
MBLK = 128
EPSILON = 1e-06
NEGATIVE = -1e30
SCALE = 1.0 / math.sqrt(HEAD_DIM)
LOG2E = math.log2(math.e)
MIB = 1 << 20
F32 = jnp.float32
BF16 = jnp.bfloat16
DP = ("chip", "core")
NT = (((1,), (1,)), ((), ()))
TN = (((0,), (0,)), ((), ()))


def dot(left, right, dims=(((1,), (0,)), ((), ()))):
    return lax.dot_general(left, right, dims, preferred_element_type=F32)


def rotary_tables(length):
    half_dim = HEAD_DIM // 2
    frequency = 10000.0 ** (-jnp.arange(half_dim, dtype=F32) / half_dim)
    angles = jnp.arange(length, dtype=jnp.int32).astype(F32)[:, None] * frequency[None, :]
    cosine, sine = jnp.cos(angles), jnp.sin(angles)
    return jnp.concatenate([cosine, cosine], 1), jnp.concatenate([-sine, sine], 1)


def qkv_kernel(heads, tok_ref, gain_ref, w_ref, cos_ref, sin_ref, qkv_ref):
    rows = tok_ref[...].astype(F32)
    factor = lax.rsqrt(jnp.mean(rows * rows, -1, keepdims=True) + EPSILON)
    normed = (rows * factor * gain_ref[...]).astype(BF16)
    cosine, sine = cos_ref[...], sin_ref[...]
    wide = heads * HEAD_DIM
    for part in range(3):
        values = dot(normed, w_ref[:, part * wide : (part + 1) * wide])
        for head in range(heads):
            value = values[:, head * HEAD_DIM : (head + 1) * HEAD_DIM]
            if part < 2:
                value = value * cosine + pltpu.roll(value, HEAD_DIM // 2, 1) * sine
            if part == 0:
                value = value * (SCALE * LOG2E)
            at = part * wide + head * HEAD_DIM
            qkv_ref[:, at : at + HEAD_DIM] = value.astype(BF16)


def project_qkv(tokens_all, gain, w_qkv, cosine, sine, heads):
    length, width = tokens_all.shape
    columns = w_qkv.shape[1]
    block = 2 * QBLK
    return pl.pallas_call(
        functools.partial(qkv_kernel, heads),
        grid=(length // block,),
        in_specs=[
            pl.BlockSpec((block, width), lambda i: (i, 0)),
            pl.BlockSpec((1, width), lambda i: (0, 0)),
            pl.BlockSpec((width, columns), lambda i: (0, 0)),
            pl.BlockSpec((block, HEAD_DIM), lambda i: (i, 0)),
            pl.BlockSpec((block, HEAD_DIM), lambda i: (i, 0)),
        ],
        out_specs=pl.BlockSpec((block, columns), lambda i: (i, 0)),
        out_shape=jax.ShapeDtypeStruct((length, columns), BF16),
        compiler_params=pltpu.CompilerParams(vmem_limit_bytes=48 * MIB),
        cost_estimate=pl.CostEstimate(
            flops=2 * length * width * columns, bytes_accessed=4 * length * (width + columns), transcendentals=0
        ),
        name="project_qkv",
    )(tokens_all, gain, w_qkv, cosine, sine)


def memory_bias(counts_ref, base, top, axis):
    shape = (1, top * MBLK) if axis == 1 else (top * MBLK, 1)
    column = lax.broadcasted_iota(jnp.int32, shape, axis)
    limit = jnp.zeros(shape, jnp.int32)
    for entry in range(top):
        inside = (column >= entry * MBLK) & (column < entry * MBLK + counts_ref[base + entry])
        limit = jnp.where(inside, 1, limit)
    return jnp.where(limit > 0, 0.0, NEGATIVE)


def pick_memory(ref, chosen_ref, base, top, columns):
    rows = [
        ref[pl.ds(pl.multiple_of(chosen_ref[base + entry] * MBLK, MBLK), MBLK), columns]
        for entry in range(top)
    ]
    return jnp.concatenate(rows, 0)


def forward_kernel(
    heads, top, chosen_ref, counts_ref, q_ref, k_ref, v_ref, mk_ref, mv_ref, out_ref, lse_ref, acc_s, peak_s
):
    block = pl.program_id(0)
    rows = q_ref.shape[0]
    subs = rows // QBLK
    own = pl.ds(pl.multiple_of(block * rows, rows), rows)
    causal = lax.broadcasted_iota(jnp.int32, (rows, rows), 0) >= lax.broadcasted_iota(jnp.int32, (rows, rows), 1)
    ones = jnp.ones((rows, HEAD_DIM), BF16)
    mem_ones = jnp.ones((top * MBLK, HEAD_DIM), BF16)
    biases = [memory_bias(counts_ref, (block * subs + sub) * top, top, 1) for sub in range(subs)]
    for head in range(heads):
        columns = slice(head * HEAD_DIM, (head + 1) * HEAD_DIM)
        remote = []
        for sub in range(subs):
            keys = pick_memory(mk_ref, chosen_ref, (block * subs + sub) * top, top, columns)
            query = q_ref[sub * QBLK : (sub + 1) * QBLK, columns]
            remote.append(dot(query, keys, NT) + biases[sub])
        local = jnp.where(causal, dot(q_ref[:, columns], k_ref[own, columns], NT), NEGATIVE)
        peak = jnp.max(local, -1, keepdims=True)
        peak = jnp.maximum(peak, jnp.concatenate([jnp.max(r, -1, keepdims=True) for r in remote], 0))
        values = jnp.concatenate([v_ref[own, columns], ones], 1)
        acc = dot(jnp.exp2(local - peak).astype(BF16), values)
        more = []
        for sub in range(subs):
            values = pick_memory(mv_ref, chosen_ref, (block * subs + sub) * top, top, columns)
            weights = jnp.exp2(remote[sub] - peak[sub * QBLK : (sub + 1) * QBLK]).astype(BF16)
            more.append(dot(weights, jnp.concatenate([values, mem_ones], 1)))
        acc_s[head] = acc + jnp.concatenate(more, 0)
        peak_s[head] = jnp.broadcast_to(peak, (rows, HEAD_DIM))

    def step(index, carry):
        there = pl.ds(pl.multiple_of(index * rows, rows), rows)
        for head in range(heads):
            columns = slice(head * HEAD_DIM, (head + 1) * HEAD_DIM)
            peak = peak_s[head][:, :1]
            scores = dot(q_ref[:, columns], k_ref[there, columns], NT)
            higher = jnp.maximum(peak, jnp.max(scores, -1, keepdims=True))
            weights = jnp.exp2(scores - higher).astype(BF16)
            values = jnp.concatenate([v_ref[there, columns], ones], 1)
            acc_s[head] = acc_s[head] * jnp.exp2(peak - higher) + dot(weights, values)
            peak_s[head] = jnp.broadcast_to(higher, (rows, HEAD_DIM))
        return carry

    lax.fori_loop(0, block, step, 0)
    for head in range(heads):
        columns = slice(head * HEAD_DIM, (head + 1) * HEAD_DIM)
        total = acc_s[head][:, HEAD_DIM:]
        out_ref[:, columns] = (acc_s[head][:, :HEAD_DIM] / total).astype(BF16)
        lse_ref[:, head : head + 1] = peak_s[head][:, :1] + jnp.log2(total[:, :1])


def attend_forward(chosen, counts, qkv, memory, heads, top):
    length = qkv.shape[0]
    wide = heads * HEAD_DIM
    rows = min(2 * QBLK, length)
    mem_rows = memory.shape[0]
    return pl.pallas_call(
        functools.partial(forward_kernel, heads, top),
        grid_spec=pltpu.PrefetchScalarGridSpec(
            num_scalar_prefetch=2,
            grid=(length // rows,),
            in_specs=[
                pl.BlockSpec((rows, wide), lambda i, *_: (i, 0)),
                pl.BlockSpec((length, wide), lambda i, *_: (0, 1)),
                pl.BlockSpec((length, wide), lambda i, *_: (0, 2)),
                pl.BlockSpec((mem_rows, wide), lambda i, *_: (0, 0)),
                pl.BlockSpec((mem_rows, wide), lambda i, *_: (0, 1)),
            ],
            out_specs=[
                pl.BlockSpec((rows, wide), lambda i, *_: (i, 0)),
                pl.BlockSpec((rows, heads), lambda i, *_: (i, 0)),
            ],
            scratch_shapes=[
                pltpu.VMEM((heads, rows, 2 * HEAD_DIM), F32),
                pltpu.VMEM((heads, rows, HEAD_DIM), F32),
            ],
        ),
        out_shape=[
            jax.ShapeDtypeStruct((length, wide), BF16),
            jax.ShapeDtypeStruct((length, heads), F32),
        ],
        compiler_params=pltpu.CompilerParams(vmem_limit_bytes=48 * MIB),
        cost_estimate=pl.CostEstimate(
            flops=4 * heads * length * HEAD_DIM * (length // 2 + top * MBLK),
            bytes_accessed=8 * length * wide,
            transcendentals=heads * length * (length // 2 + top * MBLK),
        ),
        name="attend_forward",
    )(chosen, counts, qkv, qkv, qkv, memory, memory)


def backward_kernel(
    heads, top, chosen_ref, counts_ref, q_ref, k_ref, v_ref, mk_ref, mv_ref, go_ref, out_ref, lse_ref,
    cos_ref, sin_ref, w_ref, partial_ref, grad_ref, gk_s, gv_s, gq_s,
):
    block = pl.num_programs(0) - 1 - pl.program_id(0)
    rows = q_ref.shape[0]
    subs = rows // QBLK
    wide = heads * HEAD_DIM
    own = pl.ds(pl.multiple_of(block * rows, rows), rows)
    key_at = lax.broadcasted_iota(jnp.int32, (rows, rows), 0)
    query_at = lax.broadcasted_iota(jnp.int32, (rows, rows), 1)
    causal = query_at >= key_at

    @pl.when(pl.program_id(0) == 0)
    def _():
        gk_s[...] = jnp.zeros_like(gk_s)
        gv_s[...] = jnp.zeros_like(gv_s)

    def spread(column):
        return jnp.transpose(jnp.broadcast_to(column, (rows, HEAD_DIM)))[:1]

    stats = []
    for head in range(heads):
        columns = slice(head * HEAD_DIM, (head + 1) * HEAD_DIM)
        delta = jnp.sum(go_ref[:, columns].astype(F32) * out_ref[:, columns].astype(F32), -1, keepdims=True)
        stats.append((spread(lse_ref[:, head : head + 1]), spread(delta)))

    def pair(head, queries, keys, values, mask):
        columns = slice(head * HEAD_DIM, (head + 1) * HEAD_DIM)
        lse, delta = stats[head]
        scores = mask(dot(keys, q_ref[queries, columns], NT))
        weights = jnp.exp2(scores - lse[:, queries])
        grad_weights = dot(values, go_ref[queries, columns], NT)
        return weights.astype(BF16), (weights * (grad_weights - delta[:, queries])).astype(BF16)

    every = slice(0, rows)
    for head in range(heads):
        columns = slice(head * HEAD_DIM, (head + 1) * HEAD_DIM)
        for sub in range(subs):
            base = (block * subs + sub) * top
            queries = slice(sub * QBLK, (sub + 1) * QBLK)
            keys = pick_memory(mk_ref, chosen_ref, base, top, columns)
            values = pick_memory(mv_ref, chosen_ref, base, top, columns)
            bias = memory_bias(counts_ref, base, top, 0)
            _, grad_scores = pair(head, queries, keys, values, lambda scores: scores + bias)
            gq_s[queries, columns] = dot(grad_scores, keys, TN)

    def local(head, there, mask):
        columns = slice(head * HEAD_DIM, (head + 1) * HEAD_DIM)
        keys = k_ref[there, columns]
        weights, grad_scores = pair(head, every, keys, v_ref[there, columns], mask)
        gk_s[there, columns] += dot(grad_scores, q_ref[:, columns])
        gv_s[there, columns] += dot(weights, go_ref[:, columns])
        gq_s[:, columns] += dot(grad_scores, keys, TN)

    for head in range(heads):
        local(head, own, lambda scores: jnp.where(causal, scores, NEGATIVE))

    def step(index, carry):
        for head in range(heads):
            local(head, pl.ds(pl.multiple_of(index * rows, rows), rows), lambda scores: scores)
        return carry

    lax.fori_loop(0, block, step, 0)
    cosine, sine = cos_ref[...], sin_ref[...]

    def unturn(value):
        return value * cosine - pltpu.roll(value, HEAD_DIM // 2, 1) * sine

    for head in range(heads):
        columns = slice(head * HEAD_DIM, (head + 1) * HEAD_DIM)
        at = head * HEAD_DIM
        grad_ref[:, at : at + HEAD_DIM] = unturn(gq_s[:, columns] * SCALE).astype(BF16)
        grad_key = gk_s[own, columns] * (1.0 / LOG2E)
        grad_ref[:, wide + at : wide + at + HEAD_DIM] = unturn(grad_key).astype(BF16)
        grad_ref[:, 2 * wide + at : 2 * wide + at + HEAD_DIM] = gv_s[own, columns].astype(BF16)

    partial_ref[...] = dot(grad_ref[...], w_ref[...], NT).astype(BF16)


def attend_backward(chosen, counts, qkv, memory, grad_out, out, lse, cosine, sine, w_qkv, heads, top):
    length = qkv.shape[0]
    width = w_qkv.shape[0]
    wide = heads * HEAD_DIM
    rows = min(2 * QBLK, length)
    mem_rows = memory.shape[0]
    last = length // rows - 1
    return pl.pallas_call(
        functools.partial(backward_kernel, heads, top),
        grid_spec=pltpu.PrefetchScalarGridSpec(
            num_scalar_prefetch=2,
            grid=(last + 1,),
            in_specs=[
                pl.BlockSpec((rows, wide), lambda i, *_: (last - i, 0)),
                pl.BlockSpec((length, wide), lambda i, *_: (0, 1)),
                pl.BlockSpec((length, wide), lambda i, *_: (0, 2)),
                pl.BlockSpec((mem_rows, wide), lambda i, *_: (0, 0)),
                pl.BlockSpec((mem_rows, wide), lambda i, *_: (0, 1)),
                pl.BlockSpec((rows, wide), lambda i, *_: (last - i, 0)),
                pl.BlockSpec((rows, wide), lambda i, *_: (last - i, 0)),
                pl.BlockSpec((rows, heads), lambda i, *_: (last - i, 0)),
                pl.BlockSpec((rows, HEAD_DIM), lambda i, *_: (last - i, 0)),
                pl.BlockSpec((rows, HEAD_DIM), lambda i, *_: (last - i, 0)),
                pl.BlockSpec((width, 3 * wide), lambda i, *_: (0, 0)),
            ],
            out_specs=[
                pl.BlockSpec((rows, width), lambda i, *_: (last - i, 0)),
                pl.BlockSpec((rows, 3 * wide), lambda i, *_: (last - i, 0)),
            ],
            scratch_shapes=[
                pltpu.VMEM((length, wide), F32),
                pltpu.VMEM((length, wide), F32),
                pltpu.VMEM((rows, wide), F32),
            ],
        ),
        out_shape=[
            jax.ShapeDtypeStruct((length, width), BF16),
            jax.ShapeDtypeStruct((length, 3 * wide), BF16),
        ],
        compiler_params=pltpu.CompilerParams(vmem_limit_bytes=48 * MIB),
        cost_estimate=pl.CostEstimate(
            flops=10 * heads * length * HEAD_DIM * (length // 2 + top * MBLK),
            bytes_accessed=16 * length * wide,
            transcendentals=heads * length * (length // 2 + top * MBLK),
        ),
        name="attend_backward",
    )(
        chosen, counts, qkv, qkv, qkv, memory, memory, grad_out, out, lse, cosine, sine, w_qkv
    )


def ffn_kernel(
    span, merged, tok_ref, att_ref, cot_ref, gain_ref, out_w, gate_w, up_w, down_w,
    mixed_ref, grad_mid_ref, grad_att_ref, gain_grad_ref, grads_ref, *rest,
):
    if not merged:
        down_grads_ref, rest = rest[0], rest[1:]
    middle_s, normed_s, turned_s, mixed_s, upstream_s, gate_s, up_s, down_s, out_s, sems, late_sems = rest
    step, steps = pl.program_id(0), pl.num_programs(0)
    width = tok_ref.shape[1]
    share = width // span
    wide = gate_w.shape[1]
    hidden_width = down_s.shape[0]
    tall = hidden_width // span
    lanes = width // wide
    first = tall * lanes if merged else 0
    slot = step % 2

    @pl.when(step == 0)
    def _():
        middle = tok_ref[...].astype(F32) + dot(att_ref[...], out_w[...])
        middle_s[...] = middle
        factor = lax.rsqrt(jnp.mean(middle * middle, -1, keepdims=True) + EPSILON)
        normed = (middle * factor * gain_ref[...]).astype(BF16)
        normed_s[...] = normed
        turned_s[...] = jnp.transpose(normed)
        mixed_s[...] = middle
        upstream_s[...] = jnp.zeros_like(upstream_s)

    def copy_out(kind, which, index):
        source = (gate_s, up_s)[kind].at[which]
        start = first + (lanes + kind * steps + index) * share
        target = grads_ref.at[:, pl.ds(start, share), :]
        return pltpu.make_async_copy(source, target, sems.at[kind, which])

    normed = normed_s[...]
    upstream = cot_ref[...]
    both = jnp.concatenate([gate_w[...], up_w[...]], 1)
    acts = dot(normed, both)
    gate_act, up_act = acts[:, :wide], acts[:, wide:]
    grad_hidden = dot(upstream, down_w[...], NT)
    sigmoid = jax.nn.sigmoid(gate_act)
    silu = gate_act * sigmoid
    hidden = (silu * up_act).astype(BF16)
    grad_gate = (grad_hidden * up_act * sigmoid * (1.0 + gate_act * (1.0 - sigmoid))).astype(BF16)
    grad_up = (grad_hidden * silu).astype(BF16)
    mixed_s[...] += dot(hidden, down_w[...])
    grad_acts = jnp.concatenate([grad_gate, grad_up], 1)
    upstream_s[...] += dot(grad_acts, both, NT)
    down_s[pl.ds(pl.multiple_of(step * wide, wide), wide), :] = dot(hidden, upstream, TN).astype(BF16)

    @pl.when(step >= 2)
    def _():
        copy_out(0, slot, step - 2).wait()
        copy_out(1, slot, step - 2).wait()

    weight_grads = dot(turned_s[...], grad_acts).astype(BF16)
    gate_s[slot] = weight_grads[:, :wide].reshape(span, share, wide)
    up_s[slot] = weight_grads[:, wide:].reshape(span, share, wide)
    copy_out(0, slot, step).start()
    copy_out(1, slot, step).start()

    @pl.when(step == steps - 1)
    def _():
        copies = []
        if merged:
            for place in range(span):
                for lane in range(lanes):
                    copies.append(
                        pltpu.make_async_copy(
                            down_s.at[pl.ds(place * tall, tall), pl.ds(lane * wide, wide)],
                            grads_ref.at[place, pl.ds(lane * tall, tall), :],
                            late_sems.at[len(copies)],
                        )
                    )
        else:
            copies.append(pltpu.make_async_copy(down_s, down_grads_ref, late_sems.at[0]))
        for copy in copies:
            copy.start()
        mixed_ref[...] = mixed_s[...].astype(BF16)
        middle = middle_s[...]
        grad = upstream_s[...]
        factor = lax.rsqrt(jnp.mean(middle * middle, -1, keepdims=True) + EPSILON)
        gain_grad_ref[...] = jnp.sum(grad * middle * factor, 0, keepdims=True)
        scaled = grad * gain_ref[...]
        inner = jnp.mean(scaled * middle, -1, keepdims=True)
        grad_middle = cot_ref[...].astype(F32) + factor * scaled - middle * (factor * factor * factor * inner)
        grad_mid_ref[...] = grad_middle
        branch = grad_middle.astype(BF16)
        grad_att_ref[...] = dot(branch, out_w[...], NT).astype(BF16)
        turned_att = jnp.transpose(att_ref[...])
        for lane in range(lanes):
            columns = slice(lane * wide, (lane + 1) * wide)
            out_s[lane] = dot(turned_att, branch[:, columns]).astype(BF16).reshape(span, share, wide)
            more = pltpu.make_async_copy(
                out_s.at[lane],
                grads_ref.at[:, pl.ds(first + lane * share, share), :],
                late_sems.at[len(copies)],
            )
            more.start()
            copies.append(more)
        for copy in copies:
            copy.wait()
        copy_out(0, 1 - slot, step - 1).wait()
        copy_out(1, 1 - slot, step - 1).wait()
        copy_out(0, slot, step).wait()
        copy_out(1, slot, step).wait()


def feed_forward(tokens, attended, upstream, gain, weights, w_down, span):
    rows, width = tokens.shape
    hidden_width = w_down.shape[0]
    wide = 2 * HEAD_DIM
    steps = hidden_width // wide
    lanes = width // wide
    share = width // span
    tall = hidden_width // span
    merged = tall % 16 == 0
    total = (lanes + 2 * steps) * share + (lanes * tall if merged else 0)
    shapes = [
        jax.ShapeDtypeStruct((rows, width), BF16),
        jax.ShapeDtypeStruct((rows, width), F32),
        jax.ShapeDtypeStruct((rows, width), BF16),
        jax.ShapeDtypeStruct((1, width), F32),
        jax.ShapeDtypeStruct((span, total, wide), BF16),
    ]
    specs = [
        pl.BlockSpec((rows, width), lambda i: (0, 0)),
        pl.BlockSpec((rows, width), lambda i: (0, 0)),
        pl.BlockSpec((rows, width), lambda i: (0, 0)),
        pl.BlockSpec((1, width), lambda i: (0, 0)),
        pl.BlockSpec(memory_space=pl.ANY),
    ]
    if not merged:
        shapes.append(jax.ShapeDtypeStruct((hidden_width, width), BF16))
        specs.append(pl.BlockSpec(memory_space=pl.ANY))
    return pl.pallas_call(
        functools.partial(ffn_kernel, span, merged),
        grid=(steps,),
        in_specs=[
            pl.BlockSpec((rows, width), lambda i: (0, 0)),
            pl.BlockSpec((rows, width), lambda i: (0, 0)),
            pl.BlockSpec((rows, width), lambda i: (0, 0)),
            pl.BlockSpec((1, width), lambda i: (0, 0)),
            pl.BlockSpec((width, width), lambda i: (0, 0)),
            pl.BlockSpec((width, wide), lambda i: (0, lanes + i)),
            pl.BlockSpec((width, wide), lambda i: (0, lanes + steps + i)),
            pl.BlockSpec((wide, width), lambda i: (i, 0)),
        ],
        out_specs=specs,
        out_shape=shapes,
        scratch_shapes=[
            pltpu.VMEM((rows, width), F32),
            pltpu.VMEM((rows, width), BF16),
            pltpu.VMEM((width, rows), BF16),
            pltpu.VMEM((rows, width), F32),
            pltpu.VMEM((rows, width), F32),
            pltpu.VMEM((2, span, share, wide), BF16),
            pltpu.VMEM((2, span, share, wide), BF16),
            pltpu.VMEM((hidden_width, width), BF16),
            pltpu.VMEM((lanes, span, share, wide), BF16),
            pltpu.SemaphoreType.DMA((2, 2)),
            pltpu.SemaphoreType.DMA(((span * lanes if merged else 1) + lanes,)),
        ],
        compiler_params=pltpu.CompilerParams(vmem_limit_bytes=56 * MIB),
        cost_estimate=pl.CostEstimate(
            flops=6 * rows * width * (3 * hidden_width + width),
            bytes_accessed=4 * width * (3 * hidden_width + width),
            transcendentals=rows * hidden_width,
        ),
        name="feed_forward",
    )(tokens, attended, upstream, gain, weights, weights, weights, w_down)


def projection_grads_kernel(tok_ref, gain_ref, w_ref, grad_ref, grad_w_ref, gain_grad_ref, raw_s):
    step = pl.program_id(0)

    @pl.when(step == 0)
    def _():
        raw_s[...] = jnp.zeros_like(raw_s)

    tokens = tok_ref[...].astype(F32)
    tokens = tokens * lax.rsqrt(jnp.mean(tokens * tokens, -1, keepdims=True) + EPSILON)
    raw_s[...] += dot(tokens.astype(BF16), grad_ref[...], TN)

    @pl.when(step == pl.num_programs(0) - 1)
    def _():
        raw = raw_s[...]
        gain_grad_ref[...] = jnp.sum(raw * w_ref[...].astype(F32), -1, keepdims=True)
        grad_w_ref[...] = (raw * gain_ref[...]).astype(BF16)


def projection_grads(tokens_all, gain_column, w_qkv, grad):
    length, width = tokens_all.shape
    columns = grad.shape[1]
    rows = min(2 * QBLK, length)
    return pl.pallas_call(
        projection_grads_kernel,
        grid=(length // rows,),
        in_specs=[
            pl.BlockSpec((rows, width), lambda i: (i, 0)),
            pl.BlockSpec((width, 1), lambda i: (0, 0)),
            pl.BlockSpec((width, columns), lambda i: (0, 0)),
            pl.BlockSpec((rows, columns), lambda i: (i, 0)),
        ],
        out_specs=[
            pl.BlockSpec((width, columns), lambda i: (0, 0)),
            pl.BlockSpec((width, 1), lambda i: (0, 0)),
        ],
        out_shape=[
            jax.ShapeDtypeStruct((width, columns), BF16),
            jax.ShapeDtypeStruct((width, 1), F32),
        ],
        scratch_shapes=[pltpu.VMEM((width, columns), F32)],
        compiler_params=pltpu.CompilerParams(vmem_limit_bytes=48 * MIB),
        cost_estimate=pl.CostEstimate(
            flops=2 * length * width * columns, bytes_accessed=2 * length * (width + columns), transcendentals=0
        ),
        name="projection_grads",
    )(tokens_all, gain_column, w_qkv, grad)


def after(value, earlier):
    return lax.optimization_barrier((value, earlier))[0]


def chain_gather(blocks, axis):
    size = lax.axis_size(axis)
    place = lax.axis_index(axis)
    steps = []
    rising = falling = tuple(blocks)
    for step in range(size - 1):
        up = [(i, i + 1) for i in range(step, size - 1)]
        down = [(i + 1, i) for i in range(size - 1 - step)]
        rising = tuple(lax.ppermute(block, axis, up) for block in rising)
        falling = tuple(lax.ppermute(block, axis, down) for block in falling)
        if len(blocks) > 1:
            rising, falling = lax.optimization_barrier((rising, falling))
        steps.append((rising, falling))
    results = []
    for number, block in enumerate(blocks):
        ordered = []
        for index in range(size):
            cases = []
            for mine in range(size):
                if mine == index:
                    cases.append(block)
                elif mine > index:
                    cases.append(steps[mine - index - 1][0][number])
                else:
                    cases.append(steps[index - mine - 1][1][number])
            ordered.append(lax.select_n(place, *cases) if size > 2 else lax.select_n(place > 0, *cases))
        results.append(ordered)
    return results, steps


def chain_scatter(partial, axis):
    size = lax.axis_size(axis)
    place = lax.axis_index(axis)
    rows = partial.shape[0] // size

    def block(index):
        return lax.dynamic_slice_in_dim(partial, jnp.clip(index, 0, size - 1) * rows, rows, 0).astype(F32)

    rising = falling = None
    steps = []
    for step in range(size - 1):
        up, down = block(size - 1 - step + place), block(step - size + 1 + place)
        if step:
            up, down = up + rising.astype(F32), down + falling.astype(F32)
        up, down = lax.optimization_barrier((up.astype(BF16), down.astype(BF16)))
        rising = lax.ppermute(up, axis, [(i, i + 1) for i in range(step + 1)])
        falling = lax.ppermute(down, axis, [(i, i - 1) for i in range(size - 1 - step, size)])
        rising, falling = lax.optimization_barrier((rising, falling))
        steps.append((rising, falling))
    return block(place), steps


def body(
    tokens, memory_keys, memory_values, chosen, counts, w_query, w_key, w_value, w_out, w_gate, w_up, w_down,
    gain_attn, gain_ffn, cotangent,
):
    ring, span = lax.axis_size("fsdp"), lax.axis_size(DP)
    rows, width = tokens.shape[1:]
    heads = width // HEAD_DIM // ring
    wide = heads * HEAD_DIM
    length = rows * ring
    top = chosen.shape[2]
    hidden_width = w_gate.shape[1]
    share = w_query.shape[0]
    mine = tokens[0]

    extra = 8 if share % 8 == 0 else 8 - share % 8
    parts = [w.reshape(share, ring, wide).transpose(1, 0, 2) for w in (w_query, w_key, w_value)]
    choices = jnp.concatenate([chosen[0].reshape(-1), counts[0].reshape(-1)]).astype(BF16)
    notes = jnp.stack(
        [
            jnp.pad(row, (0, 3 * wide - row.shape[0]))
            for row in (jnp.concatenate([gain_attn, gain_ffn]), choices)
        ]
    )
    notes = jnp.broadcast_to(jnp.pad(notes, ((0, extra - 2), (0, 0))), (ring, extra, 3 * wide))
    parcel = jnp.concatenate([jnp.concatenate(parts, 2), notes], 1)
    parcel = lax.all_to_all(parcel, "fsdp", 0, 0, tiled=True)
    picks = parcel[:, share + 1, : choices.shape[0]].astype(jnp.int32).reshape(ring, 2, -1)
    chosen_all, counts_all = picks[:, 0].reshape(-1), picks[:, 1].reshape(-1)
    shards = jnp.concatenate([w_out, w_gate, w_up], 1)
    (near, near_down), steps = chain_gather((shards, w_down), "fsdp")
    (gathered,), token_steps = chain_gather((after(mine, steps[-2]),), "fsdp")
    parcel = lax.all_gather(after(parcel, steps[0]), DP, axis=0, tiled=True)
    w_qkv = parcel[:, :share].reshape(width, 3 * wide)
    gain_one = parcel[:, share, :share].reshape(1, width).astype(F32)
    gain_two = parcel[:, share, share : 2 * share].reshape(1, width).astype(F32)
    first = lax.all_gather(jnp.concatenate(near, 0), DP, axis=0, tiled=True)
    gathered = jnp.concatenate(gathered, 0)

    memory = jnp.concatenate(
        [m[0].reshape(-1, ring, wide).transpose(1, 0, 2) for m in (memory_keys, memory_values)], 2
    )
    memory = lax.all_to_all(after(memory, token_steps[-2]), "fsdp", 0, 0, tiled=True).reshape(-1, 2 * wide)
    down_full = lax.all_gather(jnp.concatenate(near_down, 0), DP, axis=0, tiled=True)

    cosine, sine = rotary_tables(length)
    qkv = project_qkv(gathered, gain_one, w_qkv, cosine, sine, heads)
    attended_heads, lse = attend_forward(chosen_all, counts_all, qkv, memory, heads, top)
    attended = lax.all_to_all(attended_heads, "fsdp", 0, 1, tiled=True)

    upstream = cotangent[0]
    mixed, grad_middle, grad_attended, gain_two_grad, grads, *grad_down = feed_forward(
        mine, attended, upstream, gain_two, first, down_full, span
    )
    grad_heads = lax.all_to_all(grad_attended, "fsdp", 1, 0, tiled=True)
    grads = lax.psum_scatter(grads, DP, scatter_dimension=0, tiled=True)[0]

    partial, grad_qkv = attend_backward(
        chosen_all, counts_all, qkv, memory, grad_heads, attended_heads, lse, cosine, sine, w_qkv, heads, top
    )
    own_term, steps = chain_scatter(partial, "fsdp")
    grad_w_qkv, gain_one_grad = projection_grads(gathered, gain_one.reshape(width, 1), w_qkv, grad_qkv)
    grads = after(grads, steps[-1])

    gains = jnp.stack([gain_one_grad.reshape(span, -1), gain_two_grad.reshape(span, -1)], 1)
    gains = jnp.pad(gains.astype(BF16), ((0, 0), (0, extra - 2), (0, 3 * wide - gains.shape[2])))
    late = jnp.concatenate([grad_w_qkv.reshape(span, -1, 3 * wide), gains], 1)
    late = late.reshape(span // 2, 2, late.shape[1], 3 * wide)
    core = lax.axis_index("core")
    taken = lax.ppermute(lax.dynamic_index_in_dim(late, 1 - core, 1, keepdims=False), "core", [(0, 1), (1, 0)])
    late = lax.dynamic_index_in_dim(late, core, 1, keepdims=False).astype(F32) + taken.astype(F32)
    late = after(late.astype(BF16), steps[0])
    late = jnp.sum(lax.all_to_all(late, "chip", 0, 0, tiled=True).astype(F32), 0).astype(BF16)
    gains = late[-extra : 2 - extra, : ring * share].reshape(2, ring, share).transpose(1, 0, 2)
    gains = jnp.pad(gains, ((0, 0), (0, extra - 2), (0, 3 * wide - share)))
    late = jnp.concatenate([late[:-extra].reshape(ring, share, 3 * wide), gains], 1)
    late = lax.all_to_all(late, "fsdp", 0, 0, tiled=True).astype(F32)
    projections = [
        late[:, :share, part * wide : (part + 1) * wide].transpose(1, 0, 2).reshape(share, width)
        for part in range(3)
    ]
    gain_shares = jnp.sum(late[:, share : share + 2, :share], 0)

    strip = grads.shape[1]
    lanes = width // strip
    tall = w_down.shape[0]
    if grad_down:
        down = lax.psum_scatter(grad_down[0], DP, scatter_dimension=0, tiled=True)
        down = down.reshape(ring, tall, lanes, strip).transpose(0, 2, 1, 3)
    else:
        down = grads[: ring * tall * lanes].reshape(lanes, ring, tall, strip).transpose(1, 0, 2, 3)
        grads = grads[ring * tall * lanes :]
    grads = grads.reshape(-1, ring, share, strip).transpose(1, 0, 2, 3)
    pieces = jnp.concatenate([down.reshape(ring, -1, strip), grads.reshape(ring, -1, strip)], 1)
    rising, falling = steps[-1]
    grad_normed = own_term + rising.astype(F32) + falling.astype(F32)
    own = mine.astype(F32)
    factor = lax.rsqrt(jnp.mean(own * own, -1, keepdims=True) + EPSILON)
    scaled = grad_normed * gain_one
    inner = jnp.mean(scaled * own, -1, keepdims=True)
    tokens_grad = (grad_middle + factor * scaled - own * (factor * factor * factor * inner)).astype(BF16)

    pieces = lax.psum_scatter(pieces, "fsdp", scatter_dimension=0, tiled=True)[0].astype(F32)
    down_share = pieces[: lanes * tall].reshape(lanes, tall, strip).transpose(1, 0, 2).reshape(tall, width)
    others = pieces[lanes * tall :].reshape(-1, share, strip).transpose(1, 0, 2).reshape(share, -1)
    return (
        mixed[None],
        tokens_grad[None],
        *projections,
        others[:, :width],
        others[:, width : width + hidden_width],
        others[:, width + hidden_width :],
        down_share,
        gain_shares[0],
        gain_shares[1],
    )


def solution(mesh):
    span, ring = mesh.shape["dp"], mesh.shape["fsdp"]
    fine = Mesh(mesh.devices.reshape(span // 2, 2, ring), DP + ("fsdp",))
    every = DP + ("fsdp",)
    rows, matrix, vector = P(DP, "fsdp", None), P(every, None), P(every)
    in_specs = (rows,) * 5 + (matrix,) * 7 + (vector,) * 2 + (rows,)
    out_specs = (rows,) * 2 + (matrix,) * 7 + (vector,) * 2
    return jax.shard_map(body, mesh=fine, in_specs=in_specs, out_specs=out_specs, check_vma=False)
```

```python
import functools
import math

import jax
import jax.numpy as jnp
import numpy as np
from jax import lax
from jax.experimental import pallas as pl
from jax.experimental.pallas import tpu as pltpu
from jax.sharding import Mesh
from jax.sharding import PartitionSpec as P

HEAD_DIM = 128
QBLK = 256
MBLK = 128
EPSILON = 1e-06
NEGATIVE = -1e30
SCALE = 1.0 / math.sqrt(HEAD_DIM)
LOG2E = math.log2(math.e)
MIB = 1 << 20
F32 = jnp.float32
BF16 = jnp.bfloat16
DP = ("chip", "core")
NT = (((1,), (1,)), ((), ()))
TN = (((0,), (0,)), ((), ()))


def dot(left, right, dims=(((1,), (0,)), ((), ()))):
    return lax.dot_general(left, right, dims, preferred_element_type=F32)


def rotary_tables(length):
    half_dim = HEAD_DIM // 2
    frequency = 10000.0 ** (-jnp.arange(half_dim, dtype=F32) / half_dim)
    angles = jnp.arange(length, dtype=jnp.int32).astype(F32)[:, None] * frequency[None, :]
    cosine, sine = jnp.cos(angles), jnp.sin(angles)
    return jnp.concatenate([cosine, cosine], 1), jnp.concatenate([-sine, sine], 1)


def qkv_kernel(heads, tok_ref, gain_ref, w_ref, cos_ref, sin_ref, qkv_ref):
    rows = tok_ref[...].astype(F32)
    factor = lax.rsqrt(jnp.mean(rows * rows, -1, keepdims=True) + EPSILON)
    normed = (rows * factor * gain_ref[...]).astype(BF16)
    cosine, sine = cos_ref[...], sin_ref[...]
    wide = heads * HEAD_DIM
    for part in range(3):
        values = dot(normed, w_ref[:, part * wide : (part + 1) * wide])
        for head in range(heads):
            value = values[:, head * HEAD_DIM : (head + 1) * HEAD_DIM]
            if part < 2:
                value = value * cosine + pltpu.roll(value, HEAD_DIM // 2, 1) * sine
            if part == 0:
                value = value * (SCALE * LOG2E)
            at = part * wide + head * HEAD_DIM
            qkv_ref[:, at : at + HEAD_DIM] = value.astype(BF16)


def project_qkv(tokens_all, gain, w_qkv, cosine, sine, heads):
    length, width = tokens_all.shape
    columns = w_qkv.shape[1]
    block = 2 * QBLK
    return pl.pallas_call(
        functools.partial(qkv_kernel, heads),
        grid=(length // block,),
        in_specs=[
            pl.BlockSpec((block, width), lambda i: (i, 0)),
            pl.BlockSpec((1, width), lambda i: (0, 0)),
            pl.BlockSpec((width, columns), lambda i: (0, 0)),
            pl.BlockSpec((block, HEAD_DIM), lambda i: (i, 0)),
            pl.BlockSpec((block, HEAD_DIM), lambda i: (i, 0)),
        ],
        out_specs=pl.BlockSpec((block, columns), lambda i: (i, 0)),
        out_shape=jax.ShapeDtypeStruct((length, columns), BF16),
        compiler_params=pltpu.CompilerParams(vmem_limit_bytes=48 * MIB),
        cost_estimate=pl.CostEstimate(
            flops=2 * length * width * columns, bytes_accessed=4 * length * (width + columns), transcendentals=0
        ),
        name="project_qkv",
    )(tokens_all, gain, w_qkv, cosine, sine)


def memory_bias(counts_ref, base, top, axis):
    shape = (1, top * MBLK) if axis == 1 else (top * MBLK, 1)
    column = lax.broadcasted_iota(jnp.int32, shape, axis)
    limit = jnp.zeros(shape, jnp.int32)
    for entry in range(top):
        inside = (column >= entry * MBLK) & (column < entry * MBLK + counts_ref[base + entry])
        limit = jnp.where(inside, 1, limit)
    return jnp.where(limit > 0, 0.0, NEGATIVE)


def pick_memory(ref, chosen_ref, base, top, columns):
    rows = [
        ref[pl.ds(pl.multiple_of(chosen_ref[base + entry] * MBLK, MBLK), MBLK), columns]
        for entry in range(top)
    ]
    return jnp.concatenate(rows, 0)


def forward_kernel(
    heads, top, chosen_ref, counts_ref, q_ref, k_ref, v_ref, mk_ref, mv_ref, out_ref, lse_ref, acc_s, peak_s
):
    block = pl.program_id(0)
    rows = q_ref.shape[0]
    subs = rows // QBLK
    own = pl.ds(pl.multiple_of(block * rows, rows), rows)
    causal = lax.broadcasted_iota(jnp.int32, (rows, rows), 0) >= lax.broadcasted_iota(jnp.int32, (rows, rows), 1)
    ones = jnp.ones((rows, HEAD_DIM), BF16)
    mem_ones = jnp.ones((top * MBLK, HEAD_DIM), BF16)
    biases = [memory_bias(counts_ref, (block * subs + sub) * top, top, 1) for sub in range(subs)]
    for head in range(heads):
        columns = slice(head * HEAD_DIM, (head + 1) * HEAD_DIM)
        remote = []
        for sub in range(subs):
            keys = pick_memory(mk_ref, chosen_ref, (block * subs + sub) * top, top, columns)
            query = q_ref[sub * QBLK : (sub + 1) * QBLK, columns]
            remote.append(dot(query, keys, NT) + biases[sub])
        local = jnp.where(causal, dot(q_ref[:, columns], k_ref[own, columns], NT), NEGATIVE)
        peak = jnp.max(local, -1, keepdims=True)
        peak = jnp.maximum(peak, jnp.concatenate([jnp.max(r, -1, keepdims=True) for r in remote], 0))
        values = jnp.concatenate([v_ref[own, columns], ones], 1)
        acc = dot(jnp.exp2(local - peak).astype(BF16), values)
        more = []
        for sub in range(subs):
            values = pick_memory(mv_ref, chosen_ref, (block * subs + sub) * top, top, columns)
            weights = jnp.exp2(remote[sub] - peak[sub * QBLK : (sub + 1) * QBLK]).astype(BF16)
            more.append(dot(weights, jnp.concatenate([values, mem_ones], 1)))
        acc_s[head] = acc + jnp.concatenate(more, 0)
        peak_s[head] = jnp.broadcast_to(peak, (rows, HEAD_DIM))

    def step(index, carry):
        there = pl.ds(pl.multiple_of(index * rows, rows), rows)
        for head in range(heads):
            columns = slice(head * HEAD_DIM, (head + 1) * HEAD_DIM)
            peak = peak_s[head][:, :1]
            scores = dot(q_ref[:, columns], k_ref[there, columns], NT)
            higher = jnp.maximum(peak, jnp.max(scores, -1, keepdims=True))
            weights = jnp.exp2(scores - higher).astype(BF16)
            values = jnp.concatenate([v_ref[there, columns], ones], 1)
            acc_s[head] = acc_s[head] * jnp.exp2(peak - higher) + dot(weights, values)
            peak_s[head] = jnp.broadcast_to(higher, (rows, HEAD_DIM))
        return carry

    lax.fori_loop(0, block, step, 0)
    for head in range(heads):
        columns = slice(head * HEAD_DIM, (head + 1) * HEAD_DIM)
        total = acc_s[head][:, HEAD_DIM:]
        out_ref[:, columns] = (acc_s[head][:, :HEAD_DIM] / total).astype(BF16)
        lse_ref[:, head : head + 1] = peak_s[head][:, :1] + jnp.log2(total[:, :1])


def attend_forward(chosen, counts, qkv, memory, heads, top):
    length = qkv.shape[0]
    wide = heads * HEAD_DIM
    rows = min(2 * QBLK, length)
    mem_rows = memory.shape[0]
    return pl.pallas_call(
        functools.partial(forward_kernel, heads, top),
        grid_spec=pltpu.PrefetchScalarGridSpec(
            num_scalar_prefetch=2,
            grid=(length // rows,),
            in_specs=[
                pl.BlockSpec((rows, wide), lambda i, *_: (i, 0)),
                pl.BlockSpec((length, wide), lambda i, *_: (0, 1)),
                pl.BlockSpec((length, wide), lambda i, *_: (0, 2)),
                pl.BlockSpec((mem_rows, wide), lambda i, *_: (0, 0)),
                pl.BlockSpec((mem_rows, wide), lambda i, *_: (0, 1)),
            ],
            out_specs=[
                pl.BlockSpec((rows, wide), lambda i, *_: (i, 0)),
                pl.BlockSpec((rows, heads), lambda i, *_: (i, 0)),
            ],
            scratch_shapes=[
                pltpu.VMEM((heads, rows, 2 * HEAD_DIM), F32),
                pltpu.VMEM((heads, rows, HEAD_DIM), F32),
            ],
        ),
        out_shape=[
            jax.ShapeDtypeStruct((length, wide), BF16),
            jax.ShapeDtypeStruct((length, heads), F32),
        ],
        compiler_params=pltpu.CompilerParams(vmem_limit_bytes=48 * MIB),
        cost_estimate=pl.CostEstimate(
            flops=4 * heads * length * HEAD_DIM * (length // 2 + top * MBLK),
            bytes_accessed=8 * length * wide,
            transcendentals=heads * length * (length // 2 + top * MBLK),
        ),
        name="attend_forward",
    )(chosen, counts, qkv, qkv, qkv, memory, memory)


def backward_kernel(
    heads, top, chosen_ref, counts_ref, q_ref, k_ref, v_ref, mk_ref, mv_ref, go_ref, out_ref, lse_ref,
    cos_ref, sin_ref, w_ref, partial_ref, grad_ref, gk_s, gv_s, gq_s,
):
    block = pl.num_programs(0) - 1 - pl.program_id(0)
    rows = q_ref.shape[0]
    subs = rows // QBLK
    wide = heads * HEAD_DIM
    own = pl.ds(pl.multiple_of(block * rows, rows), rows)
    key_at = lax.broadcasted_iota(jnp.int32, (rows, rows), 0)
    query_at = lax.broadcasted_iota(jnp.int32, (rows, rows), 1)
    causal = query_at >= key_at

    @pl.when(pl.program_id(0) == 0)
    def _():
        gk_s[...] = jnp.zeros_like(gk_s)
        gv_s[...] = jnp.zeros_like(gv_s)

    def spread(column):
        return jnp.transpose(jnp.broadcast_to(column, (rows, HEAD_DIM)))[:1]

    stats = []
    for head in range(heads):
        columns = slice(head * HEAD_DIM, (head + 1) * HEAD_DIM)
        delta = jnp.sum(go_ref[:, columns].astype(F32) * out_ref[:, columns].astype(F32), -1, keepdims=True)
        stats.append((spread(lse_ref[:, head : head + 1]), spread(delta)))

    def pair(head, queries, keys, values, mask):
        columns = slice(head * HEAD_DIM, (head + 1) * HEAD_DIM)
        lse, delta = stats[head]
        scores = mask(dot(keys, q_ref[queries, columns], NT))
        weights = jnp.exp2(scores - lse[:, queries])
        grad_weights = dot(values, go_ref[queries, columns], NT)
        return weights.astype(BF16), (weights * (grad_weights - delta[:, queries])).astype(BF16)

    every = slice(0, rows)
    for head in range(heads):
        columns = slice(head * HEAD_DIM, (head + 1) * HEAD_DIM)
        for sub in range(subs):
            base = (block * subs + sub) * top
            queries = slice(sub * QBLK, (sub + 1) * QBLK)
            keys = pick_memory(mk_ref, chosen_ref, base, top, columns)
            values = pick_memory(mv_ref, chosen_ref, base, top, columns)
            bias = memory_bias(counts_ref, base, top, 0)
            _, grad_scores = pair(head, queries, keys, values, lambda scores: scores + bias)
            gq_s[queries, columns] = dot(grad_scores, keys, TN)

    def local(head, there, mask):
        columns = slice(head * HEAD_DIM, (head + 1) * HEAD_DIM)
        keys = k_ref[there, columns]
        weights, grad_scores = pair(head, every, keys, v_ref[there, columns], mask)
        gk_s[there, columns] += dot(grad_scores, q_ref[:, columns])
        gv_s[there, columns] += dot(weights, go_ref[:, columns])
        gq_s[:, columns] += dot(grad_scores, keys, TN)

    for head in range(heads):
        local(head, own, lambda scores: jnp.where(causal, scores, NEGATIVE))

    def step(index, carry):
        for head in range(heads):
            local(head, pl.ds(pl.multiple_of(index * rows, rows), rows), lambda scores: scores)
        return carry

    lax.fori_loop(0, block, step, 0)
    cosine, sine = cos_ref[...], sin_ref[...]

    def unturn(value):
        return value * cosine - pltpu.roll(value, HEAD_DIM // 2, 1) * sine

    for head in range(heads):
        columns = slice(head * HEAD_DIM, (head + 1) * HEAD_DIM)
        at = head * HEAD_DIM
        grad_ref[:, at : at + HEAD_DIM] = unturn(gq_s[:, columns] * SCALE).astype(BF16)
        grad_key = gk_s[own, columns] * (1.0 / LOG2E)
        grad_ref[:, wide + at : wide + at + HEAD_DIM] = unturn(grad_key).astype(BF16)
        grad_ref[:, 2 * wide + at : 2 * wide + at + HEAD_DIM] = gv_s[own, columns].astype(BF16)

    partial_ref[...] = dot(grad_ref[...], w_ref[...], NT).astype(BF16)


def attend_backward(chosen, counts, qkv, memory, grad_out, out, lse, cosine, sine, w_qkv, heads, top):
    length = qkv.shape[0]
    width = w_qkv.shape[0]
    wide = heads * HEAD_DIM
    rows = min(2 * QBLK, length)
    mem_rows = memory.shape[0]
    last = length // rows - 1
    return pl.pallas_call(
        functools.partial(backward_kernel, heads, top),
        grid_spec=pltpu.PrefetchScalarGridSpec(
            num_scalar_prefetch=2,
            grid=(last + 1,),
            in_specs=[
                pl.BlockSpec((rows, wide), lambda i, *_: (last - i, 0)),
                pl.BlockSpec((length, wide), lambda i, *_: (0, 1)),
                pl.BlockSpec((length, wide), lambda i, *_: (0, 2)),
                pl.BlockSpec((mem_rows, wide), lambda i, *_: (0, 0)),
                pl.BlockSpec((mem_rows, wide), lambda i, *_: (0, 1)),
                pl.BlockSpec((rows, wide), lambda i, *_: (last - i, 0)),
                pl.BlockSpec((rows, wide), lambda i, *_: (last - i, 0)),
                pl.BlockSpec((rows, heads), lambda i, *_: (last - i, 0)),
                pl.BlockSpec((rows, HEAD_DIM), lambda i, *_: (last - i, 0)),
                pl.BlockSpec((rows, HEAD_DIM), lambda i, *_: (last - i, 0)),
                pl.BlockSpec((width, 3 * wide), lambda i, *_: (0, 0)),
            ],
            out_specs=[
                pl.BlockSpec((rows, width), lambda i, *_: (last - i, 0)),
                pl.BlockSpec((rows, 3 * wide), lambda i, *_: (last - i, 0)),
            ],
            scratch_shapes=[
                pltpu.VMEM((length, wide), F32),
                pltpu.VMEM((length, wide), F32),
                pltpu.VMEM((rows, wide), F32),
            ],
        ),
        out_shape=[
            jax.ShapeDtypeStruct((length, width), BF16),
            jax.ShapeDtypeStruct((length, 3 * wide), BF16),
        ],
        compiler_params=pltpu.CompilerParams(vmem_limit_bytes=48 * MIB),
        cost_estimate=pl.CostEstimate(
            flops=10 * heads * length * HEAD_DIM * (length // 2 + top * MBLK),
            bytes_accessed=16 * length * wide,
            transcendentals=heads * length * (length // 2 + top * MBLK),
        ),
        name="attend_backward",
    )(
        chosen, counts, qkv, qkv, qkv, memory, memory, grad_out, out, lse, cosine, sine, w_qkv
    )


def ffn_kernel(
    span, merged, tok_ref, att_ref, cot_ref, gain_ref, out_w, gate_w, up_w, down_w,
    mixed_ref, grad_mid_ref, grad_att_ref, gain_grad_ref, grads_ref, *rest,
):
    if not merged:
        down_grads_ref, rest = rest[0], rest[1:]
    middle_s, normed_s, turned_s, mixed_s, upstream_s, gate_s, up_s, down_s, out_s, sems, late_sems = rest
    step, steps = pl.program_id(0), pl.num_programs(0)
    width = tok_ref.shape[1]
    share = width // span
    wide = gate_w.shape[1]
    hidden_width = down_s.shape[0]
    tall = hidden_width // span
    lanes = width // wide
    first = tall * lanes if merged else 0
    slot = step % 2

    @pl.when(step == 0)
    def _():
        middle = tok_ref[...].astype(F32) + dot(att_ref[...], out_w[...])
        middle_s[...] = middle
        factor = lax.rsqrt(jnp.mean(middle * middle, -1, keepdims=True) + EPSILON)
        normed = (middle * factor * gain_ref[...]).astype(BF16)
        normed_s[...] = normed
        turned_s[...] = jnp.transpose(normed)
        mixed_s[...] = middle
        upstream_s[...] = jnp.zeros_like(upstream_s)

    def copy_out(kind, which, index):
        source = (gate_s, up_s)[kind].at[which]
        start = first + (lanes + kind * steps + index) * share
        target = grads_ref.at[:, pl.ds(start, share), :]
        return pltpu.make_async_copy(source, target, sems.at[kind, which])

    normed = normed_s[...]
    upstream = cot_ref[...]
    both = jnp.concatenate([gate_w[...], up_w[...]], 1)
    acts = dot(normed, both)
    gate_act, up_act = acts[:, :wide], acts[:, wide:]
    grad_hidden = dot(upstream, down_w[...], NT)
    sigmoid = jax.nn.sigmoid(gate_act)
    silu = gate_act * sigmoid
    hidden = (silu * up_act).astype(BF16)
    grad_gate = (grad_hidden * up_act * sigmoid * (1.0 + gate_act * (1.0 - sigmoid))).astype(BF16)
    grad_up = (grad_hidden * silu).astype(BF16)
    mixed_s[...] += dot(hidden, down_w[...])
    grad_acts = jnp.concatenate([grad_gate, grad_up], 1)
    upstream_s[...] += dot(grad_acts, both, NT)
    down_s[pl.ds(pl.multiple_of(step * wide, wide), wide), :] = dot(hidden, upstream, TN).astype(BF16)

    @pl.when(step >= 2)
    def _():
        copy_out(0, slot, step - 2).wait()
        copy_out(1, slot, step - 2).wait()

    weight_grads = dot(turned_s[...], grad_acts).astype(BF16)
    gate_s[slot] = weight_grads[:, :wide].reshape(span, share, wide)
    up_s[slot] = weight_grads[:, wide:].reshape(span, share, wide)
    copy_out(0, slot, step).start()
    copy_out(1, slot, step).start()

    @pl.when(step == steps - 1)
    def _():
        copies = []
        if merged:
            for place in range(span):
                for lane in range(lanes):
                    copies.append(
                        pltpu.make_async_copy(
                            down_s.at[pl.ds(place * tall, tall), pl.ds(lane * wide, wide)],
                            grads_ref.at[place, pl.ds(lane * tall, tall), :],
                            late_sems.at[len(copies)],
                        )
                    )
        else:
            copies.append(pltpu.make_async_copy(down_s, down_grads_ref, late_sems.at[0]))
        for copy in copies:
            copy.start()
        mixed_ref[...] = mixed_s[...].astype(BF16)
        middle = middle_s[...]
        grad = upstream_s[...]
        factor = lax.rsqrt(jnp.mean(middle * middle, -1, keepdims=True) + EPSILON)
        gain_grad_ref[...] = jnp.sum(grad * middle * factor, 0, keepdims=True)
        scaled = grad * gain_ref[...]
        inner = jnp.mean(scaled * middle, -1, keepdims=True)
        grad_middle = cot_ref[...].astype(F32) + factor * scaled - middle * (factor * factor * factor * inner)
        grad_mid_ref[...] = grad_middle
        branch = grad_middle.astype(BF16)
        grad_att_ref[...] = dot(branch, out_w[...], NT).astype(BF16)
        turned_att = jnp.transpose(att_ref[...])
        for lane in range(lanes):
            columns = slice(lane * wide, (lane + 1) * wide)
            out_s[lane] = dot(turned_att, branch[:, columns]).astype(BF16).reshape(span, share, wide)
            more = pltpu.make_async_copy(
                out_s.at[lane],
                grads_ref.at[:, pl.ds(first + lane * share, share), :],
                late_sems.at[len(copies)],
            )
            more.start()
            copies.append(more)
        for copy in copies:
            copy.wait()
        copy_out(0, 1 - slot, step - 1).wait()
        copy_out(1, 1 - slot, step - 1).wait()
        copy_out(0, slot, step).wait()
        copy_out(1, slot, step).wait()


def feed_forward(tokens, attended, upstream, gain, weights, w_down, span):
    rows, width = tokens.shape
    hidden_width = w_down.shape[0]
    wide = 2 * HEAD_DIM
    steps = hidden_width // wide
    lanes = width // wide
    share = width // span
    tall = hidden_width // span
    merged = tall % 16 == 0
    total = (lanes + 2 * steps) * share + (lanes * tall if merged else 0)
    shapes = [
        jax.ShapeDtypeStruct((rows, width), BF16),
        jax.ShapeDtypeStruct((rows, width), F32),
        jax.ShapeDtypeStruct((rows, width), BF16),
        jax.ShapeDtypeStruct((1, width), F32),
        jax.ShapeDtypeStruct((span, total, wide), BF16),
    ]
    specs = [
        pl.BlockSpec((rows, width), lambda i: (0, 0)),
        pl.BlockSpec((rows, width), lambda i: (0, 0)),
        pl.BlockSpec((rows, width), lambda i: (0, 0)),
        pl.BlockSpec((1, width), lambda i: (0, 0)),
        pl.BlockSpec(memory_space=pl.ANY),
    ]
    if not merged:
        shapes.append(jax.ShapeDtypeStruct((hidden_width, width), BF16))
        specs.append(pl.BlockSpec(memory_space=pl.ANY))
    return pl.pallas_call(
        functools.partial(ffn_kernel, span, merged),
        grid=(steps,),
        in_specs=[
            pl.BlockSpec((rows, width), lambda i: (0, 0)),
            pl.BlockSpec((rows, width), lambda i: (0, 0)),
            pl.BlockSpec((rows, width), lambda i: (0, 0)),
            pl.BlockSpec((1, width), lambda i: (0, 0)),
            pl.BlockSpec((width, width), lambda i: (0, 0)),
            pl.BlockSpec((width, wide), lambda i: (0, lanes + i)),
            pl.BlockSpec((width, wide), lambda i: (0, lanes + steps + i)),
            pl.BlockSpec((wide, width), lambda i: (i, 0)),
        ],
        out_specs=specs,
        out_shape=shapes,
        scratch_shapes=[
            pltpu.VMEM((rows, width), F32),
            pltpu.VMEM((rows, width), BF16),
            pltpu.VMEM((width, rows), BF16),
            pltpu.VMEM((rows, width), F32),
            pltpu.VMEM((rows, width), F32),
            pltpu.VMEM((2, span, share, wide), BF16),
            pltpu.VMEM((2, span, share, wide), BF16),
            pltpu.VMEM((hidden_width, width), BF16),
            pltpu.VMEM((lanes, span, share, wide), BF16),
            pltpu.SemaphoreType.DMA((2, 2)),
            pltpu.SemaphoreType.DMA(((span * lanes if merged else 1) + lanes,)),
        ],
        compiler_params=pltpu.CompilerParams(vmem_limit_bytes=56 * MIB),
        cost_estimate=pl.CostEstimate(
            flops=6 * rows * width * (3 * hidden_width + width),
            bytes_accessed=4 * width * (3 * hidden_width + width),
            transcendentals=rows * hidden_width,
        ),
        name="feed_forward",
    )(tokens, attended, upstream, gain, weights, weights, weights, w_down)


def projection_grads_kernel(tok_ref, gain_ref, w_ref, grad_ref, grad_w_ref, gain_grad_ref, raw_s):
    step = pl.program_id(0)

    @pl.when(step == 0)
    def _():
        raw_s[...] = jnp.zeros_like(raw_s)

    tokens = tok_ref[...].astype(F32)
    tokens = tokens * lax.rsqrt(jnp.mean(tokens * tokens, -1, keepdims=True) + EPSILON)
    raw_s[...] += dot(tokens.astype(BF16), grad_ref[...], TN)

    @pl.when(step == pl.num_programs(0) - 1)
    def _():
        raw = raw_s[...]
        gain_grad_ref[...] = jnp.sum(raw * w_ref[...].astype(F32), -1, keepdims=True)
        grad_w_ref[...] = (raw * gain_ref[...]).astype(BF16)


def projection_grads(tokens_all, gain_column, w_qkv, grad):
    length, width = tokens_all.shape
    columns = grad.shape[1]
    rows = min(2 * QBLK, length)
    return pl.pallas_call(
        projection_grads_kernel,
        grid=(length // rows,),
        in_specs=[
            pl.BlockSpec((rows, width), lambda i: (i, 0)),
            pl.BlockSpec((width, 1), lambda i: (0, 0)),
            pl.BlockSpec((width, columns), lambda i: (0, 0)),
            pl.BlockSpec((rows, columns), lambda i: (i, 0)),
        ],
        out_specs=[
            pl.BlockSpec((width, columns), lambda i: (0, 0)),
            pl.BlockSpec((width, 1), lambda i: (0, 0)),
        ],
        out_shape=[
            jax.ShapeDtypeStruct((width, columns), BF16),
            jax.ShapeDtypeStruct((width, 1), F32),
        ],
        scratch_shapes=[pltpu.VMEM((width, columns), F32)],
        compiler_params=pltpu.CompilerParams(vmem_limit_bytes=48 * MIB),
        cost_estimate=pl.CostEstimate(
            flops=2 * length * width * columns, bytes_accessed=2 * length * (width + columns), transcendentals=0
        ),
        name="projection_grads",
    )(tokens_all, gain_column, w_qkv, grad)


def after(value, earlier):
    return lax.optimization_barrier((value, earlier))[0]


def chain_gather(blocks, axis):
    size = lax.axis_size(axis)
    place = lax.axis_index(axis)
    steps = []
    rising = falling = tuple(blocks)
    for step in range(size - 1):
        up = [(i, i + 1) for i in range(step, size - 1)]
        down = [(i + 1, i) for i in range(size - 1 - step)]
        rising = tuple(lax.ppermute(block, axis, up) for block in rising)
        falling = tuple(lax.ppermute(block, axis, down) for block in falling)
        if len(blocks) > 1:
            rising, falling = lax.optimization_barrier((rising, falling))
        steps.append((rising, falling))
    results = []
    for number, block in enumerate(blocks):
        ordered = []
        for index in range(size):
            cases = []
            for mine in range(size):
                if mine == index:
                    cases.append(block)
                elif mine > index:
                    cases.append(steps[mine - index - 1][0][number])
                else:
                    cases.append(steps[index - mine - 1][1][number])
            ordered.append(lax.select_n(place, *cases) if size > 2 else lax.select_n(place > 0, *cases))
        results.append(ordered)
    return results, steps


def shift_gather(block, axis, meanwhile):
    size = lax.axis_size(axis)
    place = lax.axis_index(axis)
    taken = [block]
    for far in range(1, size):
        taken.append(lax.ppermute(block, axis, [(i, (i + far) % size) for i in range(size)]))
    taken = after(taken, meanwhile)
    ordered = []
    for index in range(size):
        cases = [taken[(mine - index) % size] for mine in range(size)]
        ordered.append(lax.select_n(place, *cases) if size > 2 else lax.select_n(place > 0, *cases))
    return ordered


def chain_scatter(partial, axis):
    size = lax.axis_size(axis)
    place = lax.axis_index(axis)
    rows = partial.shape[0] // size

    def block(index):
        return lax.dynamic_slice_in_dim(partial, jnp.clip(index, 0, size - 1) * rows, rows, 0).astype(F32)

    rising = falling = None
    steps = []
    for step in range(size - 1):
        up, down = block(size - 1 - step + place), block(step - size + 1 + place)
        if step:
            up, down = up + rising.astype(F32), down + falling.astype(F32)
        up, down = lax.optimization_barrier((up.astype(BF16), down.astype(BF16)))
        rising = lax.ppermute(up, axis, [(i, i + 1) for i in range(step + 1)])
        falling = lax.ppermute(down, axis, [(i, i - 1) for i in range(size - 1 - step, size)])
        rising, falling = lax.optimization_barrier((rising, falling))
        steps.append((rising, falling))
    return block(place), steps


def body(
    tokens, memory_keys, memory_values, chosen, counts, w_query, w_key, w_value, w_out, w_gate, w_up, w_down,
    gain_attn, gain_ffn, cotangent,
):
    ring, span = lax.axis_size("fsdp"), lax.axis_size(DP)
    rows, width = tokens.shape[1:]
    heads = width // HEAD_DIM // ring
    wide = heads * HEAD_DIM
    length = rows * ring
    top = chosen.shape[2]
    hidden_width = w_gate.shape[1]
    share = w_query.shape[0]
    mine = tokens[0]

    extra = 8 if share % 8 == 0 else 8 - share % 8
    parts = [w.reshape(share, ring, wide).transpose(1, 0, 2) for w in (w_query, w_key, w_value)]
    choices = jnp.concatenate([chosen[0].reshape(-1), counts[0].reshape(-1)]).astype(BF16)
    notes = jnp.stack(
        [
            jnp.pad(row, (0, 3 * wide - row.shape[0]))
            for row in (jnp.concatenate([gain_attn, gain_ffn]), choices)
        ]
    )
    notes = jnp.broadcast_to(jnp.pad(notes, ((0, extra - 2), (0, 0))), (ring, extra, 3 * wide))
    parcel = jnp.concatenate([jnp.concatenate(parts, 2), notes], 1)
    parcel = lax.all_to_all(parcel, "fsdp", 0, 0, tiled=True)
    picks = parcel[:, share + 1, : choices.shape[0]].astype(jnp.int32).reshape(ring, 2, -1)
    chosen_all, counts_all = picks[:, 0].reshape(-1), picks[:, 1].reshape(-1)
    shards = jnp.concatenate([w_out, w_gate, w_up], 1)
    (near,), steps = chain_gather((shards,), "fsdp")
    (gathered,), token_steps = chain_gather((after(mine, steps[-1]),), "fsdp")
    parcel = lax.all_gather(parcel, DP, axis=0, tiled=True)
    w_qkv = parcel[:, :share].reshape(width, 3 * wide)
    gain_one = parcel[:, share, :share].reshape(1, width).astype(F32)
    gain_two = parcel[:, share, share : 2 * share].reshape(1, width).astype(F32)
    first = lax.all_gather(after(jnp.concatenate(near, 0), parcel), DP, axis=0, tiled=True)
    gathered = jnp.concatenate(gathered, 0)

    memory = jnp.concatenate(
        [m[0].reshape(-1, ring, wide).transpose(1, 0, 2) for m in (memory_keys, memory_values)], 2
    )
    memory = lax.all_to_all(after(memory, token_steps[-2]), "fsdp", 0, 0, tiled=True).reshape(-1, 2 * wide)

    cosine, sine = rotary_tables(length)
    qkv = project_qkv(gathered, gain_one, w_qkv, cosine, sine, heads)
    near_down = jnp.concatenate(shift_gather(after(w_down, (token_steps[-1], memory)), "fsdp", qkv), 0)
    near_down = after(near_down, first)
    down_full = lax.all_gather(near_down, DP, axis=0, tiled=True)
    qkv = after(qkv, near_down)
    attended_heads, lse = attend_forward(chosen_all, counts_all, qkv, memory, heads, top)
    attended = lax.all_to_all(attended_heads, "fsdp", 0, 1, tiled=True)

    upstream = cotangent[0]
    mixed, grad_middle, grad_attended, gain_two_grad, grads, *grad_down = feed_forward(
        mine, attended, upstream, gain_two, first, down_full, span
    )
    grad_heads = lax.all_to_all(grad_attended, "fsdp", 1, 0, tiled=True)
    grads = lax.psum_scatter(grads, DP, scatter_dimension=0, tiled=True)[0]

    partial, grad_qkv = attend_backward(
        chosen_all, counts_all, qkv, memory, grad_heads, attended_heads, lse, cosine, sine, w_qkv, heads, top
    )
    own_term, steps = chain_scatter(partial, "fsdp")
    grad_w_qkv, gain_one_grad = projection_grads(gathered, gain_one.reshape(width, 1), w_qkv, grad_qkv)
    grads = after(grads, steps[-1])

    gains = jnp.stack([gain_one_grad.reshape(span, -1), gain_two_grad.reshape(span, -1)], 1)
    gains = jnp.pad(gains.astype(BF16), ((0, 0), (0, extra - 2), (0, 3 * wide - gains.shape[2])))
    late = jnp.concatenate([grad_w_qkv.reshape(span, -1, 3 * wide), gains], 1)
    late = late.reshape(span // 2, 2, late.shape[1], 3 * wide)
    core = lax.axis_index("core")
    taken = lax.ppermute(lax.dynamic_index_in_dim(late, 1 - core, 1, keepdims=False), "core", [(0, 1), (1, 0)])
    late = lax.dynamic_index_in_dim(late, core, 1, keepdims=False).astype(F32) + taken.astype(F32)
    late = after(late.astype(BF16), steps[0])
    late = jnp.sum(lax.all_to_all(late, "chip", 0, 0, tiled=True).astype(F32), 0).astype(BF16)
    gains = late[-extra : 2 - extra, : ring * share].reshape(2, ring, share).transpose(1, 0, 2)
    gains = jnp.pad(gains, ((0, 0), (0, extra - 2), (0, 3 * wide - share)))
    late = jnp.concatenate([late[:-extra].reshape(ring, share, 3 * wide), gains], 1)
    late = lax.all_to_all(late, "fsdp", 0, 0, tiled=True).astype(F32)
    projections = [
        late[:, :share, part * wide : (part + 1) * wide].transpose(1, 0, 2).reshape(share, width)
        for part in range(3)
    ]
    gain_shares = jnp.sum(late[:, share : share + 2, :share], 0)

    strip = grads.shape[1]
    lanes = width // strip
    tall = w_down.shape[0]
    if grad_down:
        down = lax.psum_scatter(grad_down[0], DP, scatter_dimension=0, tiled=True)
        down = down.reshape(ring, tall, lanes, strip).transpose(0, 2, 1, 3)
    else:
        down = grads[: ring * tall * lanes].reshape(lanes, ring, tall, strip).transpose(1, 0, 2, 3)
        grads = grads[ring * tall * lanes :]
    grads = grads.reshape(-1, ring, share, strip).transpose(1, 0, 2, 3)
    pieces = jnp.concatenate([down.reshape(ring, -1, strip), grads.reshape(ring, -1, strip)], 1)
    rising, falling = steps[-1]
    grad_normed = own_term + rising.astype(F32) + falling.astype(F32)
    own = mine.astype(F32)
    factor = lax.rsqrt(jnp.mean(own * own, -1, keepdims=True) + EPSILON)
    scaled = grad_normed * gain_one
    inner = jnp.mean(scaled * own, -1, keepdims=True)
    tokens_grad = (grad_middle + factor * scaled - own * (factor * factor * factor * inner)).astype(BF16)

    pieces = lax.psum_scatter(pieces, "fsdp", scatter_dimension=0, tiled=True)
    pieces = after(pieces, (tokens_grad, projections, gain_shares))[0].astype(F32)
    down_share = pieces[: lanes * tall].reshape(lanes, tall, strip).transpose(1, 0, 2).reshape(tall, width)
    others = pieces[lanes * tall :].reshape(-1, share, strip).transpose(1, 0, 2).reshape(share, -1)
    return (
        mixed[None],
        tokens_grad[None],
        *projections,
        others[:, :width],
        others[:, width : width + hidden_width],
        others[:, width + hidden_width :],
        down_share,
        gain_shares[0],
        gain_shares[1],
    )


def solution(mesh):
    span, ring = mesh.shape["dp"], mesh.shape["fsdp"]
    fine = Mesh(mesh.devices.reshape(span // 2, 2, ring), DP + ("fsdp",))
    every = DP + ("fsdp",)
    rows, matrix, vector = P(DP, "fsdp", None), P(every, None), P(every)
    in_specs = (rows,) * 5 + (matrix,) * 7 + (vector,) * 2 + (rows,)
    out_specs = (rows,) * 2 + (matrix,) * 7 + (vector,) * 2
    return jax.shard_map(body, mesh=fine, in_specs=in_specs, out_specs=out_specs, check_vma=False)
```

```python
import functools
import math

import jax
import jax.numpy as jnp
import numpy as np
from jax import lax
from jax.experimental import pallas as pl
from jax.experimental.pallas import tpu as pltpu
from jax.sharding import Mesh
from jax.sharding import PartitionSpec as P

HEAD_DIM = 128
QBLK = 256
MBLK = 128
EPSILON = 1e-06
NEGATIVE = -1e30
SCALE = 1.0 / math.sqrt(HEAD_DIM)
LOG2E = math.log2(math.e)
MIB = 1 << 20
F32 = jnp.float32
BF16 = jnp.bfloat16
DP = ("chip", "core")
NT = (((1,), (1,)), ((), ()))
TN = (((0,), (0,)), ((), ()))


def dot(left, right, dims=(((1,), (0,)), ((), ()))):
    return lax.dot_general(left, right, dims, preferred_element_type=F32)


def rotary_tables(length):
    half_dim = HEAD_DIM // 2
    frequency = 10000.0 ** (-jnp.arange(half_dim, dtype=F32) / half_dim)
    angles = jnp.arange(length, dtype=jnp.int32).astype(F32)[:, None] * frequency[None, :]
    cosine, sine = jnp.cos(angles), jnp.sin(angles)
    return jnp.concatenate([cosine, cosine], 1), jnp.concatenate([-sine, sine], 1)


def qkv_kernel(heads, tok_ref, gain_ref, w_ref, cos_ref, sin_ref, qkv_ref):
    rows = tok_ref[...].astype(F32)
    factor = lax.rsqrt(jnp.mean(rows * rows, -1, keepdims=True) + EPSILON)
    normed = (rows * factor * gain_ref[...]).astype(BF16)
    cosine, sine = cos_ref[...], sin_ref[...]
    wide = heads * HEAD_DIM
    for part in range(3):
        values = dot(normed, w_ref[:, part * wide : (part + 1) * wide])
        for head in range(heads):
            value = values[:, head * HEAD_DIM : (head + 1) * HEAD_DIM]
            if part < 2:
                value = value * cosine + pltpu.roll(value, HEAD_DIM // 2, 1) * sine
            if part == 0:
                value = value * (SCALE * LOG2E)
            at = part * wide + head * HEAD_DIM
            qkv_ref[:, at : at + HEAD_DIM] = value.astype(BF16)


def project_qkv(tokens_all, gain, w_qkv, cosine, sine, heads):
    length, width = tokens_all.shape
    columns = w_qkv.shape[1]
    block = 2 * QBLK
    return pl.pallas_call(
        functools.partial(qkv_kernel, heads),
        grid=(length // block,),
        in_specs=[
            pl.BlockSpec((block, width), lambda i: (i, 0)),
            pl.BlockSpec((1, width), lambda i: (0, 0)),
            pl.BlockSpec((width, columns), lambda i: (0, 0)),
            pl.BlockSpec((block, HEAD_DIM), lambda i: (i, 0)),
            pl.BlockSpec((block, HEAD_DIM), lambda i: (i, 0)),
        ],
        out_specs=pl.BlockSpec((block, columns), lambda i: (i, 0)),
        out_shape=jax.ShapeDtypeStruct((length, columns), BF16),
        compiler_params=pltpu.CompilerParams(vmem_limit_bytes=48 * MIB),
        cost_estimate=pl.CostEstimate(
            flops=2 * length * width * columns, bytes_accessed=4 * length * (width + columns), transcendentals=0
        ),
        name="project_qkv",
    )(tokens_all, gain, w_qkv, cosine, sine)


def memory_bias(counts_ref, base, top, axis):
    shape = (1, top * MBLK) if axis == 1 else (top * MBLK, 1)
    column = lax.broadcasted_iota(jnp.int32, shape, axis)
    limit = jnp.zeros(shape, jnp.int32)
    for entry in range(top):
        inside = (column >= entry * MBLK) & (column < entry * MBLK + counts_ref[base + entry])
        limit = jnp.where(inside, 1, limit)
    return jnp.where(limit > 0, 0.0, NEGATIVE)


def pick_memory(ref, chosen_ref, base, top, columns):
    rows = [
        ref[pl.ds(pl.multiple_of(chosen_ref[base + entry] * MBLK, MBLK), MBLK), columns]
        for entry in range(top)
    ]
    return jnp.concatenate(rows, 0)


def local_kernel(heads, q_ref, k_ref, v_ref, out_ref, lse_ref, acc_s, peak_s):
    block = pl.program_id(0)
    rows = q_ref.shape[0]
    own = pl.ds(pl.multiple_of(block * rows, rows), rows)
    causal = lax.broadcasted_iota(jnp.int32, (rows, rows), 0) >= lax.broadcasted_iota(jnp.int32, (rows, rows), 1)
    ones = jnp.ones((rows, HEAD_DIM), BF16)
    for head in range(heads):
        columns = slice(head * HEAD_DIM, (head + 1) * HEAD_DIM)
        scores = jnp.where(causal, dot(q_ref[:, columns], k_ref[own, columns], NT), NEGATIVE)
        peak = jnp.max(scores, -1, keepdims=True)
        values = jnp.concatenate([v_ref[own, columns], ones], 1)
        acc_s[head] = dot(jnp.exp2(scores - peak).astype(BF16), values)
        peak_s[head] = jnp.broadcast_to(peak, (rows, HEAD_DIM))

    def step(index, carry):
        there = pl.ds(pl.multiple_of(index * rows, rows), rows)
        for head in range(heads):
            columns = slice(head * HEAD_DIM, (head + 1) * HEAD_DIM)
            peak = peak_s[head][:, :1]
            scores = dot(q_ref[:, columns], k_ref[there, columns], NT)
            higher = jnp.maximum(peak, jnp.max(scores, -1, keepdims=True))
            weights = jnp.exp2(scores - higher).astype(BF16)
            values = jnp.concatenate([v_ref[there, columns], ones], 1)
            acc_s[head] = acc_s[head] * jnp.exp2(peak - higher) + dot(weights, values)
            peak_s[head] = jnp.broadcast_to(higher, (rows, HEAD_DIM))
        return carry

    lax.fori_loop(0, block, step, 0)
    for head in range(heads):
        columns = slice(head * HEAD_DIM, (head + 1) * HEAD_DIM)
        total = acc_s[head][:, HEAD_DIM:]
        out_ref[:, columns] = acc_s[head][:, :HEAD_DIM] / total
        lse_ref[:, head : head + 1] = peak_s[head][:, :1] + jnp.log2(total[:, :1])


def attend_local(qkv, heads):
    length = qkv.shape[0]
    wide = heads * HEAD_DIM
    rows = min(2 * QBLK, length)
    return pl.pallas_call(
        functools.partial(local_kernel, heads),
        grid=(length // rows,),
        in_specs=[
            pl.BlockSpec((rows, wide), lambda i: (i, 0)),
            pl.BlockSpec((length, wide), lambda i: (0, 1)),
            pl.BlockSpec((length, wide), lambda i: (0, 2)),
        ],
        out_specs=[
            pl.BlockSpec((rows, wide), lambda i: (i, 0)),
            pl.BlockSpec((rows, heads), lambda i: (i, 0)),
        ],
        out_shape=[
            jax.ShapeDtypeStruct((length, wide), F32),
            jax.ShapeDtypeStruct((length, heads), F32),
        ],
        scratch_shapes=[
            pltpu.VMEM((heads, rows, 2 * HEAD_DIM), F32),
            pltpu.VMEM((heads, rows, HEAD_DIM), F32),
        ],
        compiler_params=pltpu.CompilerParams(vmem_limit_bytes=48 * MIB),
        cost_estimate=pl.CostEstimate(
            flops=2 * heads * length * HEAD_DIM * length,
            bytes_accessed=8 * length * wide,
            transcendentals=heads * length * length // 2,
        ),
        name="attend_local",
    )(qkv, qkv, qkv)


def memory_kernel(
    heads, top, chosen_ref, counts_ref, q_ref, mk_ref, mv_ref, local_ref, local_lse_ref, out_ref, lse_ref
):
    block = pl.program_id(0)
    subs = q_ref.shape[0] // QBLK
    ones = jnp.ones((top * MBLK, HEAD_DIM), BF16)
    for sub in range(subs):
        base = (block * subs + sub) * top
        rows = slice(sub * QBLK, (sub + 1) * QBLK)
        bias = memory_bias(counts_ref, base, top, 1)
        for head in range(heads):
            columns = slice(head * HEAD_DIM, (head + 1) * HEAD_DIM)
            keys = pick_memory(mk_ref, chosen_ref, base, top, columns)
            values = pick_memory(mv_ref, chosen_ref, base, top, columns)
            scores = dot(q_ref[rows, columns], keys, NT) + bias
            local_lse = local_lse_ref[rows, head : head + 1]
            peak = jnp.maximum(jnp.max(scores, -1, keepdims=True), local_lse)
            acc = dot(jnp.exp2(scores - peak).astype(BF16), jnp.concatenate([values, ones], 1))
            local = jnp.exp2(local_lse - peak)
            total = acc[:, HEAD_DIM:] + local
            out_ref[rows, columns] = ((acc[:, :HEAD_DIM] + local_ref[rows, columns] * local) / total).astype(BF16)
            lse_ref[rows, head : head + 1] = peak + jnp.log2(total[:, :1])


def attend_memory(chosen, counts, qkv, memory, local, local_lse, heads, top):
    length = qkv.shape[0]
    wide = heads * HEAD_DIM
    rows = min(2 * QBLK, length)
    mem_rows = memory.shape[0]
    by_rows = pl.BlockSpec((rows, wide), lambda i, *_: (i, 0))
    stats = pl.BlockSpec((rows, heads), lambda i, *_: (i, 0))
    return pl.pallas_call(
        functools.partial(memory_kernel, heads, top),
        grid_spec=pltpu.PrefetchScalarGridSpec(
            num_scalar_prefetch=2,
            grid=(length // rows,),
            in_specs=[
                by_rows,
                pl.BlockSpec((mem_rows, wide), lambda i, *_: (0, 0)),
                pl.BlockSpec((mem_rows, wide), lambda i, *_: (0, 1)),
                by_rows,
                stats,
            ],
            out_specs=[by_rows, stats],
        ),
        out_shape=[
            jax.ShapeDtypeStruct((length, wide), BF16),
            jax.ShapeDtypeStruct((length, heads), F32),
        ],
        compiler_params=pltpu.CompilerParams(vmem_limit_bytes=48 * MIB),
        cost_estimate=pl.CostEstimate(
            flops=4 * heads * length * HEAD_DIM * top * MBLK,
            bytes_accessed=8 * length * wide,
            transcendentals=heads * length * top * MBLK,
        ),
        name="attend_memory",
    )(chosen, counts, qkv, memory, memory, local, local_lse)


def backward_kernel(
    heads, top, chosen_ref, counts_ref, q_ref, k_ref, v_ref, mk_ref, mv_ref, go_ref, out_ref, lse_ref,
    cos_ref, sin_ref, w_ref, partial_ref, grad_ref, gk_s, gv_s, gq_s,
):
    block = pl.num_programs(0) - 1 - pl.program_id(0)
    rows = q_ref.shape[0]
    subs = rows // QBLK
    wide = heads * HEAD_DIM
    own = pl.ds(pl.multiple_of(block * rows, rows), rows)
    key_at = lax.broadcasted_iota(jnp.int32, (rows, rows), 0)
    query_at = lax.broadcasted_iota(jnp.int32, (rows, rows), 1)
    causal = query_at >= key_at

    @pl.when(pl.program_id(0) == 0)
    def _():
        gk_s[...] = jnp.zeros_like(gk_s)
        gv_s[...] = jnp.zeros_like(gv_s)

    def spread(column):
        return jnp.transpose(jnp.broadcast_to(column, (rows, HEAD_DIM)))[:1]

    stats = []
    for head in range(heads):
        columns = slice(head * HEAD_DIM, (head + 1) * HEAD_DIM)
        delta = jnp.sum(go_ref[:, columns].astype(F32) * out_ref[:, columns].astype(F32), -1, keepdims=True)
        stats.append((spread(lse_ref[:, head : head + 1]), spread(delta)))

    def pair(head, queries, keys, values, mask):
        columns = slice(head * HEAD_DIM, (head + 1) * HEAD_DIM)
        lse, delta = stats[head]
        scores = mask(dot(keys, q_ref[queries, columns], NT))
        weights = jnp.exp2(scores - lse[:, queries])
        grad_weights = dot(values, go_ref[queries, columns], NT)
        return weights.astype(BF16), (weights * (grad_weights - delta[:, queries])).astype(BF16)

    every = slice(0, rows)
    for head in range(heads):
        columns = slice(head * HEAD_DIM, (head + 1) * HEAD_DIM)
        for sub in range(subs):
            base = (block * subs + sub) * top
            queries = slice(sub * QBLK, (sub + 1) * QBLK)
            keys = pick_memory(mk_ref, chosen_ref, base, top, columns)
            values = pick_memory(mv_ref, chosen_ref, base, top, columns)
            bias = memory_bias(counts_ref, base, top, 0)
            _, grad_scores = pair(head, queries, keys, values, lambda scores: scores + bias)
            gq_s[queries, columns] = dot(grad_scores, keys, TN)

    def local(head, there, mask):
        columns = slice(head * HEAD_DIM, (head + 1) * HEAD_DIM)
        keys = k_ref[there, columns]
        weights, grad_scores = pair(head, every, keys, v_ref[there, columns], mask)
        gk_s[there, columns] += dot(grad_scores, q_ref[:, columns])
        gv_s[there, columns] += dot(weights, go_ref[:, columns])
        gq_s[:, columns] += dot(grad_scores, keys, TN)

    for head in range(heads):
        local(head, own, lambda scores: jnp.where(causal, scores, NEGATIVE))

    def step(index, carry):
        for head in range(heads):
            local(head, pl.ds(pl.multiple_of(index * rows, rows), rows), lambda scores: scores)
        return carry

    lax.fori_loop(0, block, step, 0)
    cosine, sine = cos_ref[...], sin_ref[...]

    def unturn(value):
        return value * cosine - pltpu.roll(value, HEAD_DIM // 2, 1) * sine

    for head in range(heads):
        columns = slice(head * HEAD_DIM, (head + 1) * HEAD_DIM)
        at = head * HEAD_DIM
        grad_ref[:, at : at + HEAD_DIM] = unturn(gq_s[:, columns] * SCALE).astype(BF16)
        grad_key = gk_s[own, columns] * (1.0 / LOG2E)
        grad_ref[:, wide + at : wide + at + HEAD_DIM] = unturn(grad_key).astype(BF16)
        grad_ref[:, 2 * wide + at : 2 * wide + at + HEAD_DIM] = gv_s[own, columns].astype(BF16)

    partial_ref[...] = dot(grad_ref[...], w_ref[...], NT).astype(BF16)


def attend_backward(chosen, counts, qkv, memory, grad_out, out, lse, cosine, sine, w_qkv, heads, top):
    length = qkv.shape[0]
    width = w_qkv.shape[0]
    wide = heads * HEAD_DIM
    rows = min(2 * QBLK, length)
    mem_rows = memory.shape[0]
    last = length // rows - 1
    return pl.pallas_call(
        functools.partial(backward_kernel, heads, top),
        grid_spec=pltpu.PrefetchScalarGridSpec(
            num_scalar_prefetch=2,
            grid=(last + 1,),
            in_specs=[
                pl.BlockSpec((rows, wide), lambda i, *_: (last - i, 0)),
                pl.BlockSpec((length, wide), lambda i, *_: (0, 1)),
                pl.BlockSpec((length, wide), lambda i, *_: (0, 2)),
                pl.BlockSpec((mem_rows, wide), lambda i, *_: (0, 0)),
                pl.BlockSpec((mem_rows, wide), lambda i, *_: (0, 1)),
                pl.BlockSpec((rows, wide), lambda i, *_: (last - i, 0)),
                pl.BlockSpec((rows, wide), lambda i, *_: (last - i, 0)),
                pl.BlockSpec((rows, heads), lambda i, *_: (last - i, 0)),
                pl.BlockSpec((rows, HEAD_DIM), lambda i, *_: (last - i, 0)),
                pl.BlockSpec((rows, HEAD_DIM), lambda i, *_: (last - i, 0)),
                pl.BlockSpec((width, 3 * wide), lambda i, *_: (0, 0)),
            ],
            out_specs=[
                pl.BlockSpec((rows, width), lambda i, *_: (last - i, 0)),
                pl.BlockSpec((rows, 3 * wide), lambda i, *_: (last - i, 0)),
            ],
            scratch_shapes=[
                pltpu.VMEM((length, wide), F32),
                pltpu.VMEM((length, wide), F32),
                pltpu.VMEM((rows, wide), F32),
            ],
        ),
        out_shape=[
            jax.ShapeDtypeStruct((length, width), BF16),
            jax.ShapeDtypeStruct((length, 3 * wide), BF16),
        ],
        compiler_params=pltpu.CompilerParams(vmem_limit_bytes=48 * MIB),
        cost_estimate=pl.CostEstimate(
            flops=10 * heads * length * HEAD_DIM * (length // 2 + top * MBLK),
            bytes_accessed=16 * length * wide,
            transcendentals=heads * length * (length // 2 + top * MBLK),
        ),
        name="attend_backward",
    )(
        chosen, counts, qkv, qkv, qkv, memory, memory, grad_out, out, lse, cosine, sine, w_qkv
    )


def ffn_kernel(
    span, merged, tok_ref, att_ref, cot_ref, gain_ref, out_w, gate_w, up_w, down_w,
    mixed_ref, grad_mid_ref, grad_att_ref, gain_grad_ref, grads_ref, *rest,
):
    if not merged:
        down_grads_ref, rest = rest[0], rest[1:]
    middle_s, normed_s, turned_s, mixed_s, upstream_s, gate_s, up_s, down_s, out_s, sems, late_sems = rest
    step, steps = pl.program_id(0), pl.num_programs(0)
    width = tok_ref.shape[1]
    share = width // span
    wide = gate_w.shape[1]
    hidden_width = down_s.shape[0]
    tall = hidden_width // span
    lanes = width // wide
    first = tall * lanes if merged else 0
    slot = step % 2

    @pl.when(step == 0)
    def _():
        middle = tok_ref[...].astype(F32) + dot(att_ref[...], out_w[...])
        middle_s[...] = middle
        factor = lax.rsqrt(jnp.mean(middle * middle, -1, keepdims=True) + EPSILON)
        normed = (middle * factor * gain_ref[...]).astype(BF16)
        normed_s[...] = normed
        turned_s[...] = jnp.transpose(normed)
        mixed_s[...] = middle
        upstream_s[...] = jnp.zeros_like(upstream_s)

    def copy_out(kind, which, index):
        source = (gate_s, up_s)[kind].at[which]
        start = first + (lanes + kind * steps + index) * share
        target = grads_ref.at[:, pl.ds(start, share), :]
        return pltpu.make_async_copy(source, target, sems.at[kind, which])

    normed = normed_s[...]
    upstream = cot_ref[...]
    both = jnp.concatenate([gate_w[...], up_w[...]], 1)
    acts = dot(normed, both)
    gate_act, up_act = acts[:, :wide], acts[:, wide:]
    grad_hidden = dot(upstream, down_w[...], NT)
    sigmoid = jax.nn.sigmoid(gate_act)
    silu = gate_act * sigmoid
    hidden = (silu * up_act).astype(BF16)
    grad_gate = (grad_hidden * up_act * sigmoid * (1.0 + gate_act * (1.0 - sigmoid))).astype(BF16)
    grad_up = (grad_hidden * silu).astype(BF16)
    mixed_s[...] += dot(hidden, down_w[...])
    grad_acts = jnp.concatenate([grad_gate, grad_up], 1)
    upstream_s[...] += dot(grad_acts, both, NT)
    down_s[pl.ds(pl.multiple_of(step * wide, wide), wide), :] = dot(hidden, upstream, TN).astype(BF16)

    @pl.when(step >= 2)
    def _():
        copy_out(0, slot, step - 2).wait()
        copy_out(1, slot, step - 2).wait()

    weight_grads = dot(turned_s[...], grad_acts).astype(BF16)
    gate_s[slot] = weight_grads[:, :wide].reshape(span, share, wide)
    up_s[slot] = weight_grads[:, wide:].reshape(span, share, wide)
    copy_out(0, slot, step).start()
    copy_out(1, slot, step).start()

    @pl.when(step == steps - 1)
    def _():
        copies = []
        if merged:
            for place in range(span):
                for lane in range(lanes):
                    copies.append(
                        pltpu.make_async_copy(
                            down_s.at[pl.ds(place * tall, tall), pl.ds(lane * wide, wide)],
                            grads_ref.at[place, pl.ds(lane * tall, tall), :],
                            late_sems.at[len(copies)],
                        )
                    )
        else:
            copies.append(pltpu.make_async_copy(down_s, down_grads_ref, late_sems.at[0]))
        for copy in copies:
            copy.start()
        mixed_ref[...] = mixed_s[...].astype(BF16)
        middle = middle_s[...]
        grad = upstream_s[...]
        factor = lax.rsqrt(jnp.mean(middle * middle, -1, keepdims=True) + EPSILON)
        gain_grad_ref[...] = jnp.sum(grad * middle * factor, 0, keepdims=True)
        scaled = grad * gain_ref[...]
        inner = jnp.mean(scaled * middle, -1, keepdims=True)
        grad_middle = cot_ref[...].astype(F32) + factor * scaled - middle * (factor * factor * factor * inner)
        grad_mid_ref[...] = grad_middle
        branch = grad_middle.astype(BF16)
        grad_att_ref[...] = dot(branch, out_w[...], NT).astype(BF16)
        turned_att = jnp.transpose(att_ref[...])
        for lane in range(lanes):
            columns = slice(lane * wide, (lane + 1) * wide)
            out_s[lane] = dot(turned_att, branch[:, columns]).astype(BF16).reshape(span, share, wide)
            more = pltpu.make_async_copy(
                out_s.at[lane],
                grads_ref.at[:, pl.ds(first + lane * share, share), :],
                late_sems.at[len(copies)],
            )
            more.start()
            copies.append(more)
        for copy in copies:
            copy.wait()
        copy_out(0, 1 - slot, step - 1).wait()
        copy_out(1, 1 - slot, step - 1).wait()
        copy_out(0, slot, step).wait()
        copy_out(1, slot, step).wait()


def feed_forward(tokens, attended, upstream, gain, weights, w_down, span):
    rows, width = tokens.shape
    hidden_width = w_down.shape[0]
    wide = 2 * HEAD_DIM
    steps = hidden_width // wide
    lanes = width // wide
    share = width // span
    tall = hidden_width // span
    merged = tall % 16 == 0
    total = (lanes + 2 * steps) * share + (lanes * tall if merged else 0)
    shapes = [
        jax.ShapeDtypeStruct((rows, width), BF16),
        jax.ShapeDtypeStruct((rows, width), F32),
        jax.ShapeDtypeStruct((rows, width), BF16),
        jax.ShapeDtypeStruct((1, width), F32),
        jax.ShapeDtypeStruct((span, total, wide), BF16),
    ]
    specs = [
        pl.BlockSpec((rows, width), lambda i: (0, 0)),
        pl.BlockSpec((rows, width), lambda i: (0, 0)),
        pl.BlockSpec((rows, width), lambda i: (0, 0)),
        pl.BlockSpec((1, width), lambda i: (0, 0)),
        pl.BlockSpec(memory_space=pl.ANY),
    ]
    if not merged:
        shapes.append(jax.ShapeDtypeStruct((hidden_width, width), BF16))
        specs.append(pl.BlockSpec(memory_space=pl.ANY))
    return pl.pallas_call(
        functools.partial(ffn_kernel, span, merged),
        grid=(steps,),
        in_specs=[
            pl.BlockSpec((rows, width), lambda i: (0, 0)),
            pl.BlockSpec((rows, width), lambda i: (0, 0)),
            pl.BlockSpec((rows, width), lambda i: (0, 0)),
            pl.BlockSpec((1, width), lambda i: (0, 0)),
            pl.BlockSpec((width, width), lambda i: (0, 0)),
            pl.BlockSpec((width, wide), lambda i: (0, lanes + i)),
            pl.BlockSpec((width, wide), lambda i: (0, lanes + steps + i)),
            pl.BlockSpec((wide, width), lambda i: (i, 0)),
        ],
        out_specs=specs,
        out_shape=shapes,
        scratch_shapes=[
            pltpu.VMEM((rows, width), F32),
            pltpu.VMEM((rows, width), BF16),
            pltpu.VMEM((width, rows), BF16),
            pltpu.VMEM((rows, width), F32),
            pltpu.VMEM((rows, width), F32),
            pltpu.VMEM((2, span, share, wide), BF16),
            pltpu.VMEM((2, span, share, wide), BF16),
            pltpu.VMEM((hidden_width, width), BF16),
            pltpu.VMEM((lanes, span, share, wide), BF16),
            pltpu.SemaphoreType.DMA((2, 2)),
            pltpu.SemaphoreType.DMA(((span * lanes if merged else 1) + lanes,)),
        ],
        compiler_params=pltpu.CompilerParams(vmem_limit_bytes=56 * MIB),
        cost_estimate=pl.CostEstimate(
            flops=6 * rows * width * (3 * hidden_width + width),
            bytes_accessed=4 * width * (3 * hidden_width + width),
            transcendentals=rows * hidden_width,
        ),
        name="feed_forward",
    )(tokens, attended, upstream, gain, weights, weights, weights, w_down)


def projection_grads_kernel(tok_ref, gain_ref, w_ref, grad_ref, grad_w_ref, gain_grad_ref, raw_s):
    step = pl.program_id(0)

    @pl.when(step == 0)
    def _():
        raw_s[...] = jnp.zeros_like(raw_s)

    tokens = tok_ref[...].astype(F32)
    tokens = tokens * lax.rsqrt(jnp.mean(tokens * tokens, -1, keepdims=True) + EPSILON)
    raw_s[...] += dot(tokens.astype(BF16), grad_ref[...], TN)

    @pl.when(step == pl.num_programs(0) - 1)
    def _():
        raw = raw_s[...]
        gain_grad_ref[...] = jnp.sum(raw * w_ref[...].astype(F32), -1, keepdims=True)
        grad_w_ref[...] = (raw * gain_ref[...]).astype(BF16)


def projection_grads(tokens_all, gain_column, w_qkv, grad):
    length, width = tokens_all.shape
    columns = grad.shape[1]
    rows = min(2 * QBLK, length)
    return pl.pallas_call(
        projection_grads_kernel,
        grid=(length // rows,),
        in_specs=[
            pl.BlockSpec((rows, width), lambda i: (i, 0)),
            pl.BlockSpec((width, 1), lambda i: (0, 0)),
            pl.BlockSpec((width, columns), lambda i: (0, 0)),
            pl.BlockSpec((rows, columns), lambda i: (i, 0)),
        ],
        out_specs=[
            pl.BlockSpec((width, columns), lambda i: (0, 0)),
            pl.BlockSpec((width, 1), lambda i: (0, 0)),
        ],
        out_shape=[
            jax.ShapeDtypeStruct((width, columns), BF16),
            jax.ShapeDtypeStruct((width, 1), F32),
        ],
        scratch_shapes=[pltpu.VMEM((width, columns), F32)],
        compiler_params=pltpu.CompilerParams(vmem_limit_bytes=48 * MIB),
        cost_estimate=pl.CostEstimate(
            flops=2 * length * width * columns, bytes_accessed=2 * length * (width + columns), transcendentals=0
        ),
        name="projection_grads",
    )(tokens_all, gain_column, w_qkv, grad)


def after(value, earlier):
    return lax.optimization_barrier((value, earlier))[0]


def chain_gather(blocks, axis):
    size = lax.axis_size(axis)
    place = lax.axis_index(axis)
    steps = []
    rising = falling = tuple(blocks)
    for step in range(size - 1):
        up = [(i, i + 1) for i in range(step, size - 1)]
        down = [(i + 1, i) for i in range(size - 1 - step)]
        rising = tuple(lax.ppermute(block, axis, up) for block in rising)
        falling = tuple(lax.ppermute(block, axis, down) for block in falling)
        if len(blocks) > 1:
            rising, falling = lax.optimization_barrier((rising, falling))
        steps.append((rising, falling))
    results = []
    for number, block in enumerate(blocks):
        ordered = []
        for index in range(size):
            cases = []
            for mine in range(size):
                if mine == index:
                    cases.append(block)
                elif mine > index:
                    cases.append(steps[mine - index - 1][0][number])
                else:
                    cases.append(steps[index - mine - 1][1][number])
            ordered.append(lax.select_n(place, *cases) if size > 2 else lax.select_n(place > 0, *cases))
        results.append(ordered)
    return results, steps


def chain_scatter(partial, axis):
    size = lax.axis_size(axis)
    place = lax.axis_index(axis)
    rows = partial.shape[0] // size

    def block(index):
        return lax.dynamic_slice_in_dim(partial, jnp.clip(index, 0, size - 1) * rows, rows, 0).astype(F32)

    arrived = []
    for step in range(size - 1):
        up, down = block(size - 1 - step + place), block(step - size + 1 + place)
        if step:
            up, down = up + arrived[-1][0].astype(F32), down + arrived[-1][1].astype(F32)
        up, down = lax.optimization_barrier((up.astype(BF16), down.astype(BF16)))
        rising = lax.ppermute(up, axis, [(i, i + 1) for i in range(step + 1)])
        falling = lax.ppermute(down, axis, [(i, i - 1) for i in range(size - 1 - step, size)])
        arrived.append(lax.optimization_barrier((rising, falling)))
    return block(place), arrived


def direct_exchange(blocks, axis):
    size = lax.axis_size(axis)
    place = lax.axis_index(axis)
    taken = [lax.dynamic_index_in_dim(blocks, place, 0, keepdims=False)]
    for far in range(1, size):
        give = lax.dynamic_index_in_dim(blocks, (place + far) % size, 0, keepdims=False)
        taken.append(lax.ppermute(give, axis, [(i, (i + far) % size) for i in range(size)]))
    return taken


def body(
    tokens, memory_keys, memory_values, chosen, counts, w_query, w_key, w_value, w_out, w_gate, w_up, w_down,
    gain_attn, gain_ffn, cotangent,
):
    ring, span = lax.axis_size("fsdp"), lax.axis_size(DP)
    rows, width = tokens.shape[1:]
    heads = width // HEAD_DIM // ring
    wide = heads * HEAD_DIM
    length = rows * ring
    top = chosen.shape[2]
    hidden_width = w_gate.shape[1]
    share = w_query.shape[0]
    mine = tokens[0]

    extra = 8 if share % 8 == 0 else 8 - share % 8
    parts = [w.reshape(share, ring, wide).transpose(1, 0, 2) for w in (w_query, w_key, w_value)]
    choices = jnp.concatenate([chosen[0].reshape(-1), counts[0].reshape(-1)]).astype(BF16)
    notes = jnp.stack(
        [
            jnp.pad(row, (0, 3 * wide - row.shape[0]))
            for row in (jnp.concatenate([gain_attn, gain_ffn]), choices)
        ]
    )
    notes = jnp.broadcast_to(jnp.pad(notes, ((0, extra - 2), (0, 0))), (ring, extra, 3 * wide))
    parcel = jnp.concatenate([jnp.concatenate(parts, 2), notes], 1)
    parcel = lax.all_to_all(parcel, "fsdp", 0, 0, tiled=True)
    picks = parcel[:, share + 1, : choices.shape[0]].astype(jnp.int32).reshape(ring, 2, -1)
    chosen_all, counts_all = picks[:, 0].reshape(-1), picks[:, 1].reshape(-1)
    shards = jnp.concatenate([w_out, w_gate, w_up], 1)
    (near, near_down), steps = chain_gather((shards, w_down), "fsdp")
    (gathered,), token_steps = chain_gather((after(mine, steps[-2]),), "fsdp")
    parcel = lax.all_gather(parcel, DP, axis=0, tiled=True)
    w_qkv = parcel[:, :share].reshape(width, 3 * wide)
    gain_one = parcel[:, share, :share].reshape(1, width).astype(F32)
    gain_two = parcel[:, share, share : 2 * share].reshape(1, width).astype(F32)
    first = lax.all_gather(jnp.concatenate(near, 0), DP, axis=0, tiled=True)
    gathered = jnp.concatenate(gathered, 0)

    memory = jnp.concatenate(
        [m[0].reshape(-1, ring, wide).transpose(1, 0, 2) for m in (memory_keys, memory_values)], 2
    )
    memory = lax.all_to_all(after(memory, token_steps[-1]), "fsdp", 0, 0, tiled=True).reshape(-1, 2 * wide)
    down_full = lax.all_gather(jnp.concatenate(near_down, 0), DP, axis=0, tiled=True)

    cosine, sine = rotary_tables(length)
    qkv = project_qkv(gathered, gain_one, w_qkv, cosine, sine, heads)
    local, local_lse = attend_local(qkv, heads)
    attended_heads, lse = attend_memory(chosen_all, counts_all, qkv, memory, local, local_lse, heads, top)
    attended = lax.all_to_all(attended_heads, "fsdp", 0, 1, tiled=True)

    upstream = cotangent[0]
    mixed, grad_middle, grad_attended, gain_two_grad, grads, *grad_down = feed_forward(
        mine, attended, upstream, gain_two, first, down_full, span
    )
    grad_heads = lax.all_to_all(grad_attended, "fsdp", 1, 0, tiled=True)
    grads = lax.psum_scatter(grads, DP, scatter_dimension=0, tiled=True)[0]

    partial, grad_qkv = attend_backward(
        chosen_all, counts_all, qkv, memory, grad_heads, attended_heads, lse, cosine, sine, w_qkv, heads, top
    )
    own_term, arrived = chain_scatter(partial, "fsdp")
    grads = after(grads, arrived[-1])

    grad_w_qkv, gain_one_grad = projection_grads(gathered, gain_one.reshape(width, 1), w_qkv, grad_qkv)
    gains = jnp.stack([gain_one_grad.reshape(span, -1), gain_two_grad.reshape(span, -1)], 1)
    gains = jnp.pad(gains.astype(BF16), ((0, 0), (0, extra - 2), (0, 3 * wide - gains.shape[2])))
    late = jnp.concatenate([grad_w_qkv.reshape(span, -1, 3 * wide), gains], 1)
    late = late.reshape(span // 2, 2, late.shape[1], 3 * wide)
    core = lax.axis_index("core")
    taken = lax.ppermute(lax.dynamic_index_in_dim(late, 1 - core, 1, keepdims=False), "core", [(0, 1), (1, 0)])
    late = lax.dynamic_index_in_dim(late, core, 1, keepdims=False).astype(F32) + taken.astype(F32)
    late = after(late.astype(BF16), arrived[0])
    late = sum(piece.astype(F32) for piece in direct_exchange(late, "chip")).astype(BF16)
    strip = grads.shape[1]
    lanes = width // strip
    tall = w_down.shape[0]
    if grad_down:
        down = lax.psum_scatter(grad_down[0], DP, scatter_dimension=0, tiled=True)
        down = down.reshape(ring, tall, lanes, strip).transpose(0, 2, 1, 3)
    else:
        down = grads[: ring * tall * lanes].reshape(lanes, ring, tall, strip).transpose(1, 0, 2, 3)
        grads = grads[ring * tall * lanes :]
    grads = grads.reshape(-1, ring, share, strip).transpose(1, 0, 2, 3)
    pieces = jnp.concatenate([down.reshape(ring, -1, strip), grads.reshape(ring, -1, strip)], 1)
    rising, falling = arrived[-1]
    grad_normed = own_term + rising.astype(F32) + falling.astype(F32)
    own = mine.astype(F32)
    factor = lax.rsqrt(jnp.mean(own * own, -1, keepdims=True) + EPSILON)
    scaled = grad_normed * gain_one
    inner = jnp.mean(scaled * own, -1, keepdims=True)
    tokens_grad = (grad_middle + factor * scaled - own * (factor * factor * factor * inner)).astype(BF16)

    gains = late[-extra : 2 - extra, : ring * share].reshape(2, ring, share).transpose(1, 0, 2)
    gains = jnp.pad(gains, ((0, 0), (0, extra - 2), (0, 3 * wide - share)))
    late = jnp.concatenate([late[:-extra].reshape(ring, share, 3 * wide), gains], 1)
    late = after(lax.all_to_all(late, "fsdp", 0, 0, tiled=True), tokens_grad).astype(F32)
    projections = [
        late[:, :share, part * wide : (part + 1) * wide].transpose(1, 0, 2).reshape(share, width)
        for part in range(3)
    ]
    gain_shares = jnp.sum(late[:, share : share + 2, :share], 0)

    pieces = lax.psum_scatter(pieces, "fsdp", scatter_dimension=0, tiled=True)
    pieces = after(pieces, (tokens_grad, projections, gain_shares))[0].astype(F32)
    down_share = pieces[: lanes * tall].reshape(lanes, tall, strip).transpose(1, 0, 2).reshape(tall, width)
    others = pieces[lanes * tall :].reshape(-1, share, strip).transpose(1, 0, 2).reshape(share, -1)
    return (
        mixed[None],
        tokens_grad[None],
        *projections,
        others[:, :width],
        others[:, width : width + hidden_width],
        others[:, width + hidden_width :],
        down_share,
        gain_shares[0],
        gain_shares[1],
    )


def solution(mesh):
    span, ring = mesh.shape["dp"], mesh.shape["fsdp"]
    fine = Mesh(mesh.devices.reshape(span // 2, 2, ring), DP + ("fsdp",))
    every = DP + ("fsdp",)
    rows, matrix, vector = P(DP, "fsdp", None), P(every, None), P(every)
    in_specs = (rows,) * 5 + (matrix,) * 7 + (vector,) * 2 + (rows,)
    out_specs = (rows,) * 2 + (matrix,) * 7 + (vector,) * 2
    return jax.shard_map(body, mesh=fine, in_specs=in_specs, out_specs=out_specs, check_vma=False)
```

```python
import functools
import math

import jax
import jax.numpy as jnp
import numpy as np
from jax import lax
from jax.experimental import pallas as pl
from jax.experimental.pallas import tpu as pltpu
from jax.sharding import Mesh
from jax.sharding import PartitionSpec as P

HEAD_DIM = 128
QBLK = 256
MBLK = 128
EPSILON = 1e-06
NEGATIVE = -1e30
SCALE = 1.0 / math.sqrt(HEAD_DIM)
LOG2E = math.log2(math.e)
MIB = 1 << 20
F32 = jnp.float32
BF16 = jnp.bfloat16
DP = ("chip", "core")
NT = (((1,), (1,)), ((), ()))
TN = (((0,), (0,)), ((), ()))


def dot(left, right, dims=(((1,), (0,)), ((), ()))):
    return lax.dot_general(left, right, dims, preferred_element_type=F32)


def rotary_tables(length):
    half_dim = HEAD_DIM // 2
    frequency = 10000.0 ** (-jnp.arange(half_dim, dtype=F32) / half_dim)
    angles = jnp.arange(length, dtype=jnp.int32).astype(F32)[:, None] * frequency[None, :]
    cosine, sine = jnp.cos(angles), jnp.sin(angles)
    return jnp.concatenate([cosine, cosine], 1), jnp.concatenate([-sine, sine], 1)


def qkv_kernel(heads, tok_ref, gain_ref, w_ref, cos_ref, sin_ref, qkv_ref):
    rows = tok_ref[...].astype(F32)
    factor = lax.rsqrt(jnp.mean(rows * rows, -1, keepdims=True) + EPSILON)
    normed = (rows * factor * gain_ref[...]).astype(BF16)
    cosine, sine = cos_ref[...], sin_ref[...]
    wide = heads * HEAD_DIM
    for part in range(3):
        values = dot(normed, w_ref[:, part * wide : (part + 1) * wide])
        for head in range(heads):
            value = values[:, head * HEAD_DIM : (head + 1) * HEAD_DIM]
            if part < 2:
                value = value * cosine + pltpu.roll(value, HEAD_DIM // 2, 1) * sine
            if part == 0:
                value = value * (SCALE * LOG2E)
            at = part * wide + head * HEAD_DIM
            qkv_ref[:, at : at + HEAD_DIM] = value.astype(BF16)


def project_qkv(tokens_all, gain, w_qkv, cosine, sine, heads):
    length, width = tokens_all.shape
    columns = w_qkv.shape[1]
    block = 2 * QBLK
    return pl.pallas_call(
        functools.partial(qkv_kernel, heads),
        grid=(length // block,),
        in_specs=[
            pl.BlockSpec((block, width), lambda i: (i, 0)),
            pl.BlockSpec((1, width), lambda i: (0, 0)),
            pl.BlockSpec((width, columns), lambda i: (0, 0)),
            pl.BlockSpec((block, HEAD_DIM), lambda i: (i, 0)),
            pl.BlockSpec((block, HEAD_DIM), lambda i: (i, 0)),
        ],
        out_specs=pl.BlockSpec((block, columns), lambda i: (i, 0)),
        out_shape=jax.ShapeDtypeStruct((length, columns), BF16),
        compiler_params=pltpu.CompilerParams(vmem_limit_bytes=48 * MIB),
        cost_estimate=pl.CostEstimate(
            flops=2 * length * width * columns, bytes_accessed=4 * length * (width + columns), transcendentals=0
        ),
        name="project_qkv",
    )(tokens_all, gain, w_qkv, cosine, sine)


def memory_bias(counts_ref, base, top, axis):
    shape = (1, top * MBLK) if axis == 1 else (top * MBLK, 1)
    column = lax.broadcasted_iota(jnp.int32, shape, axis)
    limit = jnp.zeros(shape, jnp.int32)
    for entry in range(top):
        inside = (column >= entry * MBLK) & (column < entry * MBLK + counts_ref[base + entry])
        limit = jnp.where(inside, 1, limit)
    return jnp.where(limit > 0, 0.0, NEGATIVE)


def pick_memory(ref, chosen_ref, base, top, columns):
    rows = [
        ref[pl.ds(pl.multiple_of(chosen_ref[base + entry] * MBLK, MBLK), MBLK), columns]
        for entry in range(top)
    ]
    return jnp.concatenate(rows, 0)


def forward_kernel(
    heads, top, chosen_ref, counts_ref, q_ref, k_ref, v_ref, mk_ref, mv_ref, out_ref, lse_ref, acc_s, peak_s
):
    block = pl.program_id(0)
    rows = q_ref.shape[0]
    subs = rows // QBLK
    own = pl.ds(pl.multiple_of(block * rows, rows), rows)
    causal = lax.broadcasted_iota(jnp.int32, (rows, rows), 0) >= lax.broadcasted_iota(jnp.int32, (rows, rows), 1)
    ones = jnp.ones((rows, HEAD_DIM), BF16)
    mem_ones = jnp.ones((top * MBLK, HEAD_DIM), BF16)
    biases = [memory_bias(counts_ref, (block * subs + sub) * top, top, 1) for sub in range(subs)]
    for head in range(heads):
        columns = slice(head * HEAD_DIM, (head + 1) * HEAD_DIM)
        remote = []
        for sub in range(subs):
            keys = pick_memory(mk_ref, chosen_ref, (block * subs + sub) * top, top, columns)
            query = q_ref[sub * QBLK : (sub + 1) * QBLK, columns]
            remote.append(dot(query, keys, NT) + biases[sub])
        local = jnp.where(causal, dot(q_ref[:, columns], k_ref[own, columns], NT), NEGATIVE)
        peak = jnp.max(local, -1, keepdims=True)
        peak = jnp.maximum(peak, jnp.concatenate([jnp.max(r, -1, keepdims=True) for r in remote], 0))
        values = jnp.concatenate([v_ref[own, columns], ones], 1)
        acc = dot(jnp.exp2(local - peak).astype(BF16), values)
        more = []
        for sub in range(subs):
            values = pick_memory(mv_ref, chosen_ref, (block * subs + sub) * top, top, columns)
            weights = jnp.exp2(remote[sub] - peak[sub * QBLK : (sub + 1) * QBLK]).astype(BF16)
            more.append(dot(weights, jnp.concatenate([values, mem_ones], 1)))
        acc_s[head] = acc + jnp.concatenate(more, 0)
        peak_s[head] = jnp.broadcast_to(peak, (rows, HEAD_DIM))

    def step(index, carry):
        there = pl.ds(pl.multiple_of(index * rows, rows), rows)
        for head in range(heads):
            columns = slice(head * HEAD_DIM, (head + 1) * HEAD_DIM)
            peak = peak_s[head][:, :1]
            scores = dot(q_ref[:, columns], k_ref[there, columns], NT)
            higher = jnp.maximum(peak, jnp.max(scores, -1, keepdims=True))
            weights = jnp.exp2(scores - higher).astype(BF16)
            values = jnp.concatenate([v_ref[there, columns], ones], 1)
            acc_s[head] = acc_s[head] * jnp.exp2(peak - higher) + dot(weights, values)
            peak_s[head] = jnp.broadcast_to(higher, (rows, HEAD_DIM))
        return carry

    lax.fori_loop(0, block, step, 0)
    for head in range(heads):
        columns = slice(head * HEAD_DIM, (head + 1) * HEAD_DIM)
        total = acc_s[head][:, HEAD_DIM:]
        out_ref[:, columns] = (acc_s[head][:, :HEAD_DIM] / total).astype(BF16)
        lse_ref[:, head : head + 1] = peak_s[head][:, :1] + jnp.log2(total[:, :1])


def attend_forward(chosen, counts, qkv, memory, heads, top):
    length = qkv.shape[0]
    wide = heads * HEAD_DIM
    rows = min(2 * QBLK, length)
    mem_rows = memory.shape[0]
    return pl.pallas_call(
        functools.partial(forward_kernel, heads, top),
        grid_spec=pltpu.PrefetchScalarGridSpec(
            num_scalar_prefetch=2,
            grid=(length // rows,),
            in_specs=[
                pl.BlockSpec((rows, wide), lambda i, *_: (i, 0)),
                pl.BlockSpec((length, wide), lambda i, *_: (0, 1)),
                pl.BlockSpec((length, wide), lambda i, *_: (0, 2)),
                pl.BlockSpec((mem_rows, wide), lambda i, *_: (0, 0)),
                pl.BlockSpec((mem_rows, wide), lambda i, *_: (0, 1)),
            ],
            out_specs=[
                pl.BlockSpec((rows, wide), lambda i, *_: (i, 0)),
                pl.BlockSpec((rows, heads), lambda i, *_: (i, 0)),
            ],
            scratch_shapes=[
                pltpu.VMEM((heads, rows, 2 * HEAD_DIM), F32),
                pltpu.VMEM((heads, rows, HEAD_DIM), F32),
            ],
        ),
        out_shape=[
            jax.ShapeDtypeStruct((length, wide), BF16),
            jax.ShapeDtypeStruct((length, heads), F32),
        ],
        compiler_params=pltpu.CompilerParams(vmem_limit_bytes=48 * MIB),
        cost_estimate=pl.CostEstimate(
            flops=4 * heads * length * HEAD_DIM * (length // 2 + top * MBLK),
            bytes_accessed=8 * length * wide,
            transcendentals=heads * length * (length // 2 + top * MBLK),
        ),
        name="attend_forward",
    )(chosen, counts, qkv, qkv, qkv, memory, memory)


def spread_rows(column):
    rows = column.shape[0]
    return jnp.transpose(jnp.broadcast_to(column, (rows, HEAD_DIM)))[:1]


def score_grads(query, grad_out, out, lse, keys, values, mask):
    delta = jnp.sum(grad_out.astype(F32) * out.astype(F32), -1, keepdims=True)
    weights = jnp.exp2(mask(dot(keys, query, NT)) - spread_rows(lse))
    grad_weights = dot(values, grad_out, NT)
    return weights.astype(BF16), (weights * (grad_weights - spread_rows(delta))).astype(BF16)


def causal_mask(rows):
    key_at = lax.broadcasted_iota(jnp.int32, (rows, rows), 0)
    query_at = lax.broadcasted_iota(jnp.int32, (rows, rows), 1)
    return lambda scores: jnp.where(query_at >= key_at, scores, NEGATIVE)


def memory_query_grad(chosen_ref, counts_ref, base, top, query, grad_out, out, lse, mk_ref, mv_ref, columns):
    keys = pick_memory(mk_ref, chosen_ref, base, top, columns)
    values = pick_memory(mv_ref, chosen_ref, base, top, columns)
    bias = memory_bias(counts_ref, base, top, 0)
    _, grad_scores = score_grads(query, grad_out, out, lse, keys, values, lambda scores: scores + bias)
    return dot(grad_scores, keys, TN)


def block_grads(heads, grad_query, grad_key, grad_value, cosine, sine):
    def unturn(value):
        return (value * cosine - pltpu.roll(value, HEAD_DIM // 2, 1) * sine).astype(BF16)

    parts = []
    for part, array in enumerate((grad_query * SCALE, grad_key * (1.0 / LOG2E), grad_value)):
        for head in range(heads):
            value = array[:, head * HEAD_DIM : (head + 1) * HEAD_DIM]
            parts.append(unturn(value) if part < 2 else value.astype(BF16))
    return jnp.concatenate(parts, 1)


def first_block_kernel(
    heads, top, chosen_ref, counts_ref, plan_ref, qkv_ref, mk_ref, mv_ref, go_ref, out_ref, lse_ref, cos_ref, sin_ref,
    w_ref, partial_ref, grad_ref, gq_ref, gk_ref, gv_ref,
):
    rows = partial_ref.shape[0]
    subs = rows // QBLK
    wide = heads * HEAD_DIM
    others = go_ref.shape[0] // rows - 1
    block, is_last = plan_ref[0], plan_ref[1]
    own = pl.ds(pl.multiple_of(block * rows, rows), rows)
    gq_ref[...] = jnp.zeros_like(gq_ref)
    gk_ref[...] = jnp.zeros_like(gk_ref)
    gv_ref[...] = jnp.zeros_like(gv_ref)

    def pair(queries, keys, mask):
        for head in range(heads):
            at = head * HEAD_DIM
            columns = slice(at, at + HEAD_DIM)
            query, grad_out = qkv_ref[queries, columns], go_ref[queries, columns]
            key = qkv_ref[keys, wide + at : wide + at + HEAD_DIM]
            value = qkv_ref[keys, 2 * wide + at : 2 * wide + at + HEAD_DIM]
            lse = lse_ref[queries, head : head + 1]
            weights, grad_scores = score_grads(query, grad_out, out_ref[queries, columns], lse, key, value, mask)
            gk_ref[keys, columns] += dot(grad_scores, query)
            gv_ref[keys, columns] += dot(weights, grad_out)
            gq_ref[queries, columns] += dot(grad_scores, key, TN)

    for head in range(heads):
        columns = slice(head * HEAD_DIM, (head + 1) * HEAD_DIM)
        for sub in range(subs):
            here = pl.ds(pl.multiple_of(block * rows + sub * QBLK, QBLK), QBLK)
            gq_ref[here, columns] += memory_query_grad(
                chosen_ref, counts_ref, (block * subs + sub) * top, top, qkv_ref[here, columns], go_ref[here, columns],
                out_ref[here, columns], lse_ref[here, head : head + 1], mk_ref, mv_ref, columns,
            )
    pair(own, own, causal_mask(rows))

    def step(index, carry):
        other = jnp.where(is_last == 1, index, index + 1)
        queries = jnp.where(is_last == 1, block, other)
        keys = jnp.where(is_last == 1, other, block)
        pair(
            pl.ds(pl.multiple_of(queries * rows, rows), rows),
            pl.ds(pl.multiple_of(keys * rows, rows), rows),
            lambda scores: scores,
        )
        return carry

    lax.fori_loop(0, others, step, 0)
    grad = block_grads(
        heads, gq_ref[own, :], gk_ref[own, :], gv_ref[own, :], cos_ref[own, :], sin_ref[own, :]
    )
    grad_ref[...] = grad
    partial_ref[...] = dot(grad, w_ref[...], NT).astype(BF16)


def first_block(plan, chosen, counts, qkv, memory, grad_out, out, lse, cosine, sine, w_qkv, heads, top):
    length = qkv.shape[0]
    width = w_qkv.shape[0]
    wide = heads * HEAD_DIM
    rows = min(2 * QBLK, length)
    mem_rows = memory.shape[0]

    def whole(array):
        return pl.BlockSpec(array.shape, lambda i, *_: (0, 0))

    sums = pl.BlockSpec((length, wide), lambda i, *_: (0, 0))
    return pl.pallas_call(
        functools.partial(first_block_kernel, heads, top),
        grid_spec=pltpu.PrefetchScalarGridSpec(
            num_scalar_prefetch=3,
            grid=(1,),
            in_specs=[
                whole(qkv),
                pl.BlockSpec((mem_rows, wide), lambda i, *_: (0, 0)),
                pl.BlockSpec((mem_rows, wide), lambda i, *_: (0, 1)),
                whole(grad_out),
                whole(out),
                whole(lse),
                whole(cosine),
                whole(sine),
                whole(w_qkv),
            ],
            out_specs=[
                pl.BlockSpec((rows, width), lambda i, *_: (0, 0)),
                pl.BlockSpec((rows, 3 * wide), lambda i, *_: (0, 0)),
                sums,
                sums,
                sums,
            ],
        ),
        out_shape=[
            jax.ShapeDtypeStruct((rows, width), BF16),
            jax.ShapeDtypeStruct((rows, 3 * wide), BF16),
            *[jax.ShapeDtypeStruct((length, wide), F32)] * 3,
        ],
        compiler_params=pltpu.CompilerParams(vmem_limit_bytes=60 * MIB),
        cost_estimate=pl.CostEstimate(
            flops=4 * heads * length * HEAD_DIM * length,
            bytes_accessed=40 * length * wide,
            transcendentals=heads * length * rows,
        ),
        name="first_block",
    )(chosen, counts, plan, qkv, memory, memory, grad_out, out, lse, cosine, sine, w_qkv)


def other_blocks_kernel(
    heads, top, chosen_ref, counts_ref, plan_ref, q_ref, k_ref, v_ref, mk_ref, mv_ref, go_ref, out_ref, lse_ref,
    cos_ref, sin_ref, w_ref, gq_in, gk_in, gv_in, partial_ref, grad_ref, gk_s, gv_s, gq_s,
):
    low = plan_ref[0]
    block = low + pl.num_programs(0) - 1 - pl.program_id(0)
    rows = q_ref.shape[0]
    subs = rows // QBLK
    own = pl.ds(pl.multiple_of(block * rows, rows), rows)

    @pl.when(pl.program_id(0) == 0)
    def _():
        gk_s[...] = gk_in[...]
        gv_s[...] = gv_in[...]

    for head in range(heads):
        columns = slice(head * HEAD_DIM, (head + 1) * HEAD_DIM)
        for sub in range(subs):
            here = slice(sub * QBLK, (sub + 1) * QBLK)
            gq_s[here, columns] = gq_in[here, columns] + memory_query_grad(
                chosen_ref, counts_ref, (block * subs + sub) * top, top, q_ref[here, columns], go_ref[here, columns],
                out_ref[here, columns], lse_ref[here, head : head + 1], mk_ref, mv_ref, columns,
            )

    def local(there, mask):
        for head in range(heads):
            columns = slice(head * HEAD_DIM, (head + 1) * HEAD_DIM)
            query, grad_out = q_ref[:, columns], go_ref[:, columns]
            key = k_ref[there, columns]
            weights, grad_scores = score_grads(
                query, grad_out, out_ref[:, columns], lse_ref[:, head : head + 1], key, v_ref[there, columns], mask
            )
            gk_s[there, columns] += dot(grad_scores, query)
            gv_s[there, columns] += dot(weights, grad_out)
            gq_s[:, columns] += dot(grad_scores, key, TN)

    local(own, causal_mask(rows))

    def step(index, carry):
        local(pl.ds(pl.multiple_of(index * rows, rows), rows), lambda scores: scores)
        return carry

    lax.fori_loop(low, block, step, 0)
    grad = block_grads(heads, gq_s[...], gk_s[own, :], gv_s[own, :], cos_ref[...], sin_ref[...])
    grad_ref[...] = grad
    partial_ref[...] = dot(grad, w_ref[...], NT).astype(BF16)


def other_blocks(plan, chosen, counts, qkv, memory, grad_out, out, lse, cosine, sine, w_qkv, sums, heads, top):
    length = qkv.shape[0]
    width = w_qkv.shape[0]
    wide = heads * HEAD_DIM
    rows = min(2 * QBLK, length)
    count = length // rows - 1
    mem_rows = memory.shape[0]

    def by_rows(columns, at=0):
        return pl.BlockSpec((rows, columns), lambda i, c, n, plan: (plan[0] + count - 1 - i, at))

    def result(columns):
        return pl.BlockSpec((rows, columns), lambda i, *_: (count - 1 - i, 0))

    return pl.pallas_call(
        functools.partial(other_blocks_kernel, heads, top),
        grid_spec=pltpu.PrefetchScalarGridSpec(
            num_scalar_prefetch=3,
            grid=(count,),
            in_specs=[
                by_rows(wide),
                pl.BlockSpec((length, wide), lambda i, *_: (0, 1)),
                pl.BlockSpec((length, wide), lambda i, *_: (0, 2)),
                pl.BlockSpec((mem_rows, wide), lambda i, *_: (0, 0)),
                pl.BlockSpec((mem_rows, wide), lambda i, *_: (0, 1)),
                by_rows(wide),
                by_rows(wide),
                by_rows(heads),
                by_rows(HEAD_DIM),
                by_rows(HEAD_DIM),
                pl.BlockSpec((width, 3 * wide), lambda i, *_: (0, 0)),
                by_rows(wide),
                pl.BlockSpec((length, wide), lambda i, *_: (0, 0)),
                pl.BlockSpec((length, wide), lambda i, *_: (0, 0)),
            ],
            out_specs=[result(width), result(3 * wide)],
            scratch_shapes=[
                pltpu.VMEM((length, wide), F32),
                pltpu.VMEM((length, wide), F32),
                pltpu.VMEM((rows, wide), F32),
            ],
        ),
        out_shape=[
            jax.ShapeDtypeStruct((count * rows, width), BF16),
            jax.ShapeDtypeStruct((count * rows, 3 * wide), BF16),
        ],
        compiler_params=pltpu.CompilerParams(vmem_limit_bytes=60 * MIB),
        cost_estimate=pl.CostEstimate(
            flops=6 * heads * length * HEAD_DIM * (length + top * MBLK),
            bytes_accessed=40 * length * wide,
            transcendentals=heads * length * (length // 3 + top * MBLK),
        ),
        name="other_blocks",
    )(chosen, counts, plan, qkv, qkv, qkv, memory, memory, grad_out, out, lse, cosine, sine, w_qkv, *sums)


def ffn_kernel(
    span, merged, tok_ref, att_ref, cot_ref, gain_ref, out_w, gate_w, up_w, down_w,
    mixed_ref, grad_mid_ref, grad_att_ref, gain_grad_ref, grads_ref, *rest,
):
    if not merged:
        down_grads_ref, rest = rest[0], rest[1:]
    middle_s, normed_s, turned_s, mixed_s, upstream_s, gate_s, up_s, down_s, out_s, sems, late_sems = rest
    step, steps = pl.program_id(0), pl.num_programs(0)
    width = tok_ref.shape[1]
    share = width // span
    wide = gate_w.shape[1]
    hidden_width = down_s.shape[0]
    tall = hidden_width // span
    lanes = width // wide
    first = tall * lanes if merged else 0
    slot = step % 2

    @pl.when(step == 0)
    def _():
        middle = tok_ref[...].astype(F32) + dot(att_ref[...], out_w[...])
        middle_s[...] = middle
        factor = lax.rsqrt(jnp.mean(middle * middle, -1, keepdims=True) + EPSILON)
        normed = (middle * factor * gain_ref[...]).astype(BF16)
        normed_s[...] = normed
        turned_s[...] = jnp.transpose(normed)
        mixed_s[...] = middle
        upstream_s[...] = jnp.zeros_like(upstream_s)

    def copy_out(kind, which, index):
        source = (gate_s, up_s)[kind].at[which]
        start = first + (lanes + kind * steps + index) * share
        target = grads_ref.at[:, pl.ds(start, share), :]
        return pltpu.make_async_copy(source, target, sems.at[kind, which])

    normed = normed_s[...]
    upstream = cot_ref[...]
    both = jnp.concatenate([gate_w[...], up_w[...]], 1)
    acts = dot(normed, both)
    gate_act, up_act = acts[:, :wide], acts[:, wide:]
    grad_hidden = dot(upstream, down_w[...], NT)
    sigmoid = jax.nn.sigmoid(gate_act)
    silu = gate_act * sigmoid
    hidden = (silu * up_act).astype(BF16)
    grad_gate = (grad_hidden * up_act * sigmoid * (1.0 + gate_act * (1.0 - sigmoid))).astype(BF16)
    grad_up = (grad_hidden * silu).astype(BF16)
    mixed_s[...] += dot(hidden, down_w[...])
    grad_acts = jnp.concatenate([grad_gate, grad_up], 1)
    upstream_s[...] += dot(grad_acts, both, NT)
    down_s[pl.ds(pl.multiple_of(step * wide, wide), wide), :] = dot(hidden, upstream, TN).astype(BF16)

    @pl.when(step >= 2)
    def _():
        copy_out(0, slot, step - 2).wait()
        copy_out(1, slot, step - 2).wait()

    weight_grads = dot(turned_s[...], grad_acts).astype(BF16)
    gate_s[slot] = weight_grads[:, :wide].reshape(span, share, wide)
    up_s[slot] = weight_grads[:, wide:].reshape(span, share, wide)
    copy_out(0, slot, step).start()
    copy_out(1, slot, step).start()

    @pl.when(step == steps - 1)
    def _():
        copies = []
        if merged:
            for place in range(span):
                for lane in range(lanes):
                    copies.append(
                        pltpu.make_async_copy(
                            down_s.at[pl.ds(place * tall, tall), pl.ds(lane * wide, wide)],
                            grads_ref.at[place, pl.ds(lane * tall, tall), :],
                            late_sems.at[len(copies)],
                        )
                    )
        else:
            copies.append(pltpu.make_async_copy(down_s, down_grads_ref, late_sems.at[0]))
        for copy in copies:
            copy.start()
        mixed_ref[...] = mixed_s[...].astype(BF16)
        middle = middle_s[...]
        grad = upstream_s[...]
        factor = lax.rsqrt(jnp.mean(middle * middle, -1, keepdims=True) + EPSILON)
        gain_grad_ref[...] = jnp.sum(grad * middle * factor, 0, keepdims=True)
        scaled = grad * gain_ref[...]
        inner = jnp.mean(scaled * middle, -1, keepdims=True)
        grad_middle = cot_ref[...].astype(F32) + factor * scaled - middle * (factor * factor * factor * inner)
        grad_mid_ref[...] = grad_middle
        branch = grad_middle.astype(BF16)
        grad_att_ref[...] = dot(branch, out_w[...], NT).astype(BF16)
        turned_att = jnp.transpose(att_ref[...])
        for lane in range(lanes):
            columns = slice(lane * wide, (lane + 1) * wide)
            out_s[lane] = dot(turned_att, branch[:, columns]).astype(BF16).reshape(span, share, wide)
            more = pltpu.make_async_copy(
                out_s.at[lane],
                grads_ref.at[:, pl.ds(first + lane * share, share), :],
                late_sems.at[len(copies)],
            )
            more.start()
            copies.append(more)
        for copy in copies:
            copy.wait()
        copy_out(0, 1 - slot, step - 1).wait()
        copy_out(1, 1 - slot, step - 1).wait()
        copy_out(0, slot, step).wait()
        copy_out(1, slot, step).wait()


def feed_forward(tokens, attended, upstream, gain, weights, w_down, span):
    rows, width = tokens.shape
    hidden_width = w_down.shape[0]
    wide = 2 * HEAD_DIM
    steps = hidden_width // wide
    lanes = width // wide
    share = width // span
    tall = hidden_width // span
    merged = tall % 16 == 0
    total = (lanes + 2 * steps) * share + (lanes * tall if merged else 0)
    shapes = [
        jax.ShapeDtypeStruct((rows, width), BF16),
        jax.ShapeDtypeStruct((rows, width), F32),
        jax.ShapeDtypeStruct((rows, width), BF16),
        jax.ShapeDtypeStruct((1, width), F32),
        jax.ShapeDtypeStruct((span, total, wide), BF16),
    ]
    specs = [
        pl.BlockSpec((rows, width), lambda i: (0, 0)),
        pl.BlockSpec((rows, width), lambda i: (0, 0)),
        pl.BlockSpec((rows, width), lambda i: (0, 0)),
        pl.BlockSpec((1, width), lambda i: (0, 0)),
        pl.BlockSpec(memory_space=pl.ANY),
    ]
    if not merged:
        shapes.append(jax.ShapeDtypeStruct((hidden_width, width), BF16))
        specs.append(pl.BlockSpec(memory_space=pl.ANY))
    return pl.pallas_call(
        functools.partial(ffn_kernel, span, merged),
        grid=(steps,),
        in_specs=[
            pl.BlockSpec((rows, width), lambda i: (0, 0)),
            pl.BlockSpec((rows, width), lambda i: (0, 0)),
            pl.BlockSpec((rows, width), lambda i: (0, 0)),
            pl.BlockSpec((1, width), lambda i: (0, 0)),
            pl.BlockSpec((width, width), lambda i: (0, 0)),
            pl.BlockSpec((width, wide), lambda i: (0, lanes + i)),
            pl.BlockSpec((width, wide), lambda i: (0, lanes + steps + i)),
            pl.BlockSpec((wide, width), lambda i: (i, 0)),
        ],
        out_specs=specs,
        out_shape=shapes,
        scratch_shapes=[
            pltpu.VMEM((rows, width), F32),
            pltpu.VMEM((rows, width), BF16),
            pltpu.VMEM((width, rows), BF16),
            pltpu.VMEM((rows, width), F32),
            pltpu.VMEM((rows, width), F32),
            pltpu.VMEM((2, span, share, wide), BF16),
            pltpu.VMEM((2, span, share, wide), BF16),
            pltpu.VMEM((hidden_width, width), BF16),
            pltpu.VMEM((lanes, span, share, wide), BF16),
            pltpu.SemaphoreType.DMA((2, 2)),
            pltpu.SemaphoreType.DMA(((span * lanes if merged else 1) + lanes,)),
        ],
        compiler_params=pltpu.CompilerParams(vmem_limit_bytes=56 * MIB),
        cost_estimate=pl.CostEstimate(
            flops=6 * rows * width * (3 * hidden_width + width),
            bytes_accessed=4 * width * (3 * hidden_width + width),
            transcendentals=rows * hidden_width,
        ),
        name="feed_forward",
    )(tokens, attended, upstream, gain, weights, weights, weights, w_down)


def projection_grads_kernel(order_ref, tok_ref, gain_ref, w_ref, grad_ref, grad_w_ref, gain_grad_ref, raw_s):
    step = pl.program_id(0)

    @pl.when(step == 0)
    def _():
        raw_s[...] = jnp.zeros_like(raw_s)

    tokens = tok_ref[...].astype(F32)
    tokens = tokens * lax.rsqrt(jnp.mean(tokens * tokens, -1, keepdims=True) + EPSILON)
    raw_s[...] += dot(tokens.astype(BF16), grad_ref[...], TN)

    @pl.when(step == pl.num_programs(0) - 1)
    def _():
        raw = raw_s[...]
        gain_grad_ref[...] = jnp.sum(raw * w_ref[...].astype(F32), -1, keepdims=True)
        grad_w_ref[...] = (raw * gain_ref[...]).astype(BF16)


def projection_grads(order, tokens_all, gain_column, w_qkv, grad):
    length, width = tokens_all.shape
    columns = grad.shape[1]
    rows = min(2 * QBLK, length)
    return pl.pallas_call(
        projection_grads_kernel,
        grid_spec=pltpu.PrefetchScalarGridSpec(
            num_scalar_prefetch=1,
            grid=(length // rows,),
            in_specs=[
                pl.BlockSpec((rows, width), lambda i, order: (order[i], 0)),
                pl.BlockSpec((width, 1), lambda i, _: (0, 0)),
                pl.BlockSpec((width, columns), lambda i, _: (0, 0)),
                pl.BlockSpec((rows, columns), lambda i, _: (i, 0)),
            ],
            out_specs=[
                pl.BlockSpec((width, columns), lambda i, _: (0, 0)),
                pl.BlockSpec((width, 1), lambda i, _: (0, 0)),
            ],
            scratch_shapes=[pltpu.VMEM((width, columns), F32)],
        ),
        out_shape=[
            jax.ShapeDtypeStruct((width, columns), BF16),
            jax.ShapeDtypeStruct((width, 1), F32),
        ],
        compiler_params=pltpu.CompilerParams(vmem_limit_bytes=48 * MIB),
        cost_estimate=pl.CostEstimate(
            flops=2 * length * width * columns, bytes_accessed=2 * length * (width + columns), transcendentals=0
        ),
        name="projection_grads",
    )(order, tokens_all, gain_column, w_qkv, grad)


def after(value, earlier):
    return lax.optimization_barrier((value, earlier))[0]


def chain_gather(blocks, axis):
    size = lax.axis_size(axis)
    place = lax.axis_index(axis)
    steps = []
    rising = falling = tuple(blocks)
    for step in range(size - 1):
        up = [(i, i + 1) for i in range(step, size - 1)]
        down = [(i + 1, i) for i in range(size - 1 - step)]
        rising = tuple(lax.ppermute(block, axis, up) for block in rising)
        falling = tuple(lax.ppermute(block, axis, down) for block in falling)
        if len(blocks) > 1:
            rising, falling = lax.optimization_barrier((rising, falling))
        steps.append((rising, falling))
    results = []
    for number, block in enumerate(blocks):
        ordered = []
        for index in range(size):
            cases = []
            for mine in range(size):
                if mine == index:
                    cases.append(block)
                elif mine > index:
                    cases.append(steps[mine - index - 1][0][number])
                else:
                    cases.append(steps[index - mine - 1][1][number])
            ordered.append(lax.select_n(place, *cases) if size > 2 else lax.select_n(place > 0, *cases))
        results.append(ordered)
    return results, steps


def chain_scatter(block, axis):
    size = lax.axis_size(axis)
    place = lax.axis_index(axis)
    arrived = []
    for step in range(size - 1):
        up, down = block(step, size - 1 - step + place), block(step, step - size + 1 + place)
        if step:
            up, down = up + arrived[-1][0].astype(F32), down + arrived[-1][1].astype(F32)
        up, down = lax.optimization_barrier((up.astype(BF16), down.astype(BF16)))
        rising = lax.ppermute(up, axis, [(i, i + 1) for i in range(step + 1)])
        falling = lax.ppermute(down, axis, [(i, i - 1) for i in range(size - 1 - step, size)])
        arrived.append(lax.optimization_barrier((rising, falling)))
    return block(size, place), arrived


def direct_exchange(blocks, axis):
    size = lax.axis_size(axis)
    place = lax.axis_index(axis)
    taken = [lax.dynamic_index_in_dim(blocks, place, 0, keepdims=False)]
    for far in range(1, size):
        give = lax.dynamic_index_in_dim(blocks, (place + far) % size, 0, keepdims=False)
        taken.append(lax.ppermute(give, axis, [(i, (i + far) % size) for i in range(size)]))
    return taken


def body(
    tokens, memory_keys, memory_values, chosen, counts, w_query, w_key, w_value, w_out, w_gate, w_up, w_down,
    gain_attn, gain_ffn, cotangent,
):
    ring, span = lax.axis_size("fsdp"), lax.axis_size(DP)
    rows, width = tokens.shape[1:]
    heads = width // HEAD_DIM // ring
    wide = heads * HEAD_DIM
    length = rows * ring
    top = chosen.shape[2]
    hidden_width = w_gate.shape[1]
    share = w_query.shape[0]
    mine = tokens[0]

    extra = 8 if share % 8 == 0 else 8 - share % 8
    parts = [w.reshape(share, ring, wide).transpose(1, 0, 2) for w in (w_query, w_key, w_value)]
    choices = jnp.concatenate([chosen[0].reshape(-1), counts[0].reshape(-1)]).astype(BF16)
    notes = jnp.stack(
        [
            jnp.pad(row, (0, 3 * wide - row.shape[0]))
            for row in (jnp.concatenate([gain_attn, gain_ffn]), choices)
        ]
    )
    notes = jnp.broadcast_to(jnp.pad(notes, ((0, extra - 2), (0, 0))), (ring, extra, 3 * wide))
    parcel = jnp.concatenate([jnp.concatenate(parts, 2), notes], 1)
    parcel = lax.all_to_all(parcel, "fsdp", 0, 0, tiled=True)
    picks = parcel[:, share + 1, : choices.shape[0]].astype(jnp.int32).reshape(ring, 2, -1)
    chosen_all, counts_all = picks[:, 0].reshape(-1), picks[:, 1].reshape(-1)
    shards = jnp.concatenate([w_out, w_gate, w_up], 1)
    (near, near_down), steps = chain_gather((shards, w_down), "fsdp")
    (gathered,), token_steps = chain_gather((after(mine, steps[-2]),), "fsdp")
    parcel = lax.all_gather(parcel, DP, axis=0, tiled=True)
    w_qkv = parcel[:, :share].reshape(width, 3 * wide)
    gain_one = parcel[:, share, :share].reshape(1, width).astype(F32)
    gain_two = parcel[:, share, share : 2 * share].reshape(1, width).astype(F32)
    first = lax.all_gather(jnp.concatenate(near, 0), DP, axis=0, tiled=True)
    gathered = jnp.concatenate(gathered, 0)

    memory = jnp.concatenate(
        [m[0].reshape(-1, ring, wide).transpose(1, 0, 2) for m in (memory_keys, memory_values)], 2
    )
    memory = lax.all_to_all(after(memory, token_steps[-2]), "fsdp", 0, 0, tiled=True).reshape(-1, 2 * wide)
    down_full = lax.all_gather(jnp.concatenate(near_down, 0), DP, axis=0, tiled=True)

    cosine, sine = rotary_tables(length)
    qkv = project_qkv(gathered, gain_one, w_qkv, cosine, sine, heads)
    attended_heads, lse = attend_forward(chosen_all, counts_all, qkv, memory, heads, top)
    attended = lax.all_to_all(attended_heads, "fsdp", 0, 1, tiled=True)

    upstream = cotangent[0]
    mixed, grad_middle, grad_attended, gain_two_grad, grads, *grad_down = feed_forward(
        mine, attended, upstream, gain_two, first, down_full, span
    )
    grad_heads = lax.all_to_all(grad_attended, "fsdp", 1, 0, tiled=True)
    grads = lax.psum_scatter(grads, DP, scatter_dimension=0, tiled=True)[0]

    place = lax.axis_index("fsdp").astype(jnp.int32)
    count = length // min(2 * QBLK, length)
    is_last = (place < ring // 2).astype(jnp.int32)
    first_number = jnp.where(is_last == 1, count - 1, 0).astype(jnp.int32)
    low = 1 - is_last
    first_partial, first_grad, *sums = first_block(
        jnp.stack([first_number, is_last]), chosen_all, counts_all, qkv, memory, grad_heads, attended_heads, lse,
        cosine, sine, w_qkv, heads, top,
    )
    other_partial, other_grad = other_blocks(
        low.reshape(1), chosen_all, counts_all, qkv, memory, grad_heads, attended_heads, lse, cosine, sine, w_qkv,
        sums, heads, top,
    )
    grad_qkv = jnp.concatenate([first_grad, other_grad], 0)
    order = jnp.concatenate([first_number.reshape(1), low + jnp.arange(count - 1, dtype=jnp.int32)])
    block_rows = first_partial.shape[0]

    def term(step, index):
        start = jnp.clip(index, 0, ring - 1) * rows
        at = jnp.clip(start - low * block_rows, 0, other_partial.shape[0] - rows)
        near = jnp.clip(start - first_number * block_rows, 0, block_rows - rows)
        from_first = lax.dynamic_slice_in_dim(first_partial, near, rows, 0)
        if step == 0:
            return from_first.astype(F32)
        from_others = lax.dynamic_slice_in_dim(other_partial, at, rows, 0)
        inside = (start >= first_number * block_rows) & (start < (first_number + 1) * block_rows)
        return jnp.where(inside, from_first, from_others).astype(F32)

    own_term, arrived = chain_scatter(term, "fsdp")
    grads = after(grads, arrived[-1])

    grad_w_qkv, gain_one_grad = projection_grads(order, gathered, gain_one.reshape(width, 1), w_qkv, grad_qkv)
    gains = jnp.stack([gain_one_grad.reshape(span, -1), gain_two_grad.reshape(span, -1)], 1)
    gains = jnp.pad(gains.astype(BF16), ((0, 0), (0, extra - 2), (0, 3 * wide - gains.shape[2])))
    late = jnp.concatenate([grad_w_qkv.reshape(span, -1, 3 * wide), gains], 1)
    late = late.reshape(span // 2, 2, late.shape[1], 3 * wide)
    core = lax.axis_index("core")
    taken = lax.ppermute(lax.dynamic_index_in_dim(late, 1 - core, 1, keepdims=False), "core", [(0, 1), (1, 0)])
    late = lax.dynamic_index_in_dim(late, core, 1, keepdims=False).astype(F32) + taken.astype(F32)
    late = after(late.astype(BF16), arrived[0])
    late = sum(piece.astype(F32) for piece in direct_exchange(late, "chip")).astype(BF16)
    strip = grads.shape[1]
    lanes = width // strip
    tall = w_down.shape[0]
    if grad_down:
        down = lax.psum_scatter(grad_down[0], DP, scatter_dimension=0, tiled=True)
        down = down.reshape(ring, tall, lanes, strip).transpose(0, 2, 1, 3)
    else:
        down = grads[: ring * tall * lanes].reshape(lanes, ring, tall, strip).transpose(1, 0, 2, 3)
        grads = grads[ring * tall * lanes :]
    grads = grads.reshape(-1, ring, share, strip).transpose(1, 0, 2, 3)
    pieces = jnp.concatenate([down.reshape(ring, -1, strip), grads.reshape(ring, -1, strip)], 1)
    rising, falling = arrived[-1]
    grad_normed = own_term + rising.astype(F32) + falling.astype(F32)
    own = mine.astype(F32)
    factor = lax.rsqrt(jnp.mean(own * own, -1, keepdims=True) + EPSILON)
    scaled = grad_normed * gain_one
    inner = jnp.mean(scaled * own, -1, keepdims=True)
    tokens_grad = (grad_middle + factor * scaled - own * (factor * factor * factor * inner)).astype(BF16)

    gains = late[-extra : 2 - extra, : ring * share].reshape(2, ring, share).transpose(1, 0, 2)
    gains = jnp.pad(gains, ((0, 0), (0, extra - 2), (0, 3 * wide - share)))
    late = jnp.concatenate([late[:-extra].reshape(ring, share, 3 * wide), gains], 1)
    late = after(lax.all_to_all(late, "fsdp", 0, 0, tiled=True), tokens_grad).astype(F32)
    projections = [
        late[:, :share, part * wide : (part + 1) * wide].transpose(1, 0, 2).reshape(share, width)
        for part in range(3)
    ]
    gain_shares = jnp.sum(late[:, share : share + 2, :share], 0)

    pieces = lax.psum_scatter(pieces, "fsdp", scatter_dimension=0, tiled=True)
    pieces = after(pieces, (tokens_grad, projections, gain_shares))[0].astype(F32)
    down_share = pieces[: lanes * tall].reshape(lanes, tall, strip).transpose(1, 0, 2).reshape(tall, width)
    others = pieces[lanes * tall :].reshape(-1, share, strip).transpose(1, 0, 2).reshape(share, -1)
    return (
        mixed[None],
        tokens_grad[None],
        *projections,
        others[:, :width],
        others[:, width : width + hidden_width],
        others[:, width + hidden_width :],
        down_share,
        gain_shares[0],
        gain_shares[1],
    )


def solution(mesh):
    span, ring = mesh.shape["dp"], mesh.shape["fsdp"]
    fine = Mesh(mesh.devices.reshape(span // 2, 2, ring), DP + ("fsdp",))
    every = DP + ("fsdp",)
    rows, matrix, vector = P(DP, "fsdp", None), P(every, None), P(every)
    in_specs = (rows,) * 5 + (matrix,) * 7 + (vector,) * 2 + (rows,)
    out_specs = (rows,) * 2 + (matrix,) * 7 + (vector,) * 2
    return jax.shard_map(body, mesh=fine, in_specs=in_specs, out_specs=out_specs, check_vma=False)
```

```python
import functools
import math

import jax
import jax.numpy as jnp
import numpy as np
from jax import lax
from jax.experimental import pallas as pl
from jax.experimental.pallas import tpu as pltpu
from jax.sharding import Mesh
from jax.sharding import PartitionSpec as P

HEAD_DIM = 128
QBLK = 256
MBLK = 128
EPSILON = 1e-06
NEGATIVE = -1e30
SCALE = 1.0 / math.sqrt(HEAD_DIM)
LOG2E = math.log2(math.e)
MIB = 1 << 20
F32 = jnp.float32
BF16 = jnp.bfloat16
DP = ("chip", "core")
NT = (((1,), (1,)), ((), ()))
TN = (((0,), (0,)), ((), ()))


def dot(left, right, dims=(((1,), (0,)), ((), ()))):
    return lax.dot_general(left, right, dims, preferred_element_type=F32)


def rotary_tables(length):
    half_dim = HEAD_DIM // 2
    frequency = 10000.0 ** (-jnp.arange(half_dim, dtype=F32) / half_dim)
    angles = jnp.arange(length, dtype=jnp.int32).astype(F32)[:, None] * frequency[None, :]
    cosine, sine = jnp.cos(angles), jnp.sin(angles)
    return jnp.concatenate([cosine, cosine], 1), jnp.concatenate([-sine, sine], 1)


def qkv_kernel(heads, count, which_ref, gain_ref, w_ref, cos_ref, sin_ref, *refs):
    sources = refs[:count]
    qkv_ref, tokens_ref, held, sems = refs[count:]
    step, steps = pl.program_id(0), pl.num_programs(0)
    slot = step % 2

    def fetch(index, place):
        for number, source in enumerate(sources):

            @pl.when(which_ref[index] == number)
            def _():
                pltpu.make_async_copy(source, held.at[place], sems.at[place]).start()

    @pl.when(step == 0)
    def _():
        fetch(0, 0)

    @pl.when(step + 1 < steps)
    def _():
        fetch(step + 1, 1 - slot)

    pltpu.make_async_copy(sources[0], held.at[slot], sems.at[slot]).wait()
    tokens = held[slot]
    tokens_ref[...] = tokens
    rows = tokens.astype(F32)
    factor = lax.rsqrt(jnp.mean(rows * rows, -1, keepdims=True) + EPSILON)
    normed = (rows * factor * gain_ref[...]).astype(BF16)
    cosine, sine = cos_ref[...], sin_ref[...]
    wide = heads * HEAD_DIM
    for part in range(3):
        values = dot(normed, w_ref[:, part * wide : (part + 1) * wide])
        for head in range(heads):
            value = values[:, head * HEAD_DIM : (head + 1) * HEAD_DIM]
            if part < 2:
                value = value * cosine + pltpu.roll(value, HEAD_DIM // 2, 1) * sine
            if part == 0:
                value = value * (SCALE * LOG2E)
            at = part * wide + head * HEAD_DIM
            qkv_ref[:, at : at + HEAD_DIM] = value.astype(BF16)


def project_qkv(which, blocks, gain, w_qkv, cosine, sine, heads):
    rows, width = blocks[0].shape
    columns = w_qkv.shape[1]
    size = which.shape[0]
    length = size * rows
    return pl.pallas_call(
        functools.partial(qkv_kernel, heads, len(blocks)),
        grid_spec=pltpu.PrefetchScalarGridSpec(
            num_scalar_prefetch=1,
            grid=(size,),
            in_specs=[
                pl.BlockSpec((1, width), lambda i, _: (0, 0)),
                pl.BlockSpec((width, columns), lambda i, _: (0, 0)),
                pl.BlockSpec((rows, HEAD_DIM), lambda i, _: (i, 0)),
                pl.BlockSpec((rows, HEAD_DIM), lambda i, _: (i, 0)),
                *[pl.BlockSpec(memory_space=pl.ANY) for _ in blocks],
            ],
            out_specs=[
                pl.BlockSpec((rows, columns), lambda i, _: (i, 0)),
                pl.BlockSpec((rows, width), lambda i, _: (i, 0)),
            ],
            scratch_shapes=[pltpu.VMEM((2, rows, width), BF16), pltpu.SemaphoreType.DMA((2,))],
        ),
        out_shape=[
            jax.ShapeDtypeStruct((length, columns), BF16),
            jax.ShapeDtypeStruct((length, width), BF16),
        ],
        compiler_params=pltpu.CompilerParams(vmem_limit_bytes=60 * MIB),
        cost_estimate=pl.CostEstimate(
            flops=2 * length * width * columns, bytes_accessed=4 * length * (width + columns), transcendentals=0
        ),
        name="project_qkv",
    )(which, gain, w_qkv, cosine, sine, *blocks)


def memory_bias(counts_ref, base, top, axis):
    shape = (1, top * MBLK) if axis == 1 else (top * MBLK, 1)
    column = lax.broadcasted_iota(jnp.int32, shape, axis)
    limit = jnp.zeros(shape, jnp.int32)
    for entry in range(top):
        inside = (column >= entry * MBLK) & (column < entry * MBLK + counts_ref[base + entry])
        limit = jnp.where(inside, 1, limit)
    return jnp.where(limit > 0, 0.0, NEGATIVE)


def pick_memory(ref, chosen_ref, base, top, columns):
    rows = [
        ref[pl.ds(pl.multiple_of(chosen_ref[base + entry] * MBLK, MBLK), MBLK), columns]
        for entry in range(top)
    ]
    return jnp.concatenate(rows, 0)


def forward_kernel(
    heads, top, chosen_ref, counts_ref, q_ref, k_ref, v_ref, mk_ref, mv_ref, out_ref, lse_ref, acc_s, peak_s
):
    block = pl.program_id(0)
    rows = q_ref.shape[0]
    subs = rows // QBLK
    own = pl.ds(pl.multiple_of(block * rows, rows), rows)
    causal = lax.broadcasted_iota(jnp.int32, (rows, rows), 0) >= lax.broadcasted_iota(jnp.int32, (rows, rows), 1)
    ones = jnp.ones((rows, HEAD_DIM), BF16)
    mem_ones = jnp.ones((top * MBLK, HEAD_DIM), BF16)
    biases = [memory_bias(counts_ref, (block * subs + sub) * top, top, 1) for sub in range(subs)]
    for head in range(heads):
        columns = slice(head * HEAD_DIM, (head + 1) * HEAD_DIM)
        remote = []
        for sub in range(subs):
            keys = pick_memory(mk_ref, chosen_ref, (block * subs + sub) * top, top, columns)
            query = q_ref[sub * QBLK : (sub + 1) * QBLK, columns]
            remote.append(dot(query, keys, NT) + biases[sub])
        local = jnp.where(causal, dot(q_ref[:, columns], k_ref[own, columns], NT), NEGATIVE)
        peak = jnp.max(local, -1, keepdims=True)
        peak = jnp.maximum(peak, jnp.concatenate([jnp.max(r, -1, keepdims=True) for r in remote], 0))
        values = jnp.concatenate([v_ref[own, columns], ones], 1)
        acc = dot(jnp.exp2(local - peak).astype(BF16), values)
        more = []
        for sub in range(subs):
            values = pick_memory(mv_ref, chosen_ref, (block * subs + sub) * top, top, columns)
            weights = jnp.exp2(remote[sub] - peak[sub * QBLK : (sub + 1) * QBLK]).astype(BF16)
            more.append(dot(weights, jnp.concatenate([values, mem_ones], 1)))
        acc_s[head] = acc + jnp.concatenate(more, 0)
        peak_s[head] = jnp.broadcast_to(peak, (rows, HEAD_DIM))

    def step(index, carry):
        there = pl.ds(pl.multiple_of(index * rows, rows), rows)
        for head in range(heads):
            columns = slice(head * HEAD_DIM, (head + 1) * HEAD_DIM)
            peak = peak_s[head][:, :1]
            scores = dot(q_ref[:, columns], k_ref[there, columns], NT)
            higher = jnp.maximum(peak, jnp.max(scores, -1, keepdims=True))
            weights = jnp.exp2(scores - higher).astype(BF16)
            values = jnp.concatenate([v_ref[there, columns], ones], 1)
            acc_s[head] = acc_s[head] * jnp.exp2(peak - higher) + dot(weights, values)
            peak_s[head] = jnp.broadcast_to(higher, (rows, HEAD_DIM))
        return carry

    lax.fori_loop(0, block, step, 0)
    for head in range(heads):
        columns = slice(head * HEAD_DIM, (head + 1) * HEAD_DIM)
        total = acc_s[head][:, HEAD_DIM:]
        out_ref[:, columns] = (acc_s[head][:, :HEAD_DIM] / total).astype(BF16)
        lse_ref[:, head : head + 1] = peak_s[head][:, :1] + jnp.log2(total[:, :1])


def attend_forward(chosen, counts, qkv, memory, heads, top):
    length = qkv.shape[0]
    wide = heads * HEAD_DIM
    rows = min(2 * QBLK, length)
    mem_rows = memory.shape[0]
    return pl.pallas_call(
        functools.partial(forward_kernel, heads, top),
        grid_spec=pltpu.PrefetchScalarGridSpec(
            num_scalar_prefetch=2,
            grid=(length // rows,),
            in_specs=[
                pl.BlockSpec((rows, wide), lambda i, *_: (i, 0)),
                pl.BlockSpec((length, wide), lambda i, *_: (0, 1)),
                pl.BlockSpec((length, wide), lambda i, *_: (0, 2)),
                pl.BlockSpec((mem_rows, wide), lambda i, *_: (0, 0)),
                pl.BlockSpec((mem_rows, wide), lambda i, *_: (0, 1)),
            ],
            out_specs=[
                pl.BlockSpec((rows, wide), lambda i, *_: (i, 0)),
                pl.BlockSpec((rows, heads), lambda i, *_: (i, 0)),
            ],
            scratch_shapes=[
                pltpu.VMEM((heads, rows, 2 * HEAD_DIM), F32),
                pltpu.VMEM((heads, rows, HEAD_DIM), F32),
            ],
        ),
        out_shape=[
            jax.ShapeDtypeStruct((length, wide), BF16),
            jax.ShapeDtypeStruct((length, heads), F32),
        ],
        compiler_params=pltpu.CompilerParams(vmem_limit_bytes=48 * MIB),
        cost_estimate=pl.CostEstimate(
            flops=4 * heads * length * HEAD_DIM * (length // 2 + top * MBLK),
            bytes_accessed=8 * length * wide,
            transcendentals=heads * length * (length // 2 + top * MBLK),
        ),
        name="attend_forward",
    )(chosen, counts, qkv, qkv, qkv, memory, memory)


def spread_rows(column):
    rows = column.shape[0]
    return jnp.transpose(jnp.broadcast_to(column, (rows, HEAD_DIM)))[:1]


def score_grads(query, grad_out, out, lse, keys, values, mask):
    delta = jnp.sum(grad_out.astype(F32) * out.astype(F32), -1, keepdims=True)
    weights = jnp.exp2(mask(dot(keys, query, NT)) - spread_rows(lse))
    grad_weights = dot(values, grad_out, NT)
    return weights.astype(BF16), (weights * (grad_weights - spread_rows(delta))).astype(BF16)


def causal_mask(rows):
    key_at = lax.broadcasted_iota(jnp.int32, (rows, rows), 0)
    query_at = lax.broadcasted_iota(jnp.int32, (rows, rows), 1)
    return lambda scores: jnp.where(query_at >= key_at, scores, NEGATIVE)


def memory_query_grad(chosen_ref, counts_ref, base, top, query, grad_out, out, lse, mk_ref, mv_ref, columns):
    keys = pick_memory(mk_ref, chosen_ref, base, top, columns)
    values = pick_memory(mv_ref, chosen_ref, base, top, columns)
    bias = memory_bias(counts_ref, base, top, 0)
    _, grad_scores = score_grads(query, grad_out, out, lse, keys, values, lambda scores: scores + bias)
    return dot(grad_scores, keys, TN)


def block_grads(heads, grad_query, grad_key, grad_value, cosine, sine):
    def unturn(value):
        return (value * cosine - pltpu.roll(value, HEAD_DIM // 2, 1) * sine).astype(BF16)

    parts = []
    for part, array in enumerate((grad_query * SCALE, grad_key * (1.0 / LOG2E), grad_value)):
        for head in range(heads):
            value = array[:, head * HEAD_DIM : (head + 1) * HEAD_DIM]
            parts.append(unturn(value) if part < 2 else value.astype(BF16))
    return jnp.concatenate(parts, 1)


def first_block_kernel(
    heads, top, chosen_ref, counts_ref, plan_ref, qkv_ref, mk_ref, mv_ref, go_ref, out_ref, lse_ref, cos_ref, sin_ref,
    w_ref, partial_ref, grad_ref, gq_ref, gk_ref, gv_ref,
):
    rows = partial_ref.shape[0]
    subs = rows // QBLK
    wide = heads * HEAD_DIM
    others = go_ref.shape[0] // rows - 1
    block, is_last = plan_ref[0], plan_ref[1]
    own = pl.ds(pl.multiple_of(block * rows, rows), rows)
    gq_ref[...] = jnp.zeros_like(gq_ref)
    gk_ref[...] = jnp.zeros_like(gk_ref)
    gv_ref[...] = jnp.zeros_like(gv_ref)

    def pair(queries, keys, mask):
        for head in range(heads):
            at = head * HEAD_DIM
            columns = slice(at, at + HEAD_DIM)
            query, grad_out = qkv_ref[queries, columns], go_ref[queries, columns]
            key = qkv_ref[keys, wide + at : wide + at + HEAD_DIM]
            value = qkv_ref[keys, 2 * wide + at : 2 * wide + at + HEAD_DIM]
            lse = lse_ref[queries, head : head + 1]
            weights, grad_scores = score_grads(query, grad_out, out_ref[queries, columns], lse, key, value, mask)
            gk_ref[keys, columns] += dot(grad_scores, query)
            gv_ref[keys, columns] += dot(weights, grad_out)
            gq_ref[queries, columns] += dot(grad_scores, key, TN)

    for head in range(heads):
        columns = slice(head * HEAD_DIM, (head + 1) * HEAD_DIM)
        for sub in range(subs):
            here = pl.ds(pl.multiple_of(block * rows + sub * QBLK, QBLK), QBLK)
            gq_ref[here, columns] += memory_query_grad(
                chosen_ref, counts_ref, (block * subs + sub) * top, top, qkv_ref[here, columns], go_ref[here, columns],
                out_ref[here, columns], lse_ref[here, head : head + 1], mk_ref, mv_ref, columns,
            )
    pair(own, own, causal_mask(rows))

    def step(index, carry):
        other = jnp.where(is_last == 1, index, index + 1)
        queries = jnp.where(is_last == 1, block, other)
        keys = jnp.where(is_last == 1, other, block)
        pair(
            pl.ds(pl.multiple_of(queries * rows, rows), rows),
            pl.ds(pl.multiple_of(keys * rows, rows), rows),
            lambda scores: scores,
        )
        return carry

    lax.fori_loop(0, others, step, 0)
    grad = block_grads(
        heads, gq_ref[own, :], gk_ref[own, :], gv_ref[own, :], cos_ref[...], sin_ref[...]
    )
    grad_ref[...] = grad
    partial_ref[...] = dot(grad, w_ref[...], NT).astype(BF16)


def first_block(plan, chosen, counts, qkv, memory, grad_out, out, lse, cosine, sine, w_qkv, heads, top):
    length = qkv.shape[0]
    width = w_qkv.shape[0]
    wide = heads * HEAD_DIM
    rows = min(2 * QBLK, length)
    mem_rows = memory.shape[0]

    def whole(array):
        return pl.BlockSpec(array.shape, lambda i, *_: (0, 0))

    sums = pl.BlockSpec((length, wide), lambda i, *_: (0, 0))
    return pl.pallas_call(
        functools.partial(first_block_kernel, heads, top),
        grid_spec=pltpu.PrefetchScalarGridSpec(
            num_scalar_prefetch=3,
            grid=(1,),
            in_specs=[
                whole(qkv),
                pl.BlockSpec((mem_rows, wide), lambda i, *_: (0, 0)),
                pl.BlockSpec((mem_rows, wide), lambda i, *_: (0, 1)),
                whole(grad_out),
                whole(out),
                whole(lse),
                pl.BlockSpec((rows, HEAD_DIM), lambda i, c, n, plan: (plan[0], 0)),
                pl.BlockSpec((rows, HEAD_DIM), lambda i, c, n, plan: (plan[0], 0)),
                whole(w_qkv),
            ],
            out_specs=[
                pl.BlockSpec((rows, width), lambda i, *_: (0, 0)),
                pl.BlockSpec((rows, 3 * wide), lambda i, *_: (0, 0)),
                sums,
                sums,
                sums,
            ],
        ),
        out_shape=[
            jax.ShapeDtypeStruct((rows, width), BF16),
            jax.ShapeDtypeStruct((rows, 3 * wide), BF16),
            *[jax.ShapeDtypeStruct((length, wide), F32)] * 3,
        ],
        compiler_params=pltpu.CompilerParams(vmem_limit_bytes=60 * MIB),
        cost_estimate=pl.CostEstimate(
            flops=4 * heads * length * HEAD_DIM * length,
            bytes_accessed=40 * length * wide,
            transcendentals=heads * length * rows,
        ),
        name="first_block",
    )(chosen, counts, plan, qkv, memory, memory, grad_out, out, lse, cosine, sine, w_qkv)


def other_blocks_kernel(
    heads, top, chosen_ref, counts_ref, plan_ref, q_ref, k_ref, v_ref, mk_ref, mv_ref, go_ref, out_ref, lse_ref,
    cos_ref, sin_ref, w_ref, gq_in, gk_in, gv_in, partial_ref, grad_ref, gk_s, gv_s, gq_s,
):
    low = plan_ref[0]
    block = low + pl.num_programs(0) - 1 - pl.program_id(0)
    rows = q_ref.shape[0]
    subs = rows // QBLK
    own = pl.ds(pl.multiple_of(block * rows, rows), rows)

    @pl.when(pl.program_id(0) == 0)
    def _():
        gk_s[...] = gk_in[...]
        gv_s[...] = gv_in[...]

    for head in range(heads):
        columns = slice(head * HEAD_DIM, (head + 1) * HEAD_DIM)
        for sub in range(subs):
            here = slice(sub * QBLK, (sub + 1) * QBLK)
            gq_s[here, columns] = gq_in[here, columns] + memory_query_grad(
                chosen_ref, counts_ref, (block * subs + sub) * top, top, q_ref[here, columns], go_ref[here, columns],
                out_ref[here, columns], lse_ref[here, head : head + 1], mk_ref, mv_ref, columns,
            )

    def local(there, mask):
        for head in range(heads):
            columns = slice(head * HEAD_DIM, (head + 1) * HEAD_DIM)
            query, grad_out = q_ref[:, columns], go_ref[:, columns]
            key = k_ref[there, columns]
            weights, grad_scores = score_grads(
                query, grad_out, out_ref[:, columns], lse_ref[:, head : head + 1], key, v_ref[there, columns], mask
            )
            gk_s[there, columns] += dot(grad_scores, query)
            gv_s[there, columns] += dot(weights, grad_out)
            gq_s[:, columns] += dot(grad_scores, key, TN)

    local(own, causal_mask(rows))

    def step(index, carry):
        local(pl.ds(pl.multiple_of(index * rows, rows), rows), lambda scores: scores)
        return carry

    lax.fori_loop(low, block, step, 0)
    grad = block_grads(heads, gq_s[...], gk_s[own, :], gv_s[own, :], cos_ref[...], sin_ref[...])
    grad_ref[...] = grad
    partial_ref[...] = dot(grad, w_ref[...], NT).astype(BF16)


def other_blocks(plan, chosen, counts, qkv, memory, grad_out, out, lse, cosine, sine, w_qkv, sums, heads, top):
    length = qkv.shape[0]
    width = w_qkv.shape[0]
    wide = heads * HEAD_DIM
    rows = min(2 * QBLK, length)
    count = length // rows - 1
    mem_rows = memory.shape[0]

    def by_rows(columns, at=0):
        return pl.BlockSpec((rows, columns), lambda i, c, n, plan: (plan[0] + count - 1 - i, at))

    def result(columns):
        return pl.BlockSpec((rows, columns), lambda i, *_: (count - 1 - i, 0))

    return pl.pallas_call(
        functools.partial(other_blocks_kernel, heads, top),
        grid_spec=pltpu.PrefetchScalarGridSpec(
            num_scalar_prefetch=3,
            grid=(count,),
            in_specs=[
                by_rows(wide),
                pl.BlockSpec((length, wide), lambda i, *_: (0, 1)),
                pl.BlockSpec((length, wide), lambda i, *_: (0, 2)),
                pl.BlockSpec((mem_rows, wide), lambda i, *_: (0, 0)),
                pl.BlockSpec((mem_rows, wide), lambda i, *_: (0, 1)),
                by_rows(wide),
                by_rows(wide),
                by_rows(heads),
                by_rows(HEAD_DIM),
                by_rows(HEAD_DIM),
                pl.BlockSpec((width, 3 * wide), lambda i, *_: (0, 0)),
                by_rows(wide),
                pl.BlockSpec((length, wide), lambda i, *_: (0, 0)),
                pl.BlockSpec((length, wide), lambda i, *_: (0, 0)),
            ],
            out_specs=[result(width), result(3 * wide)],
            scratch_shapes=[
                pltpu.VMEM((length, wide), F32),
                pltpu.VMEM((length, wide), F32),
                pltpu.VMEM((rows, wide), F32),
            ],
        ),
        out_shape=[
            jax.ShapeDtypeStruct((count * rows, width), BF16),
            jax.ShapeDtypeStruct((count * rows, 3 * wide), BF16),
        ],
        compiler_params=pltpu.CompilerParams(vmem_limit_bytes=60 * MIB),
        cost_estimate=pl.CostEstimate(
            flops=6 * heads * length * HEAD_DIM * (length + top * MBLK),
            bytes_accessed=40 * length * wide,
            transcendentals=heads * length * (length // 3 + top * MBLK),
        ),
        name="other_blocks",
    )(chosen, counts, plan, qkv, qkv, qkv, memory, memory, grad_out, out, lse, cosine, sine, w_qkv, *sums)


def ffn_kernel(
    span, merged, tok_ref, att_ref, cot_ref, gain_ref, out_w, gate_w, up_w, down_w,
    mixed_ref, grad_mid_ref, grad_att_ref, gain_grad_ref, grads_ref, *rest,
):
    if not merged:
        down_grads_ref, rest = rest[0], rest[1:]
    middle_s, normed_s, turned_s, mixed_s, upstream_s, gate_s, up_s, down_s, out_s, sems, late_sems = rest
    step, steps = pl.program_id(0), pl.num_programs(0)
    width = tok_ref.shape[1]
    share = width // span
    wide = gate_w.shape[1]
    hidden_width = down_s.shape[0]
    tall = hidden_width // span
    lanes = width // wide
    first = tall * lanes if merged else 0
    slot = step % 2

    @pl.when(step == 0)
    def _():
        middle = tok_ref[...].astype(F32) + dot(att_ref[...], out_w[...])
        middle_s[...] = middle
        factor = lax.rsqrt(jnp.mean(middle * middle, -1, keepdims=True) + EPSILON)
        normed = (middle * factor * gain_ref[...]).astype(BF16)
        normed_s[...] = normed
        turned_s[...] = jnp.transpose(normed)
        mixed_s[...] = middle
        upstream_s[...] = jnp.zeros_like(upstream_s)

    def copy_out(kind, which, index):
        source = (gate_s, up_s)[kind].at[which]
        start = first + (lanes + kind * steps + index) * share
        target = grads_ref.at[:, pl.ds(start, share), :]
        return pltpu.make_async_copy(source, target, sems.at[kind, which])

    normed = normed_s[...]
    upstream = cot_ref[...]
    both = jnp.concatenate([gate_w[...], up_w[...]], 1)
    acts = dot(normed, both)
    gate_act, up_act = acts[:, :wide], acts[:, wide:]
    grad_hidden = dot(upstream, down_w[...], NT)
    sigmoid = jax.nn.sigmoid(gate_act)
    silu = gate_act * sigmoid
    hidden = (silu * up_act).astype(BF16)
    grad_gate = (grad_hidden * up_act * sigmoid * (1.0 + gate_act * (1.0 - sigmoid))).astype(BF16)
    grad_up = (grad_hidden * silu).astype(BF16)
    mixed_s[...] += dot(hidden, down_w[...])
    grad_acts = jnp.concatenate([grad_gate, grad_up], 1)
    upstream_s[...] += dot(grad_acts, both, NT)
    down_s[pl.ds(pl.multiple_of(step * wide, wide), wide), :] = dot(hidden, upstream, TN).astype(BF16)

    @pl.when(step >= 2)
    def _():
        copy_out(0, slot, step - 2).wait()
        copy_out(1, slot, step - 2).wait()

    weight_grads = dot(turned_s[...], grad_acts).astype(BF16)
    gate_s[slot] = weight_grads[:, :wide].reshape(span, share, wide)
    up_s[slot] = weight_grads[:, wide:].reshape(span, share, wide)
    copy_out(0, slot, step).start()
    copy_out(1, slot, step).start()

    @pl.when(step == steps - 1)
    def _():
        copies = []
        if merged:
            for place in range(span):
                for lane in range(lanes):
                    copies.append(
                        pltpu.make_async_copy(
                            down_s.at[pl.ds(place * tall, tall), pl.ds(lane * wide, wide)],
                            grads_ref.at[place, pl.ds(lane * tall, tall), :],
                            late_sems.at[len(copies)],
                        )
                    )
        else:
            copies.append(pltpu.make_async_copy(down_s, down_grads_ref, late_sems.at[0]))
        for copy in copies:
            copy.start()
        mixed_ref[...] = mixed_s[...].astype(BF16)
        middle = middle_s[...]
        grad = upstream_s[...]
        factor = lax.rsqrt(jnp.mean(middle * middle, -1, keepdims=True) + EPSILON)
        gain_grad_ref[...] = jnp.sum(grad * middle * factor, 0, keepdims=True)
        scaled = grad * gain_ref[...]
        inner = jnp.mean(scaled * middle, -1, keepdims=True)
        grad_middle = cot_ref[...].astype(F32) + factor * scaled - middle * (factor * factor * factor * inner)
        grad_mid_ref[...] = grad_middle
        branch = grad_middle.astype(BF16)
        grad_att_ref[...] = dot(branch, out_w[...], NT).astype(BF16)
        turned_att = jnp.transpose(att_ref[...])
        for lane in range(lanes):
            columns = slice(lane * wide, (lane + 1) * wide)
            out_s[lane] = dot(turned_att, branch[:, columns]).astype(BF16).reshape(span, share, wide)
            more = pltpu.make_async_copy(
                out_s.at[lane],
                grads_ref.at[:, pl.ds(first + lane * share, share), :],
                late_sems.at[len(copies)],
            )
            more.start()
            copies.append(more)
        for copy in copies:
            copy.wait()
        copy_out(0, 1 - slot, step - 1).wait()
        copy_out(1, 1 - slot, step - 1).wait()
        copy_out(0, slot, step).wait()
        copy_out(1, slot, step).wait()


def feed_forward(tokens, attended, upstream, gain, weights, w_down, span):
    rows, width = tokens.shape
    hidden_width = w_down.shape[0]
    wide = 2 * HEAD_DIM
    steps = hidden_width // wide
    lanes = width // wide
    share = width // span
    tall = hidden_width // span
    merged = tall % 16 == 0
    total = (lanes + 2 * steps) * share + (lanes * tall if merged else 0)
    shapes = [
        jax.ShapeDtypeStruct((rows, width), BF16),
        jax.ShapeDtypeStruct((rows, width), F32),
        jax.ShapeDtypeStruct((rows, width), BF16),
        jax.ShapeDtypeStruct((1, width), F32),
        jax.ShapeDtypeStruct((span, total, wide), BF16),
    ]
    specs = [
        pl.BlockSpec((rows, width), lambda i: (0, 0)),
        pl.BlockSpec((rows, width), lambda i: (0, 0)),
        pl.BlockSpec((rows, width), lambda i: (0, 0)),
        pl.BlockSpec((1, width), lambda i: (0, 0)),
        pl.BlockSpec(memory_space=pl.ANY),
    ]
    if not merged:
        shapes.append(jax.ShapeDtypeStruct((hidden_width, width), BF16))
        specs.append(pl.BlockSpec(memory_space=pl.ANY))
    return pl.pallas_call(
        functools.partial(ffn_kernel, span, merged),
        grid=(steps,),
        in_specs=[
            pl.BlockSpec((rows, width), lambda i: (0, 0)),
            pl.BlockSpec((rows, width), lambda i: (0, 0)),
            pl.BlockSpec((rows, width), lambda i: (0, 0)),
            pl.BlockSpec((1, width), lambda i: (0, 0)),
            pl.BlockSpec((width, width), lambda i: (0, 0)),
            pl.BlockSpec((width, wide), lambda i: (0, lanes + i)),
            pl.BlockSpec((width, wide), lambda i: (0, lanes + steps + i)),
            pl.BlockSpec((wide, width), lambda i: (i, 0)),
        ],
        out_specs=specs,
        out_shape=shapes,
        scratch_shapes=[
            pltpu.VMEM((rows, width), F32),
            pltpu.VMEM((rows, width), BF16),
            pltpu.VMEM((width, rows), BF16),
            pltpu.VMEM((rows, width), F32),
            pltpu.VMEM((rows, width), F32),
            pltpu.VMEM((2, span, share, wide), BF16),
            pltpu.VMEM((2, span, share, wide), BF16),
            pltpu.VMEM((hidden_width, width), BF16),
            pltpu.VMEM((lanes, span, share, wide), BF16),
            pltpu.SemaphoreType.DMA((2, 2)),
            pltpu.SemaphoreType.DMA(((span * lanes if merged else 1) + lanes,)),
        ],
        compiler_params=pltpu.CompilerParams(vmem_limit_bytes=56 * MIB),
        cost_estimate=pl.CostEstimate(
            flops=6 * rows * width * (3 * hidden_width + width),
            bytes_accessed=4 * width * (3 * hidden_width + width),
            transcendentals=rows * hidden_width,
        ),
        name="feed_forward",
    )(tokens, attended, upstream, gain, weights, weights, weights, w_down)


def projection_grads_kernel(order_ref, tok_ref, gain_ref, w_ref, grad_ref, grad_w_ref, gain_grad_ref, raw_s):
    step = pl.program_id(0)

    @pl.when(step == 0)
    def _():
        raw_s[...] = jnp.zeros_like(raw_s)

    tokens = tok_ref[...].astype(F32)
    tokens = tokens * lax.rsqrt(jnp.mean(tokens * tokens, -1, keepdims=True) + EPSILON)
    raw_s[...] += dot(tokens.astype(BF16), grad_ref[...], TN)

    @pl.when(step == pl.num_programs(0) - 1)
    def _():
        raw = raw_s[...]
        gain_grad_ref[...] = jnp.sum(raw * w_ref[...].astype(F32), -1, keepdims=True)
        grad_w_ref[...] = (raw * gain_ref[...]).astype(BF16)


def projection_grads(order, tokens_all, gain_column, w_qkv, grad):
    length, width = tokens_all.shape
    columns = grad.shape[1]
    rows = min(2 * QBLK, length)
    return pl.pallas_call(
        projection_grads_kernel,
        grid_spec=pltpu.PrefetchScalarGridSpec(
            num_scalar_prefetch=1,
            grid=(length // rows,),
            in_specs=[
                pl.BlockSpec((rows, width), lambda i, order: (order[i], 0)),
                pl.BlockSpec((width, 1), lambda i, _: (0, 0)),
                pl.BlockSpec((width, columns), lambda i, _: (0, 0)),
                pl.BlockSpec((rows, columns), lambda i, _: (i, 0)),
            ],
            out_specs=[
                pl.BlockSpec((width, columns), lambda i, _: (0, 0)),
                pl.BlockSpec((width, 1), lambda i, _: (0, 0)),
            ],
            scratch_shapes=[pltpu.VMEM((width, columns), F32)],
        ),
        out_shape=[
            jax.ShapeDtypeStruct((width, columns), BF16),
            jax.ShapeDtypeStruct((width, 1), F32),
        ],
        compiler_params=pltpu.CompilerParams(vmem_limit_bytes=48 * MIB),
        cost_estimate=pl.CostEstimate(
            flops=2 * length * width * columns, bytes_accessed=2 * length * (width + columns), transcendentals=0
        ),
        name="projection_grads",
    )(order, tokens_all, gain_column, w_qkv, grad)


def after(value, earlier):
    return lax.optimization_barrier((value, earlier))[0]


def chain_gather(blocks, axis):
    size = lax.axis_size(axis)
    place = lax.axis_index(axis)
    steps = []
    rising = falling = tuple(blocks)
    for step in range(size - 1):
        up = [(i, i + 1) for i in range(step, size - 1)]
        down = [(i + 1, i) for i in range(size - 1 - step)]
        rising = tuple(lax.ppermute(block, axis, up) for block in rising)
        falling = tuple(lax.ppermute(block, axis, down) for block in falling)
        if len(blocks) > 1:
            rising, falling = lax.optimization_barrier((rising, falling))
        steps.append((rising, falling))
    results = []
    for number, block in enumerate(blocks):
        ordered = []
        for index in range(size):
            cases = []
            for mine in range(size):
                if mine == index:
                    cases.append(block)
                elif mine > index:
                    cases.append(steps[mine - index - 1][0][number])
                else:
                    cases.append(steps[index - mine - 1][1][number])
            ordered.append(lax.select_n(place, *cases) if size > 2 else lax.select_n(place > 0, *cases))
        results.append(ordered)
    return results, steps


def chain_scatter(block, axis):
    size = lax.axis_size(axis)
    place = lax.axis_index(axis)
    arrived = []
    for step in range(size - 1):
        up, down = block(step, size - 1 - step + place), block(step, step - size + 1 + place)
        if step:
            up, down = up + arrived[-1][0].astype(F32), down + arrived[-1][1].astype(F32)
        up, down = lax.optimization_barrier((up.astype(BF16), down.astype(BF16)))
        rising = lax.ppermute(up, axis, [(i, i + 1) for i in range(step + 1)])
        falling = lax.ppermute(down, axis, [(i, i - 1) for i in range(size - 1 - step, size)])
        arrived.append(lax.optimization_barrier((rising, falling)))
    return block(size, place), arrived


def direct_exchange(blocks, axis):
    size = lax.axis_size(axis)
    place = lax.axis_index(axis)
    taken = [lax.dynamic_index_in_dim(blocks, place, 0, keepdims=False)]
    for far in range(1, size):
        give = lax.dynamic_index_in_dim(blocks, (place + far) % size, 0, keepdims=False)
        taken.append(lax.ppermute(give, axis, [(i, (i + far) % size) for i in range(size)]))
    return taken


def body(
    tokens, memory_keys, memory_values, chosen, counts, w_query, w_key, w_value, w_out, w_gate, w_up, w_down,
    gain_attn, gain_ffn, cotangent,
):
    ring, span = lax.axis_size("fsdp"), lax.axis_size(DP)
    rows, width = tokens.shape[1:]
    heads = width // HEAD_DIM // ring
    wide = heads * HEAD_DIM
    length = rows * ring
    top = chosen.shape[2]
    hidden_width = w_gate.shape[1]
    share = w_query.shape[0]
    mine = tokens[0]

    extra = 8 if share % 8 == 0 else 8 - share % 8
    parts = [w.reshape(share, ring, wide).transpose(1, 0, 2) for w in (w_query, w_key, w_value)]
    choices = jnp.concatenate([chosen[0].reshape(-1), counts[0].reshape(-1)]).astype(BF16)
    notes = jnp.stack(
        [
            jnp.pad(row, (0, 3 * wide - row.shape[0]))
            for row in (jnp.concatenate([gain_attn, gain_ffn]), choices)
        ]
    )
    notes = jnp.broadcast_to(jnp.pad(notes, ((0, extra - 2), (0, 0))), (ring, extra, 3 * wide))
    parcel = jnp.concatenate([jnp.concatenate(parts, 2), notes], 1)
    parcel = lax.all_to_all(parcel, "fsdp", 0, 0, tiled=True)
    picks = parcel[:, share + 1, : choices.shape[0]].astype(jnp.int32).reshape(ring, 2, -1)
    chosen_all, counts_all = picks[:, 0].reshape(-1), picks[:, 1].reshape(-1)
    shards = jnp.concatenate([w_out, w_gate, w_up], 1)
    (near, near_down), steps = chain_gather((shards, w_down), "fsdp")
    _, token_steps = chain_gather((after(mine, steps[-2]),), "fsdp")
    parcel = lax.all_gather(after(parcel, steps[0]), DP, axis=0, tiled=True)
    w_qkv = parcel[:, :share].reshape(width, 3 * wide)
    gain_one = parcel[:, share, :share].reshape(1, width).astype(F32)
    gain_two = parcel[:, share, share : 2 * share].reshape(1, width).astype(F32)
    first = lax.all_gather(jnp.concatenate(near, 0), DP, axis=0, tiled=True)

    memory = jnp.concatenate(
        [m[0].reshape(-1, ring, wide).transpose(1, 0, 2) for m in (memory_keys, memory_values)], 2
    )
    memory = lax.all_to_all(after(memory, token_steps[-2]), "fsdp", 0, 0, tiled=True).reshape(-1, 2 * wide)
    down_full = lax.all_gather(jnp.concatenate(near_down, 0), DP, axis=0, tiled=True)

    cosine, sine = rotary_tables(length)
    place = lax.axis_index("fsdp").astype(jnp.int32)
    spots = jnp.arange(ring, dtype=jnp.int32)
    which = jnp.where(spots <= place, place - spots, ring - 1 + spots - place)
    arrivals = [mine, *[step[0][0] for step in token_steps], *[step[1][0] for step in token_steps]]
    qkv, gathered = project_qkv(which, arrivals, gain_one, w_qkv, cosine, sine, heads)
    attended_heads, lse = attend_forward(chosen_all, counts_all, qkv, memory, heads, top)
    attended = lax.all_to_all(attended_heads, "fsdp", 0, 1, tiled=True)

    upstream = cotangent[0]
    mixed, grad_middle, grad_attended, gain_two_grad, grads, *grad_down = feed_forward(
        mine, attended, upstream, gain_two, first, down_full, span
    )
    grad_heads = lax.all_to_all(grad_attended, "fsdp", 1, 0, tiled=True)
    grads = lax.psum_scatter(grads, DP, scatter_dimension=0, tiled=True)[0]

    count = length // min(2 * QBLK, length)
    is_last = (place < ring // 2).astype(jnp.int32)
    first_number = jnp.where(is_last == 1, count - 1, 0).astype(jnp.int32)
    low = 1 - is_last
    first_partial, first_grad, *sums = first_block(
        jnp.stack([first_number, is_last]), chosen_all, counts_all, qkv, memory, grad_heads, attended_heads, lse,
        cosine, sine, w_qkv, heads, top,
    )
    other_partial, other_grad = other_blocks(
        low.reshape(1), chosen_all, counts_all, qkv, memory, grad_heads, attended_heads, lse, cosine, sine, w_qkv,
        sums, heads, top,
    )
    grad_qkv = jnp.concatenate([first_grad, other_grad], 0)
    order = jnp.concatenate([first_number.reshape(1), low + jnp.arange(count - 1, dtype=jnp.int32)])
    block_rows = first_partial.shape[0]

    def term(step, index):
        start = jnp.clip(index, 0, ring - 1) * rows
        at = jnp.clip(start - low * block_rows, 0, other_partial.shape[0] - rows)
        near = jnp.clip(start - first_number * block_rows, 0, block_rows - rows)
        from_first = lax.dynamic_slice_in_dim(first_partial, near, rows, 0)
        if step == 0:
            return from_first.astype(F32)
        from_others = lax.dynamic_slice_in_dim(other_partial, at, rows, 0)
        inside = (start >= first_number * block_rows) & (start < (first_number + 1) * block_rows)
        return jnp.where(inside, from_first, from_others).astype(F32)

    own_term, arrived = chain_scatter(term, "fsdp")
    grads = after(grads, arrived[-1])

    grad_w_qkv, gain_one_grad = projection_grads(order, gathered, gain_one.reshape(width, 1), w_qkv, grad_qkv)
    gains = jnp.stack([gain_one_grad.reshape(span, -1), gain_two_grad.reshape(span, -1)], 1)
    gains = jnp.pad(gains.astype(BF16), ((0, 0), (0, extra - 2), (0, 3 * wide - gains.shape[2])))
    late = jnp.concatenate([grad_w_qkv.reshape(span, -1, 3 * wide), gains], 1)
    late = late.reshape(span // 2, 2, late.shape[1], 3 * wide)
    core = lax.axis_index("core")
    taken = lax.ppermute(lax.dynamic_index_in_dim(late, 1 - core, 1, keepdims=False), "core", [(0, 1), (1, 0)])
    late = lax.dynamic_index_in_dim(late, core, 1, keepdims=False).astype(F32) + taken.astype(F32)
    late = after(late.astype(BF16), arrived[0])
    late = sum(piece.astype(F32) for piece in direct_exchange(late, "chip")).astype(BF16)
    strip = grads.shape[1]
    lanes = width // strip
    tall = w_down.shape[0]
    if grad_down:
        down = lax.psum_scatter(grad_down[0], DP, scatter_dimension=0, tiled=True)
        down = down.reshape(ring, tall, lanes, strip).transpose(0, 2, 1, 3)
    else:
        down = grads[: ring * tall * lanes].reshape(lanes, ring, tall, strip).transpose(1, 0, 2, 3)
        grads = grads[ring * tall * lanes :]
    grads = grads.reshape(-1, ring, share, strip).transpose(1, 0, 2, 3)
    pieces = jnp.concatenate([down.reshape(ring, -1, strip), grads.reshape(ring, -1, strip)], 1)
    rising, falling = arrived[-1]
    grad_normed = own_term + rising.astype(F32) + falling.astype(F32)
    own = mine.astype(F32)
    factor = lax.rsqrt(jnp.mean(own * own, -1, keepdims=True) + EPSILON)
    scaled = grad_normed * gain_one
    inner = jnp.mean(scaled * own, -1, keepdims=True)
    tokens_grad = (grad_middle + factor * scaled - own * (factor * factor * factor * inner)).astype(BF16)

    gains = late[-extra : 2 - extra, : ring * share].reshape(2, ring, share).transpose(1, 0, 2)
    gains = jnp.pad(gains, ((0, 0), (0, extra - 2), (0, 3 * wide - share)))
    late = jnp.concatenate([late[:-extra].reshape(ring, share, 3 * wide), gains], 1)
    late = after(lax.all_to_all(late, "fsdp", 0, 0, tiled=True), tokens_grad).astype(F32)
    projections = [
        late[:, :share, part * wide : (part + 1) * wide].transpose(1, 0, 2).reshape(share, width)
        for part in range(3)
    ]
    gain_shares = jnp.sum(late[:, share : share + 2, :share], 0)

    pieces = lax.psum_scatter(pieces, "fsdp", scatter_dimension=0, tiled=True)
    pieces = after(pieces, (tokens_grad, projections, gain_shares))[0].astype(F32)
    down_share = pieces[: lanes * tall].reshape(lanes, tall, strip).transpose(1, 0, 2).reshape(tall, width)
    others = pieces[lanes * tall :].reshape(-1, share, strip).transpose(1, 0, 2).reshape(share, -1)
    return (
        mixed[None],
        tokens_grad[None],
        *projections,
        others[:, :width],
        others[:, width : width + hidden_width],
        others[:, width + hidden_width :],
        down_share,
        gain_shares[0],
        gain_shares[1],
    )


def solution(mesh):
    span, ring = mesh.shape["dp"], mesh.shape["fsdp"]
    fine = Mesh(mesh.devices.reshape(span // 2, 2, ring), DP + ("fsdp",))
    every = DP + ("fsdp",)
    rows, matrix, vector = P(DP, "fsdp", None), P(every, None), P(every)
    in_specs = (rows,) * 5 + (matrix,) * 7 + (vector,) * 2 + (rows,)
    out_specs = (rows,) * 2 + (matrix,) * 7 + (vector,) * 2
    return jax.shard_map(body, mesh=fine, in_specs=in_specs, out_specs=out_specs, check_vma=False)
```

```python
import functools
import math

import jax
import jax.numpy as jnp
import numpy as np
from jax import lax
from jax.experimental import pallas as pl
from jax.experimental.pallas import tpu as pltpu
from jax.sharding import Mesh
from jax.sharding import PartitionSpec as P

HEAD_DIM = 128
QBLK = 256
MBLK = 128
EPSILON = 1e-06
NEGATIVE = -1e30
SCALE = 1.0 / math.sqrt(HEAD_DIM)
LOG2E = math.log2(math.e)
MIB = 1 << 20
F32 = jnp.float32
BF16 = jnp.bfloat16
DP = ("chip", "core")
NT = (((1,), (1,)), ((), ()))
TN = (((0,), (0,)), ((), ()))


def dot(left, right, dims=(((1,), (0,)), ((), ()))):
    return lax.dot_general(left, right, dims, preferred_element_type=F32)


def rotary_tables(length):
    half_dim = HEAD_DIM // 2
    frequency = 10000.0 ** (-jnp.arange(half_dim, dtype=F32) / half_dim)
    angles = jnp.arange(length, dtype=jnp.int32).astype(F32)[:, None] * frequency[None, :]
    cosine, sine = jnp.cos(angles), jnp.sin(angles)
    return jnp.concatenate([cosine, cosine], 1), jnp.concatenate([-sine, sine], 1)


def qkv_kernel(heads, tok_ref, gain_ref, w_ref, cos_ref, sin_ref, qkv_ref):
    rows = tok_ref[...].astype(F32)
    factor = lax.rsqrt(jnp.mean(rows * rows, -1, keepdims=True) + EPSILON)
    normed = (rows * factor * gain_ref[...]).astype(BF16)
    cosine, sine = cos_ref[...], sin_ref[...]
    wide = heads * HEAD_DIM
    for part in range(3):
        values = dot(normed, w_ref[:, part * wide : (part + 1) * wide])
        for head in range(heads):
            value = values[:, head * HEAD_DIM : (head + 1) * HEAD_DIM]
            if part < 2:
                value = value * cosine + pltpu.roll(value, HEAD_DIM // 2, 1) * sine
            if part == 0:
                value = value * (SCALE * LOG2E)
            at = part * wide + head * HEAD_DIM
            qkv_ref[:, at : at + HEAD_DIM] = value.astype(BF16)


def project_qkv(tokens_all, gain, w_qkv, cosine, sine, heads):
    length, width = tokens_all.shape
    columns = w_qkv.shape[1]
    block = 2 * QBLK
    return pl.pallas_call(
        functools.partial(qkv_kernel, heads),
        grid=(length // block,),
        in_specs=[
            pl.BlockSpec((block, width), lambda i: (i, 0)),
            pl.BlockSpec((1, width), lambda i: (0, 0)),
            pl.BlockSpec((width, columns), lambda i: (0, 0)),
            pl.BlockSpec((block, HEAD_DIM), lambda i: (i, 0)),
            pl.BlockSpec((block, HEAD_DIM), lambda i: (i, 0)),
        ],
        out_specs=pl.BlockSpec((block, columns), lambda i: (i, 0)),
        out_shape=jax.ShapeDtypeStruct((length, columns), BF16),
        compiler_params=pltpu.CompilerParams(vmem_limit_bytes=48 * MIB),
        cost_estimate=pl.CostEstimate(
            flops=2 * length * width * columns, bytes_accessed=4 * length * (width + columns), transcendentals=0
        ),
        name="project_qkv",
    )(tokens_all, gain, w_qkv, cosine, sine)


def memory_bias(counts_ref, base, top, axis):
    shape = (1, top * MBLK) if axis == 1 else (top * MBLK, 1)
    column = lax.broadcasted_iota(jnp.int32, shape, axis)
    limit = jnp.zeros(shape, jnp.int32)
    for entry in range(top):
        inside = (column >= entry * MBLK) & (column < entry * MBLK + counts_ref[base + entry])
        limit = jnp.where(inside, 1, limit)
    return jnp.where(limit > 0, 0.0, NEGATIVE)


def pick_memory(ref, chosen_ref, base, top, columns):
    rows = [
        ref[pl.ds(pl.multiple_of(chosen_ref[base + entry] * MBLK, MBLK), MBLK), columns]
        for entry in range(top)
    ]
    return jnp.concatenate(rows, 0)


def forward_kernel(
    heads, top, chosen_ref, counts_ref, q_ref, k_ref, v_ref, mk_ref, mv_ref, out_ref, lse_ref, acc_s, peak_s
):
    block = pl.program_id(0)
    rows = q_ref.shape[0]
    subs = rows // QBLK
    own = pl.ds(pl.multiple_of(block * rows, rows), rows)
    causal = lax.broadcasted_iota(jnp.int32, (rows, rows), 0) >= lax.broadcasted_iota(jnp.int32, (rows, rows), 1)
    ones = jnp.ones((rows, HEAD_DIM), BF16)
    mem_ones = jnp.ones((top * MBLK, HEAD_DIM), BF16)
    biases = [memory_bias(counts_ref, (block * subs + sub) * top, top, 1) for sub in range(subs)]
    for head in range(heads):
        columns = slice(head * HEAD_DIM, (head + 1) * HEAD_DIM)
        remote = []
        for sub in range(subs):
            keys = pick_memory(mk_ref, chosen_ref, (block * subs + sub) * top, top, columns)
            query = q_ref[sub * QBLK : (sub + 1) * QBLK, columns]
            remote.append(dot(query, keys, NT) + biases[sub])
        local = jnp.where(causal, dot(q_ref[:, columns], k_ref[own, columns], NT), NEGATIVE)
        peak = jnp.max(local, -1, keepdims=True)
        peak = jnp.maximum(peak, jnp.concatenate([jnp.max(r, -1, keepdims=True) for r in remote], 0))
        values = jnp.concatenate([v_ref[own, columns], ones], 1)
        acc = dot(jnp.exp2(local - peak).astype(BF16), values)
        more = []
        for sub in range(subs):
            values = pick_memory(mv_ref, chosen_ref, (block * subs + sub) * top, top, columns)
            weights = jnp.exp2(remote[sub] - peak[sub * QBLK : (sub + 1) * QBLK]).astype(BF16)
            more.append(dot(weights, jnp.concatenate([values, mem_ones], 1)))
        acc_s[head] = acc + jnp.concatenate(more, 0)
        peak_s[head] = jnp.broadcast_to(peak, (rows, HEAD_DIM))

    def step(index, carry):
        there = pl.ds(pl.multiple_of(index * rows, rows), rows)
        for head in range(heads):
            columns = slice(head * HEAD_DIM, (head + 1) * HEAD_DIM)
            peak = peak_s[head][:, :1]
            scores = dot(q_ref[:, columns], k_ref[there, columns], NT)
            higher = jnp.maximum(peak, jnp.max(scores, -1, keepdims=True))
            weights = jnp.exp2(scores - higher).astype(BF16)
            values = jnp.concatenate([v_ref[there, columns], ones], 1)
            acc_s[head] = acc_s[head] * jnp.exp2(peak - higher) + dot(weights, values)
            peak_s[head] = jnp.broadcast_to(higher, (rows, HEAD_DIM))
        return carry

    lax.fori_loop(0, block, step, 0)
    for head in range(heads):
        columns = slice(head * HEAD_DIM, (head + 1) * HEAD_DIM)
        total = acc_s[head][:, HEAD_DIM:]
        out_ref[:, columns] = (acc_s[head][:, :HEAD_DIM] / total).astype(BF16)
        lse_ref[:, head : head + 1] = peak_s[head][:, :1] + jnp.log2(total[:, :1])


def attend_forward(chosen, counts, qkv, memory, heads, top):
    length = qkv.shape[0]
    wide = heads * HEAD_DIM
    rows = min(2 * QBLK, length)
    mem_rows = memory.shape[0]
    return pl.pallas_call(
        functools.partial(forward_kernel, heads, top),
        grid_spec=pltpu.PrefetchScalarGridSpec(
            num_scalar_prefetch=2,
            grid=(length // rows,),
            in_specs=[
                pl.BlockSpec((rows, wide), lambda i, *_: (i, 0)),
                pl.BlockSpec((length, wide), lambda i, *_: (0, 1)),
                pl.BlockSpec((length, wide), lambda i, *_: (0, 2)),
                pl.BlockSpec((mem_rows, wide), lambda i, *_: (0, 0)),
                pl.BlockSpec((mem_rows, wide), lambda i, *_: (0, 1)),
            ],
            out_specs=[
                pl.BlockSpec((rows, wide), lambda i, *_: (i, 0)),
                pl.BlockSpec((rows, heads), lambda i, *_: (i, 0)),
            ],
            scratch_shapes=[
                pltpu.VMEM((heads, rows, 2 * HEAD_DIM), F32),
                pltpu.VMEM((heads, rows, HEAD_DIM), F32),
            ],
        ),
        out_shape=[
            jax.ShapeDtypeStruct((length, wide), BF16),
            jax.ShapeDtypeStruct((length, heads), F32),
        ],
        compiler_params=pltpu.CompilerParams(vmem_limit_bytes=48 * MIB),
        cost_estimate=pl.CostEstimate(
            flops=4 * heads * length * HEAD_DIM * (length // 2 + top * MBLK),
            bytes_accessed=8 * length * wide,
            transcendentals=heads * length * (length // 2 + top * MBLK),
        ),
        name="attend_forward",
    )(chosen, counts, qkv, qkv, qkv, memory, memory)


def spread_rows(column):
    rows = column.shape[0]
    return jnp.transpose(jnp.broadcast_to(column, (rows, HEAD_DIM)))[:1]


def row_stats(grad_out, out, lse):
    delta = jnp.sum(grad_out.astype(F32) * out.astype(F32), -1, keepdims=True)
    return jnp.concatenate([spread_rows(lse), spread_rows(delta)], 0)


def score_grads(query, grad_out, stats, keys, values, mask):
    weights = jnp.exp2(mask(dot(keys, query, NT)) - stats[:1])
    grad_weights = dot(values, grad_out, NT)
    return weights.astype(BF16), (weights * (grad_weights - stats[1:2])).astype(BF16)


def causal_mask(rows):
    key_at = lax.broadcasted_iota(jnp.int32, (rows, rows), 0)
    query_at = lax.broadcasted_iota(jnp.int32, (rows, rows), 1)
    return lambda scores: jnp.where(query_at >= key_at, scores, NEGATIVE)


def memory_query_grad(chosen_ref, counts_ref, base, top, query, grad_out, stats, mk_ref, mv_ref, columns):
    keys = pick_memory(mk_ref, chosen_ref, base, top, columns)
    values = pick_memory(mv_ref, chosen_ref, base, top, columns)
    bias = memory_bias(counts_ref, base, top, 0)
    _, grad_scores = score_grads(query, grad_out, stats, keys, values, lambda scores: scores + bias)
    return dot(grad_scores, keys, TN)


def block_grads(heads, grad_query, grad_key, grad_value, cosine, sine):
    def unturn(value):
        return (value * cosine - pltpu.roll(value, HEAD_DIM // 2, 1) * sine).astype(BF16)

    parts = []
    for part, array in enumerate((grad_query * SCALE, grad_key * (1.0 / LOG2E), grad_value)):
        for head in range(heads):
            value = array[:, head * HEAD_DIM : (head + 1) * HEAD_DIM]
            parts.append(unturn(value) if part < 2 else value.astype(BF16))
    return jnp.concatenate(parts, 1)


def first_block_kernel(
    heads, top, chosen_ref, counts_ref, plan_ref, qkv_ref, mk_ref, mv_ref, go_ref, out_ref, lse_ref, cos_ref, sin_ref,
    w_ref, partial_ref, grad_ref, gq_ref, gk_ref, gv_ref, stats_s,
):
    rows = partial_ref.shape[0]
    subs = rows // QBLK
    wide = heads * HEAD_DIM
    others = go_ref.shape[0] // rows - 1
    block, is_last = plan_ref[0], plan_ref[1]
    own = pl.ds(pl.multiple_of(block * rows, rows), rows)
    gq_ref[...] = jnp.zeros_like(gq_ref)
    gk_ref[...] = jnp.zeros_like(gk_ref)
    gv_ref[...] = jnp.zeros_like(gv_ref)

    def note_stats(slot, here):
        for head in range(heads):
            columns = slice(head * HEAD_DIM, (head + 1) * HEAD_DIM)
            stats_s[slot, head] = row_stats(go_ref[here, columns], out_ref[here, columns], lse_ref[here, head : head + 1])

    note_stats(0, own)

    def pair(slot, queries, keys, mask):
        for head in range(heads):
            at = head * HEAD_DIM
            columns = slice(at, at + HEAD_DIM)
            query, grad_out = qkv_ref[queries, columns], go_ref[queries, columns]
            key = qkv_ref[keys, wide + at : wide + at + HEAD_DIM]
            value = qkv_ref[keys, 2 * wide + at : 2 * wide + at + HEAD_DIM]
            weights, grad_scores = score_grads(query, grad_out, stats_s[slot, head], key, value, mask)
            gk_ref[keys, columns] += dot(grad_scores, query)
            gv_ref[keys, columns] += dot(weights, grad_out)
            gq_ref[queries, columns] += dot(grad_scores, key, TN)

    for head in range(heads):
        columns = slice(head * HEAD_DIM, (head + 1) * HEAD_DIM)
        for sub in range(subs):
            here = pl.ds(pl.multiple_of(block * rows + sub * QBLK, QBLK), QBLK)
            gq_ref[here, columns] += memory_query_grad(
                chosen_ref, counts_ref, (block * subs + sub) * top, top, qkv_ref[here, columns], go_ref[here, columns],
                stats_s[0, head][:, sub * QBLK : (sub + 1) * QBLK], mk_ref, mv_ref, columns,
            )
    pair(0, own, own, causal_mask(rows))

    def step(index, carry):
        other = jnp.where(is_last == 1, index, index + 1)
        there = pl.ds(pl.multiple_of(other * rows, rows), rows)

        @pl.when(is_last == 1)
        def _():
            pair(0, own, there, lambda scores: scores)

        @pl.when(is_last == 0)
        def _():
            note_stats(1, there)
            pair(1, there, own, lambda scores: scores)

        return carry

    lax.fori_loop(0, others, step, 0)
    grad = block_grads(
        heads, gq_ref[own, :], gk_ref[own, :], gv_ref[own, :], cos_ref[...], sin_ref[...]
    )
    grad_ref[...] = grad
    partial_ref[...] = dot(grad, w_ref[...], NT).astype(BF16)


def first_block(plan, chosen, counts, qkv, memory, grad_out, out, lse, cosine, sine, w_qkv, heads, top):
    length = qkv.shape[0]
    width = w_qkv.shape[0]
    wide = heads * HEAD_DIM
    rows = min(2 * QBLK, length)
    mem_rows = memory.shape[0]

    def whole(array):
        return pl.BlockSpec(array.shape, lambda i, *_: (0, 0))

    sums = pl.BlockSpec((length, wide), lambda i, *_: (0, 0))
    return pl.pallas_call(
        functools.partial(first_block_kernel, heads, top),
        grid_spec=pltpu.PrefetchScalarGridSpec(
            num_scalar_prefetch=3,
            grid=(1,),
            in_specs=[
                whole(qkv),
                pl.BlockSpec((mem_rows, wide), lambda i, *_: (0, 0)),
                pl.BlockSpec((mem_rows, wide), lambda i, *_: (0, 1)),
                whole(grad_out),
                whole(out),
                whole(lse),
                pl.BlockSpec((rows, HEAD_DIM), lambda i, c, n, plan: (plan[0], 0)),
                pl.BlockSpec((rows, HEAD_DIM), lambda i, c, n, plan: (plan[0], 0)),
                whole(w_qkv),
            ],
            out_specs=[
                pl.BlockSpec((rows, width), lambda i, *_: (0, 0)),
                pl.BlockSpec((rows, 3 * wide), lambda i, *_: (0, 0)),
                sums,
                sums,
                sums,
            ],
            scratch_shapes=[pltpu.VMEM((2, heads, 2, rows), F32)],
        ),
        out_shape=[
            jax.ShapeDtypeStruct((rows, width), BF16),
            jax.ShapeDtypeStruct((rows, 3 * wide), BF16),
            *[jax.ShapeDtypeStruct((length, wide), F32)] * 3,
        ],
        compiler_params=pltpu.CompilerParams(vmem_limit_bytes=60 * MIB),
        cost_estimate=pl.CostEstimate(
            flops=4 * heads * length * HEAD_DIM * length,
            bytes_accessed=40 * length * wide,
            transcendentals=heads * length * rows,
        ),
        name="first_block",
    )(chosen, counts, plan, qkv, memory, memory, grad_out, out, lse, cosine, sine, w_qkv)


def other_blocks_kernel(
    heads, top, chosen_ref, counts_ref, plan_ref, q_ref, k_ref, v_ref, mk_ref, mv_ref, go_ref, out_ref, lse_ref,
    cos_ref, sin_ref, w_ref, gq_in, gk_in, gv_in, partial_ref, grad_ref, gk_s, gv_s, gq_s,
):
    low = plan_ref[0]
    block = low + pl.num_programs(0) - 1 - pl.program_id(0)
    rows = q_ref.shape[0]
    subs = rows // QBLK
    own = pl.ds(pl.multiple_of(block * rows, rows), rows)

    @pl.when(pl.program_id(0) == 0)
    def _():
        gk_s[...] = gk_in[...]
        gv_s[...] = gv_in[...]

    stats = []
    for head in range(heads):
        columns = slice(head * HEAD_DIM, (head + 1) * HEAD_DIM)
        stats.append(row_stats(go_ref[:, columns], out_ref[:, columns], lse_ref[:, head : head + 1]))
        for sub in range(subs):
            here = slice(sub * QBLK, (sub + 1) * QBLK)
            gq_s[here, columns] = gq_in[here, columns] + memory_query_grad(
                chosen_ref, counts_ref, (block * subs + sub) * top, top, q_ref[here, columns], go_ref[here, columns],
                stats[head][:, here], mk_ref, mv_ref, columns,
            )

    def local(there, mask):
        for head in range(heads):
            columns = slice(head * HEAD_DIM, (head + 1) * HEAD_DIM)
            query, grad_out = q_ref[:, columns], go_ref[:, columns]
            key = k_ref[there, columns]
            weights, grad_scores = score_grads(query, grad_out, stats[head], key, v_ref[there, columns], mask)
            gk_s[there, columns] += dot(grad_scores, query)
            gv_s[there, columns] += dot(weights, grad_out)
            gq_s[:, columns] += dot(grad_scores, key, TN)

    local(own, causal_mask(rows))

    def step(index, carry):
        local(pl.ds(pl.multiple_of(index * rows, rows), rows), lambda scores: scores)
        return carry

    lax.fori_loop(low, block, step, 0)
    grad = block_grads(heads, gq_s[...], gk_s[own, :], gv_s[own, :], cos_ref[...], sin_ref[...])
    grad_ref[...] = grad
    partial_ref[...] = dot(grad, w_ref[...], NT).astype(BF16)


def other_blocks(plan, chosen, counts, qkv, memory, grad_out, out, lse, cosine, sine, w_qkv, sums, heads, top):
    length = qkv.shape[0]
    width = w_qkv.shape[0]
    wide = heads * HEAD_DIM
    rows = min(2 * QBLK, length)
    count = length // rows - 1
    mem_rows = memory.shape[0]

    def by_rows(columns, at=0):
        return pl.BlockSpec((rows, columns), lambda i, c, n, plan: (plan[0] + count - 1 - i, at))

    def result(columns):
        return pl.BlockSpec((rows, columns), lambda i, *_: (count - 1 - i, 0))

    return pl.pallas_call(
        functools.partial(other_blocks_kernel, heads, top),
        grid_spec=pltpu.PrefetchScalarGridSpec(
            num_scalar_prefetch=3,
            grid=(count,),
            in_specs=[
                by_rows(wide),
                pl.BlockSpec((length, wide), lambda i, *_: (0, 1)),
                pl.BlockSpec((length, wide), lambda i, *_: (0, 2)),
                pl.BlockSpec((mem_rows, wide), lambda i, *_: (0, 0)),
                pl.BlockSpec((mem_rows, wide), lambda i, *_: (0, 1)),
                by_rows(wide),
                by_rows(wide),
                by_rows(heads),
                by_rows(HEAD_DIM),
                by_rows(HEAD_DIM),
                pl.BlockSpec((width, 3 * wide), lambda i, *_: (0, 0)),
                by_rows(wide),
                pl.BlockSpec((length, wide), lambda i, *_: (0, 0)),
                pl.BlockSpec((length, wide), lambda i, *_: (0, 0)),
            ],
            out_specs=[result(width), result(3 * wide)],
            scratch_shapes=[
                pltpu.VMEM((length, wide), F32),
                pltpu.VMEM((length, wide), F32),
                pltpu.VMEM((rows, wide), F32),
            ],
        ),
        out_shape=[
            jax.ShapeDtypeStruct((count * rows, width), BF16),
            jax.ShapeDtypeStruct((count * rows, 3 * wide), BF16),
        ],
        compiler_params=pltpu.CompilerParams(vmem_limit_bytes=60 * MIB),
        cost_estimate=pl.CostEstimate(
            flops=6 * heads * length * HEAD_DIM * (length + top * MBLK),
            bytes_accessed=40 * length * wide,
            transcendentals=heads * length * (length // 3 + top * MBLK),
        ),
        name="other_blocks",
    )(chosen, counts, plan, qkv, qkv, qkv, memory, memory, grad_out, out, lse, cosine, sine, w_qkv, *sums)


def ffn_kernel(
    span, merged, tok_ref, att_ref, cot_ref, gain_ref, out_w, gate_w, up_w, down_w,
    mixed_ref, grad_mid_ref, grad_att_ref, gain_grad_ref, grads_ref, *rest,
):
    if not merged:
        down_grads_ref, rest = rest[0], rest[1:]
    middle_s, normed_s, turned_s, mixed_s, upstream_s, gate_s, up_s, down_s, out_s, sems, late_sems = rest
    step, steps = pl.program_id(0), pl.num_programs(0)
    width = tok_ref.shape[1]
    share = width // span
    wide = gate_w.shape[1]
    hidden_width = down_s.shape[0]
    tall = hidden_width // span
    lanes = width // wide
    first = tall * lanes if merged else 0
    slot = step % 2

    @pl.when(step == 0)
    def _():
        middle = tok_ref[...].astype(F32) + dot(att_ref[...], out_w[...])
        middle_s[...] = middle
        factor = lax.rsqrt(jnp.mean(middle * middle, -1, keepdims=True) + EPSILON)
        normed = (middle * factor * gain_ref[...]).astype(BF16)
        normed_s[...] = normed
        turned_s[...] = jnp.transpose(normed)
        mixed_s[...] = middle
        upstream_s[...] = jnp.zeros_like(upstream_s)

    def copy_out(kind, which, index):
        source = (gate_s, up_s)[kind].at[which]
        start = first + (lanes + kind * steps + index) * share
        target = grads_ref.at[:, pl.ds(start, share), :]
        return pltpu.make_async_copy(source, target, sems.at[kind, which])

    normed = normed_s[...]
    upstream = cot_ref[...]
    both = jnp.concatenate([gate_w[...], up_w[...]], 1)
    acts = dot(normed, both)
    gate_act, up_act = acts[:, :wide], acts[:, wide:]
    grad_hidden = dot(upstream, down_w[...], NT)
    sigmoid = jax.nn.sigmoid(gate_act)
    silu = gate_act * sigmoid
    hidden = (silu * up_act).astype(BF16)
    grad_gate = (grad_hidden * up_act * sigmoid * (1.0 + gate_act * (1.0 - sigmoid))).astype(BF16)
    grad_up = (grad_hidden * silu).astype(BF16)
    mixed_s[...] += dot(hidden, down_w[...])
    grad_acts = jnp.concatenate([grad_gate, grad_up], 1)
    upstream_s[...] += dot(grad_acts, both, NT)
    down_s[pl.ds(pl.multiple_of(step * wide, wide), wide), :] = dot(hidden, upstream, TN).astype(BF16)

    @pl.when(step >= 2)
    def _():
        copy_out(0, slot, step - 2).wait()
        copy_out(1, slot, step - 2).wait()

    weight_grads = dot(turned_s[...], grad_acts).astype(BF16)
    gate_s[slot] = weight_grads[:, :wide].reshape(span, share, wide)
    up_s[slot] = weight_grads[:, wide:].reshape(span, share, wide)
    copy_out(0, slot, step).start()
    copy_out(1, slot, step).start()

    @pl.when(step == steps - 1)
    def _():
        copies = []
        if merged:
            for place in range(span):
                for lane in range(lanes):
                    copies.append(
                        pltpu.make_async_copy(
                            down_s.at[pl.ds(place * tall, tall), pl.ds(lane * wide, wide)],
                            grads_ref.at[place, pl.ds(lane * tall, tall), :],
                            late_sems.at[len(copies)],
                        )
                    )
        else:
            copies.append(pltpu.make_async_copy(down_s, down_grads_ref, late_sems.at[0]))
        for copy in copies:
            copy.start()
        mixed_ref[...] = mixed_s[...].astype(BF16)
        middle = middle_s[...]
        grad = upstream_s[...]
        factor = lax.rsqrt(jnp.mean(middle * middle, -1, keepdims=True) + EPSILON)
        gain_grad_ref[...] = jnp.sum(grad * middle * factor, 0, keepdims=True)
        scaled = grad * gain_ref[...]
        inner = jnp.mean(scaled * middle, -1, keepdims=True)
        grad_middle = cot_ref[...].astype(F32) + factor * scaled - middle * (factor * factor * factor * inner)
        grad_mid_ref[...] = grad_middle
        branch = grad_middle.astype(BF16)
        grad_att_ref[...] = dot(branch, out_w[...], NT).astype(BF16)
        turned_att = jnp.transpose(att_ref[...])
        for lane in range(lanes):
            columns = slice(lane * wide, (lane + 1) * wide)
            out_s[lane] = dot(turned_att, branch[:, columns]).astype(BF16).reshape(span, share, wide)
            more = pltpu.make_async_copy(
                out_s.at[lane],
                grads_ref.at[:, pl.ds(first + lane * share, share), :],
                late_sems.at[len(copies)],
            )
            more.start()
            copies.append(more)
        for copy in copies:
            copy.wait()
        copy_out(0, 1 - slot, step - 1).wait()
        copy_out(1, 1 - slot, step - 1).wait()
        copy_out(0, slot, step).wait()
        copy_out(1, slot, step).wait()


def feed_forward(tokens, attended, upstream, gain, weights, w_down, span):
    rows, width = tokens.shape
    hidden_width = w_down.shape[0]
    wide = 2 * HEAD_DIM
    steps = hidden_width // wide
    lanes = width // wide
    share = width // span
    tall = hidden_width // span
    merged = tall % 16 == 0
    total = (lanes + 2 * steps) * share + (lanes * tall if merged else 0)
    shapes = [
        jax.ShapeDtypeStruct((rows, width), BF16),
        jax.ShapeDtypeStruct((rows, width), F32),
        jax.ShapeDtypeStruct((rows, width), BF16),
        jax.ShapeDtypeStruct((1, width), F32),
        jax.ShapeDtypeStruct((span, total, wide), BF16),
    ]
    specs = [
        pl.BlockSpec((rows, width), lambda i: (0, 0)),
        pl.BlockSpec((rows, width), lambda i: (0, 0)),
        pl.BlockSpec((rows, width), lambda i: (0, 0)),
        pl.BlockSpec((1, width), lambda i: (0, 0)),
        pl.BlockSpec(memory_space=pl.ANY),
    ]
    if not merged:
        shapes.append(jax.ShapeDtypeStruct((hidden_width, width), BF16))
        specs.append(pl.BlockSpec(memory_space=pl.ANY))
    return pl.pallas_call(
        functools.partial(ffn_kernel, span, merged),
        grid=(steps,),
        in_specs=[
            pl.BlockSpec((rows, width), lambda i: (0, 0)),
            pl.BlockSpec((rows, width), lambda i: (0, 0)),
            pl.BlockSpec((rows, width), lambda i: (0, 0)),
            pl.BlockSpec((1, width), lambda i: (0, 0)),
            pl.BlockSpec((width, width), lambda i: (0, 0)),
            pl.BlockSpec((width, wide), lambda i: (0, lanes + i)),
            pl.BlockSpec((width, wide), lambda i: (0, lanes + steps + i)),
            pl.BlockSpec((wide, width), lambda i: (i, 0)),
        ],
        out_specs=specs,
        out_shape=shapes,
        scratch_shapes=[
            pltpu.VMEM((rows, width), F32),
            pltpu.VMEM((rows, width), BF16),
            pltpu.VMEM((width, rows), BF16),
            pltpu.VMEM((rows, width), F32),
            pltpu.VMEM((rows, width), F32),
            pltpu.VMEM((2, span, share, wide), BF16),
            pltpu.VMEM((2, span, share, wide), BF16),
            pltpu.VMEM((hidden_width, width), BF16),
            pltpu.VMEM((lanes, span, share, wide), BF16),
            pltpu.SemaphoreType.DMA((2, 2)),
            pltpu.SemaphoreType.DMA(((span * lanes if merged else 1) + lanes,)),
        ],
        compiler_params=pltpu.CompilerParams(vmem_limit_bytes=56 * MIB),
        cost_estimate=pl.CostEstimate(
            flops=6 * rows * width * (3 * hidden_width + width),
            bytes_accessed=4 * width * (3 * hidden_width + width),
            transcendentals=rows * hidden_width,
        ),
        name="feed_forward",
    )(tokens, attended, upstream, gain, weights, weights, weights, w_down)


def projection_grads_kernel(order_ref, tok_ref, gain_ref, w_ref, grad_ref, grad_w_ref, gain_grad_ref, raw_s):
    step = pl.program_id(0)

    @pl.when(step == 0)
    def _():
        raw_s[...] = jnp.zeros_like(raw_s)

    tokens = tok_ref[...].astype(F32)
    tokens = tokens * lax.rsqrt(jnp.mean(tokens * tokens, -1, keepdims=True) + EPSILON)
    raw_s[...] += dot(tokens.astype(BF16), grad_ref[...], TN)

    @pl.when(step == pl.num_programs(0) - 1)
    def _():
        raw = raw_s[...]
        gain_grad_ref[...] = jnp.sum(raw * w_ref[...].astype(F32), -1, keepdims=True)
        grad_w_ref[...] = (raw * gain_ref[...]).astype(BF16)


def projection_grads(order, tokens_all, gain_column, w_qkv, grad):
    length, width = tokens_all.shape
    columns = grad.shape[1]
    rows = min(2 * QBLK, length)
    return pl.pallas_call(
        projection_grads_kernel,
        grid_spec=pltpu.PrefetchScalarGridSpec(
            num_scalar_prefetch=1,
            grid=(length // rows,),
            in_specs=[
                pl.BlockSpec((rows, width), lambda i, order: (order[i], 0)),
                pl.BlockSpec((width, 1), lambda i, _: (0, 0)),
                pl.BlockSpec((width, columns), lambda i, _: (0, 0)),
                pl.BlockSpec((rows, columns), lambda i, _: (i, 0)),
            ],
            out_specs=[
                pl.BlockSpec((width, columns), lambda i, _: (0, 0)),
                pl.BlockSpec((width, 1), lambda i, _: (0, 0)),
            ],
            scratch_shapes=[pltpu.VMEM((width, columns), F32)],
        ),
        out_shape=[
            jax.ShapeDtypeStruct((width, columns), BF16),
            jax.ShapeDtypeStruct((width, 1), F32),
        ],
        compiler_params=pltpu.CompilerParams(vmem_limit_bytes=48 * MIB),
        cost_estimate=pl.CostEstimate(
            flops=2 * length * width * columns, bytes_accessed=2 * length * (width + columns), transcendentals=0
        ),
        name="projection_grads",
    )(order, tokens_all, gain_column, w_qkv, grad)


def after(value, earlier):
    return lax.optimization_barrier((value, earlier))[0]


def chain_gather(blocks, axis):
    size = lax.axis_size(axis)
    place = lax.axis_index(axis)
    steps = []
    rising = falling = tuple(blocks)
    for step in range(size - 1):
        up = [(i, i + 1) for i in range(step, size - 1)]
        down = [(i + 1, i) for i in range(size - 1 - step)]
        rising = tuple(lax.ppermute(block, axis, up) for block in rising)
        falling = tuple(lax.ppermute(block, axis, down) for block in falling)
        if len(blocks) > 1:
            rising, falling = lax.optimization_barrier((rising, falling))
        steps.append((rising, falling))
    results = []
    for number, block in enumerate(blocks):
        ordered = []
        for index in range(size):
            cases = []
            for mine in range(size):
                if mine == index:
                    cases.append(block)
                elif mine > index:
                    cases.append(steps[mine - index - 1][0][number])
                else:
                    cases.append(steps[index - mine - 1][1][number])
            ordered.append(lax.select_n(place, *cases) if size > 2 else lax.select_n(place > 0, *cases))
        results.append(ordered)
    return results, steps


def chain_scatter(block, axis):
    size = lax.axis_size(axis)
    place = lax.axis_index(axis)
    arrived = []
    for step in range(size - 1):
        up, down = block(step, size - 1 - step + place), block(step, step - size + 1 + place)
        if step:
            up, down = up + arrived[-1][0].astype(F32), down + arrived[-1][1].astype(F32)
        up, down = lax.optimization_barrier((up.astype(BF16), down.astype(BF16)))
        rising = lax.ppermute(up, axis, [(i, i + 1) for i in range(step + 1)])
        falling = lax.ppermute(down, axis, [(i, i - 1) for i in range(size - 1 - step, size)])
        arrived.append(lax.optimization_barrier((rising, falling)))
    return block(size, place), arrived


def direct_exchange(blocks, axis):
    size = lax.axis_size(axis)
    place = lax.axis_index(axis)
    taken = [lax.dynamic_index_in_dim(blocks, place, 0, keepdims=False)]
    for far in range(1, size):
        give = lax.dynamic_index_in_dim(blocks, (place + far) % size, 0, keepdims=False)
        taken.append(lax.ppermute(give, axis, [(i, (i + far) % size) for i in range(size)]))
    return taken


def body(
    tokens, memory_keys, memory_values, chosen, counts, w_query, w_key, w_value, w_out, w_gate, w_up, w_down,
    gain_attn, gain_ffn, cotangent,
):
    ring, span = lax.axis_size("fsdp"), lax.axis_size(DP)
    rows, width = tokens.shape[1:]
    heads = width // HEAD_DIM // ring
    wide = heads * HEAD_DIM
    length = rows * ring
    top = chosen.shape[2]
    hidden_width = w_gate.shape[1]
    share = w_query.shape[0]
    mine = tokens[0]

    extra = 8 if share % 8 == 0 else 8 - share % 8
    parts = [w.reshape(share, ring, wide).transpose(1, 0, 2) for w in (w_query, w_key, w_value)]
    choices = jnp.concatenate([chosen[0].reshape(-1), counts[0].reshape(-1)]).astype(BF16)
    notes = jnp.stack(
        [
            jnp.pad(row, (0, 3 * wide - row.shape[0]))
            for row in (jnp.concatenate([gain_attn, gain_ffn]), choices)
        ]
    )
    notes = jnp.broadcast_to(jnp.pad(notes, ((0, extra - 2), (0, 0))), (ring, extra, 3 * wide))
    parcel = jnp.concatenate([jnp.concatenate(parts, 2), notes], 1)
    parcel = lax.all_to_all(parcel, "fsdp", 0, 0, tiled=True)
    picks = parcel[:, share + 1, : choices.shape[0]].astype(jnp.int32).reshape(ring, 2, -1)
    chosen_all, counts_all = picks[:, 0].reshape(-1), picks[:, 1].reshape(-1)
    shards = jnp.concatenate([w_out, w_gate, w_up], 1)
    (near, near_down), steps = chain_gather((shards, w_down), "fsdp")
    (gathered,), token_steps = chain_gather((after(mine, steps[-2]),), "fsdp")
    parcel = lax.all_gather(after(parcel, steps[0]), DP, axis=0, tiled=True)
    w_qkv = parcel[:, :share].reshape(width, 3 * wide)
    gain_one = parcel[:, share, :share].reshape(1, width).astype(F32)
    gain_two = parcel[:, share, share : 2 * share].reshape(1, width).astype(F32)
    first = lax.all_gather(jnp.concatenate(near, 0), DP, axis=0, tiled=True)
    gathered = jnp.concatenate(gathered, 0)

    memory = jnp.concatenate(
        [m[0].reshape(-1, ring, wide).transpose(1, 0, 2) for m in (memory_keys, memory_values)], 2
    )
    memory = lax.all_to_all(after(memory, token_steps[-2]), "fsdp", 0, 0, tiled=True).reshape(-1, 2 * wide)
    down_full = lax.all_gather(jnp.concatenate(near_down, 0), DP, axis=0, tiled=True)

    cosine, sine = rotary_tables(length)
    qkv = project_qkv(gathered, gain_one, w_qkv, cosine, sine, heads)
    attended_heads, lse = attend_forward(chosen_all, counts_all, qkv, memory, heads, top)
    attended = lax.all_to_all(attended_heads, "fsdp", 0, 1, tiled=True)

    upstream = cotangent[0]
    mixed, grad_middle, grad_attended, gain_two_grad, grads, *grad_down = feed_forward(
        mine, attended, upstream, gain_two, first, down_full, span
    )
    grad_heads = lax.all_to_all(grad_attended, "fsdp", 1, 0, tiled=True)
    grads = lax.psum_scatter(grads, DP, scatter_dimension=0, tiled=True)[0]

    place = lax.axis_index("fsdp").astype(jnp.int32)
    count = length // min(2 * QBLK, length)
    is_last = (place < ring // 2).astype(jnp.int32)
    first_number = jnp.where(is_last == 1, count - 1, 0).astype(jnp.int32)
    low = 1 - is_last
    first_partial, first_grad, *sums = first_block(
        jnp.stack([first_number, is_last]), chosen_all, counts_all, qkv, memory, grad_heads, attended_heads, lse,
        cosine, sine, w_qkv, heads, top,
    )
    other_partial, other_grad = other_blocks(
        low.reshape(1), chosen_all, counts_all, qkv, memory, grad_heads, attended_heads, lse, cosine, sine, w_qkv,
        sums, heads, top,
    )
    grad_qkv = jnp.concatenate([first_grad, other_grad], 0)
    order = jnp.concatenate([first_number.reshape(1), low + jnp.arange(count - 1, dtype=jnp.int32)])
    block_rows = first_partial.shape[0]

    def term(step, index):
        start = jnp.clip(index, 0, ring - 1) * rows
        at = jnp.clip(start - low * block_rows, 0, other_partial.shape[0] - rows)
        near = jnp.clip(start - first_number * block_rows, 0, block_rows - rows)
        from_first = lax.dynamic_slice_in_dim(first_partial, near, rows, 0)
        if step == 0:
            return from_first.astype(F32)
        from_others = lax.dynamic_slice_in_dim(other_partial, at, rows, 0)
        inside = (start >= first_number * block_rows) & (start < (first_number + 1) * block_rows)
        return jnp.where(inside, from_first, from_others).astype(F32)

    own_term, arrived = chain_scatter(term, "fsdp")
    grads = after(grads, arrived[-1])

    grad_w_qkv, gain_one_grad = projection_grads(order, gathered, gain_one.reshape(width, 1), w_qkv, grad_qkv)
    gains = jnp.stack([gain_one_grad.reshape(span, -1), gain_two_grad.reshape(span, -1)], 1)
    gains = jnp.pad(gains.astype(BF16), ((0, 0), (0, extra - 2), (0, 3 * wide - gains.shape[2])))
    late = jnp.concatenate([grad_w_qkv.reshape(span, -1, 3 * wide), gains], 1)
    late = late.reshape(span // 2, 2, late.shape[1], 3 * wide)
    core = lax.axis_index("core")
    taken = lax.ppermute(lax.dynamic_index_in_dim(late, 1 - core, 1, keepdims=False), "core", [(0, 1), (1, 0)])
    late = lax.dynamic_index_in_dim(late, core, 1, keepdims=False).astype(F32) + taken.astype(F32)
    late = after(late.astype(BF16), arrived[0])
    late = sum(piece.astype(F32) for piece in direct_exchange(late, "chip")).astype(BF16)
    strip = grads.shape[1]
    lanes = width // strip
    tall = w_down.shape[0]
    if grad_down:
        down = lax.psum_scatter(grad_down[0], DP, scatter_dimension=0, tiled=True)
        down = down.reshape(ring, tall, lanes, strip).transpose(0, 2, 1, 3)
    else:
        down = grads[: ring * tall * lanes].reshape(lanes, ring, tall, strip).transpose(1, 0, 2, 3)
        grads = grads[ring * tall * lanes :]
    grads = grads.reshape(-1, ring, share, strip).transpose(1, 0, 2, 3)
    pieces = jnp.concatenate([down.reshape(ring, -1, strip), grads.reshape(ring, -1, strip)], 1)
    rising, falling = arrived[-1]
    grad_normed = own_term + rising.astype(F32) + falling.astype(F32)
    own = mine.astype(F32)
    factor = lax.rsqrt(jnp.mean(own * own, -1, keepdims=True) + EPSILON)
    scaled = grad_normed * gain_one
    inner = jnp.mean(scaled * own, -1, keepdims=True)
    tokens_grad = (grad_middle + factor * scaled - own * (factor * factor * factor * inner)).astype(BF16)

    gains = late[-extra : 2 - extra, : ring * share].reshape(2, ring, share).transpose(1, 0, 2)
    gains = jnp.pad(gains, ((0, 0), (0, extra - 2), (0, 3 * wide - share)))
    late = jnp.concatenate([late[:-extra].reshape(ring, share, 3 * wide), gains], 1)
    late = after(lax.all_to_all(late, "fsdp", 0, 0, tiled=True), tokens_grad).astype(F32)
    projections = [
        late[:, :share, part * wide : (part + 1) * wide].transpose(1, 0, 2).reshape(share, width)
        for part in range(3)
    ]
    gain_shares = jnp.sum(late[:, share : share + 2, :share], 0)

    pieces = lax.psum_scatter(pieces, "fsdp", scatter_dimension=0, tiled=True)
    pieces = after(pieces, (tokens_grad, projections, gain_shares))[0].astype(F32)
    down_share = pieces[: lanes * tall].reshape(lanes, tall, strip).transpose(1, 0, 2).reshape(tall, width)
    others = pieces[lanes * tall :].reshape(-1, share, strip).transpose(1, 0, 2).reshape(share, -1)
    return (
        mixed[None],
        tokens_grad[None],
        *projections,
        others[:, :width],
        others[:, width : width + hidden_width],
        others[:, width + hidden_width :],
        down_share,
        gain_shares[0],
        gain_shares[1],
    )


def solution(mesh):
    span, ring = mesh.shape["dp"], mesh.shape["fsdp"]
    fine = Mesh(mesh.devices.reshape(span // 2, 2, ring), DP + ("fsdp",))
    every = DP + ("fsdp",)
    rows, matrix, vector = P(DP, "fsdp", None), P(every, None), P(every)
    in_specs = (rows,) * 5 + (matrix,) * 7 + (vector,) * 2 + (rows,)
    out_specs = (rows,) * 2 + (matrix,) * 7 + (vector,) * 2
    return jax.shard_map(body, mesh=fine, in_specs=in_specs, out_specs=out_specs, check_vma=False)
```

```python
import functools
import math

import jax
import jax.numpy as jnp
import numpy as np
from jax import lax
from jax.experimental import pallas as pl
from jax.experimental.pallas import tpu as pltpu
from jax.sharding import Mesh
from jax.sharding import PartitionSpec as P

HEAD_DIM = 128
QBLK = 256
MBLK = 128
EPSILON = 1e-06
NEGATIVE = -1e30
SCALE = 1.0 / math.sqrt(HEAD_DIM)
LOG2E = math.log2(math.e)
MIB = 1 << 20
F32 = jnp.float32
BF16 = jnp.bfloat16
DP = ("chip", "core")
NT = (((1,), (1,)), ((), ()))
TN = (((0,), (0,)), ((), ()))


def dot(left, right, dims=(((1,), (0,)), ((), ()))):
    return lax.dot_general(left, right, dims, preferred_element_type=F32)


def rotary_tables(length):
    half_dim = HEAD_DIM // 2
    frequency = 10000.0 ** (-jnp.arange(half_dim, dtype=F32) / half_dim)
    angles = jnp.arange(length, dtype=jnp.int32).astype(F32)[:, None] * frequency[None, :]
    cosine, sine = jnp.cos(angles), jnp.sin(angles)
    return jnp.concatenate([cosine, cosine], 1), jnp.concatenate([-sine, sine], 1)


def qkv_kernel(heads, tok_ref, gain_ref, w_ref, cos_ref, sin_ref, qkv_ref):
    rows = tok_ref[...].astype(F32)
    factor = lax.rsqrt(jnp.mean(rows * rows, -1, keepdims=True) + EPSILON)
    normed = (rows * factor * gain_ref[...]).astype(BF16)
    cosine, sine = cos_ref[...], sin_ref[...]
    wide = heads * HEAD_DIM
    for part in range(3):
        values = dot(normed, w_ref[:, part * wide : (part + 1) * wide])
        for head in range(heads):
            value = values[:, head * HEAD_DIM : (head + 1) * HEAD_DIM]
            if part < 2:
                value = value * cosine + pltpu.roll(value, HEAD_DIM // 2, 1) * sine
            if part == 0:
                value = value * (SCALE * LOG2E)
            at = part * wide + head * HEAD_DIM
            qkv_ref[:, at : at + HEAD_DIM] = value.astype(BF16)


def project_qkv(tokens_all, gain, w_qkv, cosine, sine, heads):
    length, width = tokens_all.shape
    columns = w_qkv.shape[1]
    block = 2 * QBLK
    return pl.pallas_call(
        functools.partial(qkv_kernel, heads),
        grid=(length // block,),
        in_specs=[
            pl.BlockSpec((block, width), lambda i: (i, 0)),
            pl.BlockSpec((1, width), lambda i: (0, 0)),
            pl.BlockSpec((width, columns), lambda i: (0, 0)),
            pl.BlockSpec((block, HEAD_DIM), lambda i: (i, 0)),
            pl.BlockSpec((block, HEAD_DIM), lambda i: (i, 0)),
        ],
        out_specs=pl.BlockSpec((block, columns), lambda i: (i, 0)),
        out_shape=jax.ShapeDtypeStruct((length, columns), BF16),
        compiler_params=pltpu.CompilerParams(vmem_limit_bytes=48 * MIB),
        cost_estimate=pl.CostEstimate(
            flops=2 * length * width * columns, bytes_accessed=4 * length * (width + columns), transcendentals=0
        ),
        name="project_qkv",
    )(tokens_all, gain, w_qkv, cosine, sine)


def memory_bias(counts_ref, base, top, axis):
    shape = (1, top * MBLK) if axis == 1 else (top * MBLK, 1)
    column = lax.broadcasted_iota(jnp.int32, shape, axis)
    limit = jnp.zeros(shape, jnp.int32)
    for entry in range(top):
        inside = (column >= entry * MBLK) & (column < entry * MBLK + counts_ref[base + entry])
        limit = jnp.where(inside, 1, limit)
    return jnp.where(limit > 0, 0.0, NEGATIVE)


def pick_memory(ref, chosen_ref, base, top, columns):
    rows = [
        ref[pl.ds(pl.multiple_of(chosen_ref[base + entry] * MBLK, MBLK), MBLK), columns]
        for entry in range(top)
    ]
    return jnp.concatenate(rows, 0)


def forward_kernel(
    heads, top, chosen_ref, counts_ref, q_ref, k_ref, v_ref, mk_ref, mv_ref, out_ref, lse_ref, acc_s, peak_s
):
    block = pl.program_id(0)
    rows = q_ref.shape[0]
    subs = rows // QBLK
    ones = jnp.ones((rows, HEAD_DIM), BF16)
    mem_ones = jnp.ones((top * MBLK, HEAD_DIM), BF16)
    for sub in range(subs):
        base = (block * subs + sub) * top
        here = slice(sub * QBLK, (sub + 1) * QBLK)
        span = (sub + 1) * QBLK
        seen = pl.ds(pl.multiple_of(block * rows, rows), span)
        row = lax.broadcasted_iota(jnp.int32, (QBLK, span), 0) + sub * QBLK
        causal = row >= lax.broadcasted_iota(jnp.int32, (QBLK, span), 1)
        bias = memory_bias(counts_ref, base, top, 1)
        for head in range(heads):
            columns = slice(head * HEAD_DIM, (head + 1) * HEAD_DIM)
            query = q_ref[here, columns]
            remote = dot(query, pick_memory(mk_ref, chosen_ref, base, top, columns), NT) + bias
            local = jnp.where(causal, dot(query, k_ref[seen, columns], NT), NEGATIVE)
            peak = jnp.maximum(jnp.max(local, -1, keepdims=True), jnp.max(remote, -1, keepdims=True))
            values = jnp.concatenate([v_ref[seen, columns], ones[:span]], 1)
            acc = dot(jnp.exp2(local - peak).astype(BF16), values)
            values = jnp.concatenate([pick_memory(mv_ref, chosen_ref, base, top, columns), mem_ones], 1)
            acc_s[head, here] = acc + dot(jnp.exp2(remote - peak).astype(BF16), values)
            peak_s[head, here] = jnp.broadcast_to(peak, (QBLK, HEAD_DIM))

    def step(index, carry):
        there = pl.ds(pl.multiple_of(index * rows, rows), rows)
        for head in range(heads):
            columns = slice(head * HEAD_DIM, (head + 1) * HEAD_DIM)
            peak = peak_s[head][:, :1]
            scores = dot(q_ref[:, columns], k_ref[there, columns], NT)
            higher = jnp.maximum(peak, jnp.max(scores, -1, keepdims=True))
            weights = jnp.exp2(scores - higher).astype(BF16)
            values = jnp.concatenate([v_ref[there, columns], ones], 1)
            acc_s[head] = acc_s[head] * jnp.exp2(peak - higher) + dot(weights, values)
            peak_s[head] = jnp.broadcast_to(higher, (rows, HEAD_DIM))
        return carry

    lax.fori_loop(0, block, step, 0)
    for head in range(heads):
        columns = slice(head * HEAD_DIM, (head + 1) * HEAD_DIM)
        total = acc_s[head][:, HEAD_DIM:]
        out_ref[:, columns] = (acc_s[head][:, :HEAD_DIM] / total).astype(BF16)
        lse_ref[:, head : head + 1] = peak_s[head][:, :1] + jnp.log2(total[:, :1])


def attend_forward(chosen, counts, qkv, memory, heads, top):
    length = qkv.shape[0]
    wide = heads * HEAD_DIM
    rows = min(2 * QBLK, length)
    mem_rows = memory.shape[0]
    return pl.pallas_call(
        functools.partial(forward_kernel, heads, top),
        grid_spec=pltpu.PrefetchScalarGridSpec(
            num_scalar_prefetch=2,
            grid=(length // rows,),
            in_specs=[
                pl.BlockSpec((rows, wide), lambda i, *_: (i, 0)),
                pl.BlockSpec((length, wide), lambda i, *_: (0, 1)),
                pl.BlockSpec((length, wide), lambda i, *_: (0, 2)),
                pl.BlockSpec((mem_rows, wide), lambda i, *_: (0, 0)),
                pl.BlockSpec((mem_rows, wide), lambda i, *_: (0, 1)),
            ],
            out_specs=[
                pl.BlockSpec((rows, wide), lambda i, *_: (i, 0)),
                pl.BlockSpec((rows, heads), lambda i, *_: (i, 0)),
            ],
            scratch_shapes=[
                pltpu.VMEM((heads, rows, 2 * HEAD_DIM), F32),
                pltpu.VMEM((heads, rows, HEAD_DIM), F32),
            ],
        ),
        out_shape=[
            jax.ShapeDtypeStruct((length, wide), BF16),
            jax.ShapeDtypeStruct((length, heads), F32),
        ],
        compiler_params=pltpu.CompilerParams(vmem_limit_bytes=48 * MIB),
        cost_estimate=pl.CostEstimate(
            flops=4 * heads * length * HEAD_DIM * (length // 2 + top * MBLK),
            bytes_accessed=8 * length * wide,
            transcendentals=heads * length * (length // 2 + top * MBLK),
        ),
        name="attend_forward",
    )(chosen, counts, qkv, qkv, qkv, memory, memory)


def spread_rows(column):
    rows = column.shape[0]
    return jnp.transpose(jnp.broadcast_to(column, (rows, HEAD_DIM)))[:1]


def row_stats(grad_out, out, lse):
    delta = jnp.sum(grad_out.astype(F32) * out.astype(F32), -1, keepdims=True)
    return jnp.concatenate([spread_rows(lse), spread_rows(delta)], 0)


def score_grads(query, grad_out, stats, keys, values, mask):
    weights = jnp.exp2(mask(dot(keys, query, NT)) - stats[:1])
    grad_weights = dot(values, grad_out, NT)
    return weights.astype(BF16), (weights * (grad_weights - stats[1:2])).astype(BF16)


def causal_mask(rows):
    key_at = lax.broadcasted_iota(jnp.int32, (rows, rows), 0)
    query_at = lax.broadcasted_iota(jnp.int32, (rows, rows), 1)
    return lambda scores: jnp.where(query_at >= key_at, scores, NEGATIVE)


def memory_query_grad(chosen_ref, counts_ref, base, top, query, grad_out, stats, mk_ref, mv_ref, columns):
    keys = pick_memory(mk_ref, chosen_ref, base, top, columns)
    values = pick_memory(mv_ref, chosen_ref, base, top, columns)
    bias = memory_bias(counts_ref, base, top, 0)
    _, grad_scores = score_grads(query, grad_out, stats, keys, values, lambda scores: scores + bias)
    return dot(grad_scores, keys, TN)


def block_grads(heads, grad_query, grad_key, grad_value, cosine, sine):
    def unturn(value):
        return (value * cosine - pltpu.roll(value, HEAD_DIM // 2, 1) * sine).astype(BF16)

    parts = []
    for part, array in enumerate((grad_query * SCALE, grad_key * (1.0 / LOG2E), grad_value)):
        for head in range(heads):
            value = array[:, head * HEAD_DIM : (head + 1) * HEAD_DIM]
            parts.append(unturn(value) if part < 2 else value.astype(BF16))
    return jnp.concatenate(parts, 1)


def first_block_kernel(
    heads, top, chosen_ref, counts_ref, plan_ref, qkv_ref, mk_ref, mv_ref, go_ref, out_ref, lse_ref, cos_ref, sin_ref,
    w_ref, partial_ref, grad_ref, gq_ref, gk_ref, gv_ref, stats_s,
):
    rows = partial_ref.shape[0]
    subs = rows // QBLK
    wide = heads * HEAD_DIM
    others = go_ref.shape[0] // rows - 1
    block, is_last = plan_ref[0], plan_ref[1]
    own = pl.ds(pl.multiple_of(block * rows, rows), rows)
    gq_ref[...] = jnp.zeros_like(gq_ref)
    gk_ref[...] = jnp.zeros_like(gk_ref)
    gv_ref[...] = jnp.zeros_like(gv_ref)

    def note_stats(slot, here):
        for head in range(heads):
            columns = slice(head * HEAD_DIM, (head + 1) * HEAD_DIM)
            stats_s[slot, head] = row_stats(go_ref[here, columns], out_ref[here, columns], lse_ref[here, head : head + 1])

    note_stats(0, own)

    def pair(slot, queries, keys, mask):
        for head in range(heads):
            at = head * HEAD_DIM
            columns = slice(at, at + HEAD_DIM)
            query, grad_out = qkv_ref[queries, columns], go_ref[queries, columns]
            key = qkv_ref[keys, wide + at : wide + at + HEAD_DIM]
            value = qkv_ref[keys, 2 * wide + at : 2 * wide + at + HEAD_DIM]
            weights, grad_scores = score_grads(query, grad_out, stats_s[slot, head], key, value, mask)
            gk_ref[keys, columns] += dot(grad_scores, query)
            gv_ref[keys, columns] += dot(weights, grad_out)
            gq_ref[queries, columns] += dot(grad_scores, key, TN)

    for head in range(heads):
        columns = slice(head * HEAD_DIM, (head + 1) * HEAD_DIM)
        for sub in range(subs):
            here = pl.ds(pl.multiple_of(block * rows + sub * QBLK, QBLK), QBLK)
            gq_ref[here, columns] += memory_query_grad(
                chosen_ref, counts_ref, (block * subs + sub) * top, top, qkv_ref[here, columns], go_ref[here, columns],
                stats_s[0, head][:, sub * QBLK : (sub + 1) * QBLK], mk_ref, mv_ref, columns,
            )
    pair(0, own, own, causal_mask(rows))

    def step(index, carry):
        other = jnp.where(is_last == 1, index, index + 1)
        there = pl.ds(pl.multiple_of(other * rows, rows), rows)

        @pl.when(is_last == 1)
        def _():
            pair(0, own, there, lambda scores: scores)

        @pl.when(is_last == 0)
        def _():
            note_stats(1, there)
            pair(1, there, own, lambda scores: scores)

        return carry

    lax.fori_loop(0, others, step, 0)
    grad = block_grads(
        heads, gq_ref[own, :], gk_ref[own, :], gv_ref[own, :], cos_ref[...], sin_ref[...]
    )
    grad_ref[...] = grad
    partial_ref[...] = dot(grad, w_ref[...], NT).astype(BF16)


def first_block(plan, chosen, counts, qkv, memory, grad_out, out, lse, cosine, sine, w_qkv, heads, top):
    length = qkv.shape[0]
    width = w_qkv.shape[0]
    wide = heads * HEAD_DIM
    rows = min(2 * QBLK, length)
    mem_rows = memory.shape[0]

    def whole(array):
        return pl.BlockSpec(array.shape, lambda i, *_: (0, 0))

    sums = pl.BlockSpec((length, wide), lambda i, *_: (0, 0))
    return pl.pallas_call(
        functools.partial(first_block_kernel, heads, top),
        grid_spec=pltpu.PrefetchScalarGridSpec(
            num_scalar_prefetch=3,
            grid=(1,),
            in_specs=[
                whole(qkv),
                pl.BlockSpec((mem_rows, wide), lambda i, *_: (0, 0)),
                pl.BlockSpec((mem_rows, wide), lambda i, *_: (0, 1)),
                whole(grad_out),
                whole(out),
                whole(lse),
                pl.BlockSpec((rows, HEAD_DIM), lambda i, c, n, plan: (plan[0], 0)),
                pl.BlockSpec((rows, HEAD_DIM), lambda i, c, n, plan: (plan[0], 0)),
                whole(w_qkv),
            ],
            out_specs=[
                pl.BlockSpec((rows, width), lambda i, *_: (0, 0)),
                pl.BlockSpec((rows, 3 * wide), lambda i, *_: (0, 0)),
                sums,
                sums,
                sums,
            ],
            scratch_shapes=[pltpu.VMEM((2, heads, 2, rows), F32)],
        ),
        out_shape=[
            jax.ShapeDtypeStruct((rows, width), BF16),
            jax.ShapeDtypeStruct((rows, 3 * wide), BF16),
            *[jax.ShapeDtypeStruct((length, wide), F32)] * 3,
        ],
        compiler_params=pltpu.CompilerParams(vmem_limit_bytes=60 * MIB),
        cost_estimate=pl.CostEstimate(
            flops=4 * heads * length * HEAD_DIM * length,
            bytes_accessed=40 * length * wide,
            transcendentals=heads * length * rows,
        ),
        name="first_block",
    )(chosen, counts, plan, qkv, memory, memory, grad_out, out, lse, cosine, sine, w_qkv)


def other_blocks_kernel(
    heads, top, chosen_ref, counts_ref, plan_ref, q_ref, k_ref, v_ref, mk_ref, mv_ref, go_ref, out_ref, lse_ref,
    cos_ref, sin_ref, w_ref, gq_in, gk_in, gv_in, partial_ref, grad_ref, gk_s, gv_s, gq_s,
):
    low = plan_ref[0]
    block = low + pl.num_programs(0) - 1 - pl.program_id(0)
    rows = q_ref.shape[0]
    subs = rows // QBLK
    own = pl.ds(pl.multiple_of(block * rows, rows), rows)

    @pl.when(pl.program_id(0) == 0)
    def _():
        gk_s[...] = gk_in[...]
        gv_s[...] = gv_in[...]

    stats = []
    for head in range(heads):
        columns = slice(head * HEAD_DIM, (head + 1) * HEAD_DIM)
        stats.append(row_stats(go_ref[:, columns], out_ref[:, columns], lse_ref[:, head : head + 1]))
        for sub in range(subs):
            here = slice(sub * QBLK, (sub + 1) * QBLK)
            gq_s[here, columns] = gq_in[here, columns] + memory_query_grad(
                chosen_ref, counts_ref, (block * subs + sub) * top, top, q_ref[here, columns], go_ref[here, columns],
                stats[head][:, here], mk_ref, mv_ref, columns,
            )

    def local(there, mask):
        for head in range(heads):
            columns = slice(head * HEAD_DIM, (head + 1) * HEAD_DIM)
            query, grad_out = q_ref[:, columns], go_ref[:, columns]
            key = k_ref[there, columns]
            weights, grad_scores = score_grads(query, grad_out, stats[head], key, v_ref[there, columns], mask)
            gk_s[there, columns] += dot(grad_scores, query)
            gv_s[there, columns] += dot(weights, grad_out)
            gq_s[:, columns] += dot(grad_scores, key, TN)

    local(own, causal_mask(rows))

    def step(index, carry):
        local(pl.ds(pl.multiple_of(index * rows, rows), rows), lambda scores: scores)
        return carry

    lax.fori_loop(low, block, step, 0)
    grad = block_grads(heads, gq_s[...], gk_s[own, :], gv_s[own, :], cos_ref[...], sin_ref[...])
    grad_ref[...] = grad
    partial_ref[...] = dot(grad, w_ref[...], NT).astype(BF16)


def other_blocks(plan, chosen, counts, qkv, memory, grad_out, out, lse, cosine, sine, w_qkv, sums, heads, top):
    length = qkv.shape[0]
    width = w_qkv.shape[0]
    wide = heads * HEAD_DIM
    rows = min(2 * QBLK, length)
    count = length // rows - 1
    mem_rows = memory.shape[0]

    def by_rows(columns, at=0):
        return pl.BlockSpec((rows, columns), lambda i, c, n, plan: (plan[0] + count - 1 - i, at))

    def result(columns):
        return pl.BlockSpec((rows, columns), lambda i, *_: (count - 1 - i, 0))

    return pl.pallas_call(
        functools.partial(other_blocks_kernel, heads, top),
        grid_spec=pltpu.PrefetchScalarGridSpec(
            num_scalar_prefetch=3,
            grid=(count,),
            in_specs=[
                by_rows(wide),
                pl.BlockSpec((length, wide), lambda i, *_: (0, 1)),
                pl.BlockSpec((length, wide), lambda i, *_: (0, 2)),
                pl.BlockSpec((mem_rows, wide), lambda i, *_: (0, 0)),
                pl.BlockSpec((mem_rows, wide), lambda i, *_: (0, 1)),
                by_rows(wide),
                by_rows(wide),
                by_rows(heads),
                by_rows(HEAD_DIM),
                by_rows(HEAD_DIM),
                pl.BlockSpec((width, 3 * wide), lambda i, *_: (0, 0)),
                by_rows(wide),
                pl.BlockSpec((length, wide), lambda i, *_: (0, 0)),
                pl.BlockSpec((length, wide), lambda i, *_: (0, 0)),
            ],
            out_specs=[result(width), result(3 * wide)],
            scratch_shapes=[
                pltpu.VMEM((length, wide), F32),
                pltpu.VMEM((length, wide), F32),
                pltpu.VMEM((rows, wide), F32),
            ],
        ),
        out_shape=[
            jax.ShapeDtypeStruct((count * rows, width), BF16),
            jax.ShapeDtypeStruct((count * rows, 3 * wide), BF16),
        ],
        compiler_params=pltpu.CompilerParams(vmem_limit_bytes=60 * MIB),
        cost_estimate=pl.CostEstimate(
            flops=6 * heads * length * HEAD_DIM * (length + top * MBLK),
            bytes_accessed=40 * length * wide,
            transcendentals=heads * length * (length // 3 + top * MBLK),
        ),
        name="other_blocks",
    )(chosen, counts, plan, qkv, qkv, qkv, memory, memory, grad_out, out, lse, cosine, sine, w_qkv, *sums)


def ffn_kernel(
    span, merged, tok_ref, att_ref, cot_ref, gain_ref, out_w, gate_w, up_w, down_w,
    mixed_ref, grad_mid_ref, grad_att_ref, gain_grad_ref, out_grads_ref, grads_ref, *rest,
):
    if not merged:
        down_grads_ref, rest = rest[0], rest[1:]
    middle_s, normed_s, turned_s, mixed_s, upstream_s, gate_s, up_s, down_s, out_s, sems, late_sems = rest
    step, steps = pl.program_id(0), pl.num_programs(0)
    width = tok_ref.shape[1]
    share = width // span
    wide = gate_w.shape[1]
    hidden_width = down_s.shape[0]
    tall = hidden_width // span
    lanes = width // wide
    first = tall * lanes if merged else 0
    slot = step % 2

    @pl.when(step == 0)
    def _():
        middle = tok_ref[...].astype(F32) + dot(att_ref[...], out_w[...])
        middle_s[...] = middle
        factor = lax.rsqrt(jnp.mean(middle * middle, -1, keepdims=True) + EPSILON)
        normed = (middle * factor * gain_ref[...]).astype(BF16)
        normed_s[...] = normed
        turned_s[...] = jnp.transpose(normed)
        mixed_s[...] = middle
        upstream_s[...] = jnp.zeros_like(upstream_s)

    def copy_out(kind, which, index):
        source = (gate_s, up_s)[kind].at[which]
        start = first + (kind * steps + index) * share
        target = grads_ref.at[:, pl.ds(start, share), :]
        return pltpu.make_async_copy(source, target, sems.at[kind, which])

    normed = normed_s[...]
    upstream = cot_ref[...]
    both = jnp.concatenate([gate_w[...], up_w[...]], 1)
    acts = dot(normed, both)
    gate_act, up_act = acts[:, :wide], acts[:, wide:]
    grad_hidden = dot(upstream, down_w[...], NT)
    sigmoid = jax.nn.sigmoid(gate_act)
    silu = gate_act * sigmoid
    hidden = (silu * up_act).astype(BF16)
    grad_gate = (grad_hidden * up_act * sigmoid * (1.0 + gate_act * (1.0 - sigmoid))).astype(BF16)
    grad_up = (grad_hidden * silu).astype(BF16)
    mixed_s[...] += dot(hidden, down_w[...])
    grad_acts = jnp.concatenate([grad_gate, grad_up], 1)
    upstream_s[...] += dot(grad_acts, both, NT)
    down_s[pl.ds(pl.multiple_of(step * wide, wide), wide), :] = dot(hidden, upstream, TN).astype(BF16)

    @pl.when(step >= 2)
    def _():
        copy_out(0, slot, step - 2).wait()
        copy_out(1, slot, step - 2).wait()

    weight_grads = dot(turned_s[...], grad_acts).astype(BF16)
    gate_s[slot] = weight_grads[:, :wide].reshape(span, share, wide)
    up_s[slot] = weight_grads[:, wide:].reshape(span, share, wide)
    copy_out(0, slot, step).start()
    copy_out(1, slot, step).start()

    @pl.when(step == steps - 1)
    def _():
        copies = []
        if merged:
            for place in range(span):
                for lane in range(lanes):
                    copies.append(
                        pltpu.make_async_copy(
                            down_s.at[pl.ds(place * tall, tall), pl.ds(lane * wide, wide)],
                            grads_ref.at[place, pl.ds(lane * tall, tall), :],
                            late_sems.at[len(copies)],
                        )
                    )
        else:
            copies.append(pltpu.make_async_copy(down_s, down_grads_ref, late_sems.at[0]))
        for copy in copies:
            copy.start()
        mixed_ref[...] = mixed_s[...].astype(BF16)
        middle = middle_s[...]
        grad = upstream_s[...]
        factor = lax.rsqrt(jnp.mean(middle * middle, -1, keepdims=True) + EPSILON)
        gain_grad_ref[...] = jnp.sum(grad * middle * factor, 0, keepdims=True)
        scaled = grad * gain_ref[...]
        inner = jnp.mean(scaled * middle, -1, keepdims=True)
        grad_middle = cot_ref[...].astype(F32) + factor * scaled - middle * (factor * factor * factor * inner)
        grad_mid_ref[...] = grad_middle
        branch = grad_middle.astype(BF16)
        grad_att_ref[...] = dot(branch, out_w[...], NT).astype(BF16)
        turned_att = jnp.transpose(att_ref[...])
        for lane in range(lanes):
            columns = slice(lane * wide, (lane + 1) * wide)
            out_s[lane] = dot(turned_att, branch[:, columns]).astype(BF16).reshape(span, share, wide)
            more = pltpu.make_async_copy(
                out_s.at[lane],
                out_grads_ref.at[:, :, pl.ds(lane * wide, wide)],
                late_sems.at[len(copies)],
            )
            more.start()
            copies.append(more)
        for copy in copies:
            copy.wait()
        copy_out(0, 1 - slot, step - 1).wait()
        copy_out(1, 1 - slot, step - 1).wait()
        copy_out(0, slot, step).wait()
        copy_out(1, slot, step).wait()


def feed_forward(tokens, attended, upstream, gain, weights, w_down, span):
    rows, width = tokens.shape
    hidden_width = w_down.shape[0]
    wide = 2 * HEAD_DIM
    steps = hidden_width // wide
    lanes = width // wide
    share = width // span
    tall = hidden_width // span
    merged = tall % 16 == 0
    total = 2 * steps * share + (lanes * tall if merged else 0)
    shapes = [
        jax.ShapeDtypeStruct((rows, width), BF16),
        jax.ShapeDtypeStruct((rows, width), F32),
        jax.ShapeDtypeStruct((rows, width), BF16),
        jax.ShapeDtypeStruct((1, width), F32),
        jax.ShapeDtypeStruct((span, share, width), BF16),
        jax.ShapeDtypeStruct((span, total, wide), BF16),
    ]
    specs = [
        pl.BlockSpec((rows, width), lambda i: (0, 0)),
        pl.BlockSpec((rows, width), lambda i: (0, 0)),
        pl.BlockSpec((rows, width), lambda i: (0, 0)),
        pl.BlockSpec((1, width), lambda i: (0, 0)),
        pl.BlockSpec(memory_space=pl.ANY),
        pl.BlockSpec(memory_space=pl.ANY),
    ]
    if not merged:
        shapes.append(jax.ShapeDtypeStruct((hidden_width, width), BF16))
        specs.append(pl.BlockSpec(memory_space=pl.ANY))
    return pl.pallas_call(
        functools.partial(ffn_kernel, span, merged),
        grid=(steps,),
        in_specs=[
            pl.BlockSpec((rows, width), lambda i: (0, 0)),
            pl.BlockSpec((rows, width), lambda i: (0, 0)),
            pl.BlockSpec((rows, width), lambda i: (0, 0)),
            pl.BlockSpec((1, width), lambda i: (0, 0)),
            pl.BlockSpec((width, width), lambda i: (0, 0)),
            pl.BlockSpec((width, wide), lambda i: (0, lanes + i)),
            pl.BlockSpec((width, wide), lambda i: (0, lanes + steps + i)),
            pl.BlockSpec((wide, width), lambda i: (i, 0)),
        ],
        out_specs=specs,
        out_shape=shapes,
        scratch_shapes=[
            pltpu.VMEM((rows, width), F32),
            pltpu.VMEM((rows, width), BF16),
            pltpu.VMEM((width, rows), BF16),
            pltpu.VMEM((rows, width), F32),
            pltpu.VMEM((rows, width), F32),
            pltpu.VMEM((2, span, share, wide), BF16),
            pltpu.VMEM((2, span, share, wide), BF16),
            pltpu.VMEM((hidden_width, width), BF16),
            pltpu.VMEM((lanes, span, share, wide), BF16),
            pltpu.SemaphoreType.DMA((2, 2)),
            pltpu.SemaphoreType.DMA(((span * lanes if merged else 1) + lanes,)),
        ],
        compiler_params=pltpu.CompilerParams(vmem_limit_bytes=56 * MIB),
        cost_estimate=pl.CostEstimate(
            flops=6 * rows * width * (3 * hidden_width + width),
            bytes_accessed=4 * width * (3 * hidden_width + width),
            transcendentals=rows * hidden_width,
        ),
        name="feed_forward",
    )(tokens, attended, upstream, gain, weights, weights, weights, w_down)


def projection_grads_kernel(
    order_ref, tok_ref, gain_ref, w_ref, first_ref, other_ref, grad_w_ref, gain_grad_ref, raw_s
):
    step = pl.program_id(0)

    @pl.when(step == 0)
    def _():
        raw_s[...] = jnp.zeros_like(raw_s)

    tokens = tok_ref[...].astype(F32)
    tokens = tokens * lax.rsqrt(jnp.mean(tokens * tokens, -1, keepdims=True) + EPSILON)
    grad = jnp.where(step == 0, first_ref[...], other_ref[...])
    raw_s[...] += dot(tokens.astype(BF16), grad, TN)

    @pl.when(step == pl.num_programs(0) - 1)
    def _():
        raw = raw_s[...]
        gain_grad_ref[...] = jnp.sum(raw * w_ref[...].astype(F32), -1, keepdims=True)
        grad_w_ref[...] = (raw * gain_ref[...]).astype(BF16)


def projection_grads(order, tokens_all, gain_column, w_qkv, first_grad, other_grad):
    length, width = tokens_all.shape
    columns = first_grad.shape[1]
    rows = min(2 * QBLK, length)
    return pl.pallas_call(
        projection_grads_kernel,
        grid_spec=pltpu.PrefetchScalarGridSpec(
            num_scalar_prefetch=1,
            grid=(length // rows,),
            in_specs=[
                pl.BlockSpec((rows, width), lambda i, order: (order[i], 0)),
                pl.BlockSpec((width, 1), lambda i, _: (0, 0)),
                pl.BlockSpec((width, columns), lambda i, _: (0, 0)),
                pl.BlockSpec((rows, columns), lambda i, _: (0, 0)),
                pl.BlockSpec((rows, columns), lambda i, _: (jnp.maximum(i - 1, 0), 0)),
            ],
            out_specs=[
                pl.BlockSpec((width, columns), lambda i, _: (0, 0)),
                pl.BlockSpec((width, 1), lambda i, _: (0, 0)),
            ],
            scratch_shapes=[pltpu.VMEM((width, columns), F32)],
        ),
        out_shape=[
            jax.ShapeDtypeStruct((width, columns), BF16),
            jax.ShapeDtypeStruct((width, 1), F32),
        ],
        compiler_params=pltpu.CompilerParams(vmem_limit_bytes=48 * MIB),
        cost_estimate=pl.CostEstimate(
            flops=2 * length * width * columns, bytes_accessed=2 * length * (width + columns), transcendentals=0
        ),
        name="projection_grads",
    )(order, tokens_all, gain_column, w_qkv, first_grad, other_grad)


def after(value, earlier):
    return lax.optimization_barrier((value, earlier))[0]


def chain_gather(blocks, axis):
    size = lax.axis_size(axis)
    place = lax.axis_index(axis)
    steps = []
    rising = falling = tuple(blocks)
    for step in range(size - 1):
        up = [(i, i + 1) for i in range(step, size - 1)]
        down = [(i + 1, i) for i in range(size - 1 - step)]
        rising = tuple(lax.ppermute(block, axis, up) for block in rising)
        falling = tuple(lax.ppermute(block, axis, down) for block in falling)
        if len(blocks) > 1:
            rising, falling = lax.optimization_barrier((rising, falling))
        steps.append((rising, falling))
    results = []
    for number, block in enumerate(blocks):
        ordered = []
        for index in range(size):
            cases = []
            for mine in range(size):
                if mine == index:
                    cases.append(block)
                elif mine > index:
                    cases.append(steps[mine - index - 1][0][number])
                else:
                    cases.append(steps[index - mine - 1][1][number])
            ordered.append(lax.select_n(place, *cases) if size > 2 else lax.select_n(place > 0, *cases))
        results.append(ordered)
    return results, steps


def chain_scatter(block, axis, waits):
    size = lax.axis_size(axis)
    place = lax.axis_index(axis)
    arrived = []
    for step in range(size - 1):
        up, down = block(step, size - 1 - step + place), block(step, step - size + 1 + place)
        if step:
            up, down = up + arrived[-1][0].astype(F32), down + arrived[-1][1].astype(F32)
        ready = waits[step - 1](sent) if 0 < step <= len(waits) else None
        up, down, _ = lax.optimization_barrier((up.astype(BF16), down.astype(BF16), ready))
        sent = up, down
        rising = lax.ppermute(up, axis, [(i, i + 1) for i in range(step + 1)])
        falling = lax.ppermute(down, axis, [(i, i - 1) for i in range(size - 1 - step, size)])
        arrived.append(lax.optimization_barrier((rising, falling)))
    return block(size, place), arrived


def direct_exchange(blocks, axis):
    size = lax.axis_size(axis)
    place = lax.axis_index(axis)
    taken = [lax.dynamic_index_in_dim(blocks, place, 0, keepdims=False)]
    for far in range(1, size):
        give = lax.dynamic_index_in_dim(blocks, (place + far) % size, 0, keepdims=False)
        taken.append(lax.ppermute(give, axis, [(i, (i + far) % size) for i in range(size)]))
    return taken


def body(
    tokens, memory_keys, memory_values, chosen, counts, w_query, w_key, w_value, w_out, w_gate, w_up, w_down,
    gain_attn, gain_ffn, cotangent,
):
    ring, span = lax.axis_size("fsdp"), lax.axis_size(DP)
    rows, width = tokens.shape[1:]
    heads = width // HEAD_DIM // ring
    wide = heads * HEAD_DIM
    length = rows * ring
    top = chosen.shape[2]
    hidden_width = w_gate.shape[1]
    share = w_query.shape[0]
    mine = tokens[0]

    extra = 8 if share % 8 == 0 else 8 - share % 8
    parts = [w.reshape(share, ring, wide).transpose(1, 0, 2) for w in (w_query, w_key, w_value)]
    choices = jnp.concatenate([chosen[0].reshape(-1), counts[0].reshape(-1)]).astype(BF16)
    notes = jnp.stack(
        [
            jnp.pad(row, (0, 3 * wide - row.shape[0]))
            for row in (jnp.concatenate([gain_attn, gain_ffn]), choices)
        ]
    )
    notes = jnp.broadcast_to(jnp.pad(notes, ((0, extra - 2), (0, 0))), (ring, extra, 3 * wide))
    parcel = jnp.concatenate([jnp.concatenate(parts, 2), notes], 1)
    parcel = lax.all_to_all(parcel, "fsdp", 0, 0, tiled=True)
    picks = parcel[:, share + 1, : choices.shape[0]].astype(jnp.int32).reshape(ring, 2, -1)
    chosen_all, counts_all = picks[:, 0].reshape(-1), picks[:, 1].reshape(-1)
    shards = jnp.concatenate([w_out, w_gate, w_up], 1)
    (near, near_down), steps = chain_gather((shards, w_down), "fsdp")
    (gathered,), token_steps = chain_gather((after(mine, steps[-2]),), "fsdp")
    parcel = lax.all_gather(after(parcel, steps[0]), DP, axis=0, tiled=True)
    w_qkv = parcel[:, :share].reshape(width, 3 * wide)
    gain_one = parcel[:, share, :share].reshape(1, width).astype(F32)
    gain_two = parcel[:, share, share : 2 * share].reshape(1, width).astype(F32)
    first = lax.all_gather(jnp.concatenate(near, 0), DP, axis=0, tiled=True)
    gathered = jnp.concatenate(gathered, 0)

    memory = jnp.concatenate(
        [m[0].reshape(-1, ring, wide).transpose(1, 0, 2) for m in (memory_keys, memory_values)], 2
    )
    memory = lax.all_to_all(after(memory, token_steps[-2]), "fsdp", 0, 0, tiled=True).reshape(-1, 2 * wide)
    down_full = lax.all_gather(jnp.concatenate(near_down, 0), DP, axis=0, tiled=True)

    cosine, sine = rotary_tables(length)
    qkv = project_qkv(gathered, gain_one, w_qkv, cosine, sine, heads)
    attended_heads, lse = attend_forward(chosen_all, counts_all, qkv, memory, heads, top)
    attended = lax.all_to_all(attended_heads, "fsdp", 0, 1, tiled=True)

    upstream = cotangent[0]
    mixed, grad_middle, grad_attended, gain_two_grad, out_grads, grads, *grad_down = feed_forward(
        mine, attended, upstream, gain_two, first, down_full, span
    )
    grad_heads = lax.all_to_all(grad_attended, "fsdp", 1, 0, tiled=True)
    grads = lax.psum_scatter(grads, DP, scatter_dimension=0, tiled=True)[0]

    core = lax.axis_index("core")

    def over_cores(array):
        array = array.reshape((span // 2, 2) + array.shape[1:])
        taken = lax.ppermute(lax.dynamic_index_in_dim(array, 1 - core, 1, keepdims=False), "core", [(0, 1), (1, 0)])
        return (lax.dynamic_index_in_dim(array, core, 1, keepdims=False).astype(F32) + taken.astype(F32)).astype(BF16)

    def over_chips(array):
        return sum(piece.astype(F32) for piece in direct_exchange(array, "chip")).astype(BF16)

    out_grads = over_cores(out_grads)
    grad_heads = after(grad_heads, out_grads)
    out_grads = over_chips(out_grads)

    place = lax.axis_index("fsdp").astype(jnp.int32)
    count = length // min(2 * QBLK, length)
    is_last = (place < ring // 2).astype(jnp.int32)
    first_number = jnp.where(is_last == 1, count - 1, 0).astype(jnp.int32)
    low = 1 - is_last
    first_partial, first_grad, *sums = first_block(
        jnp.stack([first_number, is_last]), chosen_all, counts_all, qkv, memory, grad_heads, attended_heads, lse,
        cosine, sine, w_qkv, heads, top,
    )
    other_partial, other_grad = other_blocks(
        low.reshape(1), chosen_all, counts_all, qkv, memory, grad_heads, attended_heads, lse, cosine, sine, w_qkv,
        sums, heads, top,
    )
    order = jnp.concatenate([first_number.reshape(1), low + jnp.arange(count - 1, dtype=jnp.int32)])
    block_rows = first_partial.shape[0]

    def term(step, index):
        start = jnp.clip(index, 0, ring - 1) * rows
        at = jnp.clip(start - low * block_rows, 0, other_partial.shape[0] - rows)
        near = jnp.clip(start - first_number * block_rows, 0, block_rows - rows)
        from_first = lax.dynamic_slice_in_dim(first_partial, near, rows, 0)
        if step == 0:
            return from_first.astype(F32)
        from_others = lax.dynamic_slice_in_dim(other_partial, at, rows, 0)
        inside = (start >= first_number * block_rows) & (start < (first_number + 1) * block_rows)
        return jnp.where(inside, from_first, from_others).astype(F32)

    kept = []

    def make_projection_grads(sent):
        kept.extend(
            projection_grads(
                order, gathered, gain_one.reshape(width, 1), w_qkv, after(first_grad, sent), after(other_grad, sent)
            )
        )
        return kept

    own_term, arrived = chain_scatter(term, "fsdp", [lambda sent: out_grads, make_projection_grads])
    grad_w_qkv, gain_one_grad = kept
    grads = after(grads, arrived[-1])

    gains = jnp.stack([gain_one_grad.reshape(span, -1), gain_two_grad.reshape(span, -1)], 1)
    gains = jnp.pad(gains.astype(BF16), ((0, 0), (0, extra - 2), (0, 3 * wide - gains.shape[2])))
    late = jnp.concatenate([grad_w_qkv.reshape(span, -1, 3 * wide), gains], 1)
    late = over_chips(after(over_cores(late), arrived[0]))
    strip = grads.shape[1]
    lanes = width // strip
    tall = w_down.shape[0]
    if grad_down:
        down = lax.psum_scatter(grad_down[0], DP, scatter_dimension=0, tiled=True)
        down = down.reshape(ring, tall, lanes, strip).transpose(0, 2, 1, 3)
    else:
        down = grads[: ring * tall * lanes].reshape(lanes, ring, tall, strip).transpose(1, 0, 2, 3)
        grads = grads[ring * tall * lanes :]
    grads = grads.reshape(-1, ring, share, strip).transpose(1, 0, 2, 3)
    pieces = jnp.concatenate([down.reshape(ring, -1, strip), grads.reshape(ring, -1, strip)], 1)
    rising, falling = arrived[-1]
    grad_normed = own_term + rising.astype(F32) + falling.astype(F32)
    own = mine.astype(F32)
    factor = lax.rsqrt(jnp.mean(own * own, -1, keepdims=True) + EPSILON)
    scaled = grad_normed * gain_one
    inner = jnp.mean(scaled * own, -1, keepdims=True)
    tokens_grad = (grad_middle + factor * scaled - own * (factor * factor * factor * inner)).astype(BF16)

    gains = late[-extra : 2 - extra, : ring * share].reshape(2, ring, share).transpose(1, 0, 2)
    gains = jnp.pad(gains, ((0, 0), (0, extra - 2), (0, 3 * wide - share)))
    late = jnp.concatenate([late[:-extra].reshape(ring, share, 3 * wide), gains], 1)
    out_grads = jnp.pad(out_grads.reshape(ring, share, width), ((0, 0), (0, extra), (0, 0)))
    late = jnp.concatenate([late, out_grads], 2)
    late = after(lax.all_to_all(late, "fsdp", 0, 0, tiled=True), tokens_grad).astype(F32)
    out_share = jnp.sum(late[:, :share, 3 * wide :], 0)
    projections = [
        late[:, :share, part * wide : (part + 1) * wide].transpose(1, 0, 2).reshape(share, width)
        for part in range(3)
    ]
    gain_shares = jnp.sum(late[:, share : share + 2, :share], 0)

    pieces = lax.psum_scatter(pieces, "fsdp", scatter_dimension=0, tiled=True)
    pieces = after(pieces, (tokens_grad, projections, out_share, gain_shares))[0].astype(F32)
    down_share = pieces[: lanes * tall].reshape(lanes, tall, strip).transpose(1, 0, 2).reshape(tall, width)
    others = pieces[lanes * tall :].reshape(-1, share, strip).transpose(1, 0, 2).reshape(share, -1)
    return (
        mixed[None],
        tokens_grad[None],
        *projections,
        out_share,
        others[:, :hidden_width],
        others[:, hidden_width:],
        down_share,
        gain_shares[0],
        gain_shares[1],
    )


def solution(mesh):
    span, ring = mesh.shape["dp"], mesh.shape["fsdp"]
    fine = Mesh(mesh.devices.reshape(span // 2, 2, ring), DP + ("fsdp",))
    every = DP + ("fsdp",)
    rows, matrix, vector = P(DP, "fsdp", None), P(every, None), P(every)
    in_specs = (rows,) * 5 + (matrix,) * 7 + (vector,) * 2 + (rows,)
    out_specs = (rows,) * 2 + (matrix,) * 7 + (vector,) * 2
    return jax.shard_map(body, mesh=fine, in_specs=in_specs, out_specs=out_specs, check_vma=False)
```

```python
import functools
import math

import jax
import jax.numpy as jnp
import numpy as np
from jax import lax
from jax.experimental import pallas as pl
from jax.experimental.pallas import tpu as pltpu
from jax.sharding import Mesh
from jax.sharding import PartitionSpec as P

HEAD_DIM = 128
QBLK = 256
MBLK = 128
EPSILON = 1e-06
NEGATIVE = -1e30
SCALE = 1.0 / math.sqrt(HEAD_DIM)
LOG2E = math.log2(math.e)
MIB = 1 << 20
F32 = jnp.float32
BF16 = jnp.bfloat16
DP = ("chip", "core")
NT = (((1,), (1,)), ((), ()))
TN = (((0,), (0,)), ((), ()))


def dot(left, right, dims=(((1,), (0,)), ((), ()))):
    return lax.dot_general(left, right, dims, preferred_element_type=F32)


def rotary_tables(length):
    half_dim = HEAD_DIM // 2
    frequency = 10000.0 ** (-jnp.arange(half_dim, dtype=F32) / half_dim)
    angles = jnp.arange(length, dtype=jnp.int32).astype(F32)[:, None] * frequency[None, :]
    cosine, sine = jnp.cos(angles), jnp.sin(angles)
    return jnp.concatenate([cosine, cosine], 1), jnp.concatenate([-sine, sine], 1)


def qkv_kernel(heads, tok_ref, gain_ref, w_ref, cos_ref, sin_ref, qkv_ref):
    rows = tok_ref[...].astype(F32)
    factor = lax.rsqrt(jnp.mean(rows * rows, -1, keepdims=True) + EPSILON)
    normed = (rows * factor * gain_ref[...]).astype(BF16)
    cosine, sine = cos_ref[...], sin_ref[...]
    wide = heads * HEAD_DIM
    for part in range(3):
        values = dot(normed, w_ref[:, part * wide : (part + 1) * wide])
        for head in range(heads):
            value = values[:, head * HEAD_DIM : (head + 1) * HEAD_DIM]
            if part < 2:
                value = value * cosine + pltpu.roll(value, HEAD_DIM // 2, 1) * sine
            if part == 0:
                value = value * (SCALE * LOG2E)
            at = part * wide + head * HEAD_DIM
            qkv_ref[:, at : at + HEAD_DIM] = value.astype(BF16)


def project_qkv(tokens_all, gain, w_qkv, cosine, sine, heads):
    length, width = tokens_all.shape
    columns = w_qkv.shape[1]
    block = 2 * QBLK
    return pl.pallas_call(
        functools.partial(qkv_kernel, heads),
        grid=(length // block,),
        in_specs=[
            pl.BlockSpec((block, width), lambda i: (i, 0)),
            pl.BlockSpec((1, width), lambda i: (0, 0)),
            pl.BlockSpec((width, columns), lambda i: (0, 0)),
            pl.BlockSpec((block, HEAD_DIM), lambda i: (i, 0)),
            pl.BlockSpec((block, HEAD_DIM), lambda i: (i, 0)),
        ],
        out_specs=pl.BlockSpec((block, columns), lambda i: (i, 0)),
        out_shape=jax.ShapeDtypeStruct((length, columns), BF16),
        compiler_params=pltpu.CompilerParams(vmem_limit_bytes=48 * MIB),
        cost_estimate=pl.CostEstimate(
            flops=2 * length * width * columns, bytes_accessed=4 * length * (width + columns), transcendentals=0
        ),
        name="project_qkv",
    )(tokens_all, gain, w_qkv, cosine, sine)


def memory_bias(counts_ref, base, top, axis):
    shape = (1, top * MBLK) if axis == 1 else (top * MBLK, 1)
    column = lax.broadcasted_iota(jnp.int32, shape, axis)
    limit = jnp.zeros(shape, jnp.int32)
    for entry in range(top):
        inside = (column >= entry * MBLK) & (column < entry * MBLK + counts_ref[base + entry])
        limit = jnp.where(inside, 1, limit)
    return jnp.where(limit > 0, 0.0, NEGATIVE)


def pick_memory(ref, chosen_ref, base, top, columns):
    rows = [
        ref[pl.ds(pl.multiple_of(chosen_ref[base + entry] * MBLK, MBLK), MBLK), columns]
        for entry in range(top)
    ]
    return jnp.concatenate(rows, 0)


def forward_kernel(
    heads, top, chosen_ref, counts_ref, q_ref, k_ref, v_ref, mk_ref, mv_ref, out_ref, lse_ref, acc_s, peak_s
):
    block = pl.program_id(0)
    rows = q_ref.shape[0]
    subs = rows // QBLK
    ones = jnp.ones((rows, HEAD_DIM), BF16)
    mem_ones = jnp.ones((top * MBLK, HEAD_DIM), BF16)
    for sub in range(subs):
        base = (block * subs + sub) * top
        here = slice(sub * QBLK, (sub + 1) * QBLK)
        span = (sub + 1) * QBLK
        seen = pl.ds(pl.multiple_of(block * rows, rows), span)
        row = lax.broadcasted_iota(jnp.int32, (QBLK, span), 0) + sub * QBLK
        causal = row >= lax.broadcasted_iota(jnp.int32, (QBLK, span), 1)
        bias = memory_bias(counts_ref, base, top, 1)
        for head in range(heads):
            columns = slice(head * HEAD_DIM, (head + 1) * HEAD_DIM)
            query = q_ref[here, columns]
            remote = dot(query, pick_memory(mk_ref, chosen_ref, base, top, columns), NT) + bias
            local = jnp.where(causal, dot(query, k_ref[seen, columns], NT), NEGATIVE)
            peak = jnp.maximum(jnp.max(local, -1, keepdims=True), jnp.max(remote, -1, keepdims=True))
            values = jnp.concatenate([v_ref[seen, columns], ones[:span]], 1)
            acc = dot(jnp.exp2(local - peak).astype(BF16), values)
            values = jnp.concatenate([pick_memory(mv_ref, chosen_ref, base, top, columns), mem_ones], 1)
            acc_s[head, here] = acc + dot(jnp.exp2(remote - peak).astype(BF16), values)
            peak_s[head, here] = jnp.broadcast_to(peak, (QBLK, HEAD_DIM))

    def step(index, carry):
        there = pl.ds(pl.multiple_of(index * rows, rows), rows)
        for head in range(heads):
            columns = slice(head * HEAD_DIM, (head + 1) * HEAD_DIM)
            peak = peak_s[head][:, :1]
            scores = dot(q_ref[:, columns], k_ref[there, columns], NT)
            higher = jnp.maximum(peak, jnp.max(scores, -1, keepdims=True))
            weights = jnp.exp2(scores - higher).astype(BF16)
            values = jnp.concatenate([v_ref[there, columns], ones], 1)
            acc_s[head] = acc_s[head] * jnp.exp2(peak - higher) + dot(weights, values)
            peak_s[head] = jnp.broadcast_to(higher, (rows, HEAD_DIM))
        return carry

    lax.fori_loop(0, block, step, 0)
    for head in range(heads):
        columns = slice(head * HEAD_DIM, (head + 1) * HEAD_DIM)
        total = acc_s[head][:, HEAD_DIM:]
        out_ref[:, columns] = (acc_s[head][:, :HEAD_DIM] / total).astype(BF16)
        lse_ref[:, head : head + 1] = peak_s[head][:, :1] + jnp.log2(total[:, :1])


def attend_forward(chosen, counts, qkv, memory, heads, top):
    length = qkv.shape[0]
    wide = heads * HEAD_DIM
    rows = min(2 * QBLK, length)
    mem_rows = memory.shape[0]
    return pl.pallas_call(
        functools.partial(forward_kernel, heads, top),
        grid_spec=pltpu.PrefetchScalarGridSpec(
            num_scalar_prefetch=2,
            grid=(length // rows,),
            in_specs=[
                pl.BlockSpec((rows, wide), lambda i, *_: (i, 0)),
                pl.BlockSpec((length, wide), lambda i, *_: (0, 1)),
                pl.BlockSpec((length, wide), lambda i, *_: (0, 2)),
                pl.BlockSpec((mem_rows, wide), lambda i, *_: (0, 0)),
                pl.BlockSpec((mem_rows, wide), lambda i, *_: (0, 1)),
            ],
            out_specs=[
                pl.BlockSpec((rows, wide), lambda i, *_: (i, 0)),
                pl.BlockSpec((rows, heads), lambda i, *_: (i, 0)),
            ],
            scratch_shapes=[
                pltpu.VMEM((heads, rows, 2 * HEAD_DIM), F32),
                pltpu.VMEM((heads, rows, HEAD_DIM), F32),
            ],
        ),
        out_shape=[
            jax.ShapeDtypeStruct((length, wide), BF16),
            jax.ShapeDtypeStruct((length, heads), F32),
        ],
        compiler_params=pltpu.CompilerParams(vmem_limit_bytes=48 * MIB),
        cost_estimate=pl.CostEstimate(
            flops=4 * heads * length * HEAD_DIM * (length // 2 + top * MBLK),
            bytes_accessed=8 * length * wide,
            transcendentals=heads * length * (length // 2 + top * MBLK),
        ),
        name="attend_forward",
    )(chosen, counts, qkv, qkv, qkv, memory, memory)


def spread_rows(column):
    rows = column.shape[0]
    return jnp.transpose(jnp.broadcast_to(column, (rows, HEAD_DIM)))[:1]


def row_stats(grad_out, out, lse):
    delta = jnp.sum(grad_out.astype(F32) * out.astype(F32), -1, keepdims=True)
    return jnp.concatenate([spread_rows(lse), spread_rows(delta)], 0)


def score_grads(query, grad_out, stats, keys, values, mask):
    weights = jnp.exp2(mask(dot(keys, query, NT)) - stats[:1])
    grad_weights = dot(values, grad_out, NT)
    return weights.astype(BF16), (weights * (grad_weights - stats[1:2])).astype(BF16)


def causal_mask(rows):
    key_at = lax.broadcasted_iota(jnp.int32, (rows, rows), 0)
    query_at = lax.broadcasted_iota(jnp.int32, (rows, rows), 1)
    return lambda scores: jnp.where(query_at >= key_at, scores, NEGATIVE)


def memory_query_grad(chosen_ref, counts_ref, base, top, query, grad_out, stats, mk_ref, mv_ref, columns):
    keys = pick_memory(mk_ref, chosen_ref, base, top, columns)
    values = pick_memory(mv_ref, chosen_ref, base, top, columns)
    bias = memory_bias(counts_ref, base, top, 0)
    _, grad_scores = score_grads(query, grad_out, stats, keys, values, lambda scores: scores + bias)
    return dot(grad_scores, keys, TN)


def block_grads(heads, grad_query, grad_key, grad_value, cosine, sine):
    def unturn(value):
        return (value * cosine - pltpu.roll(value, HEAD_DIM // 2, 1) * sine).astype(BF16)

    parts = []
    for part, array in enumerate((grad_query * SCALE, grad_key * (1.0 / LOG2E), grad_value)):
        for head in range(heads):
            value = array[:, head * HEAD_DIM : (head + 1) * HEAD_DIM]
            parts.append(unturn(value) if part < 2 else value.astype(BF16))
    return jnp.concatenate(parts, 1)


def first_block_kernel(
    heads, top, chosen_ref, counts_ref, plan_ref, qkv_ref, mk_ref, mv_ref, go_ref, out_ref, lse_ref, cos_ref, sin_ref,
    w_ref, partial_ref, grad_ref, gq_ref, gk_ref, gv_ref, stats_s,
):
    rows = partial_ref.shape[0]
    subs = rows // QBLK
    wide = heads * HEAD_DIM
    others = go_ref.shape[0] // rows - 1
    block, is_last = plan_ref[0], plan_ref[1]
    own = pl.ds(pl.multiple_of(block * rows, rows), rows)
    gq_ref[...] = jnp.zeros_like(gq_ref)
    gk_ref[...] = jnp.zeros_like(gk_ref)
    gv_ref[...] = jnp.zeros_like(gv_ref)

    def note_stats(slot, here):
        for head in range(heads):
            columns = slice(head * HEAD_DIM, (head + 1) * HEAD_DIM)
            stats_s[slot, head] = row_stats(go_ref[here, columns], out_ref[here, columns], lse_ref[here, head : head + 1])

    note_stats(0, own)

    def pair(slot, queries, keys, mask):
        for head in range(heads):
            at = head * HEAD_DIM
            columns = slice(at, at + HEAD_DIM)
            query, grad_out = qkv_ref[queries, columns], go_ref[queries, columns]
            key = qkv_ref[keys, wide + at : wide + at + HEAD_DIM]
            value = qkv_ref[keys, 2 * wide + at : 2 * wide + at + HEAD_DIM]
            weights, grad_scores = score_grads(query, grad_out, stats_s[slot, head], key, value, mask)
            gk_ref[keys, columns] += dot(grad_scores, query)
            gv_ref[keys, columns] += dot(weights, grad_out)
            gq_ref[queries, columns] += dot(grad_scores, key, TN)

    for head in range(heads):
        columns = slice(head * HEAD_DIM, (head + 1) * HEAD_DIM)
        for sub in range(subs):
            here = pl.ds(pl.multiple_of(block * rows + sub * QBLK, QBLK), QBLK)
            gq_ref[here, columns] += memory_query_grad(
                chosen_ref, counts_ref, (block * subs + sub) * top, top, qkv_ref[here, columns], go_ref[here, columns],
                stats_s[0, head][:, sub * QBLK : (sub + 1) * QBLK], mk_ref, mv_ref, columns,
            )
    pair(0, own, own, causal_mask(rows))

    def step(index, carry):
        other = jnp.where(is_last == 1, index, index + 1)
        there = pl.ds(pl.multiple_of(other * rows, rows), rows)

        @pl.when(is_last == 1)
        def _():
            pair(0, own, there, lambda scores: scores)

        @pl.when(is_last == 0)
        def _():
            note_stats(1, there)
            pair(1, there, own, lambda scores: scores)

        return carry

    lax.fori_loop(0, others, step, 0)
    grad = block_grads(
        heads, gq_ref[own, :], gk_ref[own, :], gv_ref[own, :], cos_ref[...], sin_ref[...]
    )
    grad_ref[...] = grad
    partial_ref[...] = dot(grad, w_ref[...], NT).astype(BF16)


def first_block(plan, chosen, counts, qkv, memory, grad_out, out, lse, cosine, sine, w_qkv, heads, top):
    length = qkv.shape[0]
    width = w_qkv.shape[0]
    wide = heads * HEAD_DIM
    rows = min(2 * QBLK, length)
    mem_rows = memory.shape[0]

    def whole(array):
        return pl.BlockSpec(array.shape, lambda i, *_: (0, 0))

    sums = pl.BlockSpec((length, wide), lambda i, *_: (0, 0))
    return pl.pallas_call(
        functools.partial(first_block_kernel, heads, top),
        grid_spec=pltpu.PrefetchScalarGridSpec(
            num_scalar_prefetch=3,
            grid=(1,),
            in_specs=[
                whole(qkv),
                pl.BlockSpec((mem_rows, wide), lambda i, *_: (0, 0)),
                pl.BlockSpec((mem_rows, wide), lambda i, *_: (0, 1)),
                whole(grad_out),
                whole(out),
                whole(lse),
                pl.BlockSpec((rows, HEAD_DIM), lambda i, c, n, plan: (plan[0], 0)),
                pl.BlockSpec((rows, HEAD_DIM), lambda i, c, n, plan: (plan[0], 0)),
                whole(w_qkv),
            ],
            out_specs=[
                pl.BlockSpec((rows, width), lambda i, *_: (0, 0)),
                pl.BlockSpec((rows, 3 * wide), lambda i, *_: (0, 0)),
                sums,
                sums,
                sums,
            ],
            scratch_shapes=[pltpu.VMEM((2, heads, 2, rows), F32)],
        ),
        out_shape=[
            jax.ShapeDtypeStruct((rows, width), BF16),
            jax.ShapeDtypeStruct((rows, 3 * wide), BF16),
            *[jax.ShapeDtypeStruct((length, wide), F32)] * 3,
        ],
        compiler_params=pltpu.CompilerParams(vmem_limit_bytes=60 * MIB),
        cost_estimate=pl.CostEstimate(
            flops=4 * heads * length * HEAD_DIM * length,
            bytes_accessed=40 * length * wide,
            transcendentals=heads * length * rows,
        ),
        name="first_block",
    )(chosen, counts, plan, qkv, memory, memory, grad_out, out, lse, cosine, sine, w_qkv)


def other_blocks_kernel(
    heads, top, chosen_ref, counts_ref, plan_ref, q_ref, k_ref, v_ref, mk_ref, mv_ref, go_ref, out_ref, lse_ref,
    cos_ref, sin_ref, w_ref, gq_in, gk_in, gv_in, partial_ref, grad_ref, gk_s, gv_s, gq_s,
):
    low = plan_ref[0]
    block = low + pl.num_programs(0) - 1 - pl.program_id(0)
    rows = q_ref.shape[0]
    subs = rows // QBLK
    own = pl.ds(pl.multiple_of(block * rows, rows), rows)

    @pl.when(pl.program_id(0) == 0)
    def _():
        gk_s[...] = gk_in[...]
        gv_s[...] = gv_in[...]

    stats = []
    for head in range(heads):
        columns = slice(head * HEAD_DIM, (head + 1) * HEAD_DIM)
        stats.append(row_stats(go_ref[:, columns], out_ref[:, columns], lse_ref[:, head : head + 1]))
        for sub in range(subs):
            here = slice(sub * QBLK, (sub + 1) * QBLK)
            gq_s[here, columns] = gq_in[here, columns] + memory_query_grad(
                chosen_ref, counts_ref, (block * subs + sub) * top, top, q_ref[here, columns], go_ref[here, columns],
                stats[head][:, here], mk_ref, mv_ref, columns,
            )

    def local(there, mask):
        for head in range(heads):
            columns = slice(head * HEAD_DIM, (head + 1) * HEAD_DIM)
            query, grad_out = q_ref[:, columns], go_ref[:, columns]
            key = k_ref[there, columns]
            weights, grad_scores = score_grads(query, grad_out, stats[head], key, v_ref[there, columns], mask)
            gk_s[there, columns] += dot(grad_scores, query)
            gv_s[there, columns] += dot(weights, grad_out)
            gq_s[:, columns] += dot(grad_scores, key, TN)

    local(own, causal_mask(rows))

    def step(index, carry):
        local(pl.ds(pl.multiple_of(index * rows, rows), rows), lambda scores: scores)
        return carry

    lax.fori_loop(low, block, step, 0)
    grad = block_grads(heads, gq_s[...], gk_s[own, :], gv_s[own, :], cos_ref[...], sin_ref[...])
    grad_ref[...] = grad
    partial_ref[...] = dot(grad, w_ref[...], NT).astype(BF16)


def other_blocks(plan, chosen, counts, qkv, memory, grad_out, out, lse, cosine, sine, w_qkv, sums, heads, top):
    length = qkv.shape[0]
    width = w_qkv.shape[0]
    wide = heads * HEAD_DIM
    rows = min(2 * QBLK, length)
    count = length // rows - 1
    mem_rows = memory.shape[0]

    def by_rows(columns, at=0):
        return pl.BlockSpec((rows, columns), lambda i, c, n, plan: (plan[0] + count - 1 - i, at))

    def result(columns):
        return pl.BlockSpec((rows, columns), lambda i, *_: (count - 1 - i, 0))

    return pl.pallas_call(
        functools.partial(other_blocks_kernel, heads, top),
        grid_spec=pltpu.PrefetchScalarGridSpec(
            num_scalar_prefetch=3,
            grid=(count,),
            in_specs=[
                by_rows(wide),
                pl.BlockSpec((length, wide), lambda i, *_: (0, 1)),
                pl.BlockSpec((length, wide), lambda i, *_: (0, 2)),
                pl.BlockSpec((mem_rows, wide), lambda i, *_: (0, 0)),
                pl.BlockSpec((mem_rows, wide), lambda i, *_: (0, 1)),
                by_rows(wide),
                by_rows(wide),
                by_rows(heads),
                by_rows(HEAD_DIM),
                by_rows(HEAD_DIM),
                pl.BlockSpec((width, 3 * wide), lambda i, *_: (0, 0)),
                by_rows(wide),
                pl.BlockSpec((length, wide), lambda i, *_: (0, 0)),
                pl.BlockSpec((length, wide), lambda i, *_: (0, 0)),
            ],
            out_specs=[result(width), result(3 * wide)],
            scratch_shapes=[
                pltpu.VMEM((length, wide), F32),
                pltpu.VMEM((length, wide), F32),
                pltpu.VMEM((rows, wide), F32),
            ],
        ),
        out_shape=[
            jax.ShapeDtypeStruct((count * rows, width), BF16),
            jax.ShapeDtypeStruct((count * rows, 3 * wide), BF16),
        ],
        compiler_params=pltpu.CompilerParams(vmem_limit_bytes=60 * MIB),
        cost_estimate=pl.CostEstimate(
            flops=6 * heads * length * HEAD_DIM * (length + top * MBLK),
            bytes_accessed=40 * length * wide,
            transcendentals=heads * length * (length // 3 + top * MBLK),
        ),
        name="other_blocks",
    )(chosen, counts, plan, qkv, qkv, qkv, memory, memory, grad_out, out, lse, cosine, sine, w_qkv, *sums)


def ffn_kernel(
    span, merged, tok_ref, att_ref, cot_ref, gain_ref, out_w, gate_w, up_w, down_w,
    mixed_ref, grad_mid_ref, grad_att_ref, gain_grad_ref, out_grads_ref, grads_ref, *rest,
):
    if not merged:
        down_grads_ref, rest = rest[0], rest[1:]
    middle_s, normed_s, turned_s, mixed_s, upstream_s, gate_s, up_s, down_s, out_s, sems, late_sems = rest
    step, steps = pl.program_id(0), pl.num_programs(0)
    width = tok_ref.shape[1]
    share = width // span
    wide = gate_w.shape[1]
    hidden_width = down_s.shape[0]
    tall = hidden_width // span
    lanes = width // wide
    first = tall * lanes if merged else 0
    slot = step % 2

    @pl.when(step == 0)
    def _():
        middle = tok_ref[...].astype(F32) + dot(att_ref[...], out_w[...])
        middle_s[...] = middle
        factor = lax.rsqrt(jnp.mean(middle * middle, -1, keepdims=True) + EPSILON)
        normed = (middle * factor * gain_ref[...]).astype(BF16)
        normed_s[...] = normed
        turned_s[...] = jnp.transpose(normed)
        mixed_s[...] = middle
        upstream_s[...] = jnp.zeros_like(upstream_s)

    def copy_out(kind, which, index):
        source = (gate_s, up_s)[kind].at[which]
        start = first + (kind * steps + index) * share
        target = grads_ref.at[:, pl.ds(start, share), :]
        return pltpu.make_async_copy(source, target, sems.at[kind, which])

    normed = normed_s[...]
    upstream = cot_ref[...]
    both = jnp.concatenate([gate_w[...], up_w[...]], 1)
    acts = dot(normed, both)
    gate_act, up_act = acts[:, :wide], acts[:, wide:]
    grad_hidden = dot(upstream, down_w[...], NT)
    sigmoid = jax.nn.sigmoid(gate_act)
    silu = gate_act * sigmoid
    hidden = (silu * up_act).astype(BF16)
    grad_gate = (grad_hidden * up_act * sigmoid * (1.0 + gate_act * (1.0 - sigmoid))).astype(BF16)
    grad_up = (grad_hidden * silu).astype(BF16)
    mixed_s[...] += dot(hidden, down_w[...])
    grad_acts = jnp.concatenate([grad_gate, grad_up], 1)
    upstream_s[...] += dot(grad_acts, both, NT)
    down_s[pl.ds(pl.multiple_of(step * wide, wide), wide), :] = dot(hidden, upstream, TN).astype(BF16)

    @pl.when(step >= 2)
    def _():
        copy_out(0, slot, step - 2).wait()
        copy_out(1, slot, step - 2).wait()

    weight_grads = dot(turned_s[...], grad_acts).astype(BF16)
    gate_s[slot] = weight_grads[:, :wide].reshape(span, share, wide)
    up_s[slot] = weight_grads[:, wide:].reshape(span, share, wide)
    copy_out(0, slot, step).start()
    copy_out(1, slot, step).start()

    @pl.when(step == steps - 1)
    def _():
        copies = []
        if merged:
            for place in range(span):
                for lane in range(lanes):
                    copies.append(
                        pltpu.make_async_copy(
                            down_s.at[pl.ds(place * tall, tall), pl.ds(lane * wide, wide)],
                            grads_ref.at[place, pl.ds(lane * tall, tall), :],
                            late_sems.at[len(copies)],
                        )
                    )
        else:
            copies.append(pltpu.make_async_copy(down_s, down_grads_ref, late_sems.at[0]))
        for copy in copies:
            copy.start()
        mixed_ref[...] = mixed_s[...].astype(BF16)
        middle = middle_s[...]
        grad = upstream_s[...]
        factor = lax.rsqrt(jnp.mean(middle * middle, -1, keepdims=True) + EPSILON)
        gain_grad_ref[...] = jnp.sum(grad * middle * factor, 0, keepdims=True)
        scaled = grad * gain_ref[...]
        inner = jnp.mean(scaled * middle, -1, keepdims=True)
        grad_middle = cot_ref[...].astype(F32) + factor * scaled - middle * (factor * factor * factor * inner)
        grad_mid_ref[...] = grad_middle
        branch = grad_middle.astype(BF16)
        grad_att_ref[...] = dot(branch, out_w[...], NT).astype(BF16)
        turned_att = jnp.transpose(att_ref[...])
        for lane in range(lanes):
            columns = slice(lane * wide, (lane + 1) * wide)
            out_s[lane] = dot(turned_att, branch[:, columns]).astype(BF16).reshape(span, share, wide)
            more = pltpu.make_async_copy(
                out_s.at[lane],
                out_grads_ref.at[:, :, pl.ds(lane * wide, wide)],
                late_sems.at[len(copies)],
            )
            more.start()
            copies.append(more)
        for copy in copies:
            copy.wait()
        copy_out(0, 1 - slot, step - 1).wait()
        copy_out(1, 1 - slot, step - 1).wait()
        copy_out(0, slot, step).wait()
        copy_out(1, slot, step).wait()


def feed_forward(tokens, attended, upstream, gain, weights, w_down, span):
    rows, width = tokens.shape
    hidden_width = w_down.shape[0]
    wide = 2 * HEAD_DIM
    steps = hidden_width // wide
    lanes = width // wide
    share = width // span
    tall = hidden_width // span
    merged = tall % 16 == 0
    total = 2 * steps * share + (lanes * tall if merged else 0)
    shapes = [
        jax.ShapeDtypeStruct((rows, width), BF16),
        jax.ShapeDtypeStruct((rows, width), F32),
        jax.ShapeDtypeStruct((rows, width), BF16),
        jax.ShapeDtypeStruct((1, width), F32),
        jax.ShapeDtypeStruct((span, share, width), BF16),
        jax.ShapeDtypeStruct((span, total, wide), BF16),
    ]
    specs = [
        pl.BlockSpec((rows, width), lambda i: (0, 0)),
        pl.BlockSpec((rows, width), lambda i: (0, 0)),
        pl.BlockSpec((rows, width), lambda i: (0, 0)),
        pl.BlockSpec((1, width), lambda i: (0, 0)),
        pl.BlockSpec(memory_space=pl.ANY),
        pl.BlockSpec(memory_space=pl.ANY),
    ]
    if not merged:
        shapes.append(jax.ShapeDtypeStruct((hidden_width, width), BF16))
        specs.append(pl.BlockSpec(memory_space=pl.ANY))
    return pl.pallas_call(
        functools.partial(ffn_kernel, span, merged),
        grid=(steps,),
        in_specs=[
            pl.BlockSpec((rows, width), lambda i: (0, 0)),
            pl.BlockSpec((rows, width), lambda i: (0, 0)),
            pl.BlockSpec((rows, width), lambda i: (0, 0)),
            pl.BlockSpec((1, width), lambda i: (0, 0)),
            pl.BlockSpec((width, width), lambda i: (0, 0)),
            pl.BlockSpec((width, wide), lambda i: (0, lanes + i)),
            pl.BlockSpec((width, wide), lambda i: (0, lanes + steps + i)),
            pl.BlockSpec((wide, width), lambda i: (i, 0)),
        ],
        out_specs=specs,
        out_shape=shapes,
        scratch_shapes=[
            pltpu.VMEM((rows, width), F32),
            pltpu.VMEM((rows, width), BF16),
            pltpu.VMEM((width, rows), BF16),
            pltpu.VMEM((rows, width), F32),
            pltpu.VMEM((rows, width), F32),
            pltpu.VMEM((2, span, share, wide), BF16),
            pltpu.VMEM((2, span, share, wide), BF16),
            pltpu.VMEM((hidden_width, width), BF16),
            pltpu.VMEM((lanes, span, share, wide), BF16),
            pltpu.SemaphoreType.DMA((2, 2)),
            pltpu.SemaphoreType.DMA(((span * lanes if merged else 1) + lanes,)),
        ],
        compiler_params=pltpu.CompilerParams(vmem_limit_bytes=56 * MIB),
        cost_estimate=pl.CostEstimate(
            flops=6 * rows * width * (3 * hidden_width + width),
            bytes_accessed=4 * width * (3 * hidden_width + width),
            transcendentals=rows * hidden_width,
        ),
        name="feed_forward",
    )(tokens, attended, upstream, gain, weights, weights, weights, w_down)


def projection_grads_kernel(
    order_ref, tok_ref, gain_ref, w_ref, first_ref, other_ref, grad_w_ref, gain_grad_ref, raw_s
):
    step = pl.program_id(0)

    @pl.when(step == 0)
    def _():
        raw_s[...] = jnp.zeros_like(raw_s)

    tokens = tok_ref[...].astype(F32)
    tokens = tokens * lax.rsqrt(jnp.mean(tokens * tokens, -1, keepdims=True) + EPSILON)
    grad = jnp.where(step == 0, first_ref[...], other_ref[...])
    raw_s[...] += dot(tokens.astype(BF16), grad, TN)

    @pl.when(step == pl.num_programs(0) - 1)
    def _():
        raw = raw_s[...]
        gain_grad_ref[...] = jnp.sum(raw * w_ref[...].astype(F32), -1, keepdims=True)
        grad_w_ref[...] = (raw * gain_ref[...]).astype(BF16)


def projection_grads(order, tokens_all, gain_column, w_qkv, first_grad, other_grad):
    length, width = tokens_all.shape
    columns = first_grad.shape[1]
    rows = min(2 * QBLK, length)
    return pl.pallas_call(
        projection_grads_kernel,
        grid_spec=pltpu.PrefetchScalarGridSpec(
            num_scalar_prefetch=1,
            grid=(length // rows,),
            in_specs=[
                pl.BlockSpec((rows, width), lambda i, order: (order[i], 0)),
                pl.BlockSpec((width, 1), lambda i, _: (0, 0)),
                pl.BlockSpec((width, columns), lambda i, _: (0, 0)),
                pl.BlockSpec((rows, columns), lambda i, _: (0, 0)),
                pl.BlockSpec((rows, columns), lambda i, _: (jnp.maximum(i - 1, 0), 0)),
            ],
            out_specs=[
                pl.BlockSpec((width, columns), lambda i, _: (0, 0)),
                pl.BlockSpec((width, 1), lambda i, _: (0, 0)),
            ],
            scratch_shapes=[pltpu.VMEM((width, columns), F32)],
        ),
        out_shape=[
            jax.ShapeDtypeStruct((width, columns), BF16),
            jax.ShapeDtypeStruct((width, 1), F32),
        ],
        compiler_params=pltpu.CompilerParams(vmem_limit_bytes=48 * MIB),
        cost_estimate=pl.CostEstimate(
            flops=2 * length * width * columns, bytes_accessed=2 * length * (width + columns), transcendentals=0
        ),
        name="projection_grads",
    )(order, tokens_all, gain_column, w_qkv, first_grad, other_grad)


def after(value, earlier):
    return lax.optimization_barrier((value, earlier))[0]


def chain_gather(blocks, axis):
    size = lax.axis_size(axis)
    place = lax.axis_index(axis)
    steps = []
    rising = falling = tuple(blocks)
    for step in range(size - 1):
        up = [(i, i + 1) for i in range(step, size - 1)]
        down = [(i + 1, i) for i in range(size - 1 - step)]
        rising = tuple(lax.ppermute(block, axis, up) for block in rising)
        falling = tuple(lax.ppermute(block, axis, down) for block in falling)
        if len(blocks) > 1:
            rising, falling = lax.optimization_barrier((rising, falling))
        steps.append((rising, falling))
    results = []
    for number, block in enumerate(blocks):
        ordered = []
        for index in range(size):
            cases = []
            for mine in range(size):
                if mine == index:
                    cases.append(block)
                elif mine > index:
                    cases.append(steps[mine - index - 1][0][number])
                else:
                    cases.append(steps[index - mine - 1][1][number])
            ordered.append(lax.select_n(place, *cases) if size > 2 else lax.select_n(place > 0, *cases))
        results.append(ordered)
    return results, steps


def chain_scatter(block, axis, waits):
    size = lax.axis_size(axis)
    place = lax.axis_index(axis)
    arrived = []
    for step in range(size - 1):
        up, down = block(step, size - 1 - step + place), block(step, step - size + 1 + place)
        if step:
            up, down = up + arrived[-1][0].astype(F32), down + arrived[-1][1].astype(F32)
        ready = waits[step - 1](sent) if 0 < step <= len(waits) else None
        up, down, _ = lax.optimization_barrier((up.astype(BF16), down.astype(BF16), ready))
        sent = up, down
        rising = lax.ppermute(up, axis, [(i, i + 1) for i in range(step + 1)])
        falling = lax.ppermute(down, axis, [(i, i - 1) for i in range(size - 1 - step, size)])
        arrived.append(lax.optimization_barrier((rising, falling)))
    return block(size, place), arrived


def direct_exchange(blocks, axis):
    size = lax.axis_size(axis)
    place = lax.axis_index(axis)
    taken = [lax.dynamic_index_in_dim(blocks, place, 0, keepdims=False)]
    for far in range(1, size):
        give = lax.dynamic_index_in_dim(blocks, (place + far) % size, 0, keepdims=False)
        taken.append(lax.ppermute(give, axis, [(i, (i + far) % size) for i in range(size)]))
    return taken


def body(
    tokens, memory_keys, memory_values, chosen, counts, w_query, w_key, w_value, w_out, w_gate, w_up, w_down,
    gain_attn, gain_ffn, cotangent,
):
    ring, span = lax.axis_size("fsdp"), lax.axis_size(DP)
    rows, width = tokens.shape[1:]
    heads = width // HEAD_DIM // ring
    wide = heads * HEAD_DIM
    length = rows * ring
    top = chosen.shape[2]
    hidden_width = w_gate.shape[1]
    share = w_query.shape[0]
    mine = tokens[0]

    extra = 8 if share % 8 == 0 else 8 - share % 8
    parts = [w.reshape(share, ring, wide).transpose(1, 0, 2) for w in (w_query, w_key, w_value)]
    choices = jnp.concatenate([chosen[0].reshape(-1), counts[0].reshape(-1)]).astype(BF16)
    notes = jnp.stack(
        [
            jnp.pad(row, (0, 3 * wide - row.shape[0]))
            for row in (jnp.concatenate([gain_attn, gain_ffn]), choices)
        ]
    )
    notes = jnp.broadcast_to(jnp.pad(notes, ((0, extra - 2), (0, 0))), (ring, extra, 3 * wide))
    parcel = jnp.concatenate([jnp.concatenate(parts, 2), notes], 1)
    parcel = lax.all_to_all(parcel, "fsdp", 0, 0, tiled=True)
    picks = parcel[:, share + 1, : choices.shape[0]].astype(jnp.int32).reshape(ring, 2, -1)
    chosen_all, counts_all = picks[:, 0].reshape(-1), picks[:, 1].reshape(-1)
    shards = jnp.concatenate([w_out, w_gate, w_up], 1)
    (near, near_down), steps = chain_gather((shards, w_down), "fsdp")
    (gathered,), token_steps = chain_gather((after(mine, steps[-2]),), "fsdp")
    parcel = lax.all_gather(after(parcel, steps[0]), DP, axis=0, tiled=True)
    w_qkv = parcel[:, :share].reshape(width, 3 * wide)
    gain_one = parcel[:, share, :share].reshape(1, width).astype(F32)
    gain_two = parcel[:, share, share : 2 * share].reshape(1, width).astype(F32)
    first = lax.all_gather(jnp.concatenate(near, 0), DP, axis=0, tiled=True)
    gathered = jnp.concatenate(gathered, 0)

    memory = jnp.concatenate(
        [m[0].reshape(-1, ring, wide).transpose(1, 0, 2) for m in (memory_keys, memory_values)], 2
    )
    memory = lax.all_to_all(after(memory, token_steps[-2]), "fsdp", 0, 0, tiled=True).reshape(-1, 2 * wide)
    down_full = lax.all_gather(jnp.concatenate(near_down, 0), DP, axis=0, tiled=True)

    cosine, sine = rotary_tables(length)
    qkv = project_qkv(gathered, gain_one, w_qkv, cosine, sine, heads)
    attended_heads, lse = attend_forward(chosen_all, counts_all, qkv, memory, heads, top)
    attended = lax.all_to_all(attended_heads, "fsdp", 0, 1, tiled=True)

    upstream = cotangent[0]
    mixed, grad_middle, grad_attended, gain_two_grad, out_grads, grads, *grad_down = feed_forward(
        mine, attended, upstream, gain_two, first, down_full, span
    )
    grad_heads = lax.all_to_all(grad_attended, "fsdp", 1, 0, tiled=True)
    grads = lax.psum_scatter(grads, DP, scatter_dimension=0, tiled=True)[0]

    core = lax.axis_index("core")

    def over_cores(array):
        array = array.reshape((span // 2, 2) + array.shape[1:])
        taken = lax.ppermute(lax.dynamic_index_in_dim(array, 1 - core, 1, keepdims=False), "core", [(0, 1), (1, 0)])
        return (lax.dynamic_index_in_dim(array, core, 1, keepdims=False).astype(F32) + taken.astype(F32)).astype(BF16)

    def over_chips(array):
        return sum(piece.astype(F32) for piece in direct_exchange(array, "chip")).astype(BF16)

    place = lax.axis_index("fsdp").astype(jnp.int32)
    count = length // min(2 * QBLK, length)
    is_last = (place < ring // 2).astype(jnp.int32)
    first_number = jnp.where(is_last == 1, count - 1, 0).astype(jnp.int32)
    low = 1 - is_last
    first_partial, first_grad, *sums = first_block(
        jnp.stack([first_number, is_last]), chosen_all, counts_all, qkv, memory, grad_heads, attended_heads, lse,
        cosine, sine, w_qkv, heads, top,
    )
    other_partial, other_grad = other_blocks(
        low.reshape(1), chosen_all, counts_all, qkv, memory, grad_heads, attended_heads, lse, cosine, sine, w_qkv,
        sums, heads, top,
    )
    order = jnp.concatenate([first_number.reshape(1), low + jnp.arange(count - 1, dtype=jnp.int32)])
    block_rows = first_partial.shape[0]

    def term(step, index):
        start = jnp.clip(index, 0, ring - 1) * rows
        at = jnp.clip(start - low * block_rows, 0, other_partial.shape[0] - rows)
        near = jnp.clip(start - first_number * block_rows, 0, block_rows - rows)
        from_first = lax.dynamic_slice_in_dim(first_partial, near, rows, 0)
        if step == 0:
            return from_first.astype(F32)
        from_others = lax.dynamic_slice_in_dim(other_partial, at, rows, 0)
        inside = (start >= first_number * block_rows) & (start < (first_number + 1) * block_rows)
        return jnp.where(inside, from_first, from_others).astype(F32)

    kept = []

    def make_projection_grads(sent):
        kept.extend(
            projection_grads(
                order, gathered, gain_one.reshape(width, 1), w_qkv, after(first_grad, sent), after(other_grad, sent)
            )
        )
        return kept

    own_term, arrived = chain_scatter(term, "fsdp", [lambda sent: None, make_projection_grads])
    grad_w_qkv, gain_one_grad = kept
    grads = after(grads, arrived[-1])

    strip = grads.shape[1]
    lanes = width // strip
    tall = w_down.shape[0]
    if grad_down:
        down = lax.psum_scatter(grad_down[0], DP, scatter_dimension=0, tiled=True)
        down = down.reshape(ring, tall, lanes, strip).transpose(0, 2, 1, 3)
    else:
        down = grads[: ring * tall * lanes].reshape(lanes, ring, tall, strip).transpose(1, 0, 2, 3)
        grads = grads[ring * tall * lanes :]
    grads = grads.reshape(-1, ring, share, strip).transpose(1, 0, 2, 3)
    pieces = jnp.concatenate([down.reshape(ring, -1, strip), grads.reshape(ring, -1, strip)], 1)

    gains = jnp.stack([gain_one_grad.reshape(span, -1), gain_two_grad.reshape(span, -1)], 1)
    gains = jnp.pad(gains.astype(BF16), ((0, 0), (0, extra - 2), (0, 3 * wide - gains.shape[2])))
    late = jnp.concatenate([grad_w_qkv.reshape(span, -1, 3 * wide), gains], 1)
    late = jnp.concatenate([late, jnp.pad(out_grads, ((0, 0), (0, extra), (0, 0)))], 2)
    late = over_chips(over_cores(after(late, pieces)))
    late, out_grads = late[:, : 3 * wide], late[:-extra, 3 * wide :]

    rising, falling = arrived[-1]
    grad_normed = own_term + rising.astype(F32) + falling.astype(F32)
    own = mine.astype(F32)
    factor = lax.rsqrt(jnp.mean(own * own, -1, keepdims=True) + EPSILON)
    scaled = grad_normed * gain_one
    inner = jnp.mean(scaled * own, -1, keepdims=True)
    tokens_grad = (grad_middle + factor * scaled - own * (factor * factor * factor * inner)).astype(BF16)

    gains = late[-extra : 2 - extra, : ring * share].reshape(2, ring, share).transpose(1, 0, 2)
    gains = jnp.pad(gains, ((0, 0), (0, extra - 2), (0, 3 * wide - share)))
    late = jnp.concatenate([late[:-extra].reshape(ring, share, 3 * wide), gains], 1)
    out_grads = jnp.pad(out_grads.reshape(ring, share, width), ((0, 0), (0, extra), (0, 0)))
    late = jnp.concatenate([late, out_grads], 2)
    late = after(lax.all_to_all(late, "fsdp", 0, 0, tiled=True), tokens_grad).astype(F32)
    out_share = jnp.sum(late[:, :share, 3 * wide :], 0)
    projections = [
        late[:, :share, part * wide : (part + 1) * wide].transpose(1, 0, 2).reshape(share, width)
        for part in range(3)
    ]
    gain_shares = jnp.sum(late[:, share : share + 2, :share], 0)

    pieces = lax.psum_scatter(pieces, "fsdp", scatter_dimension=0, tiled=True)
    pieces = after(pieces, (tokens_grad, projections, out_share, gain_shares))[0].astype(F32)
    down_share = pieces[: lanes * tall].reshape(lanes, tall, strip).transpose(1, 0, 2).reshape(tall, width)
    others = pieces[lanes * tall :].reshape(-1, share, strip).transpose(1, 0, 2).reshape(share, -1)
    return (
        mixed[None],
        tokens_grad[None],
        *projections,
        out_share,
        others[:, :hidden_width],
        others[:, hidden_width:],
        down_share,
        gain_shares[0],
        gain_shares[1],
    )


def solution(mesh):
    span, ring = mesh.shape["dp"], mesh.shape["fsdp"]
    fine = Mesh(mesh.devices.reshape(span // 2, 2, ring), DP + ("fsdp",))
    every = DP + ("fsdp",)
    rows, matrix, vector = P(DP, "fsdp", None), P(every, None), P(every)
    in_specs = (rows,) * 5 + (matrix,) * 7 + (vector,) * 2 + (rows,)
    out_specs = (rows,) * 2 + (matrix,) * 7 + (vector,) * 2
    return jax.shard_map(body, mesh=fine, in_specs=in_specs, out_specs=out_specs, check_vma=False)
```

```python
import functools
import math

import jax
import jax.numpy as jnp
import numpy as np
from jax import lax
from jax.experimental import pallas as pl
from jax.experimental.pallas import tpu as pltpu
from jax.sharding import Mesh
from jax.sharding import PartitionSpec as P

HEAD_DIM = 128
QBLK = 256
MBLK = 128
EPSILON = 1e-06
NEGATIVE = -1e30
SCALE = 1.0 / math.sqrt(HEAD_DIM)
LOG2E = math.log2(math.e)
MIB = 1 << 20
F32 = jnp.float32
BF16 = jnp.bfloat16
DP = ("chip", "core")
NT = (((1,), (1,)), ((), ()))
TN = (((0,), (0,)), ((), ()))


def dot(left, right, dims=(((1,), (0,)), ((), ()))):
    return lax.dot_general(left, right, dims, preferred_element_type=F32)


def rotary_tables(length):
    half_dim = HEAD_DIM // 2
    frequency = 10000.0 ** (-jnp.arange(half_dim, dtype=F32) / half_dim)
    angles = jnp.arange(length, dtype=jnp.int32).astype(F32)[:, None] * frequency[None, :]
    cosine, sine = jnp.cos(angles), jnp.sin(angles)
    return jnp.concatenate([cosine, cosine], 1), jnp.concatenate([-sine, sine], 1)


def qkv_kernel(heads, tok_ref, gain_ref, w_ref, cos_ref, sin_ref, qkv_ref):
    rows = tok_ref[...].astype(F32)
    factor = lax.rsqrt(jnp.mean(rows * rows, -1, keepdims=True) + EPSILON)
    normed = (rows * factor * gain_ref[...]).astype(BF16)
    cosine, sine = cos_ref[...], sin_ref[...]
    wide = heads * HEAD_DIM
    for part in range(3):
        values = dot(normed, w_ref[:, part * wide : (part + 1) * wide])
        for head in range(heads):
            value = values[:, head * HEAD_DIM : (head + 1) * HEAD_DIM]
            if part < 2:
                value = value * cosine + pltpu.roll(value, HEAD_DIM // 2, 1) * sine
            if part == 0:
                value = value * (SCALE * LOG2E)
            at = part * wide + head * HEAD_DIM
            qkv_ref[:, at : at + HEAD_DIM] = value.astype(BF16)


def project_qkv(tokens_all, gain, w_qkv, cosine, sine, heads):
    length, width = tokens_all.shape
    columns = w_qkv.shape[1]
    block = 2 * QBLK
    return pl.pallas_call(
        functools.partial(qkv_kernel, heads),
        grid=(length // block,),
        in_specs=[
            pl.BlockSpec((block, width), lambda i: (i, 0)),
            pl.BlockSpec((1, width), lambda i: (0, 0)),
            pl.BlockSpec((width, columns), lambda i: (0, 0)),
            pl.BlockSpec((block, HEAD_DIM), lambda i: (i, 0)),
            pl.BlockSpec((block, HEAD_DIM), lambda i: (i, 0)),
        ],
        out_specs=pl.BlockSpec((block, columns), lambda i: (i, 0)),
        out_shape=jax.ShapeDtypeStruct((length, columns), BF16),
        compiler_params=pltpu.CompilerParams(vmem_limit_bytes=48 * MIB),
        cost_estimate=pl.CostEstimate(
            flops=2 * length * width * columns, bytes_accessed=4 * length * (width + columns), transcendentals=0
        ),
        name="project_qkv",
    )(tokens_all, gain, w_qkv, cosine, sine)


def memory_bias(counts_ref, base, top, axis):
    shape = (1, top * MBLK) if axis == 1 else (top * MBLK, 1)
    column = lax.broadcasted_iota(jnp.int32, shape, axis)
    limit = jnp.zeros(shape, jnp.int32)
    for entry in range(top):
        inside = (column >= entry * MBLK) & (column < entry * MBLK + counts_ref[base + entry])
        limit = jnp.where(inside, 1, limit)
    return jnp.where(limit > 0, 0.0, NEGATIVE)


def pick_memory(ref, chosen_ref, base, top, columns):
    rows = [
        ref[pl.ds(pl.multiple_of(chosen_ref[base + entry] * MBLK, MBLK), MBLK), columns]
        for entry in range(top)
    ]
    return jnp.concatenate(rows, 0)


def forward_kernel(
    heads, top, chosen_ref, counts_ref, q_ref, k_ref, v_ref, mk_ref, mv_ref, out_ref, lse_ref, acc_s, peak_s
):
    block = pl.program_id(0)
    rows = q_ref.shape[0]
    subs = rows // QBLK
    ones = jnp.ones((rows, HEAD_DIM), BF16)
    mem_ones = jnp.ones((top * MBLK, HEAD_DIM), BF16)
    for sub in range(subs):
        base = (block * subs + sub) * top
        here = slice(sub * QBLK, (sub + 1) * QBLK)
        span = (sub + 1) * QBLK
        seen = pl.ds(pl.multiple_of(block * rows, rows), span)
        row = lax.broadcasted_iota(jnp.int32, (QBLK, span), 0) + sub * QBLK
        causal = row >= lax.broadcasted_iota(jnp.int32, (QBLK, span), 1)
        bias = memory_bias(counts_ref, base, top, 1)
        for head in range(heads):
            columns = slice(head * HEAD_DIM, (head + 1) * HEAD_DIM)
            query = q_ref[here, columns]
            remote = dot(query, pick_memory(mk_ref, chosen_ref, base, top, columns), NT) + bias
            local = jnp.where(causal, dot(query, k_ref[seen, columns], NT), NEGATIVE)
            peak = jnp.maximum(jnp.max(local, -1, keepdims=True), jnp.max(remote, -1, keepdims=True))
            values = jnp.concatenate([v_ref[seen, columns], ones[:span]], 1)
            acc = dot(jnp.exp2(local - peak).astype(BF16), values)
            values = jnp.concatenate([pick_memory(mv_ref, chosen_ref, base, top, columns), mem_ones], 1)
            acc_s[head, here] = acc + dot(jnp.exp2(remote - peak).astype(BF16), values)
            peak_s[head, here] = jnp.broadcast_to(peak, (QBLK, HEAD_DIM))

    def step(index, carry):
        there = pl.ds(pl.multiple_of(index * rows, rows), rows)
        for head in range(heads):
            columns = slice(head * HEAD_DIM, (head + 1) * HEAD_DIM)
            peak = peak_s[head][:, :1]
            scores = dot(q_ref[:, columns], k_ref[there, columns], NT)
            higher = jnp.maximum(peak, jnp.max(scores, -1, keepdims=True))
            weights = jnp.exp2(scores - higher).astype(BF16)
            values = jnp.concatenate([v_ref[there, columns], ones], 1)
            acc_s[head] = acc_s[head] * jnp.exp2(peak - higher) + dot(weights, values)
            peak_s[head] = jnp.broadcast_to(higher, (rows, HEAD_DIM))
        return carry

    lax.fori_loop(0, block, step, 0)
    for head in range(heads):
        columns = slice(head * HEAD_DIM, (head + 1) * HEAD_DIM)
        total = acc_s[head][:, HEAD_DIM:]
        out_ref[:, columns] = (acc_s[head][:, :HEAD_DIM] / total).astype(BF16)
        lse_ref[:, head : head + 1] = peak_s[head][:, :1] + jnp.log2(total[:, :1])


def attend_forward(chosen, counts, qkv, memory, heads, top):
    length = qkv.shape[0]
    wide = heads * HEAD_DIM
    rows = min(2 * QBLK, length)
    mem_rows = memory.shape[0]
    return pl.pallas_call(
        functools.partial(forward_kernel, heads, top),
        grid_spec=pltpu.PrefetchScalarGridSpec(
            num_scalar_prefetch=2,
            grid=(length // rows,),
            in_specs=[
                pl.BlockSpec((rows, wide), lambda i, *_: (i, 0)),
                pl.BlockSpec((length, wide), lambda i, *_: (0, 1)),
                pl.BlockSpec((length, wide), lambda i, *_: (0, 2)),
                pl.BlockSpec((mem_rows, wide), lambda i, *_: (0, 0)),
                pl.BlockSpec((mem_rows, wide), lambda i, *_: (0, 1)),
            ],
            out_specs=[
                pl.BlockSpec((rows, wide), lambda i, *_: (i, 0)),
                pl.BlockSpec((rows, heads), lambda i, *_: (i, 0)),
            ],
            scratch_shapes=[
                pltpu.VMEM((heads, rows, 2 * HEAD_DIM), F32),
                pltpu.VMEM((heads, rows, HEAD_DIM), F32),
            ],
        ),
        out_shape=[
            jax.ShapeDtypeStruct((length, wide), BF16),
            jax.ShapeDtypeStruct((length, heads), F32),
        ],
        compiler_params=pltpu.CompilerParams(vmem_limit_bytes=48 * MIB),
        cost_estimate=pl.CostEstimate(
            flops=4 * heads * length * HEAD_DIM * (length // 2 + top * MBLK),
            bytes_accessed=8 * length * wide,
            transcendentals=heads * length * (length // 2 + top * MBLK),
        ),
        name="attend_forward",
    )(chosen, counts, qkv, qkv, qkv, memory, memory)


def spread_rows(column):
    rows = column.shape[0]
    return jnp.transpose(jnp.broadcast_to(column, (rows, HEAD_DIM)))[:1]


def row_stats(grad_out, out, lse):
    delta = jnp.sum(grad_out.astype(F32) * out.astype(F32), -1, keepdims=True)
    return jnp.concatenate([spread_rows(lse), spread_rows(delta)], 0)


def score_grads(query, grad_out, stats, keys, values, mask):
    weights = jnp.exp2(mask(dot(keys, query, NT)) - stats[:1])
    grad_weights = dot(values, grad_out, NT)
    return weights.astype(BF16), (weights * (grad_weights - stats[1:2])).astype(BF16)


def causal_mask(rows):
    key_at = lax.broadcasted_iota(jnp.int32, (rows, rows), 0)
    query_at = lax.broadcasted_iota(jnp.int32, (rows, rows), 1)
    return lambda scores: jnp.where(query_at >= key_at, scores, NEGATIVE)


def memory_query_grad(chosen_ref, counts_ref, base, top, query, grad_out, stats, mk_ref, mv_ref, columns):
    keys = pick_memory(mk_ref, chosen_ref, base, top, columns)
    values = pick_memory(mv_ref, chosen_ref, base, top, columns)
    bias = memory_bias(counts_ref, base, top, 0)
    _, grad_scores = score_grads(query, grad_out, stats, keys, values, lambda scores: scores + bias)
    return dot(grad_scores, keys, TN)


def block_grads(heads, grad_query, grad_key, grad_value, cosine, sine):
    def unturn(value):
        return (value * cosine - pltpu.roll(value, HEAD_DIM // 2, 1) * sine).astype(BF16)

    parts = []
    for part, array in enumerate((grad_query * SCALE, grad_key * (1.0 / LOG2E), grad_value)):
        for head in range(heads):
            value = array[:, head * HEAD_DIM : (head + 1) * HEAD_DIM]
            parts.append(unturn(value) if part < 2 else value.astype(BF16))
    return jnp.concatenate(parts, 1)


def first_block_kernel(
    heads, top, chosen_ref, counts_ref, plan_ref, qkv_ref, mk_ref, mv_ref, go_ref, out_ref, lse_ref, cos_ref, sin_ref,
    w_ref, partial_ref, grad_ref, gq_ref, gk_ref, gv_ref, stats_s,
):
    rows = partial_ref.shape[0]
    subs = rows // QBLK
    wide = heads * HEAD_DIM
    others = go_ref.shape[0] // rows - 1
    block, is_last = plan_ref[0], plan_ref[1]
    own = pl.ds(pl.multiple_of(block * rows, rows), rows)
    gq_ref[...] = jnp.zeros_like(gq_ref)
    gk_ref[...] = jnp.zeros_like(gk_ref)
    gv_ref[...] = jnp.zeros_like(gv_ref)

    def note_stats(slot, here):
        for head in range(heads):
            columns = slice(head * HEAD_DIM, (head + 1) * HEAD_DIM)
            stats_s[slot, head] = row_stats(go_ref[here, columns], out_ref[here, columns], lse_ref[here, head : head + 1])

    note_stats(0, own)

    def pair(slot, queries, keys, mask):
        for head in range(heads):
            at = head * HEAD_DIM
            columns = slice(at, at + HEAD_DIM)
            query, grad_out = qkv_ref[queries, columns], go_ref[queries, columns]
            key = qkv_ref[keys, wide + at : wide + at + HEAD_DIM]
            value = qkv_ref[keys, 2 * wide + at : 2 * wide + at + HEAD_DIM]
            weights, grad_scores = score_grads(query, grad_out, stats_s[slot, head], key, value, mask)
            gk_ref[keys, columns] += dot(grad_scores, query)
            gv_ref[keys, columns] += dot(weights, grad_out)
            gq_ref[queries, columns] += dot(grad_scores, key, TN)

    for head in range(heads):
        columns = slice(head * HEAD_DIM, (head + 1) * HEAD_DIM)
        for sub in range(subs):
            here = pl.ds(pl.multiple_of(block * rows + sub * QBLK, QBLK), QBLK)
            gq_ref[here, columns] += memory_query_grad(
                chosen_ref, counts_ref, (block * subs + sub) * top, top, qkv_ref[here, columns], go_ref[here, columns],
                stats_s[0, head][:, sub * QBLK : (sub + 1) * QBLK], mk_ref, mv_ref, columns,
            )
    pair(0, own, own, causal_mask(rows))

    def step(index, carry):
        other = jnp.where(is_last == 1, index, index + 1)
        there = pl.ds(pl.multiple_of(other * rows, rows), rows)

        @pl.when(is_last == 1)
        def _():
            pair(0, own, there, lambda scores: scores)

        @pl.when(is_last == 0)
        def _():
            note_stats(1, there)
            pair(1, there, own, lambda scores: scores)

        return carry

    lax.fori_loop(0, others, step, 0)
    grad = block_grads(
        heads, gq_ref[own, :], gk_ref[own, :], gv_ref[own, :], cos_ref[...], sin_ref[...]
    )
    grad_ref[...] = grad
    partial_ref[...] = dot(grad, w_ref[...], NT).astype(BF16)


def first_block(plan, chosen, counts, qkv, memory, grad_out, out, lse, cosine, sine, w_qkv, heads, top):
    length = qkv.shape[0]
    width = w_qkv.shape[0]
    wide = heads * HEAD_DIM
    rows = min(2 * QBLK, length)
    mem_rows = memory.shape[0]

    def whole(array):
        return pl.BlockSpec(array.shape, lambda i, *_: (0, 0))

    sums = pl.BlockSpec((length, wide), lambda i, *_: (0, 0))
    return pl.pallas_call(
        functools.partial(first_block_kernel, heads, top),
        grid_spec=pltpu.PrefetchScalarGridSpec(
            num_scalar_prefetch=3,
            grid=(1,),
            in_specs=[
                whole(qkv),
                pl.BlockSpec((mem_rows, wide), lambda i, *_: (0, 0)),
                pl.BlockSpec((mem_rows, wide), lambda i, *_: (0, 1)),
                whole(grad_out),
                whole(out),
                whole(lse),
                pl.BlockSpec((rows, HEAD_DIM), lambda i, c, n, plan: (plan[0], 0)),
                pl.BlockSpec((rows, HEAD_DIM), lambda i, c, n, plan: (plan[0], 0)),
                whole(w_qkv),
            ],
            out_specs=[
                pl.BlockSpec((rows, width), lambda i, *_: (0, 0)),
                pl.BlockSpec((rows, 3 * wide), lambda i, *_: (0, 0)),
                sums,
                sums,
                sums,
            ],
            scratch_shapes=[pltpu.VMEM((2, heads, 2, rows), F32)],
        ),
        out_shape=[
            jax.ShapeDtypeStruct((rows, width), BF16),
            jax.ShapeDtypeStruct((rows, 3 * wide), BF16),
            *[jax.ShapeDtypeStruct((length, wide), F32)] * 3,
        ],
        compiler_params=pltpu.CompilerParams(vmem_limit_bytes=60 * MIB),
        cost_estimate=pl.CostEstimate(
            flops=4 * heads * length * HEAD_DIM * length,
            bytes_accessed=40 * length * wide,
            transcendentals=heads * length * rows,
        ),
        name="first_block",
    )(chosen, counts, plan, qkv, memory, memory, grad_out, out, lse, cosine, sine, w_qkv)


def other_blocks_kernel(
    heads, top, chosen_ref, counts_ref, plan_ref, q_ref, k_ref, v_ref, mk_ref, mv_ref, go_ref, out_ref, lse_ref,
    cos_ref, sin_ref, w_ref, gq_in, gk_in, gv_in, partial_ref, grad_ref, gk_s, gv_s, gq_s,
):
    low = plan_ref[0]
    block = low + pl.num_programs(0) - 1 - pl.program_id(0)
    rows = q_ref.shape[0]
    subs = rows // QBLK
    own = pl.ds(pl.multiple_of(block * rows, rows), rows)

    @pl.when(pl.program_id(0) == 0)
    def _():
        gk_s[...] = gk_in[...]
        gv_s[...] = gv_in[...]

    stats = []
    for head in range(heads):
        columns = slice(head * HEAD_DIM, (head + 1) * HEAD_DIM)
        stats.append(row_stats(go_ref[:, columns], out_ref[:, columns], lse_ref[:, head : head + 1]))
        for sub in range(subs):
            here = slice(sub * QBLK, (sub + 1) * QBLK)
            gq_s[here, columns] = gq_in[here, columns] + memory_query_grad(
                chosen_ref, counts_ref, (block * subs + sub) * top, top, q_ref[here, columns], go_ref[here, columns],
                stats[head][:, here], mk_ref, mv_ref, columns,
            )

    def local(there, mask):
        for head in range(heads):
            columns = slice(head * HEAD_DIM, (head + 1) * HEAD_DIM)
            query, grad_out = q_ref[:, columns], go_ref[:, columns]
            key = k_ref[there, columns]
            weights, grad_scores = score_grads(query, grad_out, stats[head], key, v_ref[there, columns], mask)
            gk_s[there, columns] += dot(grad_scores, query)
            gv_s[there, columns] += dot(weights, grad_out)
            gq_s[:, columns] += dot(grad_scores, key, TN)

    local(own, causal_mask(rows))

    def step(index, carry):
        local(pl.ds(pl.multiple_of(index * rows, rows), rows), lambda scores: scores)
        return carry

    lax.fori_loop(low, block, step, 0)
    grad = block_grads(heads, gq_s[...], gk_s[own, :], gv_s[own, :], cos_ref[...], sin_ref[...])
    grad_ref[...] = grad
    partial_ref[...] = dot(grad, w_ref[...], NT).astype(BF16)


def other_blocks(plan, chosen, counts, qkv, memory, grad_out, out, lse, cosine, sine, w_qkv, sums, heads, top):
    length = qkv.shape[0]
    width = w_qkv.shape[0]
    wide = heads * HEAD_DIM
    rows = min(2 * QBLK, length)
    count = length // rows - 1
    mem_rows = memory.shape[0]

    def by_rows(columns, at=0):
        return pl.BlockSpec((rows, columns), lambda i, c, n, plan: (plan[0] + count - 1 - i, at))

    def result(columns):
        return pl.BlockSpec((rows, columns), lambda i, *_: (count - 1 - i, 0))

    return pl.pallas_call(
        functools.partial(other_blocks_kernel, heads, top),
        grid_spec=pltpu.PrefetchScalarGridSpec(
            num_scalar_prefetch=3,
            grid=(count,),
            in_specs=[
                by_rows(wide),
                pl.BlockSpec((length, wide), lambda i, *_: (0, 1)),
                pl.BlockSpec((length, wide), lambda i, *_: (0, 2)),
                pl.BlockSpec((mem_rows, wide), lambda i, *_: (0, 0)),
                pl.BlockSpec((mem_rows, wide), lambda i, *_: (0, 1)),
                by_rows(wide),
                by_rows(wide),
                by_rows(heads),
                by_rows(HEAD_DIM),
                by_rows(HEAD_DIM),
                pl.BlockSpec((width, 3 * wide), lambda i, *_: (0, 0)),
                by_rows(wide),
                pl.BlockSpec((length, wide), lambda i, *_: (0, 0)),
                pl.BlockSpec((length, wide), lambda i, *_: (0, 0)),
            ],
            out_specs=[result(width), result(3 * wide)],
            scratch_shapes=[
                pltpu.VMEM((length, wide), F32),
                pltpu.VMEM((length, wide), F32),
                pltpu.VMEM((rows, wide), F32),
            ],
        ),
        out_shape=[
            jax.ShapeDtypeStruct((count * rows, width), BF16),
            jax.ShapeDtypeStruct((count * rows, 3 * wide), BF16),
        ],
        compiler_params=pltpu.CompilerParams(vmem_limit_bytes=60 * MIB),
        cost_estimate=pl.CostEstimate(
            flops=6 * heads * length * HEAD_DIM * (length + top * MBLK),
            bytes_accessed=40 * length * wide,
            transcendentals=heads * length * (length // 3 + top * MBLK),
        ),
        name="other_blocks",
    )(chosen, counts, plan, qkv, qkv, qkv, memory, memory, grad_out, out, lse, cosine, sine, w_qkv, *sums)


def ffn_kernel(
    span, merged, tok_ref, att_ref, cot_ref, gain_ref, out_w, gate_w, up_w, down_w,
    mixed_ref, grad_mid_ref, grad_att_ref, gain_grad_ref, out_grads_ref, grads_ref, *rest,
):
    if not merged:
        down_grads_ref, rest = rest[0], rest[1:]
    middle_s, normed_s, turned_s, mixed_s, upstream_s, gate_s, up_s, down_s, out_s, sems, late_sems = rest
    step, steps = pl.program_id(0), pl.num_programs(0)
    width = tok_ref.shape[1]
    share = width // span
    wide = gate_w.shape[1]
    hidden_width = down_s.shape[0]
    tall = hidden_width // span
    lanes = width // wide
    first = tall * lanes if merged else 0
    slot = step % 2

    @pl.when(step == 0)
    def _():
        middle = tok_ref[...].astype(F32) + dot(att_ref[...], out_w[...])
        middle_s[...] = middle
        factor = lax.rsqrt(jnp.mean(middle * middle, -1, keepdims=True) + EPSILON)
        normed = (middle * factor * gain_ref[...]).astype(BF16)
        normed_s[...] = normed
        turned_s[...] = jnp.transpose(normed)
        mixed_s[...] = middle
        upstream_s[...] = jnp.zeros_like(upstream_s)

    def copy_out(kind, which, index):
        source = (gate_s, up_s)[kind].at[which]
        start = first + (kind * steps + index) * share
        target = grads_ref.at[:, pl.ds(start, share), :]
        return pltpu.make_async_copy(source, target, sems.at[kind, which])

    normed = normed_s[...]
    upstream = cot_ref[...]
    both = jnp.concatenate([gate_w[...], up_w[...]], 1)
    acts = dot(normed, both)
    gate_act, up_act = acts[:, :wide], acts[:, wide:]
    grad_hidden = dot(upstream, down_w[...], NT)
    sigmoid = jax.nn.sigmoid(gate_act)
    silu = gate_act * sigmoid
    hidden = (silu * up_act).astype(BF16)
    grad_gate = (grad_hidden * up_act * sigmoid * (1.0 + gate_act * (1.0 - sigmoid))).astype(BF16)
    grad_up = (grad_hidden * silu).astype(BF16)
    mixed_s[...] += dot(hidden, down_w[...])
    grad_acts = jnp.concatenate([grad_gate, grad_up], 1)
    upstream_s[...] += dot(grad_acts, both, NT)
    down_s[pl.ds(pl.multiple_of(step * wide, wide), wide), :] = dot(hidden, upstream, TN).astype(BF16)

    @pl.when(step >= 2)
    def _():
        copy_out(0, slot, step - 2).wait()
        copy_out(1, slot, step - 2).wait()

    weight_grads = dot(turned_s[...], grad_acts).astype(BF16)
    gate_s[slot] = weight_grads[:, :wide].reshape(span, share, wide)
    up_s[slot] = weight_grads[:, wide:].reshape(span, share, wide)
    copy_out(0, slot, step).start()
    copy_out(1, slot, step).start()

    @pl.when(step == steps - 1)
    def _():
        copies = []
        if merged:
            for place in range(span):
                for lane in range(lanes):
                    copies.append(
                        pltpu.make_async_copy(
                            down_s.at[pl.ds(place * tall, tall), pl.ds(lane * wide, wide)],
                            grads_ref.at[place, pl.ds(lane * tall, tall), :],
                            late_sems.at[len(copies)],
                        )
                    )
        else:
            copies.append(pltpu.make_async_copy(down_s, down_grads_ref, late_sems.at[0]))
        for copy in copies:
            copy.start()
        mixed_ref[...] = mixed_s[...].astype(BF16)
        middle = middle_s[...]
        grad = upstream_s[...]
        factor = lax.rsqrt(jnp.mean(middle * middle, -1, keepdims=True) + EPSILON)
        gain_grad_ref[...] = jnp.sum(grad * middle * factor, 0, keepdims=True)
        scaled = grad * gain_ref[...]
        inner = jnp.mean(scaled * middle, -1, keepdims=True)
        grad_middle = cot_ref[...].astype(F32) + factor * scaled - middle * (factor * factor * factor * inner)
        grad_mid_ref[...] = grad_middle
        branch = grad_middle.astype(BF16)
        grad_att_ref[...] = dot(branch, out_w[...], NT).astype(BF16)
        turned_att = jnp.transpose(att_ref[...])
        for lane in range(lanes):
            columns = slice(lane * wide, (lane + 1) * wide)
            out_s[lane] = dot(turned_att, branch[:, columns]).astype(BF16).reshape(span, share, wide)
            more = pltpu.make_async_copy(
                out_s.at[lane],
                out_grads_ref.at[:, :, pl.ds(lane * wide, wide)],
                late_sems.at[len(copies)],
            )
            more.start()
            copies.append(more)
        for copy in copies:
            copy.wait()
        copy_out(0, 1 - slot, step - 1).wait()
        copy_out(1, 1 - slot, step - 1).wait()
        copy_out(0, slot, step).wait()
        copy_out(1, slot, step).wait()


def feed_forward(tokens, attended, upstream, gain, weights, w_down, span):
    rows, width = tokens.shape
    hidden_width = w_down.shape[0]
    wide = 2 * HEAD_DIM
    steps = hidden_width // wide
    lanes = width // wide
    share = width // span
    tall = hidden_width // span
    merged = tall % 16 == 0
    total = 2 * steps * share + (lanes * tall if merged else 0)
    shapes = [
        jax.ShapeDtypeStruct((rows, width), BF16),
        jax.ShapeDtypeStruct((rows, width), F32),
        jax.ShapeDtypeStruct((rows, width), BF16),
        jax.ShapeDtypeStruct((1, width), F32),
        jax.ShapeDtypeStruct((span, share, width), BF16),
        jax.ShapeDtypeStruct((span, total, wide), BF16),
    ]
    specs = [
        pl.BlockSpec((rows, width), lambda i: (0, 0)),
        pl.BlockSpec((rows, width), lambda i: (0, 0)),
        pl.BlockSpec((rows, width), lambda i: (0, 0)),
        pl.BlockSpec((1, width), lambda i: (0, 0)),
        pl.BlockSpec(memory_space=pl.ANY),
        pl.BlockSpec(memory_space=pl.ANY),
    ]
    if not merged:
        shapes.append(jax.ShapeDtypeStruct((hidden_width, width), BF16))
        specs.append(pl.BlockSpec(memory_space=pl.ANY))
    return pl.pallas_call(
        functools.partial(ffn_kernel, span, merged),
        grid=(steps,),
        in_specs=[
            pl.BlockSpec((rows, width), lambda i: (0, 0)),
            pl.BlockSpec((rows, width), lambda i: (0, 0)),
            pl.BlockSpec((rows, width), lambda i: (0, 0)),
            pl.BlockSpec((1, width), lambda i: (0, 0)),
            pl.BlockSpec((width, width), lambda i: (0, 0)),
            pl.BlockSpec((width, wide), lambda i: (0, lanes + i)),
            pl.BlockSpec((width, wide), lambda i: (0, lanes + steps + i)),
            pl.BlockSpec((wide, width), lambda i: (i, 0)),
        ],
        out_specs=specs,
        out_shape=shapes,
        scratch_shapes=[
            pltpu.VMEM((rows, width), F32),
            pltpu.VMEM((rows, width), BF16),
            pltpu.VMEM((width, rows), BF16),
            pltpu.VMEM((rows, width), F32),
            pltpu.VMEM((rows, width), F32),
            pltpu.VMEM((2, span, share, wide), BF16),
            pltpu.VMEM((2, span, share, wide), BF16),
            pltpu.VMEM((hidden_width, width), BF16),
            pltpu.VMEM((lanes, span, share, wide), BF16),
            pltpu.SemaphoreType.DMA((2, 2)),
            pltpu.SemaphoreType.DMA(((span * lanes if merged else 1) + lanes,)),
        ],
        compiler_params=pltpu.CompilerParams(vmem_limit_bytes=56 * MIB),
        cost_estimate=pl.CostEstimate(
            flops=6 * rows * width * (3 * hidden_width + width),
            bytes_accessed=4 * width * (3 * hidden_width + width),
            transcendentals=rows * hidden_width,
        ),
        name="feed_forward",
    )(tokens, attended, upstream, gain, weights, weights, weights, w_down)


def projection_grads_kernel(
    order_ref, tok_ref, gain_ref, w_ref, first_ref, other_ref, grad_w_ref, gain_grad_ref, raw_s
):
    step = pl.program_id(0)

    @pl.when(step == 0)
    def _():
        raw_s[...] = jnp.zeros_like(raw_s)

    tokens = tok_ref[...].astype(F32)
    tokens = tokens * lax.rsqrt(jnp.mean(tokens * tokens, -1, keepdims=True) + EPSILON)
    grad = jnp.where(step == 0, first_ref[...], other_ref[...])
    raw_s[...] += dot(tokens.astype(BF16), grad, TN)

    @pl.when(step == pl.num_programs(0) - 1)
    def _():
        raw = raw_s[...]
        gain_grad_ref[...] = jnp.sum(raw * w_ref[...].astype(F32), -1, keepdims=True)
        grad_w_ref[...] = (raw * gain_ref[...]).astype(BF16)


def projection_grads(order, tokens_all, gain_column, w_qkv, first_grad, other_grad):
    length, width = tokens_all.shape
    columns = first_grad.shape[1]
    rows = min(2 * QBLK, length)
    return pl.pallas_call(
        projection_grads_kernel,
        grid_spec=pltpu.PrefetchScalarGridSpec(
            num_scalar_prefetch=1,
            grid=(length // rows,),
            in_specs=[
                pl.BlockSpec((rows, width), lambda i, order: (order[i], 0)),
                pl.BlockSpec((width, 1), lambda i, _: (0, 0)),
                pl.BlockSpec((width, columns), lambda i, _: (0, 0)),
                pl.BlockSpec((rows, columns), lambda i, _: (0, 0)),
                pl.BlockSpec((rows, columns), lambda i, _: (jnp.maximum(i - 1, 0), 0)),
            ],
            out_specs=[
                pl.BlockSpec((width, columns), lambda i, _: (0, 0)),
                pl.BlockSpec((width, 1), lambda i, _: (0, 0)),
            ],
            scratch_shapes=[pltpu.VMEM((width, columns), F32)],
        ),
        out_shape=[
            jax.ShapeDtypeStruct((width, columns), BF16),
            jax.ShapeDtypeStruct((width, 1), F32),
        ],
        compiler_params=pltpu.CompilerParams(vmem_limit_bytes=48 * MIB),
        cost_estimate=pl.CostEstimate(
            flops=2 * length * width * columns, bytes_accessed=2 * length * (width + columns), transcendentals=0
        ),
        name="projection_grads",
    )(order, tokens_all, gain_column, w_qkv, first_grad, other_grad)


def after(value, earlier):
    return lax.optimization_barrier((value, earlier))[0]


def chain_gather(blocks, axis):
    size = lax.axis_size(axis)
    place = lax.axis_index(axis)
    steps = []
    rising = falling = tuple(blocks)
    for step in range(size - 1):
        up = [(i, i + 1) for i in range(step, size - 1)]
        down = [(i + 1, i) for i in range(size - 1 - step)]
        rising = tuple(lax.ppermute(block, axis, up) for block in rising)
        falling = tuple(lax.ppermute(block, axis, down) for block in falling)
        if len(blocks) > 1:
            rising, falling = lax.optimization_barrier((rising, falling))
        steps.append((rising, falling))
    results = []
    for number, block in enumerate(blocks):
        ordered = []
        for index in range(size):
            cases = []
            for mine in range(size):
                if mine == index:
                    cases.append(block)
                elif mine > index:
                    cases.append(steps[mine - index - 1][0][number])
                else:
                    cases.append(steps[index - mine - 1][1][number])
            ordered.append(lax.select_n(place, *cases) if size > 2 else lax.select_n(place > 0, *cases))
        results.append(ordered)
    return results, steps


def chain_scatter(block, axis, waits):
    size = lax.axis_size(axis)
    place = lax.axis_index(axis)
    arrived = []
    for step in range(size - 1):
        up, down = block(step, size - 1 - step + place), block(step, step - size + 1 + place)
        if step:
            up, down = up + arrived[-1][0].astype(F32), down + arrived[-1][1].astype(F32)
        ready = waits[step - 1](sent) if 0 < step <= len(waits) else None
        up, down, _ = lax.optimization_barrier((up.astype(BF16), down.astype(BF16), ready))
        sent = up, down
        rising = lax.ppermute(up, axis, [(i, i + 1) for i in range(step + 1)])
        falling = lax.ppermute(down, axis, [(i, i - 1) for i in range(size - 1 - step, size)])
        arrived.append(lax.optimization_barrier((rising, falling)))
    return block(size, place), arrived


def direct_exchange(blocks, axis):
    size = lax.axis_size(axis)
    place = lax.axis_index(axis)
    taken = [lax.dynamic_index_in_dim(blocks, place, 0, keepdims=False)]
    for far in range(1, size):
        give = lax.dynamic_index_in_dim(blocks, (place + far) % size, 0, keepdims=False)
        taken.append(lax.ppermute(give, axis, [(i, (i + far) % size) for i in range(size)]))
    return taken


def body(
    tokens, memory_keys, memory_values, chosen, counts, w_query, w_key, w_value, w_out, w_gate, w_up, w_down,
    gain_attn, gain_ffn, cotangent,
):
    ring, span = lax.axis_size("fsdp"), lax.axis_size(DP)
    rows, width = tokens.shape[1:]
    heads = width // HEAD_DIM // ring
    wide = heads * HEAD_DIM
    length = rows * ring
    top = chosen.shape[2]
    hidden_width = w_gate.shape[1]
    share = w_query.shape[0]
    mine = tokens[0]

    extra = 8 if share % 8 == 0 else 8 - share % 8
    parts = [w.reshape(share, ring, wide).transpose(1, 0, 2) for w in (w_query, w_key, w_value)]
    choices = jnp.concatenate([chosen[0].reshape(-1), counts[0].reshape(-1)]).astype(BF16)
    notes = jnp.stack(
        [
            jnp.pad(row, (0, 3 * wide - row.shape[0]))
            for row in (jnp.concatenate([gain_attn, gain_ffn]), choices)
        ]
    )
    notes = jnp.broadcast_to(jnp.pad(notes, ((0, extra - 2), (0, 0))), (ring, extra, 3 * wide))
    parcel = jnp.concatenate([jnp.concatenate(parts, 2), notes], 1)
    parcel = lax.all_to_all(parcel, "fsdp", 0, 0, tiled=True)
    picks = parcel[:, share + 1, : choices.shape[0]].astype(jnp.int32).reshape(ring, 2, -1)
    chosen_all, counts_all = picks[:, 0].reshape(-1), picks[:, 1].reshape(-1)
    shards = jnp.concatenate([w_out, w_gate, w_up], 1)
    (near, near_down), steps = chain_gather((shards, w_down), "fsdp")
    (gathered,), token_steps = chain_gather((after(mine, steps[-2]),), "fsdp")
    parcel = lax.all_gather(after(parcel, steps[0]), DP, axis=0, tiled=True)
    w_qkv = parcel[:, :share].reshape(width, 3 * wide)
    gain_one = parcel[:, share, :share].reshape(1, width).astype(F32)
    gain_two = parcel[:, share, share : 2 * share].reshape(1, width).astype(F32)
    first = lax.all_gather(jnp.concatenate(near, 0), DP, axis=0, tiled=True)
    gathered = jnp.concatenate(gathered, 0)

    memory = jnp.concatenate(
        [m[0].reshape(-1, ring, wide).transpose(1, 0, 2) for m in (memory_keys, memory_values)], 2
    )
    memory = lax.all_to_all(after(memory, token_steps[-2]), "fsdp", 0, 0, tiled=True).reshape(-1, 2 * wide)
    down_full = lax.all_gather(jnp.concatenate(near_down, 0), DP, axis=0, tiled=True)

    cosine, sine = rotary_tables(length)
    qkv = project_qkv(gathered, gain_one, w_qkv, cosine, sine, heads)
    attended_heads, lse = attend_forward(chosen_all, counts_all, qkv, memory, heads, top)
    attended = lax.all_to_all(attended_heads, "fsdp", 0, 1, tiled=True)

    upstream = cotangent[0]
    mixed, grad_middle, grad_attended, gain_two_grad, out_grads, grads, *grad_down = feed_forward(
        mine, attended, upstream, gain_two, first, down_full, span
    )
    grad_heads = lax.all_to_all(grad_attended, "fsdp", 1, 0, tiled=True)
    grads = lax.psum_scatter(grads, DP, scatter_dimension=0, tiled=True)[0]

    core = lax.axis_index("core")

    def over_cores(array):
        array = array.reshape((-1, 2) + array.shape[1:])
        taken = lax.ppermute(lax.dynamic_index_in_dim(array, 1 - core, 1, keepdims=False), "core", [(0, 1), (1, 0)])
        return (lax.dynamic_index_in_dim(array, core, 1, keepdims=False).astype(F32) + taken.astype(F32)).astype(BF16)

    def over_chips(array):
        return sum(piece.astype(F32) for piece in direct_exchange(array, "chip")).astype(BF16)

    out_grads = over_chips(out_grads.reshape((span // 2, 2) + out_grads.shape[1:]))

    place = lax.axis_index("fsdp").astype(jnp.int32)
    count = length // min(2 * QBLK, length)
    is_last = (place < ring // 2).astype(jnp.int32)
    first_number = jnp.where(is_last == 1, count - 1, 0).astype(jnp.int32)
    low = 1 - is_last
    first_partial, first_grad, *sums = first_block(
        jnp.stack([first_number, is_last]), chosen_all, counts_all, qkv, memory, grad_heads, attended_heads, lse,
        cosine, sine, w_qkv, heads, top,
    )
    other_partial, other_grad = other_blocks(
        low.reshape(1), chosen_all, counts_all, qkv, memory, grad_heads, attended_heads, lse, cosine, sine, w_qkv,
        sums, heads, top,
    )
    order = jnp.concatenate([first_number.reshape(1), low + jnp.arange(count - 1, dtype=jnp.int32)])
    block_rows = first_partial.shape[0]

    def term(step, index):
        start = jnp.clip(index, 0, ring - 1) * rows
        at = jnp.clip(start - low * block_rows, 0, other_partial.shape[0] - rows)
        near = jnp.clip(start - first_number * block_rows, 0, block_rows - rows)
        from_first = lax.dynamic_slice_in_dim(first_partial, near, rows, 0)
        if step == 0:
            return from_first.astype(F32)
        from_others = lax.dynamic_slice_in_dim(other_partial, at, rows, 0)
        inside = (start >= first_number * block_rows) & (start < (first_number + 1) * block_rows)
        return jnp.where(inside, from_first, from_others).astype(F32)

    kept = []

    def make_projection_grads(sent):
        kept.extend(
            projection_grads(
                order, gathered, gain_one.reshape(width, 1), w_qkv, after(first_grad, sent), after(other_grad, sent)
            )
        )
        return kept

    own_term, arrived = chain_scatter(term, "fsdp", [lambda sent: out_grads, make_projection_grads])
    grad_w_qkv, gain_one_grad = kept
    grads = after(grads, arrived[-1])

    strip = grads.shape[1]
    lanes = width // strip
    tall = w_down.shape[0]
    if grad_down:
        down = lax.psum_scatter(grad_down[0], DP, scatter_dimension=0, tiled=True)
        down = down.reshape(ring, tall, lanes, strip).transpose(0, 2, 1, 3)
    else:
        down = grads[: ring * tall * lanes].reshape(lanes, ring, tall, strip).transpose(1, 0, 2, 3)
        grads = grads[ring * tall * lanes :]
    grads = grads.reshape(-1, ring, share, strip).transpose(1, 0, 2, 3)
    pieces = jnp.concatenate([down.reshape(ring, -1, strip), grads.reshape(ring, -1, strip)], 1)

    gains = jnp.stack([gain_one_grad.reshape(span, -1), gain_two_grad.reshape(span, -1)], 1)
    gains = jnp.pad(gains.astype(BF16), ((0, 0), (0, extra - 2), (0, 3 * wide - gains.shape[2])))
    late = jnp.concatenate([grad_w_qkv.reshape(span, -1, 3 * wide), gains], 1)
    late = over_chips(over_cores(after(late, pieces)))
    out_grads = over_cores(after(out_grads, pieces))[0]

    rising, falling = arrived[-1]
    grad_normed = own_term + rising.astype(F32) + falling.astype(F32)
    own = mine.astype(F32)
    factor = lax.rsqrt(jnp.mean(own * own, -1, keepdims=True) + EPSILON)
    scaled = grad_normed * gain_one
    inner = jnp.mean(scaled * own, -1, keepdims=True)
    tokens_grad = (grad_middle + factor * scaled - own * (factor * factor * factor * inner)).astype(BF16)

    gains = late[-extra : 2 - extra, : ring * share].reshape(2, ring, share).transpose(1, 0, 2)
    gains = jnp.pad(gains, ((0, 0), (0, extra - 2), (0, 3 * wide - share)))
    late = jnp.concatenate([late[:-extra].reshape(ring, share, 3 * wide), gains], 1)
    out_grads = jnp.pad(out_grads.reshape(ring, share, width), ((0, 0), (0, extra), (0, 0)))
    late = jnp.concatenate([late, out_grads], 2)
    late = after(lax.all_to_all(late, "fsdp", 0, 0, tiled=True), tokens_grad).astype(F32)
    out_share = jnp.sum(late[:, :share, 3 * wide :], 0)
    projections = [
        late[:, :share, part * wide : (part + 1) * wide].transpose(1, 0, 2).reshape(share, width)
        for part in range(3)
    ]
    gain_shares = jnp.sum(late[:, share : share + 2, :share], 0)

    pieces = lax.psum_scatter(pieces, "fsdp", scatter_dimension=0, tiled=True)
    pieces = after(pieces, (tokens_grad, projections, out_share, gain_shares))[0].astype(F32)
    down_share = pieces[: lanes * tall].reshape(lanes, tall, strip).transpose(1, 0, 2).reshape(tall, width)
    others = pieces[lanes * tall :].reshape(-1, share, strip).transpose(1, 0, 2).reshape(share, -1)
    return (
        mixed[None],
        tokens_grad[None],
        *projections,
        out_share,
        others[:, :hidden_width],
        others[:, hidden_width:],
        down_share,
        gain_shares[0],
        gain_shares[1],
    )


def solution(mesh):
    span, ring = mesh.shape["dp"], mesh.shape["fsdp"]
    fine = Mesh(mesh.devices.reshape(span // 2, 2, ring), DP + ("fsdp",))
    every = DP + ("fsdp",)
    rows, matrix, vector = P(DP, "fsdp", None), P(every, None), P(every)
    in_specs = (rows,) * 5 + (matrix,) * 7 + (vector,) * 2 + (rows,)
    out_specs = (rows,) * 2 + (matrix,) * 7 + (vector,) * 2
    return jax.shard_map(body, mesh=fine, in_specs=in_specs, out_specs=out_specs, check_vma=False)
```

```python
import functools
import math

import jax
import jax.numpy as jnp
import numpy as np
from jax import lax
from jax.experimental import pallas as pl
from jax.experimental.pallas import tpu as pltpu
from jax.sharding import Mesh
from jax.sharding import PartitionSpec as P

HEAD_DIM = 128
QBLK = 256
MBLK = 128
EPSILON = 1e-06
NEGATIVE = -1e30
SCALE = 1.0 / math.sqrt(HEAD_DIM)
LOG2E = math.log2(math.e)
MIB = 1 << 20
F32 = jnp.float32
BF16 = jnp.bfloat16
DP = ("chip", "core")
NT = (((1,), (1,)), ((), ()))
TN = (((0,), (0,)), ((), ()))


def dot(left, right, dims=(((1,), (0,)), ((), ()))):
    return lax.dot_general(left, right, dims, preferred_element_type=F32)


def rotary_tables(length):
    half_dim = HEAD_DIM // 2
    frequency = 10000.0 ** (-jnp.arange(half_dim, dtype=F32) / half_dim)
    angles = jnp.arange(length, dtype=jnp.int32).astype(F32)[:, None] * frequency[None, :]
    cosine, sine = jnp.cos(angles), jnp.sin(angles)
    return jnp.concatenate([cosine, cosine], 1), jnp.concatenate([-sine, sine], 1)


def qkv_kernel(heads, tok_ref, gain_ref, w_ref, cos_ref, sin_ref, qkv_ref):
    rows = tok_ref[...].astype(F32)
    factor = lax.rsqrt(jnp.mean(rows * rows, -1, keepdims=True) + EPSILON)
    normed = (rows * factor * gain_ref[...]).astype(BF16)
    cosine, sine = cos_ref[...], sin_ref[...]
    wide = heads * HEAD_DIM
    for part in range(3):
        values = dot(normed, w_ref[:, part * wide : (part + 1) * wide])
        for head in range(heads):
            value = values[:, head * HEAD_DIM : (head + 1) * HEAD_DIM]
            if part < 2:
                value = value * cosine + pltpu.roll(value, HEAD_DIM // 2, 1) * sine
            if part == 0:
                value = value * (SCALE * LOG2E)
            at = part * wide + head * HEAD_DIM
            qkv_ref[:, at : at + HEAD_DIM] = value.astype(BF16)


def project_qkv(tokens_all, gain, w_qkv, cosine, sine, heads):
    length, width = tokens_all.shape
    columns = w_qkv.shape[1]
    block = 2 * QBLK
    return pl.pallas_call(
        functools.partial(qkv_kernel, heads),
        grid=(length // block,),
        in_specs=[
            pl.BlockSpec((block, width), lambda i: (i, 0)),
            pl.BlockSpec((1, width), lambda i: (0, 0)),
            pl.BlockSpec((width, columns), lambda i: (0, 0)),
            pl.BlockSpec((block, HEAD_DIM), lambda i: (i, 0)),
            pl.BlockSpec((block, HEAD_DIM), lambda i: (i, 0)),
        ],
        out_specs=pl.BlockSpec((block, columns), lambda i: (i, 0)),
        out_shape=jax.ShapeDtypeStruct((length, columns), BF16),
        compiler_params=pltpu.CompilerParams(vmem_limit_bytes=48 * MIB),
        cost_estimate=pl.CostEstimate(
            flops=2 * length * width * columns, bytes_accessed=4 * length * (width + columns), transcendentals=0
        ),
        name="project_qkv",
    )(tokens_all, gain, w_qkv, cosine, sine)


def memory_bias(counts_ref, base, top, axis):
    shape = (1, top * MBLK) if axis == 1 else (top * MBLK, 1)
    column = lax.broadcasted_iota(jnp.int32, shape, axis)
    limit = jnp.zeros(shape, jnp.int32)
    for entry in range(top):
        inside = (column >= entry * MBLK) & (column < entry * MBLK + counts_ref[base + entry])
        limit = jnp.where(inside, 1, limit)
    return jnp.where(limit > 0, 0.0, NEGATIVE)


def pick_memory(ref, chosen_ref, base, top, columns):
    rows = [
        ref[pl.ds(pl.multiple_of(chosen_ref[base + entry] * MBLK, MBLK), MBLK), columns]
        for entry in range(top)
    ]
    return jnp.concatenate(rows, 0)


def forward_kernel(
    heads, top, chosen_ref, counts_ref, q_ref, k_ref, v_ref, mk_ref, mv_ref, out_ref, lse_ref, acc_s, peak_s
):
    block = pl.program_id(0)
    rows = q_ref.shape[0]
    subs = rows // QBLK
    ones = jnp.ones((rows, HEAD_DIM), BF16)
    mem_ones = jnp.ones((top * MBLK, HEAD_DIM), BF16)
    for sub in range(subs):
        base = (block * subs + sub) * top
        here = slice(sub * QBLK, (sub + 1) * QBLK)
        span = (sub + 1) * QBLK
        seen = pl.ds(pl.multiple_of(block * rows, rows), span)
        row = lax.broadcasted_iota(jnp.int32, (QBLK, span), 0) + sub * QBLK
        causal = row >= lax.broadcasted_iota(jnp.int32, (QBLK, span), 1)
        bias = memory_bias(counts_ref, base, top, 1)
        for head in range(heads):
            columns = slice(head * HEAD_DIM, (head + 1) * HEAD_DIM)
            query = q_ref[here, columns]
            remote = dot(query, pick_memory(mk_ref, chosen_ref, base, top, columns), NT) + bias
            local = jnp.where(causal, dot(query, k_ref[seen, columns], NT), NEGATIVE)
            peak = jnp.maximum(jnp.max(local, -1, keepdims=True), jnp.max(remote, -1, keepdims=True))
            values = jnp.concatenate([v_ref[seen, columns], ones[:span]], 1)
            acc = dot(jnp.exp2(local - peak).astype(BF16), values)
            values = jnp.concatenate([pick_memory(mv_ref, chosen_ref, base, top, columns), mem_ones], 1)
            acc_s[head, here] = acc + dot(jnp.exp2(remote - peak).astype(BF16), values)
            peak_s[head, here] = jnp.broadcast_to(peak, (QBLK, HEAD_DIM))

    def step(index, carry):
        there = pl.ds(pl.multiple_of(index * rows, rows), rows)
        for head in range(heads):
            columns = slice(head * HEAD_DIM, (head + 1) * HEAD_DIM)
            peak = peak_s[head][:, :1]
            scores = dot(q_ref[:, columns], k_ref[there, columns], NT)
            higher = jnp.maximum(peak, jnp.max(scores, -1, keepdims=True))
            weights = jnp.exp2(scores - higher).astype(BF16)
            values = jnp.concatenate([v_ref[there, columns], ones], 1)
            acc_s[head] = acc_s[head] * jnp.exp2(peak - higher) + dot(weights, values)
            peak_s[head] = jnp.broadcast_to(higher, (rows, HEAD_DIM))
        return carry

    lax.fori_loop(0, block, step, 0)
    for head in range(heads):
        columns = slice(head * HEAD_DIM, (head + 1) * HEAD_DIM)
        total = acc_s[head][:, HEAD_DIM:]
        out_ref[:, columns] = (acc_s[head][:, :HEAD_DIM] / total).astype(BF16)
        lse_ref[:, head : head + 1] = peak_s[head][:, :1] + jnp.log2(total[:, :1])


def attend_forward(chosen, counts, qkv, memory, heads, top):
    length = qkv.shape[0]
    wide = heads * HEAD_DIM
    rows = min(2 * QBLK, length)
    mem_rows = memory.shape[0]
    return pl.pallas_call(
        functools.partial(forward_kernel, heads, top),
        grid_spec=pltpu.PrefetchScalarGridSpec(
            num_scalar_prefetch=2,
            grid=(length // rows,),
            in_specs=[
                pl.BlockSpec((rows, wide), lambda i, *_: (i, 0)),
                pl.BlockSpec((length, wide), lambda i, *_: (0, 1)),
                pl.BlockSpec((length, wide), lambda i, *_: (0, 2)),
                pl.BlockSpec((mem_rows, wide), lambda i, *_: (0, 0)),
                pl.BlockSpec((mem_rows, wide), lambda i, *_: (0, 1)),
            ],
            out_specs=[
                pl.BlockSpec((rows, wide), lambda i, *_: (i, 0)),
                pl.BlockSpec((rows, heads), lambda i, *_: (i, 0)),
            ],
            scratch_shapes=[
                pltpu.VMEM((heads, rows, 2 * HEAD_DIM), F32),
                pltpu.VMEM((heads, rows, HEAD_DIM), F32),
            ],
        ),
        out_shape=[
            jax.ShapeDtypeStruct((length, wide), BF16),
            jax.ShapeDtypeStruct((length, heads), F32),
        ],
        compiler_params=pltpu.CompilerParams(vmem_limit_bytes=48 * MIB),
        cost_estimate=pl.CostEstimate(
            flops=4 * heads * length * HEAD_DIM * (length // 2 + top * MBLK),
            bytes_accessed=8 * length * wide,
            transcendentals=heads * length * (length // 2 + top * MBLK),
        ),
        name="attend_forward",
    )(chosen, counts, qkv, qkv, qkv, memory, memory)


def spread_rows(column):
    rows = column.shape[0]
    return jnp.transpose(jnp.broadcast_to(column, (rows, HEAD_DIM)))[:1]


def row_stats(grad_out, out, lse):
    delta = jnp.sum(grad_out.astype(F32) * out.astype(F32), -1, keepdims=True)
    return jnp.concatenate([spread_rows(lse), spread_rows(delta)], 0)


def score_grads(query, grad_out, stats, keys, values, mask):
    weights = jnp.exp2(mask(dot(keys, query, NT)) - stats[:1])
    grad_weights = dot(values, grad_out, NT)
    return weights.astype(BF16), (weights * (grad_weights - stats[1:2])).astype(BF16)


def causal_mask(rows):
    key_at = lax.broadcasted_iota(jnp.int32, (rows, rows), 0)
    query_at = lax.broadcasted_iota(jnp.int32, (rows, rows), 1)
    return lambda scores: jnp.where(query_at >= key_at, scores, NEGATIVE)


def memory_query_grad(chosen_ref, counts_ref, base, top, query, grad_out, stats, mk_ref, mv_ref, columns):
    keys = pick_memory(mk_ref, chosen_ref, base, top, columns)
    values = pick_memory(mv_ref, chosen_ref, base, top, columns)
    bias = memory_bias(counts_ref, base, top, 0)
    _, grad_scores = score_grads(query, grad_out, stats, keys, values, lambda scores: scores + bias)
    return dot(grad_scores, keys, TN)


def block_grads(heads, grad_query, grad_key, grad_value, cosine, sine):
    def unturn(value):
        return (value * cosine - pltpu.roll(value, HEAD_DIM // 2, 1) * sine).astype(BF16)

    parts = []
    for part, array in enumerate((grad_query * SCALE, grad_key * (1.0 / LOG2E), grad_value)):
        for head in range(heads):
            value = array[:, head * HEAD_DIM : (head + 1) * HEAD_DIM]
            parts.append(unturn(value) if part < 2 else value.astype(BF16))
    return jnp.concatenate(parts, 1)


def first_block_kernel(
    heads, top, chosen_ref, counts_ref, plan_ref, qkv_ref, mk_ref, mv_ref, go_ref, out_ref, lse_ref, cos_ref, sin_ref,
    w_ref, partial_ref, whole_ref, grad_ref, gq_ref, gk_ref, gv_ref, stats_s,
):
    rows = partial_ref.shape[0]
    subs = rows // QBLK
    wide = heads * HEAD_DIM
    others = go_ref.shape[0] // rows - 1
    block, is_last = plan_ref[0], plan_ref[1]
    own = pl.ds(pl.multiple_of(block * rows, rows), rows)
    gq_ref[...] = jnp.zeros_like(gq_ref)
    gk_ref[...] = jnp.zeros_like(gk_ref)
    gv_ref[...] = jnp.zeros_like(gv_ref)

    def note_stats(slot, here):
        for head in range(heads):
            columns = slice(head * HEAD_DIM, (head + 1) * HEAD_DIM)
            stats_s[slot, head] = row_stats(go_ref[here, columns], out_ref[here, columns], lse_ref[here, head : head + 1])

    note_stats(0, own)

    def pair(slot, queries, keys, mask):
        for head in range(heads):
            at = head * HEAD_DIM
            columns = slice(at, at + HEAD_DIM)
            query, grad_out = qkv_ref[queries, columns], go_ref[queries, columns]
            key = qkv_ref[keys, wide + at : wide + at + HEAD_DIM]
            value = qkv_ref[keys, 2 * wide + at : 2 * wide + at + HEAD_DIM]
            weights, grad_scores = score_grads(query, grad_out, stats_s[slot, head], key, value, mask)
            gk_ref[keys, columns] += dot(grad_scores, query)
            gv_ref[keys, columns] += dot(weights, grad_out)
            gq_ref[queries, columns] += dot(grad_scores, key, TN)

    for head in range(heads):
        columns = slice(head * HEAD_DIM, (head + 1) * HEAD_DIM)
        for sub in range(subs):
            here = pl.ds(pl.multiple_of(block * rows + sub * QBLK, QBLK), QBLK)
            gq_ref[here, columns] += memory_query_grad(
                chosen_ref, counts_ref, (block * subs + sub) * top, top, qkv_ref[here, columns], go_ref[here, columns],
                stats_s[0, head][:, sub * QBLK : (sub + 1) * QBLK], mk_ref, mv_ref, columns,
            )
    pair(0, own, own, causal_mask(rows))

    def step(index, carry):
        other = jnp.where(is_last == 1, index, index + 1)
        there = pl.ds(pl.multiple_of(other * rows, rows), rows)

        @pl.when(is_last == 1)
        def _():
            pair(0, own, there, lambda scores: scores)

        @pl.when(is_last == 0)
        def _():
            note_stats(1, there)
            pair(1, there, own, lambda scores: scores)

        return carry

    lax.fori_loop(0, others, step, 0)
    grad = block_grads(
        heads, gq_ref[own, :], gk_ref[own, :], gv_ref[own, :], cos_ref[...], sin_ref[...]
    )
    grad_ref[...] = grad
    partial = dot(grad, w_ref[...], NT).astype(BF16)
    partial_ref[...] = partial
    whole_ref[...] = partial


def first_block(plan, chosen, counts, qkv, memory, grad_out, out, lse, cosine, sine, w_qkv, heads, top):
    length = qkv.shape[0]
    width = w_qkv.shape[0]
    wide = heads * HEAD_DIM
    rows = min(2 * QBLK, length)
    mem_rows = memory.shape[0]

    def whole(array):
        return pl.BlockSpec(array.shape, lambda i, *_: (0, 0))

    sums = pl.BlockSpec((length, wide), lambda i, *_: (0, 0))
    return pl.pallas_call(
        functools.partial(first_block_kernel, heads, top),
        grid_spec=pltpu.PrefetchScalarGridSpec(
            num_scalar_prefetch=3,
            grid=(1,),
            in_specs=[
                whole(qkv),
                pl.BlockSpec((mem_rows, wide), lambda i, *_: (0, 0)),
                pl.BlockSpec((mem_rows, wide), lambda i, *_: (0, 1)),
                whole(grad_out),
                whole(out),
                whole(lse),
                pl.BlockSpec((rows, HEAD_DIM), lambda i, c, n, plan: (plan[0], 0)),
                pl.BlockSpec((rows, HEAD_DIM), lambda i, c, n, plan: (plan[0], 0)),
                whole(w_qkv),
            ],
            out_specs=[
                pl.BlockSpec((rows, width), lambda i, *_: (0, 0)),
                pl.BlockSpec((rows, width), lambda i, c, n, plan: (plan[0], 0)),
                pl.BlockSpec((rows, 3 * wide), lambda i, *_: (0, 0)),
                sums,
                sums,
                sums,
            ],
            scratch_shapes=[pltpu.VMEM((2, heads, 2, rows), F32)],
        ),
        out_shape=[
            jax.ShapeDtypeStruct((rows, width), BF16),
            jax.ShapeDtypeStruct((length, width), BF16),
            jax.ShapeDtypeStruct((rows, 3 * wide), BF16),
            *[jax.ShapeDtypeStruct((length, wide), F32)] * 3,
        ],
        compiler_params=pltpu.CompilerParams(vmem_limit_bytes=60 * MIB),
        cost_estimate=pl.CostEstimate(
            flops=4 * heads * length * HEAD_DIM * length,
            bytes_accessed=40 * length * wide,
            transcendentals=heads * length * rows,
        ),
        name="first_block",
    )(chosen, counts, plan, qkv, memory, memory, grad_out, out, lse, cosine, sine, w_qkv)


def other_blocks_kernel(
    heads, top, chosen_ref, counts_ref, plan_ref, q_ref, k_ref, v_ref, mk_ref, mv_ref, go_ref, out_ref, lse_ref,
    cos_ref, sin_ref, w_ref, gq_in, gk_in, gv_in, _, partial_ref, grad_ref, gk_s, gv_s, gq_s,
):
    low = plan_ref[0]
    block = low + pl.num_programs(0) - 1 - pl.program_id(0)
    rows = q_ref.shape[0]
    subs = rows // QBLK
    own = pl.ds(pl.multiple_of(block * rows, rows), rows)

    @pl.when(pl.program_id(0) == 0)
    def _():
        gk_s[...] = gk_in[...]
        gv_s[...] = gv_in[...]

    stats = []
    for head in range(heads):
        columns = slice(head * HEAD_DIM, (head + 1) * HEAD_DIM)
        stats.append(row_stats(go_ref[:, columns], out_ref[:, columns], lse_ref[:, head : head + 1]))
        for sub in range(subs):
            here = slice(sub * QBLK, (sub + 1) * QBLK)
            gq_s[here, columns] = gq_in[here, columns] + memory_query_grad(
                chosen_ref, counts_ref, (block * subs + sub) * top, top, q_ref[here, columns], go_ref[here, columns],
                stats[head][:, here], mk_ref, mv_ref, columns,
            )

    def local(there, mask):
        for head in range(heads):
            columns = slice(head * HEAD_DIM, (head + 1) * HEAD_DIM)
            query, grad_out = q_ref[:, columns], go_ref[:, columns]
            key = k_ref[there, columns]
            weights, grad_scores = score_grads(query, grad_out, stats[head], key, v_ref[there, columns], mask)
            gk_s[there, columns] += dot(grad_scores, query)
            gv_s[there, columns] += dot(weights, grad_out)
            gq_s[:, columns] += dot(grad_scores, key, TN)

    local(own, causal_mask(rows))

    def step(index, carry):
        local(pl.ds(pl.multiple_of(index * rows, rows), rows), lambda scores: scores)
        return carry

    lax.fori_loop(low, block, step, 0)
    grad = block_grads(heads, gq_s[...], gk_s[own, :], gv_s[own, :], cos_ref[...], sin_ref[...])
    grad_ref[...] = grad
    partial_ref[...] = dot(grad, w_ref[...], NT).astype(BF16)


def other_blocks(plan, chosen, counts, qkv, memory, grad_out, out, lse, cosine, sine, w_qkv, sums, partials, heads, top):
    length = qkv.shape[0]
    width = w_qkv.shape[0]
    wide = heads * HEAD_DIM
    rows = min(2 * QBLK, length)
    count = length // rows - 1
    mem_rows = memory.shape[0]

    def by_rows(columns, at=0):
        return pl.BlockSpec((rows, columns), lambda i, c, n, plan: (plan[0] + count - 1 - i, at))

    def result(columns):
        return pl.BlockSpec((rows, columns), lambda i, *_: (count - 1 - i, 0))

    return pl.pallas_call(
        functools.partial(other_blocks_kernel, heads, top),
        grid_spec=pltpu.PrefetchScalarGridSpec(
            num_scalar_prefetch=3,
            grid=(count,),
            in_specs=[
                by_rows(wide),
                pl.BlockSpec((length, wide), lambda i, *_: (0, 1)),
                pl.BlockSpec((length, wide), lambda i, *_: (0, 2)),
                pl.BlockSpec((mem_rows, wide), lambda i, *_: (0, 0)),
                pl.BlockSpec((mem_rows, wide), lambda i, *_: (0, 1)),
                by_rows(wide),
                by_rows(wide),
                by_rows(heads),
                by_rows(HEAD_DIM),
                by_rows(HEAD_DIM),
                pl.BlockSpec((width, 3 * wide), lambda i, *_: (0, 0)),
                by_rows(wide),
                pl.BlockSpec((length, wide), lambda i, *_: (0, 0)),
                pl.BlockSpec((length, wide), lambda i, *_: (0, 0)),
                pl.BlockSpec(memory_space=pl.ANY),
            ],
            out_specs=[by_rows(width), result(3 * wide)],
            scratch_shapes=[
                pltpu.VMEM((length, wide), F32),
                pltpu.VMEM((length, wide), F32),
                pltpu.VMEM((rows, wide), F32),
            ],
        ),
        out_shape=[
            jax.ShapeDtypeStruct((length, width), BF16),
            jax.ShapeDtypeStruct((count * rows, 3 * wide), BF16),
        ],
        input_output_aliases={17: 0},
        compiler_params=pltpu.CompilerParams(vmem_limit_bytes=60 * MIB),
        cost_estimate=pl.CostEstimate(
            flops=6 * heads * length * HEAD_DIM * (length + top * MBLK),
            bytes_accessed=40 * length * wide,
            transcendentals=heads * length * (length // 3 + top * MBLK),
        ),
        name="other_blocks",
    )(chosen, counts, plan, qkv, qkv, qkv, memory, memory, grad_out, out, lse, cosine, sine, w_qkv, *sums, partials)


def ffn_kernel(
    span, merged, tok_ref, att_ref, cot_ref, gain_ref, out_w, gate_w, up_w, down_w,
    mixed_ref, grad_mid_ref, grad_att_ref, gain_grad_ref, out_grads_ref, grads_ref, *rest,
):
    if not merged:
        down_grads_ref, rest = rest[0], rest[1:]
    middle_s, normed_s, turned_s, mixed_s, upstream_s, gate_s, up_s, down_s, out_s, sems, late_sems = rest
    step, steps = pl.program_id(0), pl.num_programs(0)
    width = tok_ref.shape[1]
    share = width // span
    wide = gate_w.shape[1]
    hidden_width = down_s.shape[0]
    tall = hidden_width // span
    lanes = width // wide
    first = tall * lanes if merged else 0
    slot = step % 2

    @pl.when(step == 0)
    def _():
        middle = tok_ref[...].astype(F32) + dot(att_ref[...], out_w[...])
        middle_s[...] = middle
        factor = lax.rsqrt(jnp.mean(middle * middle, -1, keepdims=True) + EPSILON)
        normed = (middle * factor * gain_ref[...]).astype(BF16)
        normed_s[...] = normed
        turned_s[...] = jnp.transpose(normed)
        mixed_s[...] = middle
        upstream_s[...] = jnp.zeros_like(upstream_s)

    def copy_out(kind, which, index):
        source = (gate_s, up_s)[kind].at[which]
        start = first + (kind * steps + index) * share
        target = grads_ref.at[:, pl.ds(start, share), :]
        return pltpu.make_async_copy(source, target, sems.at[kind, which])

    normed = normed_s[...]
    upstream = cot_ref[...]
    both = jnp.concatenate([gate_w[...], up_w[...]], 1)
    acts = dot(normed, both)
    gate_act, up_act = acts[:, :wide], acts[:, wide:]
    grad_hidden = dot(upstream, down_w[...], NT)
    sigmoid = jax.nn.sigmoid(gate_act)
    silu = gate_act * sigmoid
    hidden = (silu * up_act).astype(BF16)
    grad_gate = (grad_hidden * up_act * sigmoid * (1.0 + gate_act * (1.0 - sigmoid))).astype(BF16)
    grad_up = (grad_hidden * silu).astype(BF16)
    mixed_s[...] += dot(hidden, down_w[...])
    grad_acts = jnp.concatenate([grad_gate, grad_up], 1)
    upstream_s[...] += dot(grad_acts, both, NT)
    down_s[pl.ds(pl.multiple_of(step * wide, wide), wide), :] = dot(hidden, upstream, TN).astype(BF16)

    @pl.when(step >= 2)
    def _():
        copy_out(0, slot, step - 2).wait()
        copy_out(1, slot, step - 2).wait()

    weight_grads = dot(turned_s[...], grad_acts).astype(BF16)
    gate_s[slot] = weight_grads[:, :wide].reshape(span, share, wide)
    up_s[slot] = weight_grads[:, wide:].reshape(span, share, wide)
    copy_out(0, slot, step).start()
    copy_out(1, slot, step).start()

    @pl.when(step == steps - 1)
    def _():
        copies = []
        if merged:
            for place in range(span):
                for lane in range(lanes):
                    copies.append(
                        pltpu.make_async_copy(
                            down_s.at[pl.ds(place * tall, tall), pl.ds(lane * wide, wide)],
                            grads_ref.at[place, pl.ds(lane * tall, tall), :],
                            late_sems.at[len(copies)],
                        )
                    )
        else:
            copies.append(pltpu.make_async_copy(down_s, down_grads_ref, late_sems.at[0]))
        for copy in copies:
            copy.start()
        mixed_ref[...] = mixed_s[...].astype(BF16)
        middle = middle_s[...]
        grad = upstream_s[...]
        factor = lax.rsqrt(jnp.mean(middle * middle, -1, keepdims=True) + EPSILON)
        gain_grad_ref[...] = jnp.sum(grad * middle * factor, 0, keepdims=True)
        scaled = grad * gain_ref[...]
        inner = jnp.mean(scaled * middle, -1, keepdims=True)
        grad_middle = cot_ref[...].astype(F32) + factor * scaled - middle * (factor * factor * factor * inner)
        grad_mid_ref[...] = grad_middle
        branch = grad_middle.astype(BF16)
        grad_att_ref[...] = dot(branch, out_w[...], NT).astype(BF16)
        turned_att = jnp.transpose(att_ref[...])
        for lane in range(lanes):
            columns = slice(lane * wide, (lane + 1) * wide)
            out_s[lane] = dot(turned_att, branch[:, columns]).astype(BF16).reshape(span, share, wide)
            more = pltpu.make_async_copy(
                out_s.at[lane],
                out_grads_ref.at[:, :, pl.ds(lane * wide, wide)],
                late_sems.at[len(copies)],
            )
            more.start()
            copies.append(more)
        for copy in copies:
            copy.wait()
        copy_out(0, 1 - slot, step - 1).wait()
        copy_out(1, 1 - slot, step - 1).wait()
        copy_out(0, slot, step).wait()
        copy_out(1, slot, step).wait()


def feed_forward(tokens, attended, upstream, gain, weights, w_down, span):
    rows, width = tokens.shape
    hidden_width = w_down.shape[0]
    wide = 2 * HEAD_DIM
    steps = hidden_width // wide
    lanes = width // wide
    share = width // span
    tall = hidden_width // span
    merged = tall % 16 == 0
    total = 2 * steps * share + (lanes * tall if merged else 0)
    shapes = [
        jax.ShapeDtypeStruct((rows, width), BF16),
        jax.ShapeDtypeStruct((rows, width), F32),
        jax.ShapeDtypeStruct((rows, width), BF16),
        jax.ShapeDtypeStruct((1, width), F32),
        jax.ShapeDtypeStruct((span, share, width), BF16),
        jax.ShapeDtypeStruct((span, total, wide), BF16),
    ]
    specs = [
        pl.BlockSpec((rows, width), lambda i: (0, 0)),
        pl.BlockSpec((rows, width), lambda i: (0, 0)),
        pl.BlockSpec((rows, width), lambda i: (0, 0)),
        pl.BlockSpec((1, width), lambda i: (0, 0)),
        pl.BlockSpec(memory_space=pl.ANY),
        pl.BlockSpec(memory_space=pl.ANY),
    ]
    if not merged:
        shapes.append(jax.ShapeDtypeStruct((hidden_width, width), BF16))
        specs.append(pl.BlockSpec(memory_space=pl.ANY))
    return pl.pallas_call(
        functools.partial(ffn_kernel, span, merged),
        grid=(steps,),
        in_specs=[
            pl.BlockSpec((rows, width), lambda i: (0, 0)),
            pl.BlockSpec((rows, width), lambda i: (0, 0)),
            pl.BlockSpec((rows, width), lambda i: (0, 0)),
            pl.BlockSpec((1, width), lambda i: (0, 0)),
            pl.BlockSpec((width, width), lambda i: (0, 0)),
            pl.BlockSpec((width, wide), lambda i: (0, lanes + i)),
            pl.BlockSpec((width, wide), lambda i: (0, lanes + steps + i)),
            pl.BlockSpec((wide, width), lambda i: (i, 0)),
        ],
        out_specs=specs,
        out_shape=shapes,
        scratch_shapes=[
            pltpu.VMEM((rows, width), F32),
            pltpu.VMEM((rows, width), BF16),
            pltpu.VMEM((width, rows), BF16),
            pltpu.VMEM((rows, width), F32),
            pltpu.VMEM((rows, width), F32),
            pltpu.VMEM((2, span, share, wide), BF16),
            pltpu.VMEM((2, span, share, wide), BF16),
            pltpu.VMEM((hidden_width, width), BF16),
            pltpu.VMEM((lanes, span, share, wide), BF16),
            pltpu.SemaphoreType.DMA((2, 2)),
            pltpu.SemaphoreType.DMA(((span * lanes if merged else 1) + lanes,)),
        ],
        compiler_params=pltpu.CompilerParams(vmem_limit_bytes=56 * MIB),
        cost_estimate=pl.CostEstimate(
            flops=6 * rows * width * (3 * hidden_width + width),
            bytes_accessed=4 * width * (3 * hidden_width + width),
            transcendentals=rows * hidden_width,
        ),
        name="feed_forward",
    )(tokens, attended, upstream, gain, weights, weights, weights, w_down)


def projection_grads_kernel(
    order_ref, tok_ref, gain_ref, w_ref, first_ref, other_ref, grad_w_ref, gain_grad_ref, raw_s
):
    step = pl.program_id(0)

    @pl.when(step == 0)
    def _():
        raw_s[...] = jnp.zeros_like(raw_s)

    tokens = tok_ref[...].astype(F32)
    tokens = tokens * lax.rsqrt(jnp.mean(tokens * tokens, -1, keepdims=True) + EPSILON)
    grad = jnp.where(step == 0, first_ref[...], other_ref[...])
    raw_s[...] += dot(tokens.astype(BF16), grad, TN)

    @pl.when(step == pl.num_programs(0) - 1)
    def _():
        raw = raw_s[...]
        gain_grad_ref[...] = jnp.sum(raw * w_ref[...].astype(F32), -1, keepdims=True)
        grad_w_ref[...] = (raw * gain_ref[...]).astype(BF16)


def projection_grads(order, tokens_all, gain_column, w_qkv, first_grad, other_grad):
    length, width = tokens_all.shape
    columns = first_grad.shape[1]
    rows = min(2 * QBLK, length)
    return pl.pallas_call(
        projection_grads_kernel,
        grid_spec=pltpu.PrefetchScalarGridSpec(
            num_scalar_prefetch=1,
            grid=(length // rows,),
            in_specs=[
                pl.BlockSpec((rows, width), lambda i, order: (order[i], 0)),
                pl.BlockSpec((width, 1), lambda i, _: (0, 0)),
                pl.BlockSpec((width, columns), lambda i, _: (0, 0)),
                pl.BlockSpec((rows, columns), lambda i, _: (0, 0)),
                pl.BlockSpec((rows, columns), lambda i, _: (jnp.maximum(i - 1, 0), 0)),
            ],
            out_specs=[
                pl.BlockSpec((width, columns), lambda i, _: (0, 0)),
                pl.BlockSpec((width, 1), lambda i, _: (0, 0)),
            ],
            scratch_shapes=[pltpu.VMEM((width, columns), F32)],
        ),
        out_shape=[
            jax.ShapeDtypeStruct((width, columns), BF16),
            jax.ShapeDtypeStruct((width, 1), F32),
        ],
        compiler_params=pltpu.CompilerParams(vmem_limit_bytes=48 * MIB),
        cost_estimate=pl.CostEstimate(
            flops=2 * length * width * columns, bytes_accessed=2 * length * (width + columns), transcendentals=0
        ),
        name="projection_grads",
    )(order, tokens_all, gain_column, w_qkv, first_grad, other_grad)


def after(value, earlier):
    return lax.optimization_barrier((value, earlier))[0]


def chain_gather(blocks, axis):
    size = lax.axis_size(axis)
    place = lax.axis_index(axis)
    steps = []
    rising = falling = tuple(blocks)
    for step in range(size - 1):
        up = [(i, i + 1) for i in range(step, size - 1)]
        down = [(i + 1, i) for i in range(size - 1 - step)]
        rising = tuple(lax.ppermute(block, axis, up) for block in rising)
        falling = tuple(lax.ppermute(block, axis, down) for block in falling)
        if len(blocks) > 1:
            rising, falling = lax.optimization_barrier((rising, falling))
        steps.append((rising, falling))
    results = []
    for number, block in enumerate(blocks):
        ordered = []
        for index in range(size):
            cases = []
            for mine in range(size):
                if mine == index:
                    cases.append(block)
                elif mine > index:
                    cases.append(steps[mine - index - 1][0][number])
                else:
                    cases.append(steps[index - mine - 1][1][number])
            ordered.append(lax.select_n(place, *cases) if size > 2 else lax.select_n(place > 0, *cases))
        results.append(ordered)
    return results, steps


def chain_scatter(block, axis, waits):
    size = lax.axis_size(axis)
    place = lax.axis_index(axis)
    arrived = []
    for step in range(size - 1):
        up, down = block(step, size - 1 - step + place), block(step, step - size + 1 + place)
        if step:
            up, down = up + arrived[-1][0].astype(F32), down + arrived[-1][1].astype(F32)
        ready = waits[step - 1](sent) if 0 < step <= len(waits) else None
        up, down, _ = lax.optimization_barrier((up.astype(BF16), down.astype(BF16), ready))
        sent = up, down
        rising = lax.ppermute(up, axis, [(i, i + 1) for i in range(step + 1)])
        falling = lax.ppermute(down, axis, [(i, i - 1) for i in range(size - 1 - step, size)])
        arrived.append(lax.optimization_barrier((rising, falling)))
    return block(size, place), arrived


def direct_exchange(blocks, axis):
    size = lax.axis_size(axis)
    place = lax.axis_index(axis)
    taken = [lax.dynamic_index_in_dim(blocks, place, 0, keepdims=False)]
    for far in range(1, size):
        give = lax.dynamic_index_in_dim(blocks, (place + far) % size, 0, keepdims=False)
        taken.append(lax.ppermute(give, axis, [(i, (i + far) % size) for i in range(size)]))
    return taken


def body(
    tokens, memory_keys, memory_values, chosen, counts, w_query, w_key, w_value, w_out, w_gate, w_up, w_down,
    gain_attn, gain_ffn, cotangent,
):
    ring, span = lax.axis_size("fsdp"), lax.axis_size(DP)
    rows, width = tokens.shape[1:]
    heads = width // HEAD_DIM // ring
    wide = heads * HEAD_DIM
    length = rows * ring
    top = chosen.shape[2]
    hidden_width = w_gate.shape[1]
    share = w_query.shape[0]
    mine = tokens[0]

    extra = 8 if share % 8 == 0 else 8 - share % 8
    parts = [w.reshape(share, ring, wide).transpose(1, 0, 2) for w in (w_query, w_key, w_value)]
    choices = jnp.concatenate([chosen[0].reshape(-1), counts[0].reshape(-1)]).astype(BF16)
    notes = jnp.stack(
        [
            jnp.pad(row, (0, 3 * wide - row.shape[0]))
            for row in (jnp.concatenate([gain_attn, gain_ffn]), choices)
        ]
    )
    notes = jnp.broadcast_to(jnp.pad(notes, ((0, extra - 2), (0, 0))), (ring, extra, 3 * wide))
    parcel = jnp.concatenate([jnp.concatenate(parts, 2), notes], 1)
    parcel = lax.all_to_all(parcel, "fsdp", 0, 0, tiled=True)
    picks = parcel[:, share + 1, : choices.shape[0]].astype(jnp.int32).reshape(ring, 2, -1)
    chosen_all, counts_all = picks[:, 0].reshape(-1), picks[:, 1].reshape(-1)
    shards = jnp.concatenate([w_out, w_gate, w_up], 1)
    (near, near_down), steps = chain_gather((shards, w_down), "fsdp")
    (gathered,), token_steps = chain_gather((after(mine, steps[-2]),), "fsdp")
    parcel = lax.all_gather(after(parcel, steps[0]), DP, axis=0, tiled=True)
    w_qkv = parcel[:, :share].reshape(width, 3 * wide)
    gain_one = parcel[:, share, :share].reshape(1, width).astype(F32)
    gain_two = parcel[:, share, share : 2 * share].reshape(1, width).astype(F32)
    first = lax.all_gather(jnp.concatenate(near, 0), DP, axis=0, tiled=True)
    gathered = jnp.concatenate(gathered, 0)

    memory = jnp.concatenate(
        [m[0].reshape(-1, ring, wide).transpose(1, 0, 2) for m in (memory_keys, memory_values)], 2
    )
    memory = lax.all_to_all(after(memory, token_steps[-2]), "fsdp", 0, 0, tiled=True).reshape(-1, 2 * wide)
    down_full = lax.all_gather(jnp.concatenate(near_down, 0), DP, axis=0, tiled=True)

    cosine, sine = rotary_tables(length)
    qkv = project_qkv(gathered, gain_one, w_qkv, cosine, sine, heads)
    attended_heads, lse = attend_forward(chosen_all, counts_all, qkv, memory, heads, top)
    attended = lax.all_to_all(attended_heads, "fsdp", 0, 1, tiled=True)

    upstream = cotangent[0]
    mixed, grad_middle, grad_attended, gain_two_grad, out_grads, grads, *grad_down = feed_forward(
        mine, attended, upstream, gain_two, first, down_full, span
    )
    grad_heads = lax.all_to_all(grad_attended, "fsdp", 1, 0, tiled=True)
    grads = lax.psum_scatter(grads, DP, scatter_dimension=0, tiled=True)[0]

    core = lax.axis_index("core")

    def over_cores(array):
        array = array.reshape((-1, 2) + array.shape[1:])
        taken = lax.ppermute(lax.dynamic_index_in_dim(array, 1 - core, 1, keepdims=False), "core", [(0, 1), (1, 0)])
        return (lax.dynamic_index_in_dim(array, core, 1, keepdims=False).astype(F32) + taken.astype(F32)).astype(BF16)

    def over_chips(array):
        return sum(piece.astype(F32) for piece in direct_exchange(array, "chip")).astype(BF16)

    out_grads = over_chips(out_grads.reshape((span // 2, 2) + out_grads.shape[1:]))

    place = lax.axis_index("fsdp").astype(jnp.int32)
    count = length // min(2 * QBLK, length)
    is_last = (place < ring // 2).astype(jnp.int32)
    first_number = jnp.where(is_last == 1, count - 1, 0).astype(jnp.int32)
    low = 1 - is_last
    first_partial, partials, first_grad, *sums = first_block(
        jnp.stack([first_number, is_last]), chosen_all, counts_all, qkv, memory, grad_heads, attended_heads, lse,
        cosine, sine, w_qkv, heads, top,
    )
    partials, other_grad = other_blocks(
        low.reshape(1), chosen_all, counts_all, qkv, memory, grad_heads, attended_heads, lse, cosine, sine, w_qkv,
        sums, partials, heads, top,
    )
    order = jnp.concatenate([first_number.reshape(1), low + jnp.arange(count - 1, dtype=jnp.int32)])
    block_rows = first_partial.shape[0]

    def term(step, index):
        start = jnp.clip(index, 0, ring - 1) * rows
        if step == 0:
            near = jnp.clip(start - first_number * block_rows, 0, block_rows - rows)
            return lax.dynamic_slice_in_dim(first_partial, near, rows, 0).astype(F32)
        return lax.dynamic_slice_in_dim(partials, start, rows, 0).astype(F32)

    kept = []

    def make_projection_grads(sent):
        kept.extend(
            projection_grads(
                order, gathered, gain_one.reshape(width, 1), w_qkv, after(first_grad, sent), after(other_grad, sent)
            )
        )
        return kept

    own_term, arrived = chain_scatter(term, "fsdp", [lambda sent: out_grads, make_projection_grads])
    grad_w_qkv, gain_one_grad = kept
    grads = after(grads, arrived[-1])

    strip = grads.shape[1]
    lanes = width // strip
    tall = w_down.shape[0]
    if grad_down:
        down = lax.psum_scatter(grad_down[0], DP, scatter_dimension=0, tiled=True)
        down = down.reshape(ring, tall, lanes, strip).transpose(0, 2, 1, 3)
    else:
        down = grads[: ring * tall * lanes].reshape(lanes, ring, tall, strip).transpose(1, 0, 2, 3)
        grads = grads[ring * tall * lanes :]
    grads = grads.reshape(-1, ring, share, strip).transpose(1, 0, 2, 3)
    pieces = jnp.concatenate([down.reshape(ring, -1, strip), grads.reshape(ring, -1, strip)], 1)

    gains = jnp.stack([gain_one_grad.reshape(span, -1), gain_two_grad.reshape(span, -1)], 1)
    gains = jnp.pad(gains.astype(BF16), ((0, 0), (0, extra - 2), (0, 3 * wide - gains.shape[2])))
    late = jnp.concatenate([grad_w_qkv.reshape(span, -1, 3 * wide), gains], 1)
    late = over_chips(over_cores(after(late, pieces)))
    out_grads = over_cores(after(out_grads, pieces))[0]

    rising, falling = arrived[-1]
    grad_normed = own_term + rising.astype(F32) + falling.astype(F32)
    own = mine.astype(F32)
    factor = lax.rsqrt(jnp.mean(own * own, -1, keepdims=True) + EPSILON)
    scaled = grad_normed * gain_one
    inner = jnp.mean(scaled * own, -1, keepdims=True)
    tokens_grad = (grad_middle + factor * scaled - own * (factor * factor * factor * inner)).astype(BF16)

    gains = late[-extra : 2 - extra, : ring * share].reshape(2, ring, share).transpose(1, 0, 2)
    gains = jnp.pad(gains, ((0, 0), (0, extra - 2), (0, 3 * wide - share)))
    late = jnp.concatenate([late[:-extra].reshape(ring, share, 3 * wide), gains], 1)
    out_grads = jnp.pad(out_grads.reshape(ring, share, width), ((0, 0), (0, extra), (0, 0)))
    late = jnp.concatenate([late, out_grads], 2)
    late = after(lax.all_to_all(late, "fsdp", 0, 0, tiled=True), tokens_grad).astype(F32)
    out_share = jnp.sum(late[:, :share, 3 * wide :], 0)
    projections = [
        late[:, :share, part * wide : (part + 1) * wide].transpose(1, 0, 2).reshape(share, width)
        for part in range(3)
    ]
    gain_shares = jnp.sum(late[:, share : share + 2, :share], 0)

    pieces = lax.psum_scatter(pieces, "fsdp", scatter_dimension=0, tiled=True)
    pieces = after(pieces, (tokens_grad, projections, out_share, gain_shares))[0].astype(F32)
    down_share = pieces[: lanes * tall].reshape(lanes, tall, strip).transpose(1, 0, 2).reshape(tall, width)
    others = pieces[lanes * tall :].reshape(-1, share, strip).transpose(1, 0, 2).reshape(share, -1)
    return (
        mixed[None],
        tokens_grad[None],
        *projections,
        out_share,
        others[:, :hidden_width],
        others[:, hidden_width:],
        down_share,
        gain_shares[0],
        gain_shares[1],
    )


def solution(mesh):
    span, ring = mesh.shape["dp"], mesh.shape["fsdp"]
    fine = Mesh(mesh.devices.reshape(span // 2, 2, ring), DP + ("fsdp",))
    every = DP + ("fsdp",)
    rows, matrix, vector = P(DP, "fsdp", None), P(every, None), P(every)
    in_specs = (rows,) * 5 + (matrix,) * 7 + (vector,) * 2 + (rows,)
    out_specs = (rows,) * 2 + (matrix,) * 7 + (vector,) * 2
    return jax.shard_map(body, mesh=fine, in_specs=in_specs, out_specs=out_specs, check_vma=False)
```

```python
import functools
import math

import jax
import jax.numpy as jnp
import numpy as np
from jax import lax
from jax.experimental import pallas as pl
from jax.experimental.pallas import tpu as pltpu
from jax.sharding import Mesh
from jax.sharding import PartitionSpec as P

HEAD_DIM = 128
QBLK = 256
MBLK = 128
EPSILON = 1e-06
NEGATIVE = -1e30
SCALE = 1.0 / math.sqrt(HEAD_DIM)
LOG2E = math.log2(math.e)
MIB = 1 << 20
F32 = jnp.float32
BF16 = jnp.bfloat16
DP = ("chip", "core")
NT = (((1,), (1,)), ((), ()))
TN = (((0,), (0,)), ((), ()))


def dot(left, right, dims=(((1,), (0,)), ((), ()))):
    return lax.dot_general(left, right, dims, preferred_element_type=F32)


def rotary_tables(length):
    half_dim = HEAD_DIM // 2
    frequency = 10000.0 ** (-jnp.arange(half_dim, dtype=F32) / half_dim)
    angles = jnp.arange(length, dtype=jnp.int32).astype(F32)[:, None] * frequency[None, :]
    cosine, sine = jnp.cos(angles), jnp.sin(angles)
    return jnp.concatenate([cosine, cosine], 1), jnp.concatenate([-sine, sine], 1)


def qkv_kernel(heads, tok_ref, gain_ref, w_ref, cos_ref, sin_ref, qkv_ref):
    rows = tok_ref[...].astype(F32)
    factor = lax.rsqrt(jnp.mean(rows * rows, -1, keepdims=True) + EPSILON)
    normed = (rows * factor * gain_ref[...]).astype(BF16)
    cosine, sine = cos_ref[...], sin_ref[...]
    wide = heads * HEAD_DIM
    for part in range(3):
        values = dot(normed, w_ref[:, part * wide : (part + 1) * wide])
        for head in range(heads):
            value = values[:, head * HEAD_DIM : (head + 1) * HEAD_DIM]
            if part < 2:
                value = value * cosine + pltpu.roll(value, HEAD_DIM // 2, 1) * sine
            if part == 0:
                value = value * (SCALE * LOG2E)
            at = part * wide + head * HEAD_DIM
            qkv_ref[:, at : at + HEAD_DIM] = value.astype(BF16)


def project_qkv(tokens_all, gain, w_qkv, cosine, sine, heads):
    length, width = tokens_all.shape
    columns = w_qkv.shape[1]
    block = 2 * QBLK
    return pl.pallas_call(
        functools.partial(qkv_kernel, heads),
        grid=(length // block,),
        in_specs=[
            pl.BlockSpec((block, width), lambda i: (i, 0)),
            pl.BlockSpec((1, width), lambda i: (0, 0)),
            pl.BlockSpec((width, columns), lambda i: (0, 0)),
            pl.BlockSpec((block, HEAD_DIM), lambda i: (i, 0)),
            pl.BlockSpec((block, HEAD_DIM), lambda i: (i, 0)),
        ],
        out_specs=pl.BlockSpec((block, columns), lambda i: (i, 0)),
        out_shape=jax.ShapeDtypeStruct((length, columns), BF16),
        compiler_params=pltpu.CompilerParams(vmem_limit_bytes=48 * MIB),
        cost_estimate=pl.CostEstimate(
            flops=2 * length * width * columns, bytes_accessed=4 * length * (width + columns), transcendentals=0
        ),
        name="project_qkv",
    )(tokens_all, gain, w_qkv, cosine, sine)


def memory_bias(counts_ref, base, top, axis):
    shape = (1, top * MBLK) if axis == 1 else (top * MBLK, 1)
    column = lax.broadcasted_iota(jnp.int32, shape, axis)
    limit = jnp.zeros(shape, jnp.int32)
    for entry in range(top):
        inside = (column >= entry * MBLK) & (column < entry * MBLK + counts_ref[base + entry])
        limit = jnp.where(inside, 1, limit)
    return jnp.where(limit > 0, 0.0, NEGATIVE)


def pick_memory(ref, chosen_ref, base, top, columns):
    rows = [
        ref[pl.ds(pl.multiple_of(chosen_ref[base + entry] * MBLK, MBLK), MBLK), columns]
        for entry in range(top)
    ]
    return jnp.concatenate(rows, 0)


def forward_kernel(
    heads, top, chosen_ref, counts_ref, q_ref, k_ref, v_ref, mk_ref, mv_ref, out_ref, lse_ref, acc_s, peak_s
):
    block = pl.program_id(0)
    rows = q_ref.shape[0]
    subs = rows // QBLK
    ones = jnp.ones((rows, HEAD_DIM), BF16)
    mem_ones = jnp.ones((top * MBLK, HEAD_DIM), BF16)
    for sub in range(subs):
        base = (block * subs + sub) * top
        here = slice(sub * QBLK, (sub + 1) * QBLK)
        span = (sub + 1) * QBLK
        seen = pl.ds(pl.multiple_of(block * rows, rows), span)
        row = lax.broadcasted_iota(jnp.int32, (QBLK, span), 0) + sub * QBLK
        causal = row >= lax.broadcasted_iota(jnp.int32, (QBLK, span), 1)
        bias = memory_bias(counts_ref, base, top, 1)
        for head in range(heads):
            columns = slice(head * HEAD_DIM, (head + 1) * HEAD_DIM)
            query = q_ref[here, columns]
            remote = dot(query, pick_memory(mk_ref, chosen_ref, base, top, columns), NT) + bias
            local = jnp.where(causal, dot(query, k_ref[seen, columns], NT), NEGATIVE)
            peak = jnp.maximum(jnp.max(local, -1, keepdims=True), jnp.max(remote, -1, keepdims=True))
            values = jnp.concatenate([v_ref[seen, columns], ones[:span]], 1)
            acc = dot(jnp.exp2(local - peak).astype(BF16), values)
            values = jnp.concatenate([pick_memory(mv_ref, chosen_ref, base, top, columns), mem_ones], 1)
            acc_s[head, here] = acc + dot(jnp.exp2(remote - peak).astype(BF16), values)
            peak_s[head, here] = jnp.broadcast_to(peak, (QBLK, HEAD_DIM))

    def step(index, carry):
        there = pl.ds(pl.multiple_of(index * rows, rows), rows)
        for head in range(heads):
            columns = slice(head * HEAD_DIM, (head + 1) * HEAD_DIM)
            peak = peak_s[head][:, :1]
            scores = dot(q_ref[:, columns], k_ref[there, columns], NT)
            higher = jnp.maximum(peak, jnp.max(scores, -1, keepdims=True))
            weights = jnp.exp2(scores - higher).astype(BF16)
            values = jnp.concatenate([v_ref[there, columns], ones], 1)
            acc_s[head] = acc_s[head] * jnp.exp2(peak - higher) + dot(weights, values)
            peak_s[head] = jnp.broadcast_to(higher, (rows, HEAD_DIM))
        return carry

    lax.fori_loop(0, block, step, 0)
    for head in range(heads):
        columns = slice(head * HEAD_DIM, (head + 1) * HEAD_DIM)
        total = acc_s[head][:, HEAD_DIM:]
        out_ref[:, columns] = (acc_s[head][:, :HEAD_DIM] / total).astype(BF16)
        lse_ref[:, head : head + 1] = peak_s[head][:, :1] + jnp.log2(total[:, :1])


def attend_forward(chosen, counts, qkv, memory, heads, top):
    length = qkv.shape[0]
    wide = heads * HEAD_DIM
    rows = min(2 * QBLK, length)
    mem_rows = memory.shape[0]
    return pl.pallas_call(
        functools.partial(forward_kernel, heads, top),
        grid_spec=pltpu.PrefetchScalarGridSpec(
            num_scalar_prefetch=2,
            grid=(length // rows,),
            in_specs=[
                pl.BlockSpec((rows, wide), lambda i, *_: (i, 0)),
                pl.BlockSpec((length, wide), lambda i, *_: (0, 1)),
                pl.BlockSpec((length, wide), lambda i, *_: (0, 2)),
                pl.BlockSpec((mem_rows, wide), lambda i, *_: (0, 0)),
                pl.BlockSpec((mem_rows, wide), lambda i, *_: (0, 1)),
            ],
            out_specs=[
                pl.BlockSpec((rows, wide), lambda i, *_: (i, 0)),
                pl.BlockSpec((rows, heads), lambda i, *_: (i, 0)),
            ],
            scratch_shapes=[
                pltpu.VMEM((heads, rows, 2 * HEAD_DIM), F32),
                pltpu.VMEM((heads, rows, HEAD_DIM), F32),
            ],
        ),
        out_shape=[
            jax.ShapeDtypeStruct((length, wide), BF16),
            jax.ShapeDtypeStruct((length, heads), F32),
        ],
        compiler_params=pltpu.CompilerParams(vmem_limit_bytes=48 * MIB),
        cost_estimate=pl.CostEstimate(
            flops=4 * heads * length * HEAD_DIM * (length // 2 + top * MBLK),
            bytes_accessed=8 * length * wide,
            transcendentals=heads * length * (length // 2 + top * MBLK),
        ),
        name="attend_forward",
    )(chosen, counts, qkv, qkv, qkv, memory, memory)


def spread_rows(column):
    rows = column.shape[0]
    return jnp.transpose(jnp.broadcast_to(column, (rows, HEAD_DIM)))[:1]


def row_stats(grad_out, out, lse):
    delta = jnp.sum(grad_out.astype(F32) * out.astype(F32), -1, keepdims=True)
    return jnp.concatenate([spread_rows(lse), spread_rows(delta)], 0)


def score_grads(query, grad_out, stats, keys, values, mask):
    weights = jnp.exp2(mask(dot(keys, query, NT)) - stats[:1])
    grad_weights = dot(values, grad_out, NT)
    return weights.astype(BF16), (weights * (grad_weights - stats[1:2])).astype(BF16)


def causal_mask(rows):
    key_at = lax.broadcasted_iota(jnp.int32, (rows, rows), 0)
    query_at = lax.broadcasted_iota(jnp.int32, (rows, rows), 1)
    return lambda scores: jnp.where(query_at >= key_at, scores, NEGATIVE)


def memory_query_grad(chosen_ref, counts_ref, base, top, query, grad_out, stats, mk_ref, mv_ref, columns):
    keys = pick_memory(mk_ref, chosen_ref, base, top, columns)
    values = pick_memory(mv_ref, chosen_ref, base, top, columns)
    bias = memory_bias(counts_ref, base, top, 0)
    _, grad_scores = score_grads(query, grad_out, stats, keys, values, lambda scores: scores + bias)
    return dot(grad_scores, keys, TN)


def block_grads(heads, grad_query, grad_key, grad_value, cosine, sine):
    def unturn(value):
        return (value * cosine - pltpu.roll(value, HEAD_DIM // 2, 1) * sine).astype(BF16)

    parts = []
    for part, array in enumerate((grad_query * SCALE, grad_key * (1.0 / LOG2E), grad_value)):
        for head in range(heads):
            value = array[:, head * HEAD_DIM : (head + 1) * HEAD_DIM]
            parts.append(unturn(value) if part < 2 else value.astype(BF16))
    return jnp.concatenate(parts, 1)


def first_block_kernel(
    heads, top, chosen_ref, counts_ref, plan_ref, qkv_ref, mk_ref, mv_ref, go_ref, out_ref, lse_ref, cos_ref, sin_ref,
    w_ref, partial_ref, whole_ref, grad_ref, gq_ref, gk_ref, gv_ref, stats_s,
):
    rows = partial_ref.shape[0]
    subs = rows // QBLK
    wide = heads * HEAD_DIM
    others = go_ref.shape[0] // rows - 1
    block, is_last = plan_ref[0], plan_ref[1]
    own = pl.ds(pl.multiple_of(block * rows, rows), rows)
    gq_ref[...] = jnp.zeros_like(gq_ref)
    gk_ref[...] = jnp.zeros_like(gk_ref)
    gv_ref[...] = jnp.zeros_like(gv_ref)

    def note_stats(slot, here):
        for head in range(heads):
            columns = slice(head * HEAD_DIM, (head + 1) * HEAD_DIM)
            stats_s[slot, head] = row_stats(go_ref[here, columns], out_ref[here, columns], lse_ref[here, head : head + 1])

    note_stats(0, own)

    def pair(slot, queries, keys, mask):
        for head in range(heads):
            at = head * HEAD_DIM
            columns = slice(at, at + HEAD_DIM)
            query, grad_out = qkv_ref[queries, columns], go_ref[queries, columns]
            key = qkv_ref[keys, wide + at : wide + at + HEAD_DIM]
            value = qkv_ref[keys, 2 * wide + at : 2 * wide + at + HEAD_DIM]
            weights, grad_scores = score_grads(query, grad_out, stats_s[slot, head], key, value, mask)
            gk_ref[keys, columns] += dot(grad_scores, query)
            gv_ref[keys, columns] += dot(weights, grad_out)
            gq_ref[queries, columns] += dot(grad_scores, key, TN)

    for head in range(heads):
        columns = slice(head * HEAD_DIM, (head + 1) * HEAD_DIM)
        for sub in range(subs):
            here = pl.ds(pl.multiple_of(block * rows + sub * QBLK, QBLK), QBLK)
            gq_ref[here, columns] += memory_query_grad(
                chosen_ref, counts_ref, (block * subs + sub) * top, top, qkv_ref[here, columns], go_ref[here, columns],
                stats_s[0, head][:, sub * QBLK : (sub + 1) * QBLK], mk_ref, mv_ref, columns,
            )
    pair(0, own, own, causal_mask(rows))

    def step(index, carry):
        other = jnp.where(is_last == 1, index, index + 1)
        there = pl.ds(pl.multiple_of(other * rows, rows), rows)

        @pl.when(is_last == 1)
        def _():
            pair(0, own, there, lambda scores: scores)

        @pl.when(is_last == 0)
        def _():
            note_stats(1, there)
            pair(1, there, own, lambda scores: scores)

        return carry

    lax.fori_loop(0, others, step, 0)
    grad = block_grads(
        heads, gq_ref[own, :], gk_ref[own, :], gv_ref[own, :], cos_ref[...], sin_ref[...]
    )
    grad_ref[...] = grad
    partial = dot(grad, w_ref[...], NT).astype(BF16)
    partial_ref[...] = partial
    whole_ref[...] = partial


def first_block(plan, chosen, counts, qkv, memory, grad_out, out, lse, cosine, sine, w_qkv, heads, top):
    length = qkv.shape[0]
    width = w_qkv.shape[0]
    wide = heads * HEAD_DIM
    rows = min(2 * QBLK, length)
    mem_rows = memory.shape[0]

    def whole(array):
        return pl.BlockSpec(array.shape, lambda i, *_: (0, 0))

    sums = pl.BlockSpec((length, wide), lambda i, *_: (0, 0))
    return pl.pallas_call(
        functools.partial(first_block_kernel, heads, top),
        grid_spec=pltpu.PrefetchScalarGridSpec(
            num_scalar_prefetch=3,
            grid=(1,),
            in_specs=[
                whole(qkv),
                pl.BlockSpec((mem_rows, wide), lambda i, *_: (0, 0)),
                pl.BlockSpec((mem_rows, wide), lambda i, *_: (0, 1)),
                whole(grad_out),
                whole(out),
                whole(lse),
                pl.BlockSpec((rows, HEAD_DIM), lambda i, c, n, plan: (plan[0], 0)),
                pl.BlockSpec((rows, HEAD_DIM), lambda i, c, n, plan: (plan[0], 0)),
                whole(w_qkv),
            ],
            out_specs=[
                pl.BlockSpec((rows, width), lambda i, *_: (0, 0)),
                pl.BlockSpec((rows, width), lambda i, c, n, plan: (plan[0], 0)),
                pl.BlockSpec((rows, 3 * wide), lambda i, *_: (0, 0)),
                sums,
                sums,
                sums,
            ],
            scratch_shapes=[pltpu.VMEM((2, heads, 2, rows), F32)],
        ),
        out_shape=[
            jax.ShapeDtypeStruct((rows, width), BF16),
            jax.ShapeDtypeStruct((length, width), BF16),
            jax.ShapeDtypeStruct((rows, 3 * wide), BF16),
            *[jax.ShapeDtypeStruct((length, wide), F32)] * 3,
        ],
        compiler_params=pltpu.CompilerParams(vmem_limit_bytes=60 * MIB),
        cost_estimate=pl.CostEstimate(
            flops=4 * heads * length * HEAD_DIM * length,
            bytes_accessed=40 * length * wide,
            transcendentals=heads * length * rows,
        ),
        name="first_block",
    )(chosen, counts, plan, qkv, memory, memory, grad_out, out, lse, cosine, sine, w_qkv)


def other_blocks_kernel(
    heads, top, chosen_ref, counts_ref, plan_ref, q_ref, k_ref, v_ref, mk_ref, mv_ref, go_ref, out_ref, lse_ref,
    cos_ref, sin_ref, w_ref, gq_in, gk_in, gv_in, _, partial_ref, grad_ref, gk_s, gv_s, gq_s,
):
    low = plan_ref[0]
    block = low + pl.num_programs(0) - 1 - pl.program_id(0)
    rows = q_ref.shape[0]
    subs = rows // QBLK
    own = pl.ds(pl.multiple_of(block * rows, rows), rows)

    @pl.when(pl.program_id(0) == 0)
    def _():
        gk_s[...] = gk_in[...]
        gv_s[...] = gv_in[...]

    stats = []
    for head in range(heads):
        columns = slice(head * HEAD_DIM, (head + 1) * HEAD_DIM)
        stats.append(row_stats(go_ref[:, columns], out_ref[:, columns], lse_ref[:, head : head + 1]))
        for sub in range(subs):
            here = slice(sub * QBLK, (sub + 1) * QBLK)
            gq_s[here, columns] = gq_in[here, columns] + memory_query_grad(
                chosen_ref, counts_ref, (block * subs + sub) * top, top, q_ref[here, columns], go_ref[here, columns],
                stats[head][:, here], mk_ref, mv_ref, columns,
            )

    def local(there, mask):
        for head in range(heads):
            columns = slice(head * HEAD_DIM, (head + 1) * HEAD_DIM)
            query, grad_out = q_ref[:, columns], go_ref[:, columns]
            key = k_ref[there, columns]
            weights, grad_scores = score_grads(query, grad_out, stats[head], key, v_ref[there, columns], mask)
            gk_s[there, columns] += dot(grad_scores, query)
            gv_s[there, columns] += dot(weights, grad_out)
            gq_s[:, columns] += dot(grad_scores, key, TN)

    local(own, causal_mask(rows))

    def step(index, carry):
        local(pl.ds(pl.multiple_of(index * rows, rows), rows), lambda scores: scores)
        return carry

    lax.fori_loop(low, block, step, 0)
    grad = block_grads(heads, gq_s[...], gk_s[own, :], gv_s[own, :], cos_ref[...], sin_ref[...])
    grad_ref[...] = grad
    partial_ref[...] = dot(grad, w_ref[...], NT).astype(BF16)


def other_blocks(plan, chosen, counts, qkv, memory, grad_out, out, lse, cosine, sine, w_qkv, sums, partials, heads, top):
    length = qkv.shape[0]
    width = w_qkv.shape[0]
    wide = heads * HEAD_DIM
    rows = min(2 * QBLK, length)
    count = length // rows - 1
    mem_rows = memory.shape[0]

    def by_rows(columns, at=0):
        return pl.BlockSpec((rows, columns), lambda i, c, n, plan: (plan[0] + count - 1 - i, at))

    def result(columns):
        return pl.BlockSpec((rows, columns), lambda i, *_: (count - 1 - i, 0))

    return pl.pallas_call(
        functools.partial(other_blocks_kernel, heads, top),
        grid_spec=pltpu.PrefetchScalarGridSpec(
            num_scalar_prefetch=3,
            grid=(count,),
            in_specs=[
                by_rows(wide),
                pl.BlockSpec((length, wide), lambda i, *_: (0, 1)),
                pl.BlockSpec((length, wide), lambda i, *_: (0, 2)),
                pl.BlockSpec((mem_rows, wide), lambda i, *_: (0, 0)),
                pl.BlockSpec((mem_rows, wide), lambda i, *_: (0, 1)),
                by_rows(wide),
                by_rows(wide),
                by_rows(heads),
                by_rows(HEAD_DIM),
                by_rows(HEAD_DIM),
                pl.BlockSpec((width, 3 * wide), lambda i, *_: (0, 0)),
                by_rows(wide),
                pl.BlockSpec((length, wide), lambda i, *_: (0, 0)),
                pl.BlockSpec((length, wide), lambda i, *_: (0, 0)),
                pl.BlockSpec(memory_space=pl.ANY),
            ],
            out_specs=[by_rows(width), result(3 * wide)],
            scratch_shapes=[
                pltpu.VMEM((length, wide), F32),
                pltpu.VMEM((length, wide), F32),
                pltpu.VMEM((rows, wide), F32),
            ],
        ),
        out_shape=[
            jax.ShapeDtypeStruct((length, width), BF16),
            jax.ShapeDtypeStruct((count * rows, 3 * wide), BF16),
        ],
        input_output_aliases={17: 0},
        compiler_params=pltpu.CompilerParams(vmem_limit_bytes=60 * MIB),
        cost_estimate=pl.CostEstimate(
            flops=6 * heads * length * HEAD_DIM * (length + top * MBLK),
            bytes_accessed=40 * length * wide,
            transcendentals=heads * length * (length // 3 + top * MBLK),
        ),
        name="other_blocks",
    )(chosen, counts, plan, qkv, qkv, qkv, memory, memory, grad_out, out, lse, cosine, sine, w_qkv, *sums, partials)


def ffn_kernel(
    span, merged, tok_ref, att_ref, cot_ref, gain_ref, out_w, gate_w, up_w, down_w,
    mixed_ref, grad_mid_ref, grad_att_ref, gain_grad_ref, out_grads_ref, grads_ref, *rest,
):
    if not merged:
        down_grads_ref, rest = rest[0], rest[1:]
    middle_s, normed_s, turned_s, mixed_s, upstream_s, gate_s, up_s, down_s, out_s, sems, late_sems = rest
    step, steps = pl.program_id(0), pl.num_programs(0)
    width = tok_ref.shape[1]
    share = width // span
    wide = gate_w.shape[1]
    hidden_width = down_s.shape[0]
    tall = hidden_width // span
    lanes = width // wide
    first = tall * lanes if merged else 0
    slot = step % 2

    @pl.when(step == 0)
    def _():
        middle = tok_ref[...].astype(F32) + dot(att_ref[...], out_w[...])
        middle_s[...] = middle
        factor = lax.rsqrt(jnp.mean(middle * middle, -1, keepdims=True) + EPSILON)
        normed = (middle * factor * gain_ref[...]).astype(BF16)
        normed_s[...] = normed
        turned_s[...] = jnp.transpose(normed)
        mixed_s[...] = middle
        upstream_s[...] = jnp.zeros_like(upstream_s)

    def copy_out(kind, which, index):
        source = (gate_s, up_s)[kind].at[which]
        start = first + (kind * steps + index) * share
        target = grads_ref.at[:, pl.ds(start, share), :]
        return pltpu.make_async_copy(source, target, sems.at[kind, which])

    normed = normed_s[...]
    upstream = cot_ref[...]
    both = jnp.concatenate([gate_w[...], up_w[...]], 1)
    acts = dot(normed, both)
    gate_act, up_act = acts[:, :wide], acts[:, wide:]
    grad_hidden = dot(upstream, down_w[...], NT)
    sigmoid = jax.nn.sigmoid(gate_act)
    silu = gate_act * sigmoid
    hidden = (silu * up_act).astype(BF16)
    grad_gate = (grad_hidden * up_act * sigmoid * (1.0 + gate_act * (1.0 - sigmoid))).astype(BF16)
    grad_up = (grad_hidden * silu).astype(BF16)
    mixed_s[...] += dot(hidden, down_w[...])
    grad_acts = jnp.concatenate([grad_gate, grad_up], 1)
    upstream_s[...] += dot(grad_acts, both, NT)
    down_s[pl.ds(pl.multiple_of(step * wide, wide), wide), :] = dot(hidden, upstream, TN).astype(BF16)

    @pl.when(step >= 2)
    def _():
        copy_out(0, slot, step - 2).wait()
        copy_out(1, slot, step - 2).wait()

    weight_grads = dot(turned_s[...], grad_acts).astype(BF16)
    gate_s[slot] = weight_grads[:, :wide].reshape(span, share, wide)
    up_s[slot] = weight_grads[:, wide:].reshape(span, share, wide)
    copy_out(0, slot, step).start()
    copy_out(1, slot, step).start()

    @pl.when(step == steps - 1)
    def _():
        copies = []
        if merged:
            for place in range(span):
                for lane in range(lanes):
                    copies.append(
                        pltpu.make_async_copy(
                            down_s.at[pl.ds(place * tall, tall), pl.ds(lane * wide, wide)],
                            grads_ref.at[place, pl.ds(lane * tall, tall), :],
                            late_sems.at[len(copies)],
                        )
                    )
        else:
            copies.append(pltpu.make_async_copy(down_s, down_grads_ref, late_sems.at[0]))
        for copy in copies:
            copy.start()
        mixed_ref[...] = mixed_s[...].astype(BF16)
        middle = middle_s[...]
        grad = upstream_s[...]
        factor = lax.rsqrt(jnp.mean(middle * middle, -1, keepdims=True) + EPSILON)
        gain_grad_ref[...] = jnp.sum(grad * middle * factor, 0, keepdims=True)
        scaled = grad * gain_ref[...]
        inner = jnp.mean(scaled * middle, -1, keepdims=True)
        grad_middle = cot_ref[...].astype(F32) + factor * scaled - middle * (factor * factor * factor * inner)
        grad_mid_ref[...] = grad_middle
        branch = grad_middle.astype(BF16)
        grad_att_ref[...] = dot(branch, out_w[...], NT).astype(BF16)
        turned_att = jnp.transpose(att_ref[...])
        for lane in range(lanes):
            columns = slice(lane * wide, (lane + 1) * wide)
            out_s[lane] = dot(turned_att, branch[:, columns]).astype(BF16).reshape(span, share, wide)
            more = pltpu.make_async_copy(
                out_s.at[lane],
                out_grads_ref.at[:, :, pl.ds(lane * wide, wide)],
                late_sems.at[len(copies)],
            )
            more.start()
            copies.append(more)
        for copy in copies:
            copy.wait()
        copy_out(0, 1 - slot, step - 1).wait()
        copy_out(1, 1 - slot, step - 1).wait()
        copy_out(0, slot, step).wait()
        copy_out(1, slot, step).wait()


def feed_forward(tokens, attended, upstream, gain, weights, w_down, span):
    rows, width = tokens.shape
    hidden_width = w_down.shape[0]
    wide = 2 * HEAD_DIM
    steps = hidden_width // wide
    lanes = width // wide
    share = width // span
    tall = hidden_width // span
    merged = tall % 16 == 0
    total = 2 * steps * share + (lanes * tall if merged else 0)
    shapes = [
        jax.ShapeDtypeStruct((rows, width), BF16),
        jax.ShapeDtypeStruct((rows, width), F32),
        jax.ShapeDtypeStruct((rows, width), BF16),
        jax.ShapeDtypeStruct((1, width), F32),
        jax.ShapeDtypeStruct((span, share, width), BF16),
        jax.ShapeDtypeStruct((span, total, wide), BF16),
    ]
    specs = [
        pl.BlockSpec((rows, width), lambda i: (0, 0)),
        pl.BlockSpec((rows, width), lambda i: (0, 0)),
        pl.BlockSpec((rows, width), lambda i: (0, 0)),
        pl.BlockSpec((1, width), lambda i: (0, 0)),
        pl.BlockSpec(memory_space=pl.ANY),
        pl.BlockSpec(memory_space=pl.ANY),
    ]
    if not merged:
        shapes.append(jax.ShapeDtypeStruct((hidden_width, width), BF16))
        specs.append(pl.BlockSpec(memory_space=pl.ANY))
    return pl.pallas_call(
        functools.partial(ffn_kernel, span, merged),
        grid=(steps,),
        in_specs=[
            pl.BlockSpec((rows, width), lambda i: (0, 0)),
            pl.BlockSpec((rows, width), lambda i: (0, 0)),
            pl.BlockSpec((rows, width), lambda i: (0, 0)),
            pl.BlockSpec((1, width), lambda i: (0, 0)),
            pl.BlockSpec((width, width), lambda i: (0, 0)),
            pl.BlockSpec((width, wide), lambda i: (0, lanes + i)),
            pl.BlockSpec((width, wide), lambda i: (0, lanes + steps + i)),
            pl.BlockSpec((wide, width), lambda i: (i, 0)),
        ],
        out_specs=specs,
        out_shape=shapes,
        scratch_shapes=[
            pltpu.VMEM((rows, width), F32),
            pltpu.VMEM((rows, width), BF16),
            pltpu.VMEM((width, rows), BF16),
            pltpu.VMEM((rows, width), F32),
            pltpu.VMEM((rows, width), F32),
            pltpu.VMEM((2, span, share, wide), BF16),
            pltpu.VMEM((2, span, share, wide), BF16),
            pltpu.VMEM((hidden_width, width), BF16),
            pltpu.VMEM((lanes, span, share, wide), BF16),
            pltpu.SemaphoreType.DMA((2, 2)),
            pltpu.SemaphoreType.DMA(((span * lanes if merged else 1) + lanes,)),
        ],
        compiler_params=pltpu.CompilerParams(vmem_limit_bytes=56 * MIB),
        cost_estimate=pl.CostEstimate(
            flops=6 * rows * width * (3 * hidden_width + width),
            bytes_accessed=4 * width * (3 * hidden_width + width),
            transcendentals=rows * hidden_width,
        ),
        name="feed_forward",
    )(tokens, attended, upstream, gain, weights, weights, weights, w_down)


def projection_grads_kernel(
    order_ref, tok_ref, gain_ref, w_ref, first_ref, other_ref, grad_w_ref, gain_grad_ref, raw_s
):
    step = pl.program_id(0)

    @pl.when(step == 0)
    def _():
        raw_s[...] = jnp.zeros_like(raw_s)

    tokens = tok_ref[...].astype(F32)
    tokens = tokens * lax.rsqrt(jnp.mean(tokens * tokens, -1, keepdims=True) + EPSILON)
    grad = jnp.where(step == 0, first_ref[...], other_ref[...])
    raw_s[...] += dot(tokens.astype(BF16), grad, TN)

    @pl.when(step == pl.num_programs(0) - 1)
    def _():
        raw = raw_s[...]
        gain_grad_ref[...] = jnp.sum(raw * w_ref[...].astype(F32), -1, keepdims=True)
        grad_w_ref[...] = (raw * gain_ref[...]).astype(BF16)


def projection_grads(order, tokens_all, gain_column, w_qkv, first_grad, other_grad):
    length, width = tokens_all.shape
    columns = first_grad.shape[1]
    rows = min(2 * QBLK, length)
    return pl.pallas_call(
        projection_grads_kernel,
        grid_spec=pltpu.PrefetchScalarGridSpec(
            num_scalar_prefetch=1,
            grid=(length // rows,),
            in_specs=[
                pl.BlockSpec((rows, width), lambda i, order: (order[i], 0)),
                pl.BlockSpec((width, 1), lambda i, _: (0, 0)),
                pl.BlockSpec((width, columns), lambda i, _: (0, 0)),
                pl.BlockSpec((rows, columns), lambda i, _: (0, 0)),
                pl.BlockSpec((rows, columns), lambda i, _: (jnp.maximum(i - 1, 0), 0)),
            ],
            out_specs=[
                pl.BlockSpec((width, columns), lambda i, _: (0, 0)),
                pl.BlockSpec((width, 1), lambda i, _: (0, 0)),
            ],
            scratch_shapes=[pltpu.VMEM((width, columns), F32)],
        ),
        out_shape=[
            jax.ShapeDtypeStruct((width, columns), BF16),
            jax.ShapeDtypeStruct((width, 1), F32),
        ],
        compiler_params=pltpu.CompilerParams(vmem_limit_bytes=48 * MIB),
        cost_estimate=pl.CostEstimate(
            flops=2 * length * width * columns, bytes_accessed=2 * length * (width + columns), transcendentals=0
        ),
        name="projection_grads",
    )(order, tokens_all, gain_column, w_qkv, first_grad, other_grad)


def after(value, earlier):
    return lax.optimization_barrier((value, earlier))[0]


def chain_gather(blocks, axis):
    size = lax.axis_size(axis)
    place = lax.axis_index(axis)
    steps = []
    rising = falling = tuple(blocks)
    for step in range(size - 1):
        up = [(i, i + 1) for i in range(step, size - 1)]
        down = [(i + 1, i) for i in range(size - 1 - step)]
        rising = tuple(lax.ppermute(block, axis, up) for block in rising)
        falling = tuple(lax.ppermute(block, axis, down) for block in falling)
        if len(blocks) > 1:
            rising, falling = lax.optimization_barrier((rising, falling))
        steps.append((rising, falling))
    results = []
    for number, block in enumerate(blocks):
        ordered = []
        for index in range(size):
            cases = []
            for mine in range(size):
                if mine == index:
                    cases.append(block)
                elif mine > index:
                    cases.append(steps[mine - index - 1][0][number])
                else:
                    cases.append(steps[index - mine - 1][1][number])
            ordered.append(lax.select_n(place, *cases) if size > 2 else lax.select_n(place > 0, *cases))
        results.append(ordered)
    return results, steps


def chain_scatter(block, axis, waits):
    size = lax.axis_size(axis)
    place = lax.axis_index(axis)
    arrived = []
    for step in range(size - 1):
        up, down = block(step, size - 1 - step + place), block(step, step - size + 1 + place)
        if step:
            up, down = up + arrived[-1][0].astype(F32), down + arrived[-1][1].astype(F32)
        ready = waits[step - 1](sent) if 0 < step <= len(waits) else None
        up, down, _ = lax.optimization_barrier((up.astype(BF16), down.astype(BF16), ready))
        sent = up, down
        rising = lax.ppermute(up, axis, [(i, i + 1) for i in range(step + 1)])
        falling = lax.ppermute(down, axis, [(i, i - 1) for i in range(size - 1 - step, size)])
        arrived.append(lax.optimization_barrier((rising, falling)))
    return block(size, place), arrived


def direct_exchange(blocks, axis):
    size = lax.axis_size(axis)
    place = lax.axis_index(axis)
    taken = [lax.dynamic_index_in_dim(blocks, place, 0, keepdims=False)]
    for far in range(1, size):
        give = lax.dynamic_index_in_dim(blocks, (place + far) % size, 0, keepdims=False)
        taken.append(lax.ppermute(give, axis, [(i, (i + far) % size) for i in range(size)]))
    return taken


def body(
    tokens, memory_keys, memory_values, chosen, counts, w_query, w_key, w_value, w_out, w_gate, w_up, w_down,
    gain_attn, gain_ffn, cotangent,
):
    ring, span = lax.axis_size("fsdp"), lax.axis_size(DP)
    rows, width = tokens.shape[1:]
    heads = width // HEAD_DIM // ring
    wide = heads * HEAD_DIM
    length = rows * ring
    top = chosen.shape[2]
    hidden_width = w_gate.shape[1]
    share = w_query.shape[0]
    mine = tokens[0]

    extra = 8 if share % 8 == 0 else 8 - share % 8
    parts = [w.reshape(share, ring, wide).transpose(1, 0, 2) for w in (w_query, w_key, w_value)]
    choices = jnp.concatenate([chosen[0].reshape(-1), counts[0].reshape(-1)]).astype(BF16)
    notes = jnp.stack(
        [
            jnp.pad(row, (0, 3 * wide - row.shape[0]))
            for row in (jnp.concatenate([gain_attn, gain_ffn]), choices)
        ]
    )
    notes = jnp.broadcast_to(jnp.pad(notes, ((0, extra - 2), (0, 0))), (ring, extra, 3 * wide))
    parcel = jnp.concatenate([jnp.concatenate(parts, 2), notes], 1)
    parcel = lax.all_to_all(parcel, "fsdp", 0, 0, tiled=True)
    picks = parcel[:, share + 1, : choices.shape[0]].astype(jnp.int32).reshape(ring, 2, -1)
    chosen_all, counts_all = picks[:, 0].reshape(-1), picks[:, 1].reshape(-1)
    shards = jnp.concatenate([w_out, w_gate, w_up], 1)
    (near, near_down), steps = chain_gather((shards, w_down), "fsdp")
    (gathered,), token_steps = chain_gather((after(mine, steps[-2]),), "fsdp")
    parcel = lax.all_gather(after(parcel, steps[0]), DP, axis=0, tiled=True)
    w_qkv = parcel[:, :share].reshape(width, 3 * wide)
    gain_one = parcel[:, share, :share].reshape(1, width).astype(F32)
    gain_two = parcel[:, share, share : 2 * share].reshape(1, width).astype(F32)
    first = lax.all_gather(jnp.concatenate(near, 0), DP, axis=0, tiled=True)
    gathered = jnp.concatenate(gathered, 0)

    memory = jnp.concatenate(
        [m[0].reshape(-1, ring, wide).transpose(1, 0, 2) for m in (memory_keys, memory_values)], 2
    )
    memory = lax.all_to_all(after(memory, token_steps[-2]), "fsdp", 0, 0, tiled=True).reshape(-1, 2 * wide)
    down_full = lax.all_gather(jnp.concatenate(near_down, 0), DP, axis=0, tiled=True)

    cosine, sine = rotary_tables(length)
    qkv = project_qkv(gathered, gain_one, w_qkv, cosine, sine, heads)
    attended_heads, lse = attend_forward(chosen_all, counts_all, qkv, memory, heads, top)
    attended = lax.all_to_all(attended_heads, "fsdp", 0, 1, tiled=True)

    upstream = cotangent[0]
    mixed, grad_middle, grad_attended, gain_two_grad, out_grads, grads, *grad_down = feed_forward(
        mine, attended, upstream, gain_two, first, down_full, span
    )
    grad_heads = lax.all_to_all(grad_attended, "fsdp", 1, 0, tiled=True)
    grads = lax.psum_scatter(grads, DP, scatter_dimension=0, tiled=True)[0]

    core = lax.axis_index("core")

    def over_cores(array):
        array = array.reshape((-1, 2) + array.shape[1:])
        taken = lax.ppermute(lax.dynamic_index_in_dim(array, 1 - core, 1, keepdims=False), "core", [(0, 1), (1, 0)])
        return (lax.dynamic_index_in_dim(array, core, 1, keepdims=False).astype(F32) + taken.astype(F32)).astype(BF16)

    def over_chips(array):
        return sum(piece.astype(F32) for piece in direct_exchange(array, "chip")).astype(BF16)

    out_grads = over_chips(out_grads.reshape((span // 2, 2) + out_grads.shape[1:]))

    place = lax.axis_index("fsdp").astype(jnp.int32)
    count = length // min(2 * QBLK, length)
    is_last = (place < ring // 2).astype(jnp.int32)
    first_number = jnp.where(is_last == 1, count - 1, 0).astype(jnp.int32)
    low = 1 - is_last
    first_partial, partials, first_grad, *sums = first_block(
        jnp.stack([first_number, is_last]), chosen_all, counts_all, qkv, memory, grad_heads, attended_heads, lse,
        cosine, sine, w_qkv, heads, top,
    )
    partials, other_grad = other_blocks(
        low.reshape(1), chosen_all, counts_all, qkv, memory, grad_heads, attended_heads, lse, cosine, sine, w_qkv,
        sums, partials, heads, top,
    )
    order = jnp.concatenate([first_number.reshape(1), low + jnp.arange(count - 1, dtype=jnp.int32)])
    block_rows = first_partial.shape[0]

    def term(step, index):
        start = jnp.clip(index, 0, ring - 1) * rows
        if step == 0:
            near = jnp.clip(start - first_number * block_rows, 0, block_rows - rows)
            return lax.dynamic_slice_in_dim(first_partial, near, rows, 0).astype(F32)
        return lax.dynamic_slice_in_dim(partials, start, rows, 0).astype(F32)

    kept = []

    def make_projection_grads(sent):
        kept.extend(
            projection_grads(
                order, gathered, gain_one.reshape(width, 1), w_qkv, after(first_grad, sent), after(other_grad, sent)
            )
        )
        return kept

    own_term, arrived = chain_scatter(term, "fsdp", [lambda sent: None, lambda sent: (out_grads, make_projection_grads(sent))])
    grad_w_qkv, gain_one_grad = kept
    grads = after(grads, arrived[-1])

    strip = grads.shape[1]
    lanes = width // strip
    tall = w_down.shape[0]
    if grad_down:
        down = lax.psum_scatter(grad_down[0], DP, scatter_dimension=0, tiled=True)
        down = down.reshape(ring, tall, lanes, strip).transpose(0, 2, 1, 3)
    else:
        down = grads[: ring * tall * lanes].reshape(lanes, ring, tall, strip).transpose(1, 0, 2, 3)
        grads = grads[ring * tall * lanes :]
    grads = grads.reshape(-1, ring, share, strip).transpose(1, 0, 2, 3)
    pieces = jnp.concatenate([down.reshape(ring, -1, strip), grads.reshape(ring, -1, strip)], 1)

    gains = jnp.stack([gain_one_grad.reshape(span, -1), gain_two_grad.reshape(span, -1)], 1)
    gains = jnp.pad(gains.astype(BF16), ((0, 0), (0, extra - 2), (0, 3 * wide - gains.shape[2])))
    late = jnp.concatenate([grad_w_qkv.reshape(span, -1, 3 * wide), gains], 1)
    late = over_chips(over_cores(after(late, pieces)))
    out_grads = over_cores(after(out_grads, pieces))[0]

    rising, falling = arrived[-1]
    grad_normed = own_term + rising.astype(F32) + falling.astype(F32)
    own = mine.astype(F32)
    factor = lax.rsqrt(jnp.mean(own * own, -1, keepdims=True) + EPSILON)
    scaled = grad_normed * gain_one
    inner = jnp.mean(scaled * own, -1, keepdims=True)
    tokens_grad = (grad_middle + factor * scaled - own * (factor * factor * factor * inner)).astype(BF16)

    gains = late[-extra : 2 - extra, : ring * share].reshape(2, ring, share).transpose(1, 2, 0)
    gains = jnp.pad(gains, ((0, 0), (0, 0), (0, HEAD_DIM - 2)))
    late = late[:-extra].reshape(ring, share, 3 * wide)
    late = jnp.concatenate([late, out_grads.reshape(ring, share, width), gains], 2)
    late = after(lax.all_to_all(late, "fsdp", 0, 0, tiled=True), tokens_grad).astype(F32)
    projections = [
        late[:, :, part * wide : (part + 1) * wide].transpose(1, 0, 2).reshape(share, width)
        for part in range(3)
    ]
    summed = jnp.sum(late[:, :, 3 * wide :], 0)
    out_share, gain_shares = summed[:, :width], summed[:, width : width + 2]

    pieces = lax.psum_scatter(pieces, "fsdp", scatter_dimension=0, tiled=True)
    pieces = after(pieces, (tokens_grad, projections, out_share, gain_shares))[0].astype(F32)
    down_share = pieces[: lanes * tall].reshape(lanes, tall, strip).transpose(1, 0, 2).reshape(tall, width)
    others = pieces[lanes * tall :].reshape(-1, share, strip).transpose(1, 0, 2).reshape(share, -1)
    return (
        mixed[None],
        tokens_grad[None],
        *projections,
        out_share,
        others[:, :hidden_width],
        others[:, hidden_width:],
        down_share,
        gain_shares[:, 0],
        gain_shares[:, 1],
    )


def solution(mesh):
    span, ring = mesh.shape["dp"], mesh.shape["fsdp"]
    fine = Mesh(mesh.devices.reshape(span // 2, 2, ring), DP + ("fsdp",))
    every = DP + ("fsdp",)
    rows, matrix, vector = P(DP, "fsdp", None), P(every, None), P(every)
    in_specs = (rows,) * 5 + (matrix,) * 7 + (vector,) * 2 + (rows,)
    out_specs = (rows,) * 2 + (matrix,) * 7 + (vector,) * 2
    return jax.shard_map(body, mesh=fine, in_specs=in_specs, out_specs=out_specs, check_vma=False)
```

```python
import functools
import math

import jax
import jax.numpy as jnp
import numpy as np
from jax import lax
from jax.experimental import pallas as pl
from jax.experimental.pallas import tpu as pltpu
from jax.sharding import Mesh
from jax.sharding import PartitionSpec as P

HEAD_DIM = 128
QBLK = 256
MBLK = 128
EPSILON = 1e-06
NEGATIVE = -1e30
SCALE = 1.0 / math.sqrt(HEAD_DIM)
LOG2E = math.log2(math.e)
MIB = 1 << 20
F32 = jnp.float32
BF16 = jnp.bfloat16
DP = ("chip", "core")
NT = (((1,), (1,)), ((), ()))
TN = (((0,), (0,)), ((), ()))


def dot(left, right, dims=(((1,), (0,)), ((), ()))):
    return lax.dot_general(left, right, dims, preferred_element_type=F32)


def rotary_tables(length):
    half_dim = HEAD_DIM // 2
    frequency = 10000.0 ** (-jnp.arange(half_dim, dtype=F32) / half_dim)
    angles = jnp.arange(length, dtype=jnp.int32).astype(F32)[:, None] * frequency[None, :]
    cosine, sine = jnp.cos(angles), jnp.sin(angles)
    return jnp.concatenate([cosine, cosine], 1), jnp.concatenate([-sine, sine], 1)


def qkv_kernel(heads, tok_ref, gain_ref, w_ref, cos_ref, sin_ref, qkv_ref):
    rows = tok_ref[...].astype(F32)
    factor = lax.rsqrt(jnp.mean(rows * rows, -1, keepdims=True) + EPSILON)
    normed = (rows * factor * gain_ref[...]).astype(BF16)
    cosine, sine = cos_ref[...], sin_ref[...]
    wide = heads * HEAD_DIM
    for part in range(3):
        values = dot(normed, w_ref[:, part * wide : (part + 1) * wide])
        for head in range(heads):
            value = values[:, head * HEAD_DIM : (head + 1) * HEAD_DIM]
            if part < 2:
                value = value * cosine + pltpu.roll(value, HEAD_DIM // 2, 1) * sine
            if part == 0:
                value = value * (SCALE * LOG2E)
            at = part * wide + head * HEAD_DIM
            qkv_ref[:, at : at + HEAD_DIM] = value.astype(BF16)


def project_qkv(tokens_all, gain, w_qkv, cosine, sine, heads):
    length, width = tokens_all.shape
    columns = w_qkv.shape[1]
    block = 2 * QBLK
    return pl.pallas_call(
        functools.partial(qkv_kernel, heads),
        grid=(length // block,),
        in_specs=[
            pl.BlockSpec((block, width), lambda i: (i, 0)),
            pl.BlockSpec((1, width), lambda i: (0, 0)),
            pl.BlockSpec((width, columns), lambda i: (0, 0)),
            pl.BlockSpec((block, HEAD_DIM), lambda i: (i, 0)),
            pl.BlockSpec((block, HEAD_DIM), lambda i: (i, 0)),
        ],
        out_specs=pl.BlockSpec((block, columns), lambda i: (i, 0)),
        out_shape=jax.ShapeDtypeStruct((length, columns), BF16),
        compiler_params=pltpu.CompilerParams(vmem_limit_bytes=48 * MIB),
        cost_estimate=pl.CostEstimate(
            flops=2 * length * width * columns, bytes_accessed=4 * length * (width + columns), transcendentals=0
        ),
        name="project_qkv",
    )(tokens_all, gain, w_qkv, cosine, sine)


def memory_bias(counts_ref, base, top, axis):
    shape = (1, top * MBLK) if axis == 1 else (top * MBLK, 1)
    column = lax.broadcasted_iota(jnp.int32, shape, axis)
    limit = jnp.zeros(shape, jnp.int32)
    for entry in range(top):
        inside = (column >= entry * MBLK) & (column < entry * MBLK + counts_ref[base + entry])
        limit = jnp.where(inside, 1, limit)
    return jnp.where(limit > 0, 0.0, NEGATIVE)


def pick_memory(ref, chosen_ref, base, top, columns):
    rows = [
        ref[pl.ds(pl.multiple_of(chosen_ref[base + entry] * MBLK, MBLK), MBLK), columns]
        for entry in range(top)
    ]
    return jnp.concatenate(rows, 0)


def forward_kernel(
    heads, top, chosen_ref, counts_ref, q_ref, k_ref, v_ref, mk_ref, mv_ref, out_ref, lse_ref, acc_s, peak_s
):
    block = pl.program_id(0)
    rows = q_ref.shape[0]
    subs = rows // QBLK
    ones = jnp.ones((rows, HEAD_DIM), BF16)
    mem_ones = jnp.ones((top * MBLK, HEAD_DIM), BF16)
    for sub in range(subs):
        base = (block * subs + sub) * top
        here = slice(sub * QBLK, (sub + 1) * QBLK)
        span = (sub + 1) * QBLK
        seen = pl.ds(pl.multiple_of(block * rows, rows), span)
        row = lax.broadcasted_iota(jnp.int32, (QBLK, span), 0) + sub * QBLK
        causal = row >= lax.broadcasted_iota(jnp.int32, (QBLK, span), 1)
        bias = memory_bias(counts_ref, base, top, 1)
        for head in range(heads):
            columns = slice(head * HEAD_DIM, (head + 1) * HEAD_DIM)
            query = q_ref[here, columns]
            remote = dot(query, pick_memory(mk_ref, chosen_ref, base, top, columns), NT) + bias
            local = jnp.where(causal, dot(query, k_ref[seen, columns], NT), NEGATIVE)
            peak = jnp.maximum(jnp.max(local, -1, keepdims=True), jnp.max(remote, -1, keepdims=True))
            values = jnp.concatenate([v_ref[seen, columns], ones[:span]], 1)
            acc = dot(jnp.exp2(local - peak).astype(BF16), values)
            values = jnp.concatenate([pick_memory(mv_ref, chosen_ref, base, top, columns), mem_ones], 1)
            acc_s[head, here] = acc + dot(jnp.exp2(remote - peak).astype(BF16), values)
            peak_s[head, here] = jnp.broadcast_to(peak, (QBLK, HEAD_DIM))

    def step(index, carry):
        there = pl.ds(pl.multiple_of(index * rows, rows), rows)
        for head in range(heads):
            columns = slice(head * HEAD_DIM, (head + 1) * HEAD_DIM)
            peak = peak_s[head][:, :1]
            scores = dot(q_ref[:, columns], k_ref[there, columns], NT)
            higher = jnp.maximum(peak, jnp.max(scores, -1, keepdims=True))
            weights = jnp.exp2(scores - higher).astype(BF16)
            values = jnp.concatenate([v_ref[there, columns], ones], 1)
            acc_s[head] = acc_s[head] * jnp.exp2(peak - higher) + dot(weights, values)
            peak_s[head] = jnp.broadcast_to(higher, (rows, HEAD_DIM))
        return carry

    lax.fori_loop(0, block, step, 0)
    for head in range(heads):
        columns = slice(head * HEAD_DIM, (head + 1) * HEAD_DIM)
        total = acc_s[head][:, HEAD_DIM:]
        out_ref[:, columns] = (acc_s[head][:, :HEAD_DIM] / total).astype(BF16)
        lse_ref[:, head : head + 1] = peak_s[head][:, :1] + jnp.log2(total[:, :1])


def attend_forward(chosen, counts, qkv, memory, heads, top):
    length = qkv.shape[0]
    wide = heads * HEAD_DIM
    rows = min(2 * QBLK, length)
    mem_rows = memory.shape[0]
    return pl.pallas_call(
        functools.partial(forward_kernel, heads, top),
        grid_spec=pltpu.PrefetchScalarGridSpec(
            num_scalar_prefetch=2,
            grid=(length // rows,),
            in_specs=[
                pl.BlockSpec((rows, wide), lambda i, *_: (i, 0)),
                pl.BlockSpec((length, wide), lambda i, *_: (0, 1)),
                pl.BlockSpec((length, wide), lambda i, *_: (0, 2)),
                pl.BlockSpec((mem_rows, wide), lambda i, *_: (0, 0)),
                pl.BlockSpec((mem_rows, wide), lambda i, *_: (0, 1)),
            ],
            out_specs=[
                pl.BlockSpec((rows, wide), lambda i, *_: (i, 0)),
                pl.BlockSpec((rows, heads), lambda i, *_: (i, 0)),
            ],
            scratch_shapes=[
                pltpu.VMEM((heads, rows, 2 * HEAD_DIM), F32),
                pltpu.VMEM((heads, rows, HEAD_DIM), F32),
            ],
        ),
        out_shape=[
            jax.ShapeDtypeStruct((length, wide), BF16),
            jax.ShapeDtypeStruct((length, heads), F32),
        ],
        compiler_params=pltpu.CompilerParams(vmem_limit_bytes=48 * MIB),
        cost_estimate=pl.CostEstimate(
            flops=4 * heads * length * HEAD_DIM * (length // 2 + top * MBLK),
            bytes_accessed=8 * length * wide,
            transcendentals=heads * length * (length // 2 + top * MBLK),
        ),
        name="attend_forward",
    )(chosen, counts, qkv, qkv, qkv, memory, memory)


def spread_rows(column):
    rows = column.shape[0]
    return jnp.transpose(jnp.broadcast_to(column, (rows, HEAD_DIM)))[:1]


def row_stats(grad_out, out, lse):
    delta = jnp.sum(grad_out.astype(F32) * out.astype(F32), -1, keepdims=True)
    return jnp.concatenate([spread_rows(lse), spread_rows(delta)], 0)


def score_grads(query, grad_out, stats, keys, values, mask):
    weights = jnp.exp2(mask(dot(keys, query, NT)) - stats[:1])
    grad_weights = dot(values, grad_out, NT)
    return weights.astype(BF16), (weights * (grad_weights - stats[1:2])).astype(BF16)


def causal_mask(rows):
    key_at = lax.broadcasted_iota(jnp.int32, (rows, rows), 0)
    query_at = lax.broadcasted_iota(jnp.int32, (rows, rows), 1)
    return lambda scores: jnp.where(query_at >= key_at, scores, NEGATIVE)


def memory_query_grad(chosen_ref, counts_ref, base, top, query, grad_out, stats, mk_ref, mv_ref, columns):
    keys = pick_memory(mk_ref, chosen_ref, base, top, columns)
    values = pick_memory(mv_ref, chosen_ref, base, top, columns)
    bias = memory_bias(counts_ref, base, top, 0)
    _, grad_scores = score_grads(query, grad_out, stats, keys, values, lambda scores: scores + bias)
    return dot(grad_scores, keys, TN)


def block_grads(heads, grad_query, grad_key, grad_value, cosine, sine):
    def unturn(value):
        return (value * cosine - pltpu.roll(value, HEAD_DIM // 2, 1) * sine).astype(BF16)

    parts = []
    for part, array in enumerate((grad_query * SCALE, grad_key * (1.0 / LOG2E), grad_value)):
        for head in range(heads):
            value = array[:, head * HEAD_DIM : (head + 1) * HEAD_DIM]
            parts.append(unturn(value) if part < 2 else value.astype(BF16))
    return jnp.concatenate(parts, 1)


def first_block_kernel(
    heads, top, chosen_ref, counts_ref, plan_ref, qkv_ref, mk_ref, mv_ref, go_ref, out_ref, lse_ref, cos_ref, sin_ref,
    w_ref, partial_ref, whole_ref, grad_ref, gq_ref, gk_ref, gv_ref, stats_s,
):
    rows = partial_ref.shape[0]
    subs = rows // QBLK
    wide = heads * HEAD_DIM
    others = go_ref.shape[0] // rows - 1
    block, is_last = plan_ref[0], plan_ref[1]
    own = pl.ds(pl.multiple_of(block * rows, rows), rows)
    gq_ref[...] = jnp.zeros_like(gq_ref)
    gk_ref[...] = jnp.zeros_like(gk_ref)
    gv_ref[...] = jnp.zeros_like(gv_ref)

    def note_stats(slot, here):
        for head in range(heads):
            columns = slice(head * HEAD_DIM, (head + 1) * HEAD_DIM)
            stats_s[slot, head] = row_stats(go_ref[here, columns], out_ref[here, columns], lse_ref[here, head : head + 1])

    note_stats(0, own)

    def pair(slot, queries, keys, mask):
        for head in range(heads):
            at = head * HEAD_DIM
            columns = slice(at, at + HEAD_DIM)
            query, grad_out = qkv_ref[queries, columns], go_ref[queries, columns]
            key = qkv_ref[keys, wide + at : wide + at + HEAD_DIM]
            value = qkv_ref[keys, 2 * wide + at : 2 * wide + at + HEAD_DIM]
            weights, grad_scores = score_grads(query, grad_out, stats_s[slot, head], key, value, mask)
            gk_ref[keys, columns] += dot(grad_scores, query)
            gv_ref[keys, columns] += dot(weights, grad_out)
            gq_ref[queries, columns] += dot(grad_scores, key, TN)

    for head in range(heads):
        columns = slice(head * HEAD_DIM, (head + 1) * HEAD_DIM)
        for sub in range(subs):
            here = pl.ds(pl.multiple_of(block * rows + sub * QBLK, QBLK), QBLK)
            gq_ref[here, columns] += memory_query_grad(
                chosen_ref, counts_ref, (block * subs + sub) * top, top, qkv_ref[here, columns], go_ref[here, columns],
                stats_s[0, head][:, sub * QBLK : (sub + 1) * QBLK], mk_ref, mv_ref, columns,
            )
    pair(0, own, own, causal_mask(rows))

    def step(index, carry):
        other = jnp.where(is_last == 1, index, index + 1)
        there = pl.ds(pl.multiple_of(other * rows, rows), rows)

        @pl.when(is_last == 1)
        def _():
            pair(0, own, there, lambda scores: scores)

        @pl.when(is_last == 0)
        def _():
            note_stats(1, there)
            pair(1, there, own, lambda scores: scores)

        return carry

    lax.fori_loop(0, others, step, 0)
    grad = block_grads(
        heads, gq_ref[own, :], gk_ref[own, :], gv_ref[own, :], cos_ref[...], sin_ref[...]
    )
    grad_ref[...] = grad
    partial = dot(grad, w_ref[...], NT).astype(BF16)
    partial_ref[...] = partial
    whole_ref[...] = partial


def first_block(plan, chosen, counts, qkv, memory, grad_out, out, lse, cosine, sine, w_qkv, heads, top):
    length = qkv.shape[0]
    width = w_qkv.shape[0]
    wide = heads * HEAD_DIM
    rows = min(2 * QBLK, length)
    mem_rows = memory.shape[0]

    def whole(array):
        return pl.BlockSpec(array.shape, lambda i, *_: (0, 0))

    sums = pl.BlockSpec((length, wide), lambda i, *_: (0, 0))
    return pl.pallas_call(
        functools.partial(first_block_kernel, heads, top),
        grid_spec=pltpu.PrefetchScalarGridSpec(
            num_scalar_prefetch=3,
            grid=(1,),
            in_specs=[
                whole(qkv),
                pl.BlockSpec((mem_rows, wide), lambda i, *_: (0, 0)),
                pl.BlockSpec((mem_rows, wide), lambda i, *_: (0, 1)),
                whole(grad_out),
                whole(out),
                whole(lse),
                pl.BlockSpec((rows, HEAD_DIM), lambda i, c, n, plan: (plan[0], 0)),
                pl.BlockSpec((rows, HEAD_DIM), lambda i, c, n, plan: (plan[0], 0)),
                whole(w_qkv),
            ],
            out_specs=[
                pl.BlockSpec((rows, width), lambda i, *_: (0, 0)),
                pl.BlockSpec((rows, width), lambda i, c, n, plan: (plan[0], 0)),
                pl.BlockSpec((rows, 3 * wide), lambda i, *_: (0, 0)),
                sums,
                sums,
                sums,
            ],
            scratch_shapes=[pltpu.VMEM((2, heads, 2, rows), F32)],
        ),
        out_shape=[
            jax.ShapeDtypeStruct((rows, width), BF16),
            jax.ShapeDtypeStruct((length, width), BF16),
            jax.ShapeDtypeStruct((rows, 3 * wide), BF16),
            *[jax.ShapeDtypeStruct((length, wide), F32)] * 3,
        ],
        compiler_params=pltpu.CompilerParams(vmem_limit_bytes=60 * MIB),
        cost_estimate=pl.CostEstimate(
            flops=4 * heads * length * HEAD_DIM * length,
            bytes_accessed=40 * length * wide,
            transcendentals=heads * length * rows,
        ),
        name="first_block",
    )(chosen, counts, plan, qkv, memory, memory, grad_out, out, lse, cosine, sine, w_qkv)


def other_blocks_kernel(
    heads, top, chosen_ref, counts_ref, plan_ref, q_ref, k_ref, v_ref, mk_ref, mv_ref, go_ref, out_ref, lse_ref,
    cos_ref, sin_ref, w_ref, gq_in, gk_in, gv_in, _, partial_ref, grad_ref, gk_s, gv_s, gq_s,
):
    low = plan_ref[0]
    block = low + pl.num_programs(0) - 1 - pl.program_id(0)
    rows = q_ref.shape[0]
    subs = rows // QBLK
    own = pl.ds(pl.multiple_of(block * rows, rows), rows)

    @pl.when(pl.program_id(0) == 0)
    def _():
        gk_s[...] = gk_in[...]
        gv_s[...] = gv_in[...]

    stats = []
    for head in range(heads):
        columns = slice(head * HEAD_DIM, (head + 1) * HEAD_DIM)
        stats.append(row_stats(go_ref[:, columns], out_ref[:, columns], lse_ref[:, head : head + 1]))
        for sub in range(subs):
            here = slice(sub * QBLK, (sub + 1) * QBLK)
            gq_s[here, columns] = gq_in[here, columns] + memory_query_grad(
                chosen_ref, counts_ref, (block * subs + sub) * top, top, q_ref[here, columns], go_ref[here, columns],
                stats[head][:, here], mk_ref, mv_ref, columns,
            )

    def local(there, mask):
        for head in range(heads):
            columns = slice(head * HEAD_DIM, (head + 1) * HEAD_DIM)
            query, grad_out = q_ref[:, columns], go_ref[:, columns]
            key = k_ref[there, columns]
            weights, grad_scores = score_grads(query, grad_out, stats[head], key, v_ref[there, columns], mask)
            gk_s[there, columns] += dot(grad_scores, query)
            gv_s[there, columns] += dot(weights, grad_out)
            gq_s[:, columns] += dot(grad_scores, key, TN)

    local(own, causal_mask(rows))

    def step(index, carry):
        local(pl.ds(pl.multiple_of(index * rows, rows), rows), lambda scores: scores)
        return carry

    lax.fori_loop(low, block, step, 0)
    grad = block_grads(heads, gq_s[...], gk_s[own, :], gv_s[own, :], cos_ref[...], sin_ref[...])
    grad_ref[...] = grad
    partial_ref[...] = dot(grad, w_ref[...], NT).astype(BF16)


def other_blocks(plan, chosen, counts, qkv, memory, grad_out, out, lse, cosine, sine, w_qkv, sums, partials, heads, top):
    length = qkv.shape[0]
    width = w_qkv.shape[0]
    wide = heads * HEAD_DIM
    rows = min(2 * QBLK, length)
    count = length // rows - 1
    mem_rows = memory.shape[0]

    def by_rows(columns, at=0):
        return pl.BlockSpec((rows, columns), lambda i, c, n, plan: (plan[0] + count - 1 - i, at))

    def result(columns):
        return pl.BlockSpec((rows, columns), lambda i, *_: (count - 1 - i, 0))

    return pl.pallas_call(
        functools.partial(other_blocks_kernel, heads, top),
        grid_spec=pltpu.PrefetchScalarGridSpec(
            num_scalar_prefetch=3,
            grid=(count,),
            in_specs=[
                by_rows(wide),
                pl.BlockSpec((length, wide), lambda i, *_: (0, 1)),
                pl.BlockSpec((length, wide), lambda i, *_: (0, 2)),
                pl.BlockSpec((mem_rows, wide), lambda i, *_: (0, 0)),
                pl.BlockSpec((mem_rows, wide), lambda i, *_: (0, 1)),
                by_rows(wide),
                by_rows(wide),
                by_rows(heads),
                by_rows(HEAD_DIM),
                by_rows(HEAD_DIM),
                pl.BlockSpec((width, 3 * wide), lambda i, *_: (0, 0)),
                by_rows(wide),
                pl.BlockSpec((length, wide), lambda i, *_: (0, 0)),
                pl.BlockSpec((length, wide), lambda i, *_: (0, 0)),
                pl.BlockSpec(memory_space=pl.ANY),
            ],
            out_specs=[by_rows(width), result(3 * wide)],
            scratch_shapes=[
                pltpu.VMEM((length, wide), F32),
                pltpu.VMEM((length, wide), F32),
                pltpu.VMEM((rows, wide), F32),
            ],
        ),
        out_shape=[
            jax.ShapeDtypeStruct((length, width), BF16),
            jax.ShapeDtypeStruct((count * rows, 3 * wide), BF16),
        ],
        input_output_aliases={17: 0},
        compiler_params=pltpu.CompilerParams(vmem_limit_bytes=60 * MIB),
        cost_estimate=pl.CostEstimate(
            flops=6 * heads * length * HEAD_DIM * (length + top * MBLK),
            bytes_accessed=40 * length * wide,
            transcendentals=heads * length * (length // 3 + top * MBLK),
        ),
        name="other_blocks",
    )(chosen, counts, plan, qkv, qkv, qkv, memory, memory, grad_out, out, lse, cosine, sine, w_qkv, *sums, partials)


def ffn_kernel(
    span, merged, tok_ref, att_ref, cot_ref, gain_ref, out_w, gate_w, up_w, down_w,
    mixed_ref, grad_mid_ref, grad_att_ref, gain_grad_ref, out_grads_ref, grads_ref, *rest,
):
    if not merged:
        down_grads_ref, rest = rest[0], rest[1:]
    middle_s, normed_s, turned_s, mixed_s, upstream_s, gate_s, up_s, down_s, out_s, sems, late_sems = rest
    step, steps = pl.program_id(0), pl.num_programs(0)
    width = tok_ref.shape[1]
    share = width // span
    wide = gate_w.shape[1]
    hidden_width = down_s.shape[0]
    tall = hidden_width // span
    lanes = width // wide
    first = tall * lanes if merged else 0
    slot = step % 2

    @pl.when(step == 0)
    def _():
        middle = tok_ref[...].astype(F32) + dot(att_ref[...], out_w[...])
        middle_s[...] = middle
        factor = lax.rsqrt(jnp.mean(middle * middle, -1, keepdims=True) + EPSILON)
        normed = (middle * factor * gain_ref[...]).astype(BF16)
        normed_s[...] = normed
        turned_s[...] = jnp.transpose(normed)
        mixed_s[...] = middle
        upstream_s[...] = jnp.zeros_like(upstream_s)

    def copy_out(kind, which, index):
        source = (gate_s, up_s)[kind].at[which]
        start = first + (kind * steps + index) * share
        target = grads_ref.at[:, pl.ds(start, share), :]
        return pltpu.make_async_copy(source, target, sems.at[kind, which])

    normed = normed_s[...]
    upstream = cot_ref[...]
    both = jnp.concatenate([gate_w[...], up_w[...]], 1)
    acts = dot(normed, both)
    gate_act, up_act = acts[:, :wide], acts[:, wide:]
    grad_hidden = dot(upstream, down_w[...], NT)
    sigmoid = jax.nn.sigmoid(gate_act)
    silu = gate_act * sigmoid
    hidden = (silu * up_act).astype(BF16)
    grad_gate = (grad_hidden * up_act * sigmoid * (1.0 + gate_act * (1.0 - sigmoid))).astype(BF16)
    grad_up = (grad_hidden * silu).astype(BF16)
    mixed_s[...] += dot(hidden, down_w[...])
    grad_acts = jnp.concatenate([grad_gate, grad_up], 1)
    upstream_s[...] += dot(grad_acts, both, NT)
    down_s[pl.ds(pl.multiple_of(step * wide, wide), wide), :] = dot(hidden, upstream, TN).astype(BF16)

    @pl.when(step >= 2)
    def _():
        copy_out(0, slot, step - 2).wait()
        copy_out(1, slot, step - 2).wait()

    weight_grads = dot(turned_s[...], grad_acts).astype(BF16)
    gate_s[slot] = weight_grads[:, :wide].reshape(span, share, wide)
    up_s[slot] = weight_grads[:, wide:].reshape(span, share, wide)
    copy_out(0, slot, step).start()
    copy_out(1, slot, step).start()

    @pl.when(step == steps - 1)
    def _():
        copies = []
        if merged:
            for place in range(span):
                for lane in range(lanes):
                    copies.append(
                        pltpu.make_async_copy(
                            down_s.at[pl.ds(place * tall, tall), pl.ds(lane * wide, wide)],
                            grads_ref.at[place, pl.ds(lane * tall, tall), :],
                            late_sems.at[len(copies)],
                        )
                    )
        else:
            copies.append(pltpu.make_async_copy(down_s, down_grads_ref, late_sems.at[0]))
        for copy in copies:
            copy.start()
        mixed_ref[...] = mixed_s[...].astype(BF16)
        middle = middle_s[...]
        grad = upstream_s[...]
        factor = lax.rsqrt(jnp.mean(middle * middle, -1, keepdims=True) + EPSILON)
        gain_grad_ref[...] = jnp.sum(grad * middle * factor, 0, keepdims=True)
        scaled = grad * gain_ref[...]
        inner = jnp.mean(scaled * middle, -1, keepdims=True)
        grad_middle = cot_ref[...].astype(F32) + factor * scaled - middle * (factor * factor * factor * inner)
        grad_mid_ref[...] = grad_middle
        branch = grad_middle.astype(BF16)
        grad_att_ref[...] = dot(branch, out_w[...], NT).astype(BF16)
        turned_att = jnp.transpose(att_ref[...])
        for lane in range(lanes):
            columns = slice(lane * wide, (lane + 1) * wide)
            out_s[lane] = dot(turned_att, branch[:, columns]).astype(BF16).reshape(span, share, wide)
            more = pltpu.make_async_copy(
                out_s.at[lane],
                out_grads_ref.at[:, :, pl.ds(lane * wide, wide)],
                late_sems.at[len(copies)],
            )
            more.start()
            copies.append(more)
        for copy in copies:
            copy.wait()
        copy_out(0, 1 - slot, step - 1).wait()
        copy_out(1, 1 - slot, step - 1).wait()
        copy_out(0, slot, step).wait()
        copy_out(1, slot, step).wait()


def feed_forward(tokens, attended, upstream, gain, weights, w_down, span):
    rows, width = tokens.shape
    hidden_width = w_down.shape[0]
    wide = 2 * HEAD_DIM
    steps = hidden_width // wide
    lanes = width // wide
    share = width // span
    tall = hidden_width // span
    merged = tall % 16 == 0
    total = 2 * steps * share + (lanes * tall if merged else 0)
    shapes = [
        jax.ShapeDtypeStruct((rows, width), BF16),
        jax.ShapeDtypeStruct((rows, width), F32),
        jax.ShapeDtypeStruct((rows, width), BF16),
        jax.ShapeDtypeStruct((1, width), F32),
        jax.ShapeDtypeStruct((span, share, width), BF16),
        jax.ShapeDtypeStruct((span, total, wide), BF16),
    ]
    specs = [
        pl.BlockSpec((rows, width), lambda i: (0, 0)),
        pl.BlockSpec((rows, width), lambda i: (0, 0)),
        pl.BlockSpec((rows, width), lambda i: (0, 0)),
        pl.BlockSpec((1, width), lambda i: (0, 0)),
        pl.BlockSpec(memory_space=pl.ANY),
        pl.BlockSpec(memory_space=pl.ANY),
    ]
    if not merged:
        shapes.append(jax.ShapeDtypeStruct((hidden_width, width), BF16))
        specs.append(pl.BlockSpec(memory_space=pl.ANY))
    return pl.pallas_call(
        functools.partial(ffn_kernel, span, merged),
        grid=(steps,),
        in_specs=[
            pl.BlockSpec((rows, width), lambda i: (0, 0)),
            pl.BlockSpec((rows, width), lambda i: (0, 0)),
            pl.BlockSpec((rows, width), lambda i: (0, 0)),
            pl.BlockSpec((1, width), lambda i: (0, 0)),
            pl.BlockSpec((width, width), lambda i: (0, 0)),
            pl.BlockSpec((width, wide), lambda i: (0, lanes + i)),
            pl.BlockSpec((width, wide), lambda i: (0, lanes + steps + i)),
            pl.BlockSpec((wide, width), lambda i: (i, 0)),
        ],
        out_specs=specs,
        out_shape=shapes,
        scratch_shapes=[
            pltpu.VMEM((rows, width), F32),
            pltpu.VMEM((rows, width), BF16),
            pltpu.VMEM((width, rows), BF16),
            pltpu.VMEM((rows, width), F32),
            pltpu.VMEM((rows, width), F32),
            pltpu.VMEM((2, span, share, wide), BF16),
            pltpu.VMEM((2, span, share, wide), BF16),
            pltpu.VMEM((hidden_width, width), BF16),
            pltpu.VMEM((lanes, span, share, wide), BF16),
            pltpu.SemaphoreType.DMA((2, 2)),
            pltpu.SemaphoreType.DMA(((span * lanes if merged else 1) + lanes,)),
        ],
        compiler_params=pltpu.CompilerParams(vmem_limit_bytes=56 * MIB),
        cost_estimate=pl.CostEstimate(
            flops=6 * rows * width * (3 * hidden_width + width),
            bytes_accessed=4 * width * (3 * hidden_width + width),
            transcendentals=rows * hidden_width,
        ),
        name="feed_forward",
    )(tokens, attended, upstream, gain, weights, weights, weights, w_down)


def projection_grads_kernel(
    order_ref, tok_ref, gain_ref, w_ref, first_ref, other_ref, grad_w_ref, gain_grad_ref, raw_s
):
    step = pl.program_id(0)

    @pl.when(step == 0)
    def _():
        raw_s[...] = jnp.zeros_like(raw_s)

    tokens = tok_ref[...].astype(F32)
    tokens = tokens * lax.rsqrt(jnp.mean(tokens * tokens, -1, keepdims=True) + EPSILON)
    grad = jnp.where(step == 0, first_ref[...], other_ref[...])
    raw_s[...] += dot(tokens.astype(BF16), grad, TN)

    @pl.when(step == pl.num_programs(0) - 1)
    def _():
        raw = raw_s[...]
        gain_grad_ref[...] = jnp.sum(raw * w_ref[...].astype(F32), -1, keepdims=True)
        grad_w_ref[...] = (raw * gain_ref[...]).astype(BF16)


def projection_grads(order, tokens_all, gain_column, w_qkv, first_grad, other_grad):
    length, width = tokens_all.shape
    columns = first_grad.shape[1]
    rows = min(2 * QBLK, length)
    return pl.pallas_call(
        projection_grads_kernel,
        grid_spec=pltpu.PrefetchScalarGridSpec(
            num_scalar_prefetch=1,
            grid=(length // rows,),
            in_specs=[
                pl.BlockSpec((rows, width), lambda i, order: (order[i], 0)),
                pl.BlockSpec((width, 1), lambda i, _: (0, 0)),
                pl.BlockSpec((width, columns), lambda i, _: (0, 0)),
                pl.BlockSpec((rows, columns), lambda i, _: (0, 0)),
                pl.BlockSpec((rows, columns), lambda i, _: (jnp.maximum(i - 1, 0), 0)),
            ],
            out_specs=[
                pl.BlockSpec((width, columns), lambda i, _: (0, 0)),
                pl.BlockSpec((width, 1), lambda i, _: (0, 0)),
            ],
            scratch_shapes=[pltpu.VMEM((width, columns), F32)],
        ),
        out_shape=[
            jax.ShapeDtypeStruct((width, columns), BF16),
            jax.ShapeDtypeStruct((width, 1), F32),
        ],
        compiler_params=pltpu.CompilerParams(vmem_limit_bytes=48 * MIB),
        cost_estimate=pl.CostEstimate(
            flops=2 * length * width * columns, bytes_accessed=2 * length * (width + columns), transcendentals=0
        ),
        name="projection_grads",
    )(order, tokens_all, gain_column, w_qkv, first_grad, other_grad)


def after(value, earlier):
    return lax.optimization_barrier((value, earlier))[0]


def chain_gather(blocks, axis):
    size = lax.axis_size(axis)
    place = lax.axis_index(axis)
    steps = []
    rising = falling = tuple(blocks)
    for step in range(size - 1):
        up = [(i, i + 1) for i in range(step, size - 1)]
        down = [(i + 1, i) for i in range(size - 1 - step)]
        rising = tuple(lax.ppermute(block, axis, up) for block in rising)
        falling = tuple(lax.ppermute(block, axis, down) for block in falling)
        if len(blocks) > 1:
            rising, falling = lax.optimization_barrier((rising, falling))
        steps.append((rising, falling))
    results = []
    for number, block in enumerate(blocks):
        ordered = []
        for index in range(size):
            cases = []
            for mine in range(size):
                if mine == index:
                    cases.append(block)
                elif mine > index:
                    cases.append(steps[mine - index - 1][0][number])
                else:
                    cases.append(steps[index - mine - 1][1][number])
            ordered.append(lax.select_n(place, *cases) if size > 2 else lax.select_n(place > 0, *cases))
        results.append(ordered)
    return results, steps


def chain_scatter(block, axis, waits):
    size = lax.axis_size(axis)
    place = lax.axis_index(axis)
    arrived = []
    for step in range(size - 1):
        up, down = block(step, size - 1 - step + place), block(step, step - size + 1 + place)
        if step:
            up, down = up + arrived[-1][0].astype(F32), down + arrived[-1][1].astype(F32)
        ready = waits[step - 1](sent) if 0 < step <= len(waits) else None
        up, down, _ = lax.optimization_barrier((up.astype(BF16), down.astype(BF16), ready))
        sent = up, down
        rising = lax.ppermute(up, axis, [(i, i + 1) for i in range(step + 1)])
        falling = lax.ppermute(down, axis, [(i, i - 1) for i in range(size - 1 - step, size)])
        arrived.append(lax.optimization_barrier((rising, falling)))
    return block(size, place), arrived


def direct_exchange(blocks, axis):
    size = lax.axis_size(axis)
    place = lax.axis_index(axis)
    taken = [lax.dynamic_index_in_dim(blocks, place, 0, keepdims=False)]
    for far in range(1, size):
        give = lax.dynamic_index_in_dim(blocks, (place + far) % size, 0, keepdims=False)
        taken.append(lax.ppermute(give, axis, [(i, (i + far) % size) for i in range(size)]))
    return taken


def body(
    tokens, memory_keys, memory_values, chosen, counts, w_query, w_key, w_value, w_out, w_gate, w_up, w_down,
    gain_attn, gain_ffn, cotangent,
):
    ring, span = lax.axis_size("fsdp"), lax.axis_size(DP)
    rows, width = tokens.shape[1:]
    heads = width // HEAD_DIM // ring
    wide = heads * HEAD_DIM
    length = rows * ring
    top = chosen.shape[2]
    hidden_width = w_gate.shape[1]
    share = w_query.shape[0]
    mine = tokens[0]

    extra = 8 if share % 8 == 0 else 8 - share % 8
    parts = [w.reshape(share, ring, wide).transpose(1, 0, 2) for w in (w_query, w_key, w_value)]
    choices = jnp.concatenate([chosen[0].reshape(-1), counts[0].reshape(-1)]).astype(BF16)
    notes = jnp.stack(
        [
            jnp.pad(row, (0, 3 * wide - row.shape[0]))
            for row in (jnp.concatenate([gain_attn, gain_ffn]), choices)
        ]
    )
    notes = jnp.broadcast_to(jnp.pad(notes, ((0, extra - 2), (0, 0))), (ring, extra, 3 * wide))
    parcel = jnp.concatenate([jnp.concatenate(parts, 2), notes], 1)
    parcel = lax.all_to_all(parcel, "fsdp", 0, 0, tiled=True)
    picks = parcel[:, share + 1, : choices.shape[0]].astype(jnp.int32).reshape(ring, 2, -1)
    chosen_all, counts_all = picks[:, 0].reshape(-1), picks[:, 1].reshape(-1)
    shards = jnp.concatenate([w_out, w_gate, w_up], 1)
    (near, near_down), steps = chain_gather((shards, w_down), "fsdp")
    (gathered,), token_steps = chain_gather((after(mine, steps[-2]),), "fsdp")
    parcel = lax.all_gather(after(parcel, steps[0]), DP, axis=0, tiled=True)
    w_qkv = parcel[:, :share].reshape(width, 3 * wide)
    gain_one = parcel[:, share, :share].reshape(1, width).astype(F32)
    gain_two = parcel[:, share, share : 2 * share].reshape(1, width).astype(F32)
    first = lax.all_gather(jnp.concatenate(near, 0), DP, axis=0, tiled=True)
    gathered = jnp.concatenate(gathered, 0)

    memory = jnp.concatenate(
        [m[0].reshape(-1, ring, wide).transpose(1, 0, 2) for m in (memory_keys, memory_values)], 2
    )
    memory = lax.all_to_all(after(memory, token_steps[-2]), "fsdp", 0, 0, tiled=True).reshape(-1, 2 * wide)
    down_full = lax.all_gather(jnp.concatenate(near_down, 0), DP, axis=0, tiled=True)

    cosine, sine = rotary_tables(length)
    qkv = project_qkv(gathered, gain_one, w_qkv, cosine, sine, heads)
    attended_heads, lse = attend_forward(chosen_all, counts_all, qkv, memory, heads, top)
    attended = lax.all_to_all(attended_heads, "fsdp", 0, 1, tiled=True)

    upstream = cotangent[0]
    mixed, grad_middle, grad_attended, gain_two_grad, out_grads, grads, *grad_down = feed_forward(
        mine, attended, upstream, gain_two, first, down_full, span
    )
    grad_heads = lax.all_to_all(grad_attended, "fsdp", 1, 0, tiled=True)
    grads = lax.psum_scatter(grads, DP, scatter_dimension=0, tiled=True)[0]

    core = lax.axis_index("core")

    def over_cores(array):
        array = array.reshape((-1, 2) + array.shape[1:])
        taken = lax.ppermute(lax.dynamic_index_in_dim(array, 1 - core, 1, keepdims=False), "core", [(0, 1), (1, 0)])
        return (lax.dynamic_index_in_dim(array, core, 1, keepdims=False).astype(F32) + taken.astype(F32)).astype(BF16)

    def over_chips(array):
        return sum(piece.astype(F32) for piece in direct_exchange(array, "chip")).astype(BF16)

    out_grads = over_chips(out_grads.reshape((span // 2, 2) + out_grads.shape[1:]))

    place = lax.axis_index("fsdp").astype(jnp.int32)
    count = length // min(2 * QBLK, length)
    is_last = (place < ring // 2).astype(jnp.int32)
    first_number = jnp.where(is_last == 1, count - 1, 0).astype(jnp.int32)
    low = 1 - is_last
    first_partial, partials, first_grad, *sums = first_block(
        jnp.stack([first_number, is_last]), chosen_all, counts_all, qkv, memory, grad_heads, attended_heads, lse,
        cosine, sine, w_qkv, heads, top,
    )
    partials, other_grad = other_blocks(
        low.reshape(1), chosen_all, counts_all, qkv, memory, grad_heads, attended_heads, lse, cosine, sine, w_qkv,
        sums, partials, heads, top,
    )
    order = jnp.concatenate([first_number.reshape(1), low + jnp.arange(count - 1, dtype=jnp.int32)])
    block_rows = first_partial.shape[0]

    def term(step, index):
        start = jnp.clip(index, 0, ring - 1) * rows
        if step == 0:
            near = jnp.clip(start - first_number * block_rows, 0, block_rows - rows)
            return lax.dynamic_slice_in_dim(first_partial, near, rows, 0).astype(F32)
        return lax.dynamic_slice_in_dim(partials, start, rows, 0).astype(F32)

    kept = []

    def make_projection_grads(sent):
        kept.extend(
            projection_grads(
                order, gathered, gain_one.reshape(width, 1), w_qkv, after(first_grad, sent), after(other_grad, sent)
            )
        )
        return kept

    own_term, arrived = chain_scatter(term, "fsdp", [lambda sent: out_grads, make_projection_grads])
    grad_w_qkv, gain_one_grad = kept
    grads = after(grads, arrived[-1])

    strip = grads.shape[1]
    lanes = width // strip
    tall = w_down.shape[0]
    if grad_down:
        down = lax.psum_scatter(grad_down[0], DP, scatter_dimension=0, tiled=True)
        down = down.reshape(ring, tall, lanes, strip).transpose(0, 2, 1, 3)
    else:
        down = grads[: ring * tall * lanes].reshape(lanes, ring, tall, strip).transpose(1, 0, 2, 3)
        grads = grads[ring * tall * lanes :]
    grads = grads.reshape(-1, ring, share, strip).transpose(1, 0, 2, 3)
    pieces = jnp.concatenate([down.reshape(ring, -1, strip), grads.reshape(ring, -1, strip)], 1)

    gains = jnp.stack([gain_one_grad.reshape(span, -1), gain_two_grad.reshape(span, -1)], 1)
    gains = jnp.pad(gains.astype(BF16), ((0, 0), (0, extra - 2), (0, 3 * wide - gains.shape[2])))
    late = jnp.concatenate([grad_w_qkv.reshape(span, -1, 3 * wide), gains], 1)
    late = over_chips(over_cores(after(late, pieces)))
    out_grads = over_cores(after(out_grads, pieces))[0]

    rising, falling = arrived[-1]
    grad_normed = own_term + rising.astype(F32) + falling.astype(F32)
    own = mine.astype(F32)
    factor = lax.rsqrt(jnp.mean(own * own, -1, keepdims=True) + EPSILON)
    scaled = grad_normed * gain_one
    inner = jnp.mean(scaled * own, -1, keepdims=True)
    tokens_grad = (grad_middle + factor * scaled - own * (factor * factor * factor * inner)).astype(BF16)

    gains = late[-extra : 2 - extra, : ring * share].reshape(2, ring, share).transpose(1, 2, 0)
    gains = jnp.pad(gains, ((0, 0), (0, 0), (0, HEAD_DIM - 2)))
    late = late[:-extra].reshape(ring, share, 3 * wide)
    late = jnp.concatenate([late, out_grads.reshape(ring, share, width), gains], 2)
    late = after(lax.all_to_all(late, "fsdp", 0, 0, tiled=True), tokens_grad).astype(F32)
    projections = [
        late[:, :, part * wide : (part + 1) * wide].transpose(1, 0, 2).reshape(share, width)
        for part in range(3)
    ]
    summed = jnp.sum(late[:, :, 3 * wide :], 0)
    out_share, gain_shares = summed[:, :width], summed[:, width : width + 2]

    pieces = lax.psum_scatter(pieces, "fsdp", scatter_dimension=0, tiled=True)
    pieces = after(pieces, (tokens_grad, projections, out_share, gain_shares))[0].astype(F32)
    down_share = pieces[: lanes * tall].reshape(lanes, tall, strip).transpose(1, 0, 2).reshape(tall, width)
    others = pieces[lanes * tall :].reshape(-1, share, strip).transpose(1, 0, 2).reshape(share, -1)
    return (
        mixed[None],
        tokens_grad[None],
        *projections,
        out_share,
        others[:, :hidden_width],
        others[:, hidden_width:],
        down_share,
        gain_shares[:, 0],
        gain_shares[:, 1],
    )


def solution(mesh):
    span, ring = mesh.shape["dp"], mesh.shape["fsdp"]
    fine = Mesh(mesh.devices.reshape(span // 2, 2, ring), DP + ("fsdp",))
    every = DP + ("fsdp",)
    rows, matrix, vector = P(DP, "fsdp", None), P(every, None), P(every)
    in_specs = (rows,) * 5 + (matrix,) * 7 + (vector,) * 2 + (rows,)
    out_specs = (rows,) * 2 + (matrix,) * 7 + (vector,) * 2
    return jax.shard_map(body, mesh=fine, in_specs=in_specs, out_specs=out_specs, check_vma=False)
```
